32 devices in a mesh: shard: 2 (over core), ctx: 4 (over y, x), tp: 4 (over z).
Axes of the slice: x: 2, y: 2, z: 4, core: 2. Of those that a mesh axis runs over, the one named last changes fastest.
Arguments:
- hidden_in: bfloat16 [4, 1024, 2048], P('shard', 'ctx'), may hold values from -6 to 6
- lengths: int32 [4], P('shard'), may hold values from 256 to 1024, as said below
- cotangent: bfloat16 [4, 1024, 2048], P('shard', 'ctx'), may hold values from -6 to 6
- norm_gain: bfloat16 [2048], P('shard'), may hold values from 0.5 to 1.5
- in_weight: bfloat16 [2048, 2, 4096], P('shard', None, 'tp'), may hold values from -0.125 to 0.125
- conv_weight: bfloat16 [4, 4096], P(None, ('tp', 'shard')), may hold values from -3 to 3
- conv_bias: bfloat16 [4096], P(('tp', 'shard')), may hold values from -3 to 3
- low_weight: bfloat16 [160, 4096], P(None, ('tp', 'shard')), may hold values from -0.09375 to 0.09375
- step_weight: bfloat16 [128, 4096], P(None, ('tp', 'shard')), may hold values from -0.5 to 0.5
- step_bias: bfloat16 [4096], P(('tp', 'shard')), may hold values from -10 to -2
- decay_log: bfloat16 [16, 4096], P(None, ('tp', 'shard')), may hold values from -2 to 2
- skip_gain: bfloat16 [4096], P(('tp', 'shard')), may hold values from 0.25 to 1.75
- out_weight: bfloat16 [4096, 2048], P('tp', 'shard'), may hold values from -0.1875 to 0.1875
- ffn_gain: bfloat16 [2048], P('shard'), may hold values from 0.5 to 1.5
- gate_up: bfloat16 [2048, 2, 4096], P('shard', None, 'tp'), may hold values from -0.125 to 0.125
- down_weight: bfloat16 [4096, 2048], P('tp', 'shard'), may hold values from -0.09375 to 0.09375
Outputs:
- mixed_out: bfloat16 [4, 1024, 2048], P('shard', 'ctx')
- input_grad: float32 [4, 1024, 2048], P('shard', 'ctx')
- norm_gain_grad: float32 [2048], P(('shard', 'ctx'))
- in_weight_grad: float32 [2048, 2, 4096], P(('shard', 'ctx'), None, 'tp')
- conv_weight_grad: float32 [4, 4096], P(None, ('tp', 'shard', 'ctx'))
- conv_bias_grad: float32 [4096], P(('tp', 'shard', 'ctx'))
- low_weight_grad: float32 [160, 4096], P(None, ('tp', 'shard', 'ctx'))
- step_weight_grad: float32 [128, 4096], P(None, ('tp', 'shard', 'ctx'))
- step_bias_grad: float32 [4096], P(('tp', 'shard', 'ctx'))
- decay_log_grad: float32 [16, 4096], P(None, ('tp', 'shard', 'ctx'))
- skip_gain_grad: float32 [4096], P(('tp', 'shard', 'ctx'))
- out_weight_grad: float32 [4096, 2048], P('tp', ('shard', 'ctx'))
- ffn_gain_grad: float32 [2048], P(('shard', 'ctx'))
- gate_up_grad: float32 [2048, 2, 4096], P(('shard', 'ctx'), None, 'tp')
- down_grad: float32 [4096, 2048], P('tp', ('shard', 'ctx'))
The draws below stay inside these ranges and needn't reach their ends.
Inputs may be any that keep to these rules, and one draw needn't show every extreme that they name: `lengths`: in each aligned group of 2 sequences one uses all 1024 slots; slots at or past a sequence's length are padding.
All inputs are finite; a program needn't handle non-finite values.
Results may differ from the reference program's by a relative error of at most 0.017.
Values may be sent and summed in bfloat16 or wider, within the bound.
A program may use at most 320 MiB of HBM per device.

```python
import jax
import jax.numpy as jnp
from jax import lax

D = 2048
INNER = 4096
STATE = 16
CONV = 4
DT_RANK = 128
FFN = 4096
SLOTS = 1024
SEQ_DEV = 2
SEQS = 4


def draw_lengths(key, part):
    key = jax.random.fold_in(key, 7)
    base_key, pick_key = jax.random.split(key)
    base_len = jax.random.randint(base_key, (SEQS,), SLOTS // 4, SLOTS + 1)
    groups = SEQS // SEQ_DEV
    picked = jax.random.randint(pick_key, (groups,), 0, SEQ_DEV)
    full_one = (jnp.arange(SEQ_DEV)[None, :] == picked[:, None]).reshape(SEQS)
    return jnp.where(full_one, SLOTS, base_len).astype(jnp.int32)


def levels(key, extent, cuts, low, largest):
    level, own = 1.0, jax.random.fold_in(key, 6)
    for axis_at, shards_of in cuts:
        draws = jnp.exp(jax.random.uniform(jax.random.fold_in(own, axis_at), (shards_of,), jnp.float32, low / len(cuts), largest / len(cuts)))
        level = level * jnp.repeat(draws, extent[axis_at] // shards_of).reshape([-1 if axis == axis_at else 1 for axis in range(len(extent))])
    return level


def gaussian(stream_key, dims, spread, reach, cuts=(), held_as=jnp.bfloat16):
    result = spread * jax.random.normal(stream_key, dims, jnp.float32)
    if cuts:
        result = result * levels(stream_key, dims, cuts, -0.22, 0.18)
    return jnp.clip(result, -reach, reach).astype(held_as)


def setup_inputs(seed: int = 0) -> dict:
    streams_of = jax.random.split(jax.random.key(seed), 17)
    hidden_in = gaussian(streams_of[0], (SEQS, SLOTS, D), 1.0, 6.0, ((0, 2), (1, 4)))
    lengths = draw_lengths(jax.random.fold_in(streams_of[16], 71), 0)
    cotangent = gaussian(streams_of[2], (SEQS, SLOTS, D), 1.0, 6.0, ((0, 2), (1, 4)))
    norm_gain = jnp.clip(1.0 + 0.1 * jax.random.normal(streams_of[3], (D,), jnp.float32), 0.5, 1.5).astype(jnp.bfloat16)
    in_weight = gaussian(streams_of[4], (D, 2, INNER), D ** -0.5, 0.125, ((0, 2), (2, 4)))
    conv_weight = gaussian(streams_of[5], (CONV, INNER), CONV ** -0.5, 3.0, ((1, 8),))
    conv_bias = gaussian(streams_of[6], (INNER,), 0.5, 3.0, ((0, 8),))
    low_weight = gaussian(streams_of[7], (DT_RANK + 2 * STATE, INNER), INNER ** -0.5, 0.09375, ((1, 8),))
    step_weight = gaussian(streams_of[8], (DT_RANK, INNER), DT_RANK ** -0.5, 0.5, ((1, 8),))
    step_bias = jnp.clip(-10.0 + 8.0 * jax.random.uniform(streams_of[9], (INNER,), jnp.float32) ** levels(streams_of[9], (INNER,), ((0, 8),), -0.2, 0.2), -10.0, -2.0).astype(jnp.bfloat16)
    decay_log = jnp.clip(jax.random.uniform(streams_of[10], (STATE, INNER), jnp.float32, -2.0, 2.0) * levels(streams_of[10], (STATE, INNER), ((1, 8),), -0.4, 0.0), -2.0, 2.0).astype(jnp.bfloat16)
    skip_gain = jnp.clip(0.25 + 1.5 * jax.random.uniform(streams_of[11], (INNER,), jnp.float32) ** levels(streams_of[11], (INNER,), ((0, 8),), -0.2, 0.2), 0.25, 1.75).astype(jnp.bfloat16)
    out_weight = gaussian(streams_of[12], (INNER, D), (INNER // 4) ** -0.5, 0.1875, ((0, 4), (1, 2)))
    ffn_gain = jnp.clip(1.0 + 0.1 * jax.random.normal(streams_of[13], (D,), jnp.float32), 0.5, 1.5).astype(jnp.bfloat16)
    gate_up = gaussian(streams_of[14], (D, 2, FFN), D ** -0.5, 0.125, ((0, 2), (2, 4)))
    down_weight = gaussian(streams_of[15], (FFN, D), FFN ** -0.5, 0.09375, ((0, 4), (1, 2)))
    return {"hidden_in": hidden_in, "lengths": lengths, "cotangent": cotangent, "norm_gain": norm_gain, "in_weight": in_weight, "conv_weight": conv_weight, "conv_bias": conv_bias, "low_weight": low_weight, "step_weight": step_weight, "step_bias": step_bias, "decay_log": decay_log, "skip_gain": skip_gain, "out_weight": out_weight, "ffn_gain": ffn_gain, "gate_up": gate_up, "down_weight": down_weight}


epsilon = 1e-05
highest = lax.Precision.HIGHEST

@jax.custom_vjp
def low(v):
    return lax.optimization_barrier(v.astype(jnp.bfloat16)).astype(jnp.float32)

@jax.custom_vjp
def low_back(v):
    return v

def low_keep(v):
    return (low(v), None)

def low_pass(kept, grad):
    return (grad,)

def back_keep(v):
    return (v, None)

def back_low(kept, grad):
    return (low(grad),)
low.defvjp(low_keep, low_pass)
low_back.defvjp(back_keep, back_low)

def rms_scale(source):
    return lax.rsqrt(lax.optimization_barrier(jnp.mean(source * source, axis=-1, keepdims=True)) + epsilon)

def scan_piece(carried, pieces, decay_rate):

    def one_step(state_now, inputs):
        step_now, drive_now, b_now, c_now = inputs
        state_now = jnp.exp(step_now[:, None, :] * decay_rate[None]) * state_now + drive_now[:, None, :] * b_now[:, :, None]
        return (state_now, lax.optimization_barrier(jnp.sum(state_now * c_now[:, :, None], axis=1)))
    return lax.scan(one_step, carried, tuple((jnp.moveaxis(block_arr, 1, 0) for block_arr in pieces)))

def selective(step_size, drive_in, b_in, c_out, decay_rate):
    groups, length, inner = step_size.shape
    block_count = length // 32

    def split_up(array_in):
        return jnp.moveaxis(array_in.reshape(groups, block_count, 32, array_in.shape[-1]), 1, 0)
    remat_piece = jax.checkpoint(scan_piece)

    def outer_step(carried, pieces):
        return remat_piece(carried, pieces, decay_rate)
    zero_state = jnp.zeros((groups, decay_rate.shape[0], inner), step_size.dtype)
    _, outputs = lax.scan(outer_step, zero_state, (split_up(step_size), split_up(drive_in), split_up(b_in), split_up(c_out)))
    return jnp.moveaxis(outputs, 2, 0).reshape(groups, length, inner)

def block_forward(hidden, norm_gain, in_weight, conv_weight, conv_bias, low_weight, step_weight, step_bias, decay_log, skip_gain, out_weight, ffn_gain, gate_up, down_weight):
    normed_one = low(hidden * rms_scale(hidden) * norm_gain)
    project = low_back(jnp.einsum('gtd,dce->gtce', normed_one, in_weight, precision=highest))
    conv_in = low(project[:, :, 0])
    gate_z = project[:, :, 1]
    width_k = conv_weight.shape[0]
    length = hidden.shape[1]
    padded = jnp.pad(conv_in, ((0, 0), (width_k - 1, 0), (0, 0)))
    pre_act = conv_bias + sum((conv_weight[kernel_at] * padded[:, kernel_at:kernel_at + length] for kernel_at in range(width_k)))
    act_out = low(jax.nn.silu(pre_act))
    low_all = low_back(jnp.einsum('gte,pe->gtp', act_out, low_weight, precision=highest))
    rank_n = step_weight.shape[0]
    state_n = decay_log.shape[0]
    step_low = low(low_all[:, :, :rank_n])
    b_in = low_all[:, :, rank_n:rank_n + state_n]
    c_out = low_all[:, :, rank_n + state_n:]
    step_pre = low_back(jnp.einsum('gtr,re->gte', step_low, step_weight, precision=highest) + step_bias)
    step_size = jax.nn.softplus(step_pre)
    decay_rate = -jnp.exp(decay_log)
    scan_out = selective(step_size, step_size * act_out, b_in, c_out, decay_rate) + skip_gain * act_out
    gated_out = low(scan_out * jax.nn.silu(gate_z))
    mixed_sum = low_back(jnp.einsum('gte,ed->gtd', gated_out, out_weight, precision=highest))
    middle = hidden + mixed_sum
    normed_two = low(middle * rms_scale(middle) * ffn_gain)
    gate_val = low_back(jnp.einsum('gtd,dcf->gtcf', normed_two, gate_up, precision=highest))
    hidden_ffn = low(jax.nn.silu(gate_val[:, :, 0]) * gate_val[:, :, 1])
    ffn_out = low_back(jnp.einsum('gtf,fd->gtd', hidden_ffn, down_weight, precision=highest))
    return middle + ffn_out

def reference(hidden_in, lengths, cotangent, norm_gain, in_weight, conv_weight, conv_bias, low_weight, step_weight, step_bias, decay_log, skip_gain, out_weight, ffn_gain, gate_up, down_weight):
    weights = tuple((item.astype(jnp.float32) for item in (norm_gain, in_weight, conv_weight, conv_bias, low_weight, step_weight, step_bias, decay_log, skip_gain, out_weight, ffn_gain, gate_up, down_weight)))
    groups = SEQS // SEQ_DEV

    def group_step(totals, inputs):
        hidden_grp, cot_grp, len_grp = inputs
        pad_mask = (jnp.arange(SLOTS)[None, :] < len_grp[:, None]).astype(jnp.float32)
        output, pullback = jax.vjp(block_forward, hidden_grp.astype(jnp.float32), *weights)
        grads = pullback(cot_grp.astype(jnp.float32) * pad_mask[:, :, None])
        totals = tuple((running + new_grad for running, new_grad in zip(totals, grads[1:])))
        return (totals, (output.astype(jnp.bfloat16), grads[0]))
    start_totals = tuple((jnp.zeros_like(weight_arr) for weight_arr in weights))
    stacked = (hidden_in.reshape((groups, SEQ_DEV) + hidden_in.shape[1:]), cotangent.reshape((groups, SEQ_DEV) + cotangent.shape[1:]), lengths.reshape(groups, SEQ_DEV))
    totals, (outputs, input_grad) = lax.scan(group_step, start_totals, stacked)
    mixed_out = outputs.reshape(hidden_in.shape)
    input_grad = input_grad.reshape(hidden_in.shape)
    return (mixed_out, input_grad, totals[0], totals[1], totals[2], totals[3], totals[4], totals[5], totals[6], totals[7], totals[8], totals[9], totals[10], totals[11], totals[12])
```

```python
import functools

import jax
import jax.numpy as jnp
from jax import lax
from jax.experimental import pallas as pl
from jax.experimental.pallas import tpu as pltpu
from jax.sharding import PartitionSpec as P

MESH = pl.DeviceIdType.MESH
epsilon = 1e-05
log2e = 1.4426950408889634
bf16 = jnp.bfloat16
f32 = jnp.float32
VMEM = pl.BlockSpec(memory_space=pltpu.VMEM)
HBM = pl.BlockSpec(memory_space=pl.ANY)


def inner_rows(left, right):
    return lax.dot_general(left, right, (((0,), (0,)), ((), ())), preferred_element_type=f32)


def outer_cols(left, right):
    return lax.dot_general(left, right, (((1,), (1,)), ((), ())), preferred_element_type=f32)


def silu_grad(values):
    sig_val = jax.nn.sigmoid(values)
    return sig_val * (1.0 + values * (1.0 - sig_val))


def rms_scale(source):
    return lax.rsqrt(jnp.mean(source * source, axis=-1, keepdims=True) + epsilon)


def tp_sum(partial, epilogue, extras, extra_outs, chunk, ident, out_dtype=bf16):
    rows, width = partial.shape
    count = rows // chunk
    n_ex, n_out = len(extras), len(extra_outs)

    def kernel(*refs):
        p_ref = refs[0]
        ins = refs[1 : 1 + n_ex]
        out_ref = refs[1 + n_ex]
        outs = refs[2 + n_ex : 2 + n_ex + n_out]
        got_a, pair, got_b, a_send, a_recv, b_send, b_recv, c_send, c_recv = refs[2 + n_ex + n_out :]
        me = lax.axis_index("tp")
        mate = me + 1 - 2 * (me % 2)
        across = 3 - me
        middle = jnp.logical_or(me == 1, me == 2)
        barrier = pltpu.get_barrier_semaphore()

        def at(c):
            return pl.ds(pl.multiple_of(c * chunk, chunk), chunk)

        def copy_a(c):
            return pltpu.make_async_remote_copy(
                p_ref.at[at(c)], got_a.at[at(c)], a_send.at[c], a_recv.at[c], device_id={"tp": mate}, device_id_type=MESH
            )

        def copy_b(c):
            return pltpu.make_async_remote_copy(
                pair.at[at(c)], got_b.at[at(c)], b_send.at[c], b_recv.at[c], device_id={"tp": across}, device_id_type=MESH
            )

        def copy_c(c):
            return pltpu.make_async_remote_copy(
                out_ref.at[at(c)], out_ref.at[at(c)], c_send.at[c], c_recv.at[c], device_id={"tp": mate}, device_id_type=MESH
            )

        pl.semaphore_signal(barrier, inc=1, device_id={"tp": mate}, device_id_type=MESH)

        @pl.when(middle)
        def _():
            pl.semaphore_signal(barrier, inc=1, device_id={"tp": across}, device_id_type=MESH)
            pl.semaphore_wait(barrier, 2)

            def first(c):
                copy_a(c).wait_recv()
                pair[at(c), :] = (p_ref[at(c), :].astype(f32) + got_a[at(c), :].astype(f32)).astype(bf16)
                copy_b(c).start()

            def second(c):
                copy_b(c).wait_recv()
                total = pair[at(c), :].astype(f32) + got_b[at(c), :].astype(f32)
                epilogue(c, at(c), total, ins, out_ref, outs)
                copy_c(c).start()

            first(0)

            def turn(c, _):
                first(c)
                second(c - 1)
                return 0

            lax.fori_loop(1, count, turn, 0)
            second(count - 1)

            def drain(c, _):
                copy_b(c).wait_send()
                copy_c(c).wait_send()
                return 0

            lax.fori_loop(0, count, drain, 0)

        @pl.when(jnp.logical_not(middle))
        def _():
            pl.semaphore_wait(barrier, 1)

            def send(c, _):
                copy_a(c).start()
                return 0

            lax.fori_loop(0, count, send, 0)

            def take(c, _):
                copy_c(c).wait_recv()
                copy_a(c).wait_send()
                return 0

            lax.fori_loop(0, count, take, 0)

    return pl.pallas_call(
        kernel,
        out_shape=[jax.ShapeDtypeStruct((rows, width), out_dtype)] + list(extra_outs),
        in_specs=[VMEM] * (1 + n_ex),
        out_specs=[VMEM] * (1 + n_out),
        scratch_shapes=[pltpu.VMEM((rows, width), bf16)] * 3 + [pltpu.SemaphoreType.DMA((count,))] * 6,
        compiler_params=pltpu.CompilerParams(
            collective_id=ident, has_side_effects=True, vmem_limit_bytes=48 << 20
        ),
    )(partial, *extras)


def plain_end(c, rows, total, ins, out_ref, outs):
    out_ref[rows, :] = total.astype(out_ref.dtype)


def norm_end(c, rows, total, ins, out_ref, outs):
    source_ref, gain_ref = ins
    middle = source_ref[rows, :].astype(f32) + total
    outs[0][rows, :] = middle
    out_ref[rows, :] = (middle * rms_scale(middle) * gain_ref[...]).astype(bf16)


def add_end(c, rows, total, ins, out_ref, outs):
    out_ref[rows, :] = (ins[0][rows, :] + total).astype(bf16)


def norm_back_end(c, rows, total, ins, out_ref, outs):
    source = ins[0][rows, :].astype(f32)
    inv = rms_scale(source)
    weighted = total * ins[1][...]
    back = inv * weighted - source * (inv * inv * inv) * jnp.mean(weighted * source, axis=-1, keepdims=True)
    result = ins[2][rows, :] + back
    if outs:
        outs[0][rows, :] = result
    out_ref[rows, :] = result.astype(bf16)


def shard_gather(arrays, dims, ident):
    shards = lax.axis_size("shard")
    n = len(arrays)

    def kernel(*refs):
        ins, outs, (send, recv, own) = refs[:n], refs[n : 2 * n], refs[2 * n :]
        me = lax.axis_index("shard")
        barrier = pltpu.get_barrier_semaphore()
        for step in range(1, shards):
            pl.semaphore_signal(barrier, inc=1, device_id={"shard": lax.rem(me + step, shards)}, device_id_type=MESH)
        pl.semaphore_wait(barrier, shards - 1)
        copies = []
        for i in range(n):
            size = arrays[i].shape[dims[i]]
            spot = pl.ds(pl.multiple_of(me * size, size), size)
            place = outs[i].at[tuple(spot if k == dims[i] else slice(None) for k in range(arrays[i].ndim))]
            for step in range(1, shards):
                peer = lax.rem(me + step, shards)
                copies.append(
                    pltpu.make_async_remote_copy(
                        ins[i], place, send.at[i, step], recv.at[i, step], device_id={"shard": peer}, device_id_type=MESH
                    )
                )
                copies[-1].start()
            copies.append(pltpu.make_async_copy(ins[i], place, own.at[i]))
            copies[-1].start()
        for copy in copies:
            copy.wait()

    def full(array, dim):
        return jax.ShapeDtypeStruct(
            tuple(s * shards if k == dim else s for k, s in enumerate(array.shape)), array.dtype
        )

    return pl.pallas_call(
        kernel,
        out_shape=[full(a, d) for a, d in zip(arrays, dims)],
        in_specs=[VMEM] * n,
        out_specs=[HBM] * n,
        scratch_shapes=[
            pltpu.SemaphoreType.DMA((n, shards)),
            pltpu.SemaphoreType.DMA((n, shards)),
            pltpu.SemaphoreType.DMA((n,)),
        ],
        compiler_params=pltpu.CompilerParams(
            collective_id=ident, has_side_effects=True, vmem_limit_bytes=32 << 20
        ),
    )(*arrays)


piece = 32
unroll = 4


def spread(flat_ref, natural, first):
    for j in range(8):
        flat_ref[pl.ds(first * 8 + j, 8, stride=8), :] = natural[:, j * 128 : (j + 1) * 128]


def unspread(flat_ref, first):
    return jnp.concatenate([flat_ref[pl.ds(first * 8 + j, 8, stride=8), :] for j in range(8)], axis=1)


def tile(ref, t):
    return ref[pl.ds(pl.multiple_of(t * 8, 8), 8), :]


def row(ref, t, n, states):
    return ref[pl.ds(t * states + n, 8, stride=0), :]


def exchange(ends, got, send, recv, seq, width):
    me = lax.axis_index("ctx")
    copies = []
    for step in range(1, width):
        copies.append(
            pltpu.make_async_remote_copy(
                ends.at[seq],
                got.at[me, seq],
                send.at[seq, step],
                recv.at[seq, step],
                device_id={"ctx": lax.rem(me + step, width)},
                device_id_type=MESH,
            )
        )
        copies[-1].start()
    return copies


def ctx_barrier(width):
    me = lax.axis_index("ctx")
    barrier = pltpu.get_barrier_semaphore()
    for step in range(1, width):
        pl.semaphore_signal(barrier, inc=1, device_id={"ctx": lax.rem(me + step, width)}, device_id_type=MESH)
    pl.semaphore_wait(barrier, width - 1)


def entering(got, seq, rate_ref, states, width, reverse):
    me = lax.axis_index("ctx")
    result = []
    for n in range(states):
        value = jnp.zeros((8, 128), f32)
        for k in reversed(range(width)) if reverse else range(width):
            new = jnp.exp2(got[k, seq, states] * rate_ref[n]) * value + got[k, seq, n]
            value = jnp.where(me < k if reverse else me > k, new, value)
        result.append(value)
    return result


def scan_forward(size, act, b_row, c_row, rate, seqs, ident):
    rows, channels = size.shape
    local = rows // seqs
    states = rate.shape[0]
    width = lax.axis_size("ctx")
    pieces = local // piece

    def kernel(
        size_ref, act_ref, b_ref, c_ref, rate_ref, y_ref, kept_ref, enter_ref, size3, drive3,
        y3, ends, got, held, send, recv, out_sem,
    ):
        ctx_barrier(width)

        def lay(i, _):
            first = pl.multiple_of(i * 8, 8)
            block = size_ref[pl.ds(first, 8), :]
            spread(size3, block, first)
            spread(drive3, block * act_ref[pl.ds(first, 8), :], first)
            return 0

        lax.fori_loop(0, rows // 8, lay, 0)
        copies = []
        for seq in range(seqs):

            def first_pass(i, carried):
                values, total = list(carried[:-1]), carried[-1]
                for u in range(unroll):
                    t = seq * local + i * unroll + u
                    s, d = tile(size3, t), tile(drive3, t)
                    total = total + s
                    for n in range(states):
                        values[n] = jnp.exp2(s * rate_ref[n]) * values[n] + d * row(b_ref, t, n, states)
                return tuple(values) + (total,)

            zero = tuple(jnp.zeros((8, 128), f32) for _ in range(states + 1))
            done = lax.fori_loop(0, local // unroll, first_pass, zero)
            for n in range(states + 1):
                ends[seq, n] = done[n]
            copies.append(exchange(ends, got, send, recv, seq, width))
        me = lax.axis_index("ctx")
        for seq in range(seqs):
            for copy in copies[seq]:
                copy.wait()
            got[me, seq] = ends[seq]
            start = entering(got, seq, rate_ref, states, width, False)
            for n in range(states):
                enter_ref[seq, n] = start[n]

            def save(k, slot):
                return pltpu.make_async_copy(
                    held.at[slot], kept_ref.at[pl.ds(seq * local + k * piece, piece)], out_sem.at[slot]
                )

            def one_piece(k, carried):
                slot = lax.rem(k, 2)

                @pl.when(k >= 2)
                def _():
                    save(k - 2, slot).wait()

                def second_pass(i, values):
                    values = list(values)
                    for u in range(unroll):
                        inside = i * unroll + u
                        t = seq * local + k * piece + inside
                        s, d = tile(size3, t), tile(drive3, t)
                        acc = [None] * 4
                        for n in range(states):
                            values[n] = jnp.exp2(s * rate_ref[n]) * values[n] + d * row(b_ref, t, n, states)
                            held[slot, inside, n] = values[n]
                            part = values[n] * row(c_ref, t, n, states)
                            acc[n % 4] = part if acc[n % 4] is None else acc[n % 4] + part
                        y3[pl.ds(pl.multiple_of(t * 8, 8), 8), :] = (acc[0] + acc[1]) + (acc[2] + acc[3])
                    return tuple(values)

                carried = lax.fori_loop(0, piece // unroll, second_pass, carried)
                save(k, slot).start()
                return carried

            lax.fori_loop(0, pieces, one_piece, tuple(start))
            for k in (pieces - 2, pieces - 1):
                save(k, k % 2).wait()

        def back(i, _):
            first = pl.multiple_of(i * 8, 8)
            y_ref[pl.ds(first, 8), :] = unspread(y3, first)
            return 0

        lax.fori_loop(0, rows // 8, back, 0)

    flat = jax.ShapeDtypeStruct((rows * 8, 128), f32)
    return pl.pallas_call(
        kernel,
        out_shape=[
            jax.ShapeDtypeStruct((rows, channels), f32),
            jax.ShapeDtypeStruct((rows, states, 8, 128), f32),
            jax.ShapeDtypeStruct((seqs, states, 8, 128), f32),
            flat,
            flat,
        ],
        in_specs=[VMEM] * 5,
        out_specs=[VMEM, HBM, VMEM, VMEM, VMEM],
        scratch_shapes=[
            pltpu.VMEM((rows * 8, 128), f32),
            pltpu.VMEM((seqs, states + 1, 8, 128), f32),
            pltpu.VMEM((width, seqs, states + 1, 8, 128), f32),
            pltpu.VMEM((2, piece, states, 8, 128), f32),
            pltpu.SemaphoreType.DMA((seqs, width)),
            pltpu.SemaphoreType.DMA((seqs, width)),
            pltpu.SemaphoreType.DMA((2,)),
        ],
        compiler_params=pltpu.CompilerParams(
            collective_id=ident, has_side_effects=True, vmem_limit_bytes=48 << 20
        ),
    )(size, act, b_row, c_row, rate)


def sublane_sums(parts):
    at = lax.broadcasted_iota(jnp.int32, (8, 128), 0)
    for shift in (4, 2, 1):
        low = (at // shift) % 2 == 0
        half = len(parts) // 2
        merged = []
        for one, two in zip(parts[:half], parts[half:]):
            merged.append(
                jnp.where(low, one + pltpu.roll(one, 8 - shift, 0), two + pltpu.roll(two, shift, 0))
            )
        parts = merged
    return parts[0]


def scan_backward(size3, drive3, grad, b_row, c_row, rate, kept, enter, seqs, ident):
    rows, channels = grad.shape
    local = rows // seqs
    states = rate.shape[0]
    width = lax.axis_size("ctx")
    pieces = local // piece
    unroll_b = 2

    def kernel(
        size_ref, drive_ref, grad_ref, b_ref, c_ref, rate_ref, kept_ref, enter_ref,
        tb_ref, sd_ref, bg_ref, cg_ref, dec_ref,
        grad3, tb3, sd3, ends, got, held, bpart, cpart, prior, send, recv, in_sem,
    ):
        ctx_barrier(width)

        def lay(i, _):
            first = pl.multiple_of(i * 8, 8)
            spread(grad3, grad_ref[pl.ds(first, 8), :], first)
            return 0

        lax.fori_loop(0, rows // 8, lay, 0)

        def fetch(seq, k, slot):
            return pltpu.make_async_copy(
                kept_ref.at[pl.ds(seq * local + k * piece, piece)], held.at[slot], in_sem.at[slot]
            )

        copies = []
        for seq in range(seqs):

            def first_pass(i, carried):
                values, total = list(carried[:-1]), carried[-1]
                for u in range(unroll):
                    t = seq * local + local - 1 - (i * unroll + u)
                    s, g = tile(size_ref, t), tile(grad3, t)
                    total = total + s
                    for n in range(states):
                        values[n] = jnp.exp2(s * rate_ref[n]) * (values[n] + g * row(c_ref, t, n, states))
                return tuple(values) + (total,)

            zero = tuple(jnp.zeros((8, 128), f32) for _ in range(states + 1))
            done = lax.fori_loop(0, local // unroll, first_pass, zero)
            for n in range(states + 1):
                ends[seq, n] = done[n]
            copies.append(exchange(ends, got, send, recv, seq, width))
        me = lax.axis_index("ctx")
        for n in range(states):
            dec_ref[n] = jnp.zeros((8, 128), f32)
        for seq in range(seqs):
            fetch(seq, pieces - 1, (pieces - 1) % 2).start()
            for copy in copies[seq]:
                copy.wait()
            got[me, seq] = ends[seq]
            start = entering(got, seq, rate_ref, states, width, True)
            fetch(seq, pieces - 1, (pieces - 1) % 2).wait()

            def one_slot(slot, k, inside, adjoint, decays, prior_at):
                t = seq * local + k * piece + inside
                s, d, g = tile(size_ref, t), tile(drive_ref, t), tile(grad3, t)
                tb, sd = [None] * 2, [None] * 2
                b_parts, c_parts = [], []
                for n in range(states):
                    total = adjoint[n] + g * row(c_ref, t, n, states)
                    c_parts.append(held[slot, inside, n] * g)
                    b_parts.append(total * d)
                    through = total * row(b_ref, t, n, states)
                    adjoint[n] = jnp.exp2(s * rate_ref[n]) * total
                    kept_part = adjoint[n] * prior_at(n)
                    through_size = kept_part * rate_ref[n]
                    decays[n] = decays[n] + kept_part * s
                    tb[n % 2] = through if tb[n % 2] is None else tb[n % 2] + through
                    sd[n % 2] = through_size if sd[n % 2] is None else sd[n % 2] + through_size
                here = pl.ds(pl.multiple_of(t * 8, 8), 8)
                tb3[here, :] = tb[0] + tb[1]
                sd3[here, :] = sd[0] + sd[1]
                for h in range(states // 8):
                    spot = pl.ds(pl.multiple_of(inside * states + h * 8, 8), 8)
                    bpart[spot, :] = sublane_sums(b_parts[h * 8 : h * 8 + 8])
                    cpart[spot, :] = sublane_sums(c_parts[h * 8 : h * 8 + 8])

            def one_piece(back_k, carried):
                k = pieces - 1 - back_k
                slot = lax.rem(k, 2)

                @pl.when(k > 0)
                def _():
                    fetch(seq, k - 1, 1 - slot).start()

                def slots(i, carried):
                    adjoint, decays = list(carried[:states]), list(carried[states:])
                    for u in range(unroll_b):
                        inside = piece - 1 - (i * unroll_b + u)
                        one_slot(slot, k, inside, adjoint, decays, lambda n: held[slot, inside - 1, n])
                    return tuple(adjoint) + tuple(decays)

                carried = lax.fori_loop(0, piece // unroll_b - 1, slots, carried)
                adjoint, decays = list(carried[:states]), list(carried[states:])
                for inside in reversed(range(1, unroll_b)):
                    one_slot(slot, k, inside, adjoint, decays, lambda n: held[slot, inside - 1, n])

                @pl.when(k > 0)
                def _():
                    fetch(seq, k - 1, 1 - slot).wait()
                    prior[...] = held[1 - slot, piece - 1]

                @pl.when(k == 0)
                def _():
                    prior[...] = enter_ref[seq]

                one_slot(slot, k, 0, adjoint, decays, lambda n: prior[n])
                ones = jnp.ones((8, 128), bf16)
                for part, out in ((bpart, bg_ref), (cpart, cg_ref)):
                    sums = outer_cols(ones, part[...].astype(bf16))
                    out[pl.ds(seq * pieces + k, 1)] = sums[None]
                return tuple(adjoint) + tuple(decays)

            zero = tuple(jnp.zeros((8, 128), f32) for _ in range(states))
            carried = lax.fori_loop(0, pieces, one_piece, tuple(start) + zero)
            for n in range(states):
                dec_ref[n] = dec_ref[n] + carried[states + n]

        def back(i, _):
            first = pl.multiple_of(i * 8, 8)
            tb_ref[pl.ds(first, 8), :] = unspread(tb3, first)
            sd_ref[pl.ds(first, 8), :] = unspread(sd3, first)
            return 0

        lax.fori_loop(0, rows // 8, back, 0)

    nat = jax.ShapeDtypeStruct((rows, channels), f32)
    sums = jax.ShapeDtypeStruct((rows // piece, 8, piece * states), f32)
    return pl.pallas_call(
        kernel,
        out_shape=[nat, nat, sums, sums, jax.ShapeDtypeStruct((states, 8, 128), f32)],
        in_specs=[VMEM] * 6 + [HBM, VMEM],
        out_specs=[VMEM] * 5,
        scratch_shapes=[pltpu.VMEM((rows * 8, 128), f32)] * 3
        + [
            pltpu.VMEM((seqs, states + 1, 8, 128), f32),
            pltpu.VMEM((width, seqs, states + 1, 8, 128), f32),
            pltpu.VMEM((2, piece, states, 8, 128), f32),
            pltpu.VMEM((piece * states, 128), f32),
            pltpu.VMEM((piece * states, 128), f32),
            pltpu.VMEM((states, 8, 128), f32),
            pltpu.SemaphoreType.DMA((seqs, width)),
            pltpu.SemaphoreType.DMA((seqs, width)),
            pltpu.SemaphoreType.DMA((2,)),
        ],
        compiler_params=pltpu.CompilerParams(
            collective_id=ident, has_side_effects=True, vmem_limit_bytes=52 << 20
        ),
    )(size3, drive3, grad, b_row, c_row, rate, kept, enter)


def body(
    hidden_in, lengths, cotangent, norm_gain, in_weight, conv_weight, conv_bias, low_weight, step_weight,
    step_bias, decay_log, skip_gain, out_weight, ffn_gain, gate_up, down_weight,
):
    seqs, local, width = hidden_in.shape
    rows = seqs * local
    shards, pieces = lax.axis_size("shard"), lax.axis_size("ctx")
    inner = in_weight.shape[2]
    taps = conv_weight.shape[0]
    rank = step_weight.shape[0]
    states = decay_log.shape[0]
    low_len = low_weight.shape[0]

    small = jnp.concatenate(
        [low_weight, step_weight, decay_log, conv_weight, conv_bias[None], step_bias[None], skip_gain[None]], axis=0
    )
    small = jnp.pad(small, ((0, -small.shape[0] % 16), (0, 0)))
    gains = jnp.stack([norm_gain, ffn_gain])
    gains = jnp.pad(gains, ((0, 14), (0, 0)))
    in_half = in_weight.transpose(1, 0, 2)
    small, gains, in_w = shard_gather([small, gains, in_half], [1, 1, 1], 0)
    out_parts = lax.all_gather(out_weight, "shard")
    gate_half = gate_up.transpose(1, 0, 2)
    gate_w = [lax.all_gather(gate_half[c], "shard", axis=0, tiled=True) for c in range(2)]
    down_parts = lax.all_gather(down_weight, "shard")
    part = width // shards

    low_w = small[:low_len]
    step_w = small[low_len : low_len + rank]
    at = low_len + rank
    decay_w = small[at : at + states].astype(f32)
    kernel = small[at + states : at + states + taps].astype(f32)
    conv_b = small[at + states + taps].astype(f32)
    step_b = small[at + states + taps + 1].astype(f32)
    skip_full = small[at + states + taps + 2].astype(f32)
    gain_one, gain_two = gains[0:1].astype(f32), gains[1:2].astype(f32)

    first_slot = lax.axis_index("ctx") * local
    positions = first_slot + jnp.arange(local, dtype=jnp.int32)
    pad_mask = (positions[None, :] < lengths[:, None]).astype(f32)

    ahead = lax.ppermute(hidden_in[:, local - taps + 1 :], "ctx", [(k, k + 1) for k in range(pieces - 1)])
    longer = jnp.concatenate([ahead, hidden_in], axis=1).astype(f32)
    normed_all = (longer * rms_scale(longer) * gain_one).astype(bf16)
    source = hidden_in.reshape(rows, width).astype(f32)
    normed_one = normed_all[:, taps - 1 :].reshape(rows, width)
    normed_edge = normed_all[:, : taps - 1].reshape(seqs * (taps - 1), width)
    edge_in = jnp.dot(normed_edge, in_w[0], preferred_element_type=f32).astype(bf16)
    conv_in = jnp.dot(normed_one, in_w[0], preferred_element_type=f32).astype(bf16)
    gate_z = jnp.dot(normed_one, in_w[1], preferred_element_type=f32)
    padded = jnp.concatenate(
        [edge_in.reshape(seqs, taps - 1, inner), conv_in.reshape(seqs, local, inner)], axis=1
    ).astype(f32)
    pre_act = conv_b + sum(kernel[k] * padded[:, k : k + local] for k in range(taps))
    pre_act = pre_act.reshape(rows, inner)
    act_half = jax.nn.silu(pre_act).astype(bf16)
    act_full = act_half.astype(f32)

    low_part = outer_cols(low_w, act_half).astype(bf16)
    low_all = tp_sum(low_part, plain_end, [], [], 80, 1, f32)[0]
    step_low = low_all[:rank].astype(bf16)
    b_in, c_out = low_all[rank : rank + states], low_all[rank + states :]
    b_row, c_row = (
        jnp.broadcast_to(v.T[:, :, None], (rows, states, 128)).reshape(rows * states, 128) for v in (b_in, c_out)
    )
    step_pre = inner_rows(step_low, step_w) + step_b
    step_size = jax.nn.softplus(step_pre)
    decay_rate = -jnp.exp(decay_w)
    rate = (decay_rate * log2e).reshape(states, 8, 128)
    scan_y, kept, enter, size3, drive3 = scan_forward(step_size, act_full, b_row, c_row, rate, seqs, 2)
    scan_out = scan_y + skip_full * act_full
    gate_act = jax.nn.silu(gate_z)
    gated_out = (scan_out * gate_act).astype(bf16)
    mixed_part = jnp.concatenate(
        [jnp.dot(gated_out, out_parts[k], preferred_element_type=f32) for k in range(shards)], axis=1
    ).astype(bf16)
    wide = jax.ShapeDtypeStruct((rows, width), f32)
    hidden_rows = hidden_in.reshape(rows, width)
    normed_two, middle = tp_sum(mixed_part, norm_end, [hidden_rows, gain_two], [wide], 32, 3)
    gate_lin, up_lin = (jnp.dot(normed_two, gate_w[c], preferred_element_type=f32) for c in range(2))
    hidden_ffn = (jax.nn.silu(gate_lin) * up_lin).astype(bf16)
    ffn_part = jnp.concatenate(
        [jnp.dot(hidden_ffn, down_parts[k], preferred_element_type=f32) for k in range(shards)], axis=1
    ).astype(bf16)
    mixed_out = tp_sum(ffn_part, add_end, [middle], [], 32, 4)[0].reshape(hidden_in.shape)

    upstream = cotangent.reshape(rows, width).astype(f32) * pad_mask.reshape(rows, 1)
    ffn_grad = upstream.astype(bf16)
    down_grad = inner_rows(hidden_ffn, ffn_grad)
    hidden_grad = sum(outer_cols(ffn_grad[:, k * part : (k + 1) * part], down_parts[k]) for k in range(shards))
    gate_grad = (hidden_grad * up_lin * silu_grad(gate_lin)).astype(bf16)
    up_grad = (hidden_grad * jax.nn.silu(gate_lin)).astype(bf16)
    both_grad = jnp.concatenate([gate_grad, up_grad], axis=1)
    gate_up_grad = inner_rows(normed_two, both_grad)
    back_part = (outer_cols(gate_grad, gate_w[0]) + outer_cols(up_grad, gate_w[1])).astype(bf16)
    mix_grad, middle_grad = tp_sum(back_part, norm_back_end, [middle, gain_two, upstream], [wide], 32, 5)
    ffn_gain_grad = jnp.sum(back_part.astype(f32) * normed_two.astype(f32), axis=0) / gain_two[0]

    out_weight_grad = inner_rows(gated_out, mix_grad)
    gated_grad = sum(outer_cols(mix_grad[:, k * part : (k + 1) * part], out_parts[k]) for k in range(shards))
    scan_grad = gated_grad * gate_act
    z_grad = gated_grad * scan_out * silu_grad(gate_z)
    skip_gain_grad = jnp.sum(scan_grad * act_full, axis=0)
    through_b, through_decay, b_sums, c_sums, decay_sum = scan_backward(
        size3, drive3, scan_grad, b_row, c_row, rate, kept, enter, seqs, 6
    )
    decay_log_grad = decay_sum.reshape(states, inner) * decay_rate
    size_grad = act_full * through_b + through_decay * (1.0 / log2e)
    step_grad = (size_grad * jax.nn.sigmoid(step_pre)).astype(bf16)
    step_bias_grad = jnp.sum(step_grad.astype(f32), axis=0)
    step_weight_grad = jnp.dot(step_low, step_grad, preferred_element_type=f32)
    low_back = jnp.concatenate(
        [
            outer_cols(step_w, step_grad),
            b_sums[:, 0].reshape(rows, states).T,
            c_sums[:, 0].reshape(rows, states).T,
        ],
        axis=0,
    ).astype(bf16)
    low_grad = tp_sum(low_back, plain_end, [], [], 80, 7)[0]
    low_weight_grad = jnp.dot(low_grad, act_half, preferred_element_type=f32)
    act_grad = skip_full * scan_grad + step_size * through_b + inner_rows(low_grad, low_w)
    pre_grad = (act_grad * silu_grad(pre_act)).reshape(seqs, local, inner)
    conv_bias_grad = jnp.sum(pre_grad, axis=(0, 1))
    conv_weight_grad = jnp.stack(
        [jnp.sum(pre_grad * padded[:, k : k + local], axis=(0, 1)) for k in range(taps)]
    )
    behind = lax.ppermute(pre_grad[:, : taps - 1], "ctx", [(k + 1, k) for k in range(pieces - 1)])
    pre_long = jnp.concatenate([pre_grad, behind], axis=1)
    conv_grad = sum(kernel[k] * pre_long[:, taps - 1 - k : taps - 1 - k + local] for k in range(taps))
    conv_grad = conv_grad.reshape(rows, inner).astype(bf16)
    z_half = z_grad.astype(bf16)
    project_grad = jnp.concatenate([conv_grad, z_half], axis=1)
    in_weight_grad = inner_rows(normed_one, project_grad)
    first_part = (outer_cols(conv_grad, in_w[0]) + outer_cols(z_half, in_w[1])).astype(bf16)
    norm_gain_grad = jnp.sum(first_part.astype(f32) * source * rms_scale(source), axis=0)
    input_grad = tp_sum(first_part, norm_back_end, [hidden_rows, gain_one, middle_grad], [], 32, 8)[0]
    input_grad = input_grad.astype(f32).reshape(hidden_in.shape)

    both = ("shard", "ctx")
    scatter = functools.partial(lax.psum_scatter, axis_name=both, tiled=True)
    small_grads = jnp.concatenate(
        [low_weight_grad, step_weight_grad, decay_log_grad, conv_weight_grad, conv_bias_grad[None],
         step_bias_grad[None], skip_gain_grad[None]], axis=0,
    )
    small_out = scatter(small_grads, scatter_dimension=1)
    at = low_len + rank
    gain_out = lax.psum(scatter(jnp.stack([norm_gain_grad, ffn_gain_grad]), scatter_dimension=1), "tp")
    in_out = scatter(in_weight_grad, scatter_dimension=0)
    gate_out = scatter(gate_up_grad, scatter_dimension=0)
    return (
        mixed_out,
        input_grad,
        gain_out[0],
        in_out.reshape((-1,) + in_weight.shape[1:]),
        small_out[at + states : at + states + taps],
        small_out[at + states + taps],
        small_out[:low_len],
        small_out[low_len : low_len + rank],
        small_out[at + states + taps + 1],
        small_out[at : at + states],
        small_out[at + states + taps + 2],
        scatter(out_weight_grad, scatter_dimension=1),
        gain_out[1],
        gate_out.reshape((-1,) + gate_up.shape[1:]),
        scatter(down_grad, scatter_dimension=1),
    )


def solution(mesh):
    placed = (
        P("shard", "ctx", None),
        P("shard"),
        P("shard", "ctx", None),
        P("shard"),
        P("shard", None, "tp"),
        P(None, ("tp", "shard")),
        P(("tp", "shard")),
        P(None, ("tp", "shard")),
        P(None, ("tp", "shard")),
        P(("tp", "shard")),
        P(None, ("tp", "shard")),
        P(("tp", "shard")),
        P("tp", "shard"),
        P("shard"),
        P("shard", None, "tp"),
        P("tp", "shard"),
    )
    return jax.shard_map(
        body,
        mesh=mesh,
        in_specs=placed,
        out_specs=(
            P("shard", "ctx", None),
            P("shard", "ctx", None),
            P(("shard", "ctx")),
            P(("shard", "ctx"), None, "tp"),
            P(None, ("tp", "shard", "ctx")),
            P(("tp", "shard", "ctx")),
            P(None, ("tp", "shard", "ctx")),
            P(None, ("tp", "shard", "ctx")),
            P(("tp", "shard", "ctx")),
            P(None, ("tp", "shard", "ctx")),
            P(("tp", "shard", "ctx")),
            P("tp", ("shard", "ctx")),
            P(("shard", "ctx")),
            P(("shard", "ctx"), None, "tp"),
            P("tp", ("shard", "ctx")),
        ),
        check_vma=False,
    )
```

```python
import functools

import jax
import jax.numpy as jnp
from jax import lax
from jax.experimental import pallas as pl
from jax.experimental.pallas import tpu as pltpu
from jax.sharding import PartitionSpec as P

MESH = pl.DeviceIdType.MESH
epsilon = 1e-05
log2e = 1.4426950408889634
bf16 = jnp.bfloat16
f32 = jnp.float32
VMEM = pl.BlockSpec(memory_space=pltpu.VMEM)
HBM = pl.BlockSpec(memory_space=pl.ANY)


def inner_rows(left, right):
    return lax.dot_general(left, right, (((0,), (0,)), ((), ())), preferred_element_type=f32)


def outer_cols(left, right):
    return lax.dot_general(left, right, (((1,), (1,)), ((), ())), preferred_element_type=f32)


def silu_grad(values):
    sig_val = jax.nn.sigmoid(values)
    return sig_val * (1.0 + values * (1.0 - sig_val))


def rms_scale(source):
    return lax.rsqrt(jnp.mean(source * source, axis=-1, keepdims=True) + epsilon)


class Line:
    lag = 3
    ahead = 4

    def __init__(self, shape, chunk, epilogue, extras, out_dtype):
        self.shape, self.chunk, self.epilogue, self.out_dtype = shape, chunk, epilogue, out_dtype
        self.count = shape[0] // chunk
        self.extras = [(e.shape, e.dtype) for e in extras]

    def scratch(self):
        return (
            [pltpu.VMEM(self.shape, bf16)] * 4
            + [pltpu.SemaphoreType.DMA((self.count,))] * 6
            + [pltpu.VMEM(shape, dtype) for shape, dtype in self.extras]
            + [pltpu.SemaphoreType.DMA((1 + len(self.extras),))]
        )

    def bind(self, p_ref, ins, out_ref, outs, scratch):
        self.p_ref, self.given, self.out_ref, self.outs = p_ref, ins, out_ref, outs
        (self.p, self.got_a, self.pair, self.got_b, self.a_send, self.a_recv, self.b_send, self.b_recv,
         self.c_send, self.c_recv) = scratch[:10]
        self.ins, self.in_sem = scratch[10:-1], scratch[-1]
        me = lax.axis_index("tp")
        self.mate = me + 1 - 2 * (me % 2)
        self.across = 3 - me
        self.middle = jnp.logical_or(me == 1, me == 2)

    def at(self, c):
        return pl.ds(pl.multiple_of(c * self.chunk, self.chunk), self.chunk)

    def remote(self, source, target, send, recv, c, to):
        return pltpu.make_async_remote_copy(
            source.at[self.at(c)], target.at[self.at(c)], send.at[c], recv.at[c], device_id={"tp": to}, device_id_type=MESH
        )

    def copy_a(self, c):
        return self.remote(self.p_ref, self.got_a, self.a_send, self.a_recv, c, self.mate)

    def copy_b(self, c):
        return self.remote(self.pair, self.got_b, self.b_send, self.b_recv, c, self.across)

    def copy_c(self, c):
        return self.remote(self.out_ref, self.out_ref, self.c_send, self.c_recv, c, self.mate)

    def loads(self):
        pairs = [(self.p_ref, self.p)] + list(zip(self.given, self.ins))
        return [pltpu.make_async_copy(a, b, self.in_sem.at[i]) for i, (a, b) in enumerate(pairs)]

    def begin(self, barrier, met, ends_meet=False):
        pl.semaphore_signal(barrier, inc=1, device_id={"tp": self.mate}, device_id_type=MESH)

        @pl.when(self.middle)
        def _():
            pl.semaphore_signal(barrier, inc=1, device_id={"tp": self.across}, device_id_type=MESH)
            for load in self.loads():
                load.start()
            pl.semaphore_wait(barrier, met + 2)
            for load in self.loads():
                load.wait()

        @pl.when(jnp.logical_not(self.middle))
        def _():
            if ends_meet:
                pl.semaphore_signal(barrier, inc=1, device_id={"tp": self.across}, device_id_type=MESH)
            pl.semaphore_wait(barrier, met + 2 if ends_meet else met + 1)

            for c in range(min(self.ahead, self.count)):
                self.copy_a(c).start()

    def first(self, c):
        at = self.at(c)
        self.copy_a(c).wait_recv()
        self.pair[at, :] = (self.p[at, :].astype(f32) + self.got_a[at, :].astype(f32)).astype(bf16)
        self.copy_b(c).start()

    def second(self, c):
        at = self.at(c)
        self.copy_b(c).wait_recv()
        total = self.pair[at, :].astype(f32) + self.got_b[at, :].astype(f32)
        self.epilogue(c, at, total, self.ins, self.out_ref, self.outs)
        self.copy_c(c).start()

    def tick(self, c):
        lag = min(self.lag, self.count)

        @pl.when(jnp.logical_and(self.middle, c < self.count))
        def _():
            self.first(c)

        @pl.when(jnp.logical_and(self.middle, jnp.logical_and(c >= lag, c < self.count + lag)))
        def _():
            self.second(c - lag)

        @pl.when(jnp.logical_and(jnp.logical_not(self.middle), c + self.ahead < self.count))
        def _():
            self.copy_a(c + self.ahead).start()

    def ticks(self):
        return self.count + min(self.lag, self.count)

    def finish(self):
        @pl.when(self.middle)
        def _():
            def drain(c, _):
                self.copy_b(c).wait_send()
                self.copy_c(c).wait_send()
                return 0

            lax.fori_loop(0, self.count, drain, 0)

        @pl.when(jnp.logical_not(self.middle))
        def _():
            def take(c, _):
                self.copy_c(c).wait_recv()
                self.copy_a(c).wait_send()
                return 0

            lax.fori_loop(0, self.count, take, 0)


share_lag = 2
share_ahead = 2


def halving(count, axis):
    return [(axis, 1 << k) for k in reversed(range(count.bit_length() - 1))]


def tp_sum(partial, epilogue, extras, extra_outs, chunk, ident, out_dtype=bf16, scatters=(), line_too=False):
    rows, width = partial.shape
    line = Line(partial.shape, chunk, epilogue, extras, out_dtype)
    n_line = len(line.scratch())
    n_ex, n_out, n_sc = len(extras), len(extra_outs), len(scatters)
    shards, pieces = lax.axis_size("shard"), lax.axis_size("ctx")
    bits = halving(shards, "shard") + halving(pieces, "ctx")
    depth = len(bits)
    head = shards.bit_length() - 1
    dims = list(range(depth))
    orders = (dims, dims[:head] + dims[head:][::-1])
    step_rows = 16
    blocks = [g.shape[0] // (shards * pieces) for g in scatters]
    parts = [r // step_rows for r in blocks]
    folded = [g.reshape((2,) * depth + (r, g.shape[1])) for g, r in zip(scatters, blocks)]

    def kernel(*refs):
        refs = list(refs)

        def take_refs(n):
            taken = refs[:n]
            del refs[:n]
            return taken

        (p_ref,) = take_refs(1)
        ins = take_refs(n_ex)
        full = take_refs(n_sc)
        (out_ref,) = take_refs(1)
        outs = take_refs(n_out)
        shares = take_refs(n_sc)
        line.bind(p_ref, ins, out_ref, outs, take_refs(n_line))
        own = take_refs(n_sc)
        landed = [take_refs(n_sc) for _ in range(depth if n_sc else 0)]
        r_send, r_recv, own_sem = take_refs(3) if n_sc else (None, None, None)
        tail, tail_send, tail_recv = take_refs(3) if line_too else (None, None, None)
        barrier = pltpu.get_barrier_semaphore()
        mine, partner = [], []
        for axis, bit in bits if n_sc else []:
            here = lax.axis_index(axis)
            mine.append((here // bit) % 2)
            partner.append({axis: here + bit - 2 * bit * ((here // bit) % 2)})

        def spot(c):
            return pl.ds(pl.multiple_of(c * step_rows, step_rows), step_rows)

        def pick(remaining, dim, index, c):
            return tuple(index if d == dim else slice(None) for d in remaining) + (spot(c), slice(None))

        def rest(order, j):
            return [d for d in dims if d not in order[:j]]

        def share_copy(j, a, c, order):
            source = full[a] if j == 0 else landed[j - 1][a]
            d = order[j]
            return pltpu.make_async_remote_copy(
                source.at[pick(rest(order, j), d, 1 - mine[d], c)],
                landed[j][a].at[pick(rest(order, j + 1), None, None, c)],
                r_send.at[j, a, c],
                r_recv.at[j, a, c],
                device_id=partner[d],
                device_id_type=MESH,
            )

        def own_copy(a, c, order):
            return pltpu.make_async_copy(
                full[a].at[pick(dims, order[0], mine[order[0]], c)],
                own[a].at[pick(rest(order, 1), None, None, c)],
                own_sem.at[a, c],
            )

        def share_step(j, a, c, order):
            share_copy(j, a, c, order).wait_recv()
            where = pick(rest(order, j + 1), None, None, c)
            d = order[j]
            if j == 0:
                own_copy(a, c, order).wait()
                kept = own[a][where]
            else:
                kept = landed[j - 1][a][pick(rest(order, j), d, mine[d], c)]
            total = kept.astype(f32) + landed[j][a][where].astype(f32)
            if j == depth - 1:
                shares[a][spot(c), :] = total
            else:
                landed[j][a][where] = total.astype(bf16)
                share_copy(j + 1, a, c, order).start()

        def each_part(i, fn):
            for parity in (0, 1):
                c = 2 * i + parity
                for a in range(n_sc):

                    @pl.when(jnp.logical_and(c >= 0, c < parts[a]))
                    def _():
                        fn(a, c, orders[parity])

        for who in partner:
            pl.semaphore_signal(barrier, inc=1, device_id=who, device_id_type=MESH)
        line.begin(barrier, len(partner), line_too)

        def begin(a, c, order):
            share_copy(0, a, c, order).start()
            own_copy(a, c, order).start()

        pairs = (max(parts, default=0) + 1) // 2
        if n_sc:

            for i in range(share_ahead):
                each_part(i, begin)

        def turn(i, _):
            for parity in (0, 1):
                line.tick(2 * i + parity)
            each_part(i + share_ahead, begin)
            for j in range(depth if n_sc else 0):
                each_part(i - share_lag * j, functools.partial(share_step, j))
            return 0

        turns = (line.ticks() + 1) // 2
        if n_sc:
            turns = max(turns, pairs + share_lag * (depth - 1))
        lax.fori_loop(0, turns, turn, 0)
        if line_too:
            top = shares[-1].at[pl.ds(0, 8)]
            for k, to in enumerate((line.mate, line.across)):
                copy = pltpu.make_async_remote_copy(
                    top if k == 0 else tail.at[2], tail.at[k], tail_send.at[k], tail_recv.at[k],
                    device_id={"tp": to}, device_id_type=MESH,
                )
                copy.start()
                copy.wait()
                if k == 0:
                    tail[2] = top[...] + tail[0]
            shares[-1][pl.ds(0, 8), :] = tail[2] + tail[1]
        line.finish()

        if n_sc:

            def sent(i, _):
                for j in range(depth):
                    each_part(i, lambda a, c, order: share_copy(j, a, c, order).wait_send())
                return 0

            lax.fori_loop(0, pairs, sent, 0)

    buffers = []
    if n_sc:
        buffers += [pltpu.VMEM((2,) * (depth - 1) + g.shape[depth:], bf16) for g in folded]
        for j in range(depth):
            buffers += [pltpu.VMEM((2,) * (depth - 1 - j) + g.shape[depth:], bf16) for g in folded]
        sem = pltpu.SemaphoreType.DMA((depth, n_sc, max(parts)))
        buffers += [sem, sem, pltpu.SemaphoreType.DMA((n_sc, max(parts)))]
    if line_too:
        pair_sem = pltpu.SemaphoreType.DMA((2,))
        buffers += [pltpu.VMEM((3, 8, folded[-1].shape[-1]), f32), pair_sem, pair_sem]
    return pl.pallas_call(
        kernel,
        out_shape=[jax.ShapeDtypeStruct((rows, width), out_dtype)]
        + list(extra_outs)
        + [jax.ShapeDtypeStruct(g.shape[depth:], f32) for g in folded],
        in_specs=[HBM] * (1 + n_ex + n_sc),
        out_specs=[VMEM] * (1 + n_out + n_sc),
        scratch_shapes=line.scratch() + buffers,
        compiler_params=pltpu.CompilerParams(
            collective_id=ident, has_side_effects=True, vmem_limit_bytes=56 << 20
        ),
    )(partial, *extras, *folded)


def plain_end(c, rows, total, ins, out_ref, outs):
    out_ref[rows, :] = total.astype(out_ref.dtype)


def norm_end(c, rows, total, ins, out_ref, outs):
    source_ref, gain_ref = ins
    middle = source_ref[rows, :].astype(f32) + total
    outs[0][rows, :] = middle
    out_ref[rows, :] = (middle * rms_scale(middle) * gain_ref[...]).astype(bf16)


def add_end(c, rows, total, ins, out_ref, outs):
    out_ref[rows, :] = (ins[0][rows, :] + total).astype(bf16)


def norm_back_end(c, rows, total, ins, out_ref, outs):
    source = ins[0][rows, :].astype(f32)
    inv = rms_scale(source)
    weighted = total * ins[1][...]
    back = inv * weighted - source * (inv * inv * inv) * jnp.mean(weighted * source, axis=-1, keepdims=True)
    result = ins[2][rows, :] + back
    if outs:
        outs[0][rows, :] = result
    out_ref[rows, :] = result.astype(bf16)


def shard_gather(arrays, dims, ident):
    shards = lax.axis_size("shard")
    n = len(arrays)

    def kernel(*refs):
        ins, outs, (send, recv, own) = refs[:n], refs[n : 2 * n], refs[2 * n :]
        me = lax.axis_index("shard")
        barrier = pltpu.get_barrier_semaphore()
        for step in range(1, shards):
            pl.semaphore_signal(barrier, inc=1, device_id={"shard": lax.rem(me + step, shards)}, device_id_type=MESH)
        pl.semaphore_wait(barrier, shards - 1)
        copies = []
        for i in range(n):
            size = arrays[i].shape[dims[i]]
            spot = pl.ds(pl.multiple_of(me * size, size), size)
            place = outs[i].at[tuple(spot if k == dims[i] else slice(None) for k in range(arrays[i].ndim))]
            for step in range(1, shards):
                peer = lax.rem(me + step, shards)
                copies.append(
                    pltpu.make_async_remote_copy(
                        ins[i], place, send.at[i, step], recv.at[i, step], device_id={"shard": peer}, device_id_type=MESH
                    )
                )
                copies[-1].start()
            copies.append(pltpu.make_async_copy(ins[i], place, own.at[i]))
            copies[-1].start()
        for copy in copies:
            copy.wait()

    def full(array, dim):
        return jax.ShapeDtypeStruct(
            tuple(s * shards if k == dim else s for k, s in enumerate(array.shape)), array.dtype
        )

    return pl.pallas_call(
        kernel,
        out_shape=[full(a, d) for a, d in zip(arrays, dims)],
        in_specs=[VMEM] * n,
        out_specs=[HBM] * n,
        scratch_shapes=[
            pltpu.SemaphoreType.DMA((n, shards)),
            pltpu.SemaphoreType.DMA((n, shards)),
            pltpu.SemaphoreType.DMA((n,)),
        ],
        compiler_params=pltpu.CompilerParams(
            collective_id=ident, has_side_effects=True, vmem_limit_bytes=32 << 20
        ),
    )(*arrays)


piece = 32
unroll = 4


def spread(flat_ref, natural, first):
    for j in range(8):
        flat_ref[pl.ds(first * 8 + j, 8, stride=8), :] = natural[:, j * 128 : (j + 1) * 128]


def unspread(flat_ref, first):
    return jnp.concatenate([flat_ref[pl.ds(first * 8 + j, 8, stride=8), :] for j in range(8)], axis=1)


def tile(ref, t):
    return ref[pl.ds(pl.multiple_of(t * 8, 8), 8), :]


def row(ref, t, n, states):
    return ref[pl.ds(t * states + n, 8, stride=0), :]


def exchange(ends, got, send, recv, seq, width):
    me = lax.axis_index("ctx")
    copies = []
    for step in range(1, width):
        copies.append(
            pltpu.make_async_remote_copy(
                ends.at[seq],
                got.at[me, seq],
                send.at[seq, step],
                recv.at[seq, step],
                device_id={"ctx": lax.rem(me + step, width)},
                device_id_type=MESH,
            )
        )
        copies[-1].start()
    return copies


def ctx_greet(width):
    me = lax.axis_index("ctx")
    barrier = pltpu.get_barrier_semaphore()
    for step in range(1, width):
        pl.semaphore_signal(barrier, inc=1, device_id={"ctx": lax.rem(me + step, width)}, device_id_type=MESH)
    return barrier


def entering(got, seq, rate_ref, states, width, reverse):
    me = lax.axis_index("ctx")
    result = []
    for n in range(states):
        value = jnp.zeros((8, 128), f32)
        for k in reversed(range(width)) if reverse else range(width):
            new = jnp.exp2(got[k, seq, states] * rate_ref[n]) * value + got[k, seq, n]
            value = jnp.where(me < k if reverse else me > k, new, value)
        result.append(value)
    return result


def scan_forward(size, act, b_row, c_row, rate, seqs, ident):
    rows, channels = size.shape
    local = rows // seqs
    states = rate.shape[0]
    width = lax.axis_size("ctx")
    pieces = local // piece

    def kernel(
        size_ref, act_ref, b_ref, c_ref, rate_ref, y_ref, kept_ref, enter_ref, size3, drive3,
        y3, ends, got, held, send, recv, out_sem,
    ):
        pl.semaphore_wait(ctx_greet(width), width - 1)

        def lay(i, _):
            first = pl.multiple_of(i * 8, 8)
            block = size_ref[pl.ds(first, 8), :]
            spread(size3, block, first)
            spread(drive3, block * act_ref[pl.ds(first, 8), :], first)
            return 0

        lax.fori_loop(0, rows // 8, lay, 0)
        copies = []
        for seq in range(seqs):

            def first_pass(i, carried):
                values, total = list(carried[:-1]), carried[-1]
                for u in range(unroll):
                    t = seq * local + i * unroll + u
                    s, d = tile(size3, t), tile(drive3, t)
                    total = total + s
                    for n in range(states):
                        values[n] = jnp.exp2(s * rate_ref[n]) * values[n] + d * row(b_ref, t, n, states)
                return tuple(values) + (total,)

            zero = tuple(jnp.zeros((8, 128), f32) for _ in range(states + 1))
            done = lax.fori_loop(0, local // unroll, first_pass, zero)
            for n in range(states + 1):
                ends[seq, n] = done[n]
            copies.append(exchange(ends, got, send, recv, seq, width))
        me = lax.axis_index("ctx")
        for seq in range(seqs):
            for copy in copies[seq]:
                copy.wait()
            got[me, seq] = ends[seq]
            start = entering(got, seq, rate_ref, states, width, False)
            for n in range(states):
                enter_ref[seq, n] = start[n]

            def save(k, slot):
                return pltpu.make_async_copy(
                    held.at[slot], kept_ref.at[pl.ds(seq * local + k * piece, piece)], out_sem.at[slot]
                )

            def one_piece(k, carried):
                slot = lax.rem(k, 2)

                @pl.when(k >= 2)
                def _():
                    save(k - 2, slot).wait()

                def second_pass(i, values):
                    values = list(values)
                    for u in range(unroll):
                        inside = i * unroll + u
                        t = seq * local + k * piece + inside
                        s, d = tile(size3, t), tile(drive3, t)
                        acc = [None] * 4
                        for n in range(states):
                            values[n] = jnp.exp2(s * rate_ref[n]) * values[n] + d * row(b_ref, t, n, states)
                            held[slot, inside, n] = values[n]
                            part = values[n] * row(c_ref, t, n, states)
                            acc[n % 4] = part if acc[n % 4] is None else acc[n % 4] + part
                        y3[pl.ds(pl.multiple_of(t * 8, 8), 8), :] = (acc[0] + acc[1]) + (acc[2] + acc[3])
                    return tuple(values)

                carried = lax.fori_loop(0, piece // unroll, second_pass, carried)
                save(k, slot).start()
                return carried

            lax.fori_loop(0, pieces, one_piece, tuple(start))
            for k in (pieces - 2, pieces - 1):
                save(k, k % 2).wait()

        def back(i, _):
            first = pl.multiple_of(i * 8, 8)
            y_ref[pl.ds(first, 8), :] = unspread(y3, first)
            return 0

        lax.fori_loop(0, rows // 8, back, 0)

    flat = jax.ShapeDtypeStruct((rows * 8, 128), f32)
    return pl.pallas_call(
        kernel,
        out_shape=[
            jax.ShapeDtypeStruct((rows, channels), f32),
            jax.ShapeDtypeStruct((rows, states, 8, 128), f32),
            jax.ShapeDtypeStruct((seqs, states, 8, 128), f32),
            flat,
            flat,
        ],
        in_specs=[VMEM] * 5,
        out_specs=[VMEM, HBM, VMEM, VMEM, VMEM],
        scratch_shapes=[
            pltpu.VMEM((rows * 8, 128), f32),
            pltpu.VMEM((seqs, states + 1, 8, 128), f32),
            pltpu.VMEM((width, seqs, states + 1, 8, 128), f32),
            pltpu.VMEM((2, piece, states, 8, 128), f32),
            pltpu.SemaphoreType.DMA((seqs, width)),
            pltpu.SemaphoreType.DMA((seqs, width)),
            pltpu.SemaphoreType.DMA((2,)),
        ],
        compiler_params=pltpu.CompilerParams(
            collective_id=ident, has_side_effects=True, vmem_limit_bytes=48 << 20
        ),
    )(size, act, b_row, c_row, rate)


def sublane_sums(parts):
    at = lax.broadcasted_iota(jnp.int32, (8, 128), 0)
    for shift in (4, 2, 1):
        low = (at // shift) % 2 == 0
        half = len(parts) // 2
        merged = []
        for one, two in zip(parts[:half], parts[half:]):
            merged.append(
                jnp.where(low, one + pltpu.roll(one, 8 - shift, 0), two + pltpu.roll(two, shift, 0))
            )
        parts = merged
    return parts[0]


def scan_backward(size3, drive3, grad, b_row, c_row, rate, kept, enter, seqs, ident, partial, epilogue, extras, chunk):
    rows, channels = grad.shape
    local = rows // seqs
    states = rate.shape[0]
    width = lax.axis_size("ctx")
    pieces = local // piece
    early = 2
    unroll_b = 2
    line = Line(partial.shape, chunk, epilogue, extras, bf16)
    n_line, n_ex = len(line.scratch()), len(extras)

    def kernel(*refs):
        size_ref, drive_ref, grad_ref, b_ref, c_ref, rate_ref, kept_ref, enter_ref, p_ref = refs[:9]
        tb_ref, sd_ref, bg_ref, cg_ref, dec_ref, sum_ref = refs[9 + n_ex : 15 + n_ex]
        grad3, tb3, sd3, ends, got, held, bpart, cpart, prior, send, recv, in_sem = refs[15 + n_ex : 27 + n_ex]
        line.bind(p_ref, refs[9 : 9 + n_ex], sum_ref, [], refs[27 + n_ex :])
        line.begin(ctx_greet(width), width - 1)

        def lay(i, _):
            first = pl.multiple_of(i * 8, 8)
            spread(grad3, grad_ref[pl.ds(first, 8), :], first)
            return 0

        lax.fori_loop(0, rows // 8, lay, 0)

        def fetch(seq, k, slot):
            return pltpu.make_async_copy(
                kept_ref.at[pl.ds(seq * local + k * piece, piece)], held.at[slot], in_sem.at[slot]
            )

        copies = []
        for seq in range(seqs):

            def first_pass(i, carried):
                values, total = list(carried[:-1]), carried[-1]
                for u in range(unroll):
                    t = seq * local + local - 1 - (i * unroll + u)
                    s, g = tile(size_ref, t), tile(grad3, t)
                    total = total + s
                    for n in range(states):
                        values[n] = jnp.exp2(s * rate_ref[n]) * (values[n] + g * row(c_ref, t, n, states))
                return tuple(values) + (total,)

            zero = tuple(jnp.zeros((8, 128), f32) for _ in range(states + 1))
            done = zero
            for half in range(early):
                span = local // unroll // early
                done = lax.fori_loop(half * span, (half + 1) * span, first_pass, done)
                line.tick(seq * early + half)
            for n in range(states + 1):
                ends[seq, n] = done[n]
            copies.append(exchange(ends, got, send, recv, seq, width))
        me = lax.axis_index("ctx")
        for n in range(states):
            dec_ref[n] = jnp.zeros((8, 128), f32)
        for seq in range(seqs):
            fetch(seq, pieces - 1, (pieces - 1) % 2).start()
            for copy in copies[seq]:
                copy.wait()
            got[me, seq] = ends[seq]
            start = entering(got, seq, rate_ref, states, width, True)
            fetch(seq, pieces - 1, (pieces - 1) % 2).wait()

            def one_slot(slot, k, inside, adjoint, decays, prior_at):
                t = seq * local + k * piece + inside
                s, d, g = tile(size_ref, t), tile(drive_ref, t), tile(grad3, t)
                tb, sd = [None] * 2, [None] * 2
                b_parts, c_parts = [], []
                for n in range(states):
                    total = adjoint[n] + g * row(c_ref, t, n, states)
                    c_parts.append(held[slot, inside, n] * g)
                    b_parts.append(total * d)
                    through = total * row(b_ref, t, n, states)
                    adjoint[n] = jnp.exp2(s * rate_ref[n]) * total
                    kept_part = adjoint[n] * prior_at(n)
                    through_size = kept_part * rate_ref[n]
                    decays[n] = decays[n] + kept_part * s
                    tb[n % 2] = through if tb[n % 2] is None else tb[n % 2] + through
                    sd[n % 2] = through_size if sd[n % 2] is None else sd[n % 2] + through_size
                here = pl.ds(pl.multiple_of(t * 8, 8), 8)
                tb3[here, :] = tb[0] + tb[1]
                sd3[here, :] = sd[0] + sd[1]
                for h in range(states // 8):
                    spot = pl.ds(pl.multiple_of(inside * states + h * 8, 8), 8)
                    bpart[spot, :] = sublane_sums(b_parts[h * 8 : h * 8 + 8])
                    cpart[spot, :] = sublane_sums(c_parts[h * 8 : h * 8 + 8])

            def one_piece(back_k, carried):
                k = pieces - 1 - back_k
                slot = lax.rem(k, 2)

                @pl.when(k > 0)
                def _():
                    fetch(seq, k - 1, 1 - slot).start()

                def slots(i, carried):
                    adjoint, decays = list(carried[:states]), list(carried[states:])
                    for u in range(unroll_b):
                        inside = piece - 1 - (i * unroll_b + u)
                        one_slot(slot, k, inside, adjoint, decays, lambda n: held[slot, inside - 1, n])
                    return tuple(adjoint) + tuple(decays)

                carried = lax.fori_loop(0, piece // unroll_b - 1, slots, carried)
                adjoint, decays = list(carried[:states]), list(carried[states:])
                for inside in reversed(range(1, unroll_b)):
                    one_slot(slot, k, inside, adjoint, decays, lambda n: held[slot, inside - 1, n])

                @pl.when(k > 0)
                def _():
                    fetch(seq, k - 1, 1 - slot).wait()
                    prior[...] = held[1 - slot, piece - 1]

                @pl.when(k == 0)
                def _():
                    prior[...] = enter_ref[seq]

                one_slot(slot, k, 0, adjoint, decays, lambda n: prior[n])
                ones = jnp.ones((8, 128), bf16)
                for part, out in ((bpart, bg_ref), (cpart, cg_ref)):
                    sums = outer_cols(ones, part[...].astype(bf16))
                    out[pl.ds(seq * pieces + k, 1)] = sums[None]
                line.tick(seqs * early + seq * pieces + back_k)
                return tuple(adjoint) + tuple(decays)

            zero = tuple(jnp.zeros((8, 128), f32) for _ in range(states))
            carried = lax.fori_loop(0, pieces, one_piece, tuple(start) + zero)
            for n in range(states):
                dec_ref[n] = dec_ref[n] + carried[states + n]

        def back(i, _):
            first = pl.multiple_of(i * 8, 8)
            tb_ref[pl.ds(first, 8), :] = unspread(tb3, first)
            sd_ref[pl.ds(first, 8), :] = unspread(sd3, first)
            return 0

        lax.fori_loop(0, rows // 8, back, 0)
        for c in range(seqs * (early + pieces), line.ticks()):
            line.tick(c)
        line.finish()

    nat = jax.ShapeDtypeStruct((rows, channels), f32)
    sums = jax.ShapeDtypeStruct((rows // piece, 8, piece * states), f32)
    return pl.pallas_call(
        kernel,
        out_shape=[nat, nat, sums, sums, jax.ShapeDtypeStruct((states, 8, 128), f32),
                   jax.ShapeDtypeStruct(partial.shape, bf16)],
        in_specs=[VMEM] * 6 + [HBM, VMEM] + [HBM] * (1 + n_ex),
        out_specs=[VMEM] * 6,
        scratch_shapes=[pltpu.VMEM((rows * 8, 128), f32)] * 3
        + [
            pltpu.VMEM((seqs, states + 1, 8, 128), f32),
            pltpu.VMEM((width, seqs, states + 1, 8, 128), f32),
            pltpu.VMEM((2, piece, states, 8, 128), f32),
            pltpu.VMEM((piece * states, 128), f32),
            pltpu.VMEM((piece * states, 128), f32),
            pltpu.VMEM((states, 8, 128), f32),
            pltpu.SemaphoreType.DMA((seqs, width)),
            pltpu.SemaphoreType.DMA((seqs, width)),
            pltpu.SemaphoreType.DMA((2,)),
        ]
        + line.scratch(),
        compiler_params=pltpu.CompilerParams(
            collective_id=ident, has_side_effects=True, vmem_limit_bytes=58 << 20
        ),
    )(size3, drive3, grad, b_row, c_row, rate, kept, enter, partial, *extras)


def body(
    hidden_in, lengths, cotangent, norm_gain, in_weight, conv_weight, conv_bias, low_weight, step_weight,
    step_bias, decay_log, skip_gain, out_weight, ffn_gain, gate_up, down_weight,
):
    seqs, local, width = hidden_in.shape
    rows = seqs * local
    shards, pieces = lax.axis_size("shard"), lax.axis_size("ctx")
    inner = in_weight.shape[2]
    taps = conv_weight.shape[0]
    rank = step_weight.shape[0]
    states = decay_log.shape[0]
    low_len = low_weight.shape[0]

    small = jnp.concatenate(
        [low_weight, step_weight, decay_log, conv_weight, conv_bias[None], step_bias[None], skip_gain[None]], axis=0
    )
    small = jnp.pad(small, ((0, -small.shape[0] % 16), (0, 0)))
    gains = jnp.stack([norm_gain, ffn_gain])
    gains = jnp.pad(gains, ((0, 14), (0, 0)))
    in_half = in_weight.transpose(1, 0, 2)
    small, gains, in_w = shard_gather([small, gains, in_half], [1, 1, 1], 0)
    out_parts = lax.all_gather(out_weight, "shard")
    gate_half = gate_up.transpose(1, 0, 2)
    gate_w = [lax.all_gather(gate_half[c], "shard", axis=0, tiled=True) for c in range(2)]
    down_parts = lax.all_gather(down_weight, "shard")
    part = width // shards

    low_w = small[:low_len]
    step_w = small[low_len : low_len + rank]
    at = low_len + rank
    decay_w = small[at : at + states].astype(f32)
    kernel = small[at + states : at + states + taps].astype(f32)
    conv_b = small[at + states + taps].astype(f32)
    step_b = small[at + states + taps + 1].astype(f32)
    skip_full = small[at + states + taps + 2].astype(f32)
    gain_one, gain_two = gains[0:1].astype(f32), gains[1:2].astype(f32)

    first_slot = lax.axis_index("ctx") * local
    positions = first_slot + jnp.arange(local, dtype=jnp.int32)
    pad_mask = (positions[None, :] < lengths[:, None]).astype(f32)

    ahead = lax.ppermute(hidden_in[:, local - taps + 1 :], "ctx", [(k, k + 1) for k in range(pieces - 1)])
    longer = jnp.concatenate([ahead, hidden_in], axis=1).astype(f32)
    normed_all = (longer * rms_scale(longer) * gain_one).astype(bf16)
    source = hidden_in.reshape(rows, width).astype(f32)
    normed_one = normed_all[:, taps - 1 :].reshape(rows, width)
    normed_edge = normed_all[:, : taps - 1].reshape(seqs * (taps - 1), width)
    edge_in = jnp.dot(normed_edge, in_w[0], preferred_element_type=f32).astype(bf16)
    conv_in = jnp.dot(normed_one, in_w[0], preferred_element_type=f32).astype(bf16)
    gate_z = jnp.dot(normed_one, in_w[1], preferred_element_type=f32)
    padded = jnp.concatenate(
        [edge_in.reshape(seqs, taps - 1, inner), conv_in.reshape(seqs, local, inner)], axis=1
    ).astype(f32)
    pre_act = conv_b + sum(kernel[k] * padded[:, k : k + local] for k in range(taps))
    pre_act = pre_act.reshape(rows, inner)
    act_half = jax.nn.silu(pre_act).astype(bf16)
    act_full = act_half.astype(f32)

    low_part = outer_cols(low_w, act_half).astype(bf16)
    low_all = tp_sum(low_part, plain_end, [], [], 80, 1, f32)[0]
    step_low = low_all[:rank].astype(bf16)
    b_in, c_out = low_all[rank : rank + states], low_all[rank + states :]
    b_row, c_row = (
        jnp.broadcast_to(v.T[:, :, None], (rows, states, 128)).reshape(rows * states, 128) for v in (b_in, c_out)
    )
    step_pre = inner_rows(step_low, step_w) + step_b
    step_size = jax.nn.softplus(step_pre)
    decay_rate = -jnp.exp(decay_w)
    rate = (decay_rate * log2e).reshape(states, 8, 128)
    scan_y, kept, enter, size3, drive3 = scan_forward(step_size, act_full, b_row, c_row, rate, seqs, 2)
    scan_out = scan_y + skip_full * act_full
    gate_act = jax.nn.silu(gate_z)
    gated_out = (scan_out * gate_act).astype(bf16)
    mixed_part = jnp.concatenate(
        [jnp.dot(gated_out, out_parts[k], preferred_element_type=f32) for k in range(shards)], axis=1
    ).astype(bf16)
    wide = jax.ShapeDtypeStruct((rows, width), f32)
    hidden_rows = hidden_in.reshape(rows, width)
    normed_two, middle = tp_sum(mixed_part, norm_end, [hidden_rows, gain_two], [wide], 32, 3)
    gate_lin, up_lin = (jnp.dot(normed_two, gate_w[c], preferred_element_type=f32) for c in range(2))
    hidden_ffn = (jax.nn.silu(gate_lin) * up_lin).astype(bf16)
    ffn_part = jnp.concatenate(
        [jnp.dot(hidden_ffn, down_parts[k], preferred_element_type=f32) for k in range(shards)], axis=1
    ).astype(bf16)

    upstream = cotangent.reshape(rows, width).astype(f32) * pad_mask.reshape(rows, 1)
    ffn_grad = upstream.astype(bf16)
    down_grad = inner_rows(ffn_grad, hidden_ffn).astype(bf16)
    hidden_grad = sum(outer_cols(ffn_grad[:, k * part : (k + 1) * part], down_parts[k]) for k in range(shards))
    gate_grad = (hidden_grad * up_lin * silu_grad(gate_lin)).astype(bf16)
    up_grad = (hidden_grad * jax.nn.silu(gate_lin)).astype(bf16)
    gate_up_grad = [inner_rows(normed_two, g).astype(bf16) for g in (gate_grad, up_grad)]
    back_part = (outer_cols(gate_grad, gate_w[0]) + outer_cols(up_grad, gate_w[1])).astype(bf16)
    mix_grad, middle_grad, *ffn_shares = tp_sum(
        back_part, norm_back_end, [middle, gain_two, ffn_grad], [wide], 32, 5, scatters=gate_up_grad + [down_grad]
    )
    ffn_gain_grad = jnp.sum(back_part.astype(f32) * normed_two.astype(f32), axis=0) / gain_two[0]

    out_weight_grad = inner_rows(mix_grad, gated_out).astype(bf16)
    gated_grad = sum(outer_cols(mix_grad[:, k * part : (k + 1) * part], out_parts[k]) for k in range(shards))
    scan_grad = gated_grad * gate_act
    z_grad = gated_grad * scan_out * silu_grad(gate_z)
    skip_gain_grad = jnp.sum(scan_grad * act_full, axis=0)
    through_b, through_decay, b_sums, c_sums, decay_sum, mixed_out = scan_backward(
        size3, drive3, scan_grad, b_row, c_row, rate, kept, enter, seqs, 6, ffn_part, add_end, [middle], 32
    )
    mixed_out = mixed_out.reshape(hidden_in.shape)
    decay_log_grad = decay_sum.reshape(states, inner) * decay_rate
    size_grad = act_full * through_b + through_decay * (1.0 / log2e)
    step_grad = (size_grad * jax.nn.sigmoid(step_pre)).astype(bf16)
    step_bias_grad = jnp.sum(step_grad.astype(f32), axis=0)
    step_weight_grad = jnp.dot(step_low, step_grad, preferred_element_type=f32)
    low_back = jnp.concatenate(
        [
            outer_cols(step_w, step_grad),
            b_sums[:, 0].reshape(rows, states).T,
            c_sums[:, 0].reshape(rows, states).T,
        ],
        axis=0,
    ).astype(bf16)
    low_grad = tp_sum(low_back, plain_end, [], [], 80, 7)[0]
    low_weight_grad = jnp.dot(low_grad, act_half, preferred_element_type=f32)
    act_grad = skip_full * scan_grad + step_size * through_b + inner_rows(low_grad, low_w)
    pre_grad = (act_grad * silu_grad(pre_act)).reshape(seqs, local, inner)
    conv_bias_grad = jnp.sum(pre_grad, axis=(0, 1))
    conv_weight_grad = jnp.stack(
        [jnp.sum(pre_grad * padded[:, k : k + local], axis=(0, 1)) for k in range(taps)]
    )
    behind = lax.ppermute(pre_grad[:, : taps - 1], "ctx", [(k + 1, k) for k in range(pieces - 1)])
    pre_long = jnp.concatenate([pre_grad, behind], axis=1)
    conv_grad = sum(kernel[k] * pre_long[:, taps - 1 - k : taps - 1 - k + local] for k in range(taps))
    conv_grad = conv_grad.reshape(rows, inner).astype(bf16)
    z_half = z_grad.astype(bf16)
    in_weight_grad = [inner_rows(normed_one, g).astype(bf16) for g in (conv_grad, z_half)]
    first_part = (outer_cols(conv_grad, in_w[0]) + outer_cols(z_half, in_w[1])).astype(bf16)
    norm_gain_grad = jnp.sum(first_part.astype(f32) * source * rms_scale(source), axis=0)
    small_grads = jnp.concatenate(
        [low_weight_grad, step_weight_grad, decay_log_grad, conv_weight_grad, conv_bias_grad[None],
         step_bias_grad[None], skip_gain_grad[None]], axis=0,
    )
    places = shards * pieces
    lines, lane = small_grads.shape[0], inner // places
    small_blocks = small_grads.reshape(lines, places, lane).transpose(1, 0, 2).reshape(places, lines * lane)
    small_rows = -(-lines * lane // (16 * inner)) * 16
    small_blocks = jnp.pad(small_blocks, ((0, 0), (0, small_rows * inner - lines * lane)))
    small_blocks = small_blocks.reshape(places * small_rows, inner).astype(bf16)
    share = width // places
    gain_blocks = jnp.concatenate([norm_gain_grad.reshape(places, share), ffn_gain_grad.reshape(places, share)], axis=1)
    gain_blocks = jnp.pad(gain_blocks[:, None], ((0, 0), (0, 15), (0, inner - 2 * share))).astype(bf16)
    input_grad, in_share, z_share, out_share, small_share, gain_share = tp_sum(
        first_part, norm_back_end, [hidden_rows, gain_one, middle_grad], [], 32, 8,
        scatters=in_weight_grad + [out_weight_grad, small_blocks, gain_blocks.reshape(places * 16, inner)],
        line_too=True,
    )
    input_grad = input_grad.astype(f32).reshape(hidden_in.shape)
    small_out = small_share.reshape(-1)[: lines * lane].reshape(lines, lane)
    at = low_len + rank
    return (
        mixed_out,
        input_grad,
        gain_share[0, :share],
        jnp.stack([in_share, z_share], axis=1),
        small_out[at + states : at + states + taps],
        small_out[at + states + taps],
        small_out[:low_len],
        small_out[low_len : low_len + rank],
        small_out[at + states + taps + 1],
        small_out[at : at + states],
        small_out[at + states + taps + 2],
        out_share.T,
        gain_share[0, share : 2 * share],
        jnp.stack(ffn_shares[:2], axis=1),
        ffn_shares[2].T,
    )


def solution(mesh):
    placed = (
        P("shard", "ctx", None),
        P("shard"),
        P("shard", "ctx", None),
        P("shard"),
        P("shard", None, "tp"),
        P(None, ("tp", "shard")),
        P(("tp", "shard")),
        P(None, ("tp", "shard")),
        P(None, ("tp", "shard")),
        P(("tp", "shard")),
        P(None, ("tp", "shard")),
        P(("tp", "shard")),
        P("tp", "shard"),
        P("shard"),
        P("shard", None, "tp"),
        P("tp", "shard"),
    )
    return jax.shard_map(
        body,
        mesh=mesh,
        in_specs=placed,
        out_specs=(
            P("shard", "ctx", None),
            P("shard", "ctx", None),
            P(("shard", "ctx")),
            P(("shard", "ctx"), None, "tp"),
            P(None, ("tp", "shard", "ctx")),
            P(("tp", "shard", "ctx")),
            P(None, ("tp", "shard", "ctx")),
            P(None, ("tp", "shard", "ctx")),
            P(("tp", "shard", "ctx")),
            P(None, ("tp", "shard", "ctx")),
            P(("tp", "shard", "ctx")),
            P("tp", ("shard", "ctx")),
            P(("shard", "ctx")),
            P(("shard", "ctx"), None, "tp"),
            P("tp", ("shard", "ctx")),
        ),
        check_vma=False,
    )
```

```python
import functools

import jax
import jax.numpy as jnp
from jax import lax
from jax.experimental import pallas as pl
from jax.experimental.pallas import tpu as pltpu
from jax.sharding import PartitionSpec as P

MESH = pl.DeviceIdType.MESH
epsilon = 1e-05
log2e = 1.4426950408889634
bf16 = jnp.bfloat16
f32 = jnp.float32
VMEM = pl.BlockSpec(memory_space=pltpu.VMEM)
HBM = pl.BlockSpec(memory_space=pl.ANY)


def inner_rows(left, right):
    return lax.dot_general(left, right, (((0,), (0,)), ((), ())), preferred_element_type=f32)


def outer_cols(left, right):
    return lax.dot_general(left, right, (((1,), (1,)), ((), ())), preferred_element_type=f32)


def silu_grad(values):
    sig_val = jax.nn.sigmoid(values)
    return sig_val * (1.0 + values * (1.0 - sig_val))


def rms_scale(source):
    return lax.rsqrt(jnp.mean(source * source, axis=-1, keepdims=True) + epsilon)


class Line:
    lag = 3
    ahead = 4

    def __init__(self, shape, chunk, epilogue, extras, out_dtype):
        self.shape, self.chunk, self.epilogue, self.out_dtype = shape, chunk, epilogue, out_dtype
        self.count = shape[0] // chunk
        self.extras = [(e.shape, e.dtype) for e in extras]

    def scratch(self):
        return (
            [pltpu.VMEM(self.shape, bf16)] * 4
            + [pltpu.SemaphoreType.DMA((self.count,))] * 6
            + [pltpu.VMEM(shape, dtype) for shape, dtype in self.extras]
            + [pltpu.SemaphoreType.DMA((1 + len(self.extras),))]
        )

    def bind(self, p_ref, ins, out_ref, outs, scratch):
        self.p_ref, self.given, self.out_ref, self.outs = p_ref, ins, out_ref, outs
        (self.p, self.got_a, self.pair, self.got_b, self.a_send, self.a_recv, self.b_send, self.b_recv,
         self.c_send, self.c_recv) = scratch[:10]
        self.ins, self.in_sem = scratch[10:-1], scratch[-1]
        me = lax.axis_index("tp")
        self.mate = me + 1 - 2 * (me % 2)
        self.across = 3 - me
        self.middle = jnp.logical_or(me == 1, me == 2)

    def at(self, c):
        return pl.ds(pl.multiple_of(c * self.chunk, self.chunk), self.chunk)

    def remote(self, source, target, send, recv, c, to):
        return pltpu.make_async_remote_copy(
            source.at[self.at(c)], target.at[self.at(c)], send.at[c], recv.at[c], device_id={"tp": to}, device_id_type=MESH
        )

    def copy_a(self, c):
        return self.remote(self.p_ref, self.got_a, self.a_send, self.a_recv, c, self.mate)

    def copy_b(self, c):
        return self.remote(self.pair, self.got_b, self.b_send, self.b_recv, c, self.across)

    def copy_c(self, c):
        return self.remote(self.out_ref, self.out_ref, self.c_send, self.c_recv, c, self.mate)

    def loads(self):
        pairs = [(self.p_ref, self.p)] + list(zip(self.given, self.ins))
        return [pltpu.make_async_copy(a, b, self.in_sem.at[i]) for i, (a, b) in enumerate(pairs)]

    def begin(self, barrier, met, ends_meet=False):
        pl.semaphore_signal(barrier, inc=1, device_id={"tp": self.mate}, device_id_type=MESH)

        @pl.when(self.middle)
        def _():
            pl.semaphore_signal(barrier, inc=1, device_id={"tp": self.across}, device_id_type=MESH)
            for load in self.loads():
                load.start()
            pl.semaphore_wait(barrier, met + 2)
            for load in self.loads():
                load.wait()

        @pl.when(jnp.logical_not(self.middle))
        def _():
            if ends_meet:
                pl.semaphore_signal(barrier, inc=1, device_id={"tp": self.across}, device_id_type=MESH)
            pl.semaphore_wait(barrier, met + 2 if ends_meet else met + 1)

            for c in range(min(self.ahead, self.count)):
                self.copy_a(c).start()

    def greet(self, barrier, met):
        pl.semaphore_signal(barrier, inc=1, device_id={"tp": self.mate}, device_id_type=MESH)

        @pl.when(self.middle)
        def _():
            pl.semaphore_signal(barrier, inc=1, device_id={"tp": self.across}, device_id_type=MESH)
            pl.semaphore_wait(barrier, met + 2)

        @pl.when(jnp.logical_not(self.middle))
        def _():
            pl.semaphore_wait(barrier, met + 1)

    def start(self):
        @pl.when(jnp.logical_not(self.middle))
        def _():
            for c in range(min(self.ahead, self.count)):
                self.copy_a(c).start()

    def first(self, c):
        at = self.at(c)
        self.copy_a(c).wait_recv()
        self.pair[at, :] = (self.p[at, :].astype(f32) + self.got_a[at, :].astype(f32)).astype(bf16)
        self.copy_b(c).start()

    def second(self, c):
        at = self.at(c)
        self.copy_b(c).wait_recv()
        total = self.pair[at, :].astype(f32) + self.got_b[at, :].astype(f32)
        self.epilogue(c, at, total, self.ins, self.out_ref, self.outs)
        self.copy_c(c).start()

    def tick(self, c):
        lag = min(self.lag, self.count)

        @pl.when(jnp.logical_and(self.middle, c < self.count))
        def _():
            self.first(c)

        @pl.when(jnp.logical_and(self.middle, jnp.logical_and(c >= lag, c < self.count + lag)))
        def _():
            self.second(c - lag)

        @pl.when(jnp.logical_and(jnp.logical_not(self.middle), c + self.ahead < self.count))
        def _():
            self.copy_a(c + self.ahead).start()

    def ticks(self):
        return self.count + min(self.lag, self.count)

    def finish(self):
        @pl.when(self.middle)
        def _():
            def drain(c, _):
                self.copy_b(c).wait_send()
                self.copy_c(c).wait_send()
                return 0

            lax.fori_loop(0, self.count, drain, 0)

        @pl.when(jnp.logical_not(self.middle))
        def _():
            def take(c, _):
                self.copy_c(c).wait_recv()
                self.copy_a(c).wait_send()
                return 0

            lax.fori_loop(0, self.count, take, 0)


share_lag = 2
share_ahead = 2


class Halving:
    def __init__(self, arrays, step_rows=16):
        self.step_rows = step_rows
        shards, pieces = lax.axis_size("shard"), lax.axis_size("ctx")
        self.n = len(arrays)
        self.bits = [
            (axis, 1 << k)
            for axis, size in (("shard", shards), ("ctx", pieces))
            for k in reversed(range(size.bit_length() - 1))
        ]
        self.depth = len(self.bits)
        head = shards.bit_length() - 1
        self.dims = list(range(self.depth))
        self.orders = (self.dims, self.dims[:head] + self.dims[head:][::-1])
        self.parts = [g.shape[0] // (shards * pieces) // step_rows for g in arrays]
        self.folded = [g.reshape((2,) * self.depth + (p * step_rows, g.shape[1])) for g, p in zip(arrays, self.parts)]
        self.tails = [g.shape[self.depth :] for g in self.folded]
        self.pairs = (max(self.parts, default=0) + 1) // 2
        self.turns = self.pairs + share_lag * (self.depth - 1)

    def results(self):
        return [jax.ShapeDtypeStruct(tail, f32) for tail in self.tails]

    def scratch(self):
        if not self.n:
            return []
        held = [pltpu.VMEM((2,) * (self.depth - 1) + tail, bf16) for tail in self.tails]
        for j in range(self.depth):
            held += [pltpu.VMEM((2,) * (self.depth - 1 - j) + tail, bf16) for tail in self.tails]
        sem = pltpu.SemaphoreType.DMA((self.depth, self.n, max(self.parts)))
        return held + [sem, sem, pltpu.SemaphoreType.DMA((self.n, max(self.parts)))]

    def bind(self, full, shares, scratch):
        n = self.n
        self.partner, self.mine = [], []
        if not n:
            return
        self.full, self.shares, self.own = full, shares, scratch[:n]
        self.landed = [scratch[n * (j + 1) : n * (j + 2)] for j in range(self.depth)]
        self.send, self.recv, self.own_sem = scratch[n * (self.depth + 1) :]
        for axis, bit in self.bits:
            here = lax.axis_index(axis)
            self.mine.append((here // bit) % 2)
            self.partner.append({axis: here + bit - 2 * bit * ((here // bit) % 2)})

    def greet(self, barrier):
        for who in self.partner:
            pl.semaphore_signal(barrier, inc=1, device_id=who, device_id_type=MESH)
        return len(self.partner)

    def spot(self, c):
        return pl.ds(pl.multiple_of(c * self.step_rows, self.step_rows), self.step_rows)

    def pick(self, remaining, dim, index, c):
        return tuple(index if d == dim else slice(None) for d in remaining) + (self.spot(c), slice(None))

    def rest(self, order, j):
        return [d for d in self.dims if d not in order[:j]]

    def copy(self, j, a, c, order):
        source = self.full[a] if j == 0 else self.landed[j - 1][a]
        d = order[j]
        return pltpu.make_async_remote_copy(
            source.at[self.pick(self.rest(order, j), d, 1 - self.mine[d], c)],
            self.landed[j][a].at[self.pick(self.rest(order, j + 1), None, None, c)],
            self.send.at[j, a, c],
            self.recv.at[j, a, c],
            device_id=self.partner[d],
            device_id_type=MESH,
        )

    def own_copy(self, a, c, order):
        return pltpu.make_async_copy(
            self.full[a].at[self.pick(self.dims, order[0], self.mine[order[0]], c)],
            self.own[a].at[self.pick(self.rest(order, 1), None, None, c)],
            self.own_sem.at[a, c],
        )

    def begin(self, a, c, order):
        self.copy(0, a, c, order).start()
        self.own_copy(a, c, order).start()

    def step(self, j, a, c, order):
        self.copy(j, a, c, order).wait_recv()
        where = self.pick(self.rest(order, j + 1), None, None, c)
        d = order[j]
        if j == 0:
            self.own_copy(a, c, order).wait()
            kept = self.own[a][where]
        else:
            kept = self.landed[j - 1][a][self.pick(self.rest(order, j), d, self.mine[d], c)]
        total = kept.astype(f32) + self.landed[j][a][where].astype(f32)
        if j == self.depth - 1:
            self.shares[a][self.spot(c), :] = total
        else:
            self.landed[j][a][where] = total.astype(bf16)
            self.copy(j + 1, a, c, order).start()

    def each(self, i, fn):
        for parity in (0, 1):
            c = 2 * i + parity
            for a in range(self.n):

                @pl.when(jnp.logical_and(c >= 0, c < self.parts[a]))
                def _():
                    fn(a, c, self.orders[parity])

    def start(self):
        for i in range(share_ahead if self.n else 0):
            self.each(i, self.begin)

    def tick(self, i):
        if self.n:
            self.each(i + share_ahead, self.begin)
            for j in range(self.depth):
                self.each(i - share_lag * j, functools.partial(self.step, j))

    def finish(self):
        def sent(i, _):
            for j in range(self.depth):
                self.each(i, lambda a, c, order: self.copy(j, a, c, order).wait_send())
            return 0

        if self.n:
            lax.fori_loop(0, self.pairs, sent, 0)


def tp_sum(partial, epilogue, extras, extra_outs, chunk, ident, out_dtype=bf16, scatters=(), line_too=False):
    line = Line(partial.shape, chunk, epilogue, extras, out_dtype)
    share = Halving(scatters)
    n_ex, n_out, n_sc = len(extras), len(extra_outs), len(scatters)
    n_line, n_share = len(line.scratch()), len(share.scratch())

    def kernel(*refs):
        refs = list(refs)

        def take_refs(n):
            taken = refs[:n]
            del refs[:n]
            return taken

        (p_ref,) = take_refs(1)
        ins = take_refs(n_ex)
        full = take_refs(n_sc)
        (out_ref,) = take_refs(1)
        outs = take_refs(n_out)
        shares = take_refs(n_sc)
        line.bind(p_ref, ins, out_ref, outs, take_refs(n_line))
        share.bind(full, shares, take_refs(n_share))
        tail, tail_send, tail_recv = take_refs(3) if line_too else (None, None, None)
        barrier = pltpu.get_barrier_semaphore()
        line.begin(barrier, share.greet(barrier), line_too)
        share.start()

        def turn(i, _):
            for parity in (0, 1):
                line.tick(2 * i + parity)
            share.tick(i)
            return 0

        turns = (line.ticks() + 1) // 2
        lax.fori_loop(0, max(turns, share.turns) if n_sc else turns, turn, 0)
        if line_too:
            height = shares[-1].shape[0]
            last = pl.ds(height - 8, 8)
            for k, to in enumerate((line.mate, line.across)):
                copy = pltpu.make_async_remote_copy(
                    shares[-1].at[last] if k == 0 else tail.at[2], tail.at[k], tail_send.at[k], tail_recv.at[k],
                    device_id={"tp": to}, device_id_type=MESH,
                )
                copy.start()
                copy.wait()
                if k == 0:
                    tail[2] = shares[-1][last, :] + tail[0]
            shares[-1][last, :] = tail[2] + tail[1]
        line.finish()
        share.finish()

    buffers = []
    if line_too:
        pair_sem = pltpu.SemaphoreType.DMA((2,))
        buffers += [pltpu.VMEM((3, 8, scatters[-1].shape[-1]), f32), pair_sem, pair_sem]
    return pl.pallas_call(
        kernel,
        out_shape=[jax.ShapeDtypeStruct(partial.shape, out_dtype)] + list(extra_outs) + share.results(),
        in_specs=[HBM] * (1 + n_ex + n_sc),
        out_specs=[VMEM] * (1 + n_out + n_sc),
        scratch_shapes=line.scratch() + share.scratch() + buffers,
        compiler_params=pltpu.CompilerParams(
            collective_id=ident, has_side_effects=True, vmem_limit_bytes=56 << 20
        ),
    )(partial, *extras, *share.folded)


def plain_end(c, rows, total, ins, out_ref, outs):
    out_ref[rows, :] = total.astype(out_ref.dtype)


def norm_end(c, rows, total, ins, out_ref, outs):
    source_ref, gain_ref = ins
    middle = source_ref[rows, :].astype(f32) + total
    outs[0][rows, :] = middle
    out_ref[rows, :] = (middle * rms_scale(middle) * gain_ref[...]).astype(bf16)


def add_end(c, rows, total, ins, out_ref, outs):
    out_ref[rows, :] = (ins[0][rows, :] + total).astype(bf16)


def norm_back_end(c, rows, total, ins, out_ref, outs):
    source = ins[0][rows, :].astype(f32)
    inv = rms_scale(source)
    weighted = total * ins[1][...]
    back = inv * weighted - source * (inv * inv * inv) * jnp.mean(weighted * source, axis=-1, keepdims=True)
    result = ins[2][rows, :] + back
    if outs:
        outs[0][rows, :] = result
    out_ref[rows, :] = result.astype(bf16)


halo = 16
tile_cols = 256


def front(hidden, in_half, small, gains, seqs, at_conv, taps, low_len, ident):
    rows, width = hidden.shape
    local = rows // seqs
    part, inner = in_half.shape[1:]
    shards, pieces = lax.axis_size("shard"), lax.axis_size("ctx")
    long = local + halo
    tiles = inner // tile_cols
    line = Line((low_len, rows), 80, plain_end, [], f32)
    n_line = len(line.scratch())

    def kernel(
        hid_ref, tail_ref, in_ref, small_ref, gain_ref,
        in_out, small_out, gain_out, normed_out, z_out, ext_out, pre_out, act_out, low_out,
        own_w, got_w, edge, normed, ext_n, acc, z_val, conv_f, ext_c, pre, act, low_acc, small_all, gain_all,
        send, recv, edge_sem, own_sem, out_sem, *rest
    ):
        me, ctx = lax.axis_index("shard"), lax.axis_index("ctx")
        barrier = pltpu.get_barrier_semaphore()
        line.bind(rest[0], [], low_out, [], list(rest))
        for step in range(1, shards):
            pl.semaphore_signal(barrier, inc=1, device_id={"shard": lax.rem(me + step, shards)}, device_id_type=MESH)
        pl.semaphore_signal(barrier, inc=1, device_id={"ctx": lax.rem(ctx + pieces - 1, pieces)}, device_id_type=MESH)
        load = pltpu.make_async_copy(in_ref, own_w, own_sem.at[0])
        load.start()
        small_size, gain_size = small_ref.shape[1], gain_ref.shape[1]
        small_at = pl.ds(pl.multiple_of(me * small_size, small_size), small_size)
        gain_at = pl.ds(pl.multiple_of(me * gain_size, gain_size), gain_size)
        small_all[:, small_at] = small_ref[...]
        gain_all[:, gain_at] = gain_ref[...]
        line.greet(barrier, shards)
        edge_copy = pltpu.make_async_remote_copy(
            tail_ref, edge, edge_sem.at[0], edge_sem.at[1],
            device_id={"ctx": lax.rem(ctx + 1, pieces)}, device_id_type=MESH,
        )
        copies = {}
        for step in range(1, shards):
            peer = {"shard": lax.rem(me + step, shards)}
            moves = [(gain_ref, gain_all.at[:, gain_at]), (small_ref, small_all.at[:, small_at])]
            moves += [(in_ref.at[c], got_w.at[step - 1, c]) for c in range(2)]
            for k, (source, target) in enumerate(moves):
                copies[step, k] = pltpu.make_async_remote_copy(
                    source, target, send.at[step, k], recv.at[step, k], device_id=peer, device_id_type=MESH
                )
        for k in range(4):
            for step in range(1, shards):
                copies[step, k].start()
            if k == 0:
                edge_copy.start()
        for step in range(1, shards):
            copies[step, 0].wait_recv()
        gain = gain_all[0:1, :].astype(f32)

        def norm_rows(i, _):
            at = pl.ds(pl.multiple_of(i * 16, 16), 16)
            source = hid_ref[at, :].astype(f32)
            value = (source * rms_scale(source) * gain).astype(bf16)
            normed[at, :] = value
            seq = i // (local // 16)
            ext_n[pl.ds(pl.multiple_of(i * 16 + (seq + 1) * halo, 16), 16), :] = value
            return 0

        lax.fori_loop(0, rows // 16, norm_rows, 0)
        edge_copy.wait_recv()
        for seq in range(seqs):
            source = edge[seq].astype(f32)
            value = source * rms_scale(source) * gain * (ctx > 0).astype(f32)
            ext_n[seq * long : seq * long + halo, :] = value.astype(bf16)
        outs = [(normed, normed_out)]
        pltpu.make_async_copy(normed, normed_out, out_sem.at[0]).start()

        def cols(c, j):
            return pl.ds(pl.multiple_of(c * inner + j * tile_cols, tile_cols), tile_cols)

        def finish_conv(j):
            here = pl.ds(pl.multiple_of(j * tile_cols, tile_cols), tile_cols)
            value = acc[:, cols(0, j)].astype(bf16)
            ext_c[:, here] = value
            conv_f[...] = value.astype(f32)
            weights = small_all[at_conv : at_conv + 16, here].astype(f32)
            for seq in range(seqs):
                for k in range(local // 64):
                    first = seq * long + halo + k * 64
                    total = weights[taps : taps + 1]
                    for tap in range(taps):
                        total = total + weights[tap : tap + 1] * conv_f[first - taps + 1 + tap : first - taps + 1 + tap + 64, :]
                    to = slice(seq * local + k * 64, seq * local + (k + 1) * 64)
                    pre[to, here] = total
                    act[to, here] = jax.nn.silu(total).astype(bf16)
            low = outer_cols(small_all[0:low_len, here], act[:, here])
            low_acc[...] = low_acc[...] + low

        def finish_gate(j):
            here = pl.ds(pl.multiple_of(j * tile_cols, tile_cols), tile_cols)
            for seq in range(seqs):
                z_val[seq * local : (seq + 1) * local, here] = acc[seq * long + halo : (seq + 1) * long, cols(1, j)]

        low_acc[...] = jnp.zeros_like(low_acc)
        own_place = pl.ds(pl.multiple_of(me * part, part), part)
        load.wait()
        own_save = pltpu.make_async_copy(own_w, in_out.at[:, own_place], own_sem.at[1])
        own_save.start()
        saves = []
        for step in range(shards):
            owner = lax.rem(me - step + shards, shards)
            place = pl.ds(pl.multiple_of(owner * part, part), part)
            last = step == shards - 1
            if last:
                for other in range(1, shards):
                    copies[other, 1].wait_recv()
            for c in range(2):
                weight = own_w.at[c] if step == 0 else got_w.at[step - 1, c]
                if step > 0:
                    copies[step, 2 + c].wait_recv()

                def matmul(j, _):
                    here = pl.ds(pl.multiple_of(j * tile_cols, tile_cols), tile_cols)
                    value = jnp.dot(ext_n[:, place], weight[:, here], preferred_element_type=f32)
                    acc[:, cols(c, j)] = value if step == 0 else acc[:, cols(c, j)] + value
                    if last:
                        (finish_conv, finish_gate)[c](j)
                    return 0

                lax.fori_loop(0, tiles, matmul, 0)
            if step > 0:
                saves.append(pltpu.make_async_copy(got_w.at[step - 1], in_out.at[:, place], own_sem.at[1 + step]))
                saves[-1].start()
        line.p[...] = low_acc[...].astype(bf16)
        outs += [(z_val, z_out), (ext_c, ext_out), (pre, pre_out), (act, act_out), (small_all, small_out), (gain_all, gain_out)]
        for k, (source, target) in enumerate(outs):
            if k:
                pltpu.make_async_copy(source, target, out_sem.at[k]).start()
        line.start()
        for c in range(line.ticks()):
            line.tick(c)
        line.finish()
        for save in saves + [own_save]:
            save.wait()
        for k, (source, target) in enumerate(outs):
            pltpu.make_async_copy(source, target, out_sem.at[k]).wait()
        for copy in copies.values():
            copy.wait_send()
        edge_copy.wait_send()

    sds = jax.ShapeDtypeStruct
    tails = hidden.reshape(seqs, local, width)[:, local - halo :]
    return pl.pallas_call(
        kernel,
        out_shape=[
            sds((2, shards * part, inner), bf16),
            sds((small.shape[0], small.shape[1] * shards), bf16),
            sds((gains.shape[0], gains.shape[1] * shards), bf16),
            sds((rows, width), bf16),
            sds((rows, inner), f32),
            sds((seqs * long, inner), bf16),
            sds((rows, inner), f32),
            sds((rows, inner), bf16),
            sds((low_len, rows), f32),
        ],
        in_specs=[VMEM, HBM, HBM, VMEM, VMEM],
        out_specs=[HBM] * 8 + [VMEM],
        scratch_shapes=[
            pltpu.VMEM((2, part, inner), bf16),
            pltpu.VMEM((max(shards - 1, 1), 2, part, inner), bf16),
            pltpu.VMEM((seqs, halo, width), bf16),
            pltpu.VMEM((rows, width), bf16),
            pltpu.VMEM((seqs * long, width), bf16),
            pltpu.VMEM((seqs * long, 2 * inner), f32),
            pltpu.VMEM((rows, inner), f32),
            pltpu.VMEM((seqs * long, tile_cols), f32),
            pltpu.VMEM((seqs * long, inner), bf16),
            pltpu.VMEM((rows, inner), f32),
            pltpu.VMEM((rows, inner), bf16),
            pltpu.VMEM((low_len, rows), f32),
            pltpu.VMEM((small.shape[0], small.shape[1] * shards), bf16),
            pltpu.VMEM((gains.shape[0], gains.shape[1] * shards), bf16),
            pltpu.SemaphoreType.DMA((shards, 4)),
            pltpu.SemaphoreType.DMA((shards, 4)),
            pltpu.SemaphoreType.DMA((2,)),
            pltpu.SemaphoreType.DMA((shards + 1,)),
            pltpu.SemaphoreType.DMA((7,)),
        ]
        + line.scratch(),
        compiler_params=pltpu.CompilerParams(
            collective_id=ident, has_side_effects=True, vmem_limit_bytes=56 << 20
        ),
    )(hidden, tails, in_half, small, gains)


piece = 32
unroll = 4


def spread(flat_ref, natural, first):
    for j in range(8):
        flat_ref[pl.ds(first * 8 + j, 8, stride=8), :] = natural[:, j * 128 : (j + 1) * 128]


def unspread(flat_ref, first):
    return jnp.concatenate([flat_ref[pl.ds(first * 8 + j, 8, stride=8), :] for j in range(8)], axis=1)


def tile(ref, t):
    return ref[pl.ds(pl.multiple_of(t * 8, 8), 8), :]


def row(ref, t, n, states):
    return ref[pl.ds(t * states + n, 8, stride=0), :]


def exchange(ends, got, send, recv, seq, width):
    me = lax.axis_index("ctx")
    copies = []
    for step in range(1, width):
        copies.append(
            pltpu.make_async_remote_copy(
                ends.at[seq],
                got.at[me, seq],
                send.at[seq, step],
                recv.at[seq, step],
                device_id={"ctx": lax.rem(me + step, width)},
                device_id_type=MESH,
            )
        )
        copies[-1].start()
    return copies


def ctx_greet(width):
    me = lax.axis_index("ctx")
    barrier = pltpu.get_barrier_semaphore()
    for step in range(1, width):
        pl.semaphore_signal(barrier, inc=1, device_id={"ctx": lax.rem(me + step, width)}, device_id_type=MESH)
    return barrier


def entering(got, seq, rate_ref, states, width, reverse):
    me = lax.axis_index("ctx")
    result = []
    for n in range(states):
        value = jnp.zeros((8, 128), f32)
        for k in reversed(range(width)) if reverse else range(width):
            new = jnp.exp2(got[k, seq, states] * rate_ref[n]) * value + got[k, seq, n]
            value = jnp.where(me < k if reverse else me > k, new, value)
        result.append(value)
    return result


def scan_forward(size, act, b_row, c_row, rate, seqs, ident):
    rows, channels = size.shape
    local = rows // seqs
    states = rate.shape[0]
    width = lax.axis_size("ctx")
    pieces = local // piece

    def kernel(
        size_ref, act_ref, b_ref, c_ref, rate_ref, y_ref, kept_ref, enter_ref, size3, drive3,
        y3, ends, got, held, send, recv, out_sem,
    ):
        pl.semaphore_wait(ctx_greet(width), width - 1)

        def lay(i, _):
            first = pl.multiple_of(i * 8, 8)
            block = size_ref[pl.ds(first, 8), :]
            spread(size3, block, first)
            spread(drive3, block * act_ref[pl.ds(first, 8), :], first)
            return 0

        lax.fori_loop(0, rows // 8, lay, 0)
        copies = []
        for seq in range(seqs):

            def first_pass(i, carried):
                values, total = list(carried[:-1]), carried[-1]
                for u in range(unroll):
                    t = seq * local + i * unroll + u
                    s, d = tile(size3, t), tile(drive3, t)
                    total = total + s
                    for n in range(states):
                        values[n] = jnp.exp2(s * rate_ref[n]) * values[n] + d * row(b_ref, t, n, states)
                return tuple(values) + (total,)

            zero = tuple(jnp.zeros((8, 128), f32) for _ in range(states + 1))
            done = lax.fori_loop(0, local // unroll, first_pass, zero)
            for n in range(states + 1):
                ends[seq, n] = done[n]
            copies.append(exchange(ends, got, send, recv, seq, width))
        me = lax.axis_index("ctx")
        for seq in range(seqs):
            for copy in copies[seq]:
                copy.wait()
            got[me, seq] = ends[seq]
            start = entering(got, seq, rate_ref, states, width, False)
            for n in range(states):
                enter_ref[seq, n] = start[n]

            def save(k, slot):
                return pltpu.make_async_copy(
                    held.at[slot], kept_ref.at[pl.ds(seq * local + k * piece, piece)], out_sem.at[slot]
                )

            def one_piece(k, carried):
                slot = lax.rem(k, 2)

                @pl.when(k >= 2)
                def _():
                    save(k - 2, slot).wait()

                def second_pass(i, values):
                    values = list(values)
                    for u in range(unroll):
                        inside = i * unroll + u
                        t = seq * local + k * piece + inside
                        s, d = tile(size3, t), tile(drive3, t)
                        acc = [None] * 4
                        for n in range(states):
                            values[n] = jnp.exp2(s * rate_ref[n]) * values[n] + d * row(b_ref, t, n, states)
                            held[slot, inside, n] = values[n]
                            part = values[n] * row(c_ref, t, n, states)
                            acc[n % 4] = part if acc[n % 4] is None else acc[n % 4] + part
                        y3[pl.ds(pl.multiple_of(t * 8, 8), 8), :] = (acc[0] + acc[1]) + (acc[2] + acc[3])
                    return tuple(values)

                carried = lax.fori_loop(0, piece // unroll, second_pass, carried)
                save(k, slot).start()
                return carried

            lax.fori_loop(0, pieces, one_piece, tuple(start))
            for k in (pieces - 2, pieces - 1):
                save(k, k % 2).wait()

        def back(i, _):
            first = pl.multiple_of(i * 8, 8)
            y_ref[pl.ds(first, 8), :] = unspread(y3, first)
            return 0

        lax.fori_loop(0, rows // 8, back, 0)

    flat = jax.ShapeDtypeStruct((rows * 8, 128), f32)
    return pl.pallas_call(
        kernel,
        out_shape=[
            jax.ShapeDtypeStruct((rows, channels), f32),
            jax.ShapeDtypeStruct((rows, states, 8, 128), f32),
            jax.ShapeDtypeStruct((seqs, states, 8, 128), f32),
            flat,
            flat,
        ],
        in_specs=[VMEM] * 5,
        out_specs=[VMEM, HBM, VMEM, VMEM, VMEM],
        scratch_shapes=[
            pltpu.VMEM((rows * 8, 128), f32),
            pltpu.VMEM((seqs, states + 1, 8, 128), f32),
            pltpu.VMEM((width, seqs, states + 1, 8, 128), f32),
            pltpu.VMEM((2, piece, states, 8, 128), f32),
            pltpu.SemaphoreType.DMA((seqs, width)),
            pltpu.SemaphoreType.DMA((seqs, width)),
            pltpu.SemaphoreType.DMA((2,)),
        ],
        compiler_params=pltpu.CompilerParams(
            collective_id=ident, has_side_effects=True, vmem_limit_bytes=48 << 20
        ),
    )(size, act, b_row, c_row, rate)


def sublane_sums(parts):
    at = lax.broadcasted_iota(jnp.int32, (8, 128), 0)
    for shift in (4, 2, 1):
        low = (at // shift) % 2 == 0
        half = len(parts) // 2
        merged = []
        for one, two in zip(parts[:half], parts[half:]):
            merged.append(
                jnp.where(low, one + pltpu.roll(one, 8 - shift, 0), two + pltpu.roll(two, shift, 0))
            )
        parts = merged
    return parts[0]


def scan_backward(size3, drive3, grad, b_row, c_row, rate, kept, enter, seqs, ident, partial, epilogue, extras, chunk, scatters):
    rows, channels = grad.shape
    local = rows // seqs
    states = rate.shape[0]
    width = lax.axis_size("ctx")
    pieces = local // piece
    early = 2
    unroll_b = 2
    line = Line(partial.shape, chunk, epilogue, extras, bf16)
    share = Halving(scatters, 64)
    n_line, n_ex, n_sc = len(line.scratch()), len(extras), len(scatters)

    def kernel(*refs):
        refs = list(refs)

        def take_refs(n):
            taken = refs[:n]
            del refs[:n]
            return taken

        size_ref, drive_ref, grad_ref, b_ref, c_ref, rate_ref, kept_ref, enter_ref, p_ref = take_refs(9)
        ins, full = take_refs(n_ex), take_refs(n_sc)
        tb_ref, sd_ref, bg_ref, cg_ref, dec_ref, sum_ref = take_refs(6)
        shares = take_refs(n_sc)
        grad3, tb3, sd3, ends, got, held, bpart, cpart, prior, send, recv, in_sem = take_refs(12)
        line.bind(p_ref, ins, sum_ref, [], take_refs(n_line))
        share.bind(full, shares, refs)
        barrier = ctx_greet(width)
        line.begin(barrier, width - 1 + share.greet(barrier))
        share.start()

        def lay(i, _):
            first = pl.multiple_of(i * 8, 8)
            spread(grad3, grad_ref[pl.ds(first, 8), :], first)
            return 0

        lax.fori_loop(0, rows // 8, lay, 0)

        def fetch(seq, k, slot):
            return pltpu.make_async_copy(
                kept_ref.at[pl.ds(seq * local + k * piece, piece)], held.at[slot], in_sem.at[slot]
            )

        copies = []
        for seq in range(seqs):

            def first_pass(i, carried):
                values, total = list(carried[:-1]), carried[-1]
                for u in range(unroll):
                    t = seq * local + local - 1 - (i * unroll + u)
                    s, g = tile(size_ref, t), tile(grad3, t)
                    total = total + s
                    for n in range(states):
                        values[n] = jnp.exp2(s * rate_ref[n]) * (values[n] + g * row(c_ref, t, n, states))
                return tuple(values) + (total,)

            zero = tuple(jnp.zeros((8, 128), f32) for _ in range(states + 1))
            done = zero
            for half in range(early):
                span = local // unroll // early
                done = lax.fori_loop(half * span, (half + 1) * span, first_pass, done)
                line.tick(seq * early + half)
            for n in range(states + 1):
                ends[seq, n] = done[n]
            copies.append(exchange(ends, got, send, recv, seq, width))
        me = lax.axis_index("ctx")
        for n in range(states):
            dec_ref[n] = jnp.zeros((8, 128), f32)
        for seq in range(seqs):
            fetch(seq, pieces - 1, (pieces - 1) % 2).start()
            for copy in copies[seq]:
                copy.wait()
            got[me, seq] = ends[seq]
            start = entering(got, seq, rate_ref, states, width, True)
            fetch(seq, pieces - 1, (pieces - 1) % 2).wait()

            def one_slot(slot, k, inside, adjoint, decays, prior_at):
                t = seq * local + k * piece + inside
                s, d, g = tile(size_ref, t), tile(drive_ref, t), tile(grad3, t)
                tb, sd = [None] * 2, [None] * 2
                b_parts, c_parts = [], []
                for n in range(states):
                    total = adjoint[n] + g * row(c_ref, t, n, states)
                    c_parts.append(held[slot, inside, n] * g)
                    b_parts.append(total * d)
                    through = total * row(b_ref, t, n, states)
                    adjoint[n] = jnp.exp2(s * rate_ref[n]) * total
                    kept_part = adjoint[n] * prior_at(n)
                    through_size = kept_part * rate_ref[n]
                    decays[n] = decays[n] + kept_part * s
                    tb[n % 2] = through if tb[n % 2] is None else tb[n % 2] + through
                    sd[n % 2] = through_size if sd[n % 2] is None else sd[n % 2] + through_size
                here = pl.ds(pl.multiple_of(t * 8, 8), 8)
                tb3[here, :] = tb[0] + tb[1]
                sd3[here, :] = sd[0] + sd[1]
                for h in range(states // 8):
                    spot = pl.ds(pl.multiple_of(inside * states + h * 8, 8), 8)
                    bpart[spot, :] = sublane_sums(b_parts[h * 8 : h * 8 + 8])
                    cpart[spot, :] = sublane_sums(c_parts[h * 8 : h * 8 + 8])

            def one_piece(back_k, carried):
                k = pieces - 1 - back_k
                slot = lax.rem(k, 2)

                @pl.when(k > 0)
                def _():
                    fetch(seq, k - 1, 1 - slot).start()

                def slots(i, carried):
                    adjoint, decays = list(carried[:states]), list(carried[states:])
                    for u in range(unroll_b):
                        inside = piece - 1 - (i * unroll_b + u)
                        one_slot(slot, k, inside, adjoint, decays, lambda n: held[slot, inside - 1, n])
                    return tuple(adjoint) + tuple(decays)

                carried = lax.fori_loop(0, piece // unroll_b - 1, slots, carried)
                adjoint, decays = list(carried[:states]), list(carried[states:])
                for inside in reversed(range(1, unroll_b)):
                    one_slot(slot, k, inside, adjoint, decays, lambda n: held[slot, inside - 1, n])

                @pl.when(k > 0)
                def _():
                    fetch(seq, k - 1, 1 - slot).wait()
                    prior[...] = held[1 - slot, piece - 1]

                @pl.when(k == 0)
                def _():
                    prior[...] = enter_ref[seq]

                one_slot(slot, k, 0, adjoint, decays, lambda n: prior[n])
                ones = jnp.ones((8, 128), bf16)
                for part, out in ((bpart, bg_ref), (cpart, cg_ref)):
                    sums = outer_cols(ones, part[...].astype(bf16))
                    out[pl.ds(seq * pieces + k, 1)] = sums[None]
                line.tick(seqs * early + seq * pieces + back_k)
                share.tick(seq * pieces + back_k)
                return tuple(adjoint) + tuple(decays)

            zero = tuple(jnp.zeros((8, 128), f32) for _ in range(states))
            carried = lax.fori_loop(0, pieces, one_piece, tuple(start) + zero)
            for n in range(states):
                dec_ref[n] = dec_ref[n] + carried[states + n]

        def back(i, _):
            first = pl.multiple_of(i * 8, 8)
            tb_ref[pl.ds(first, 8), :] = unspread(tb3, first)
            sd_ref[pl.ds(first, 8), :] = unspread(sd3, first)
            return 0

        lax.fori_loop(0, rows // 8, back, 0)
        for c in range(seqs * (early + pieces), line.ticks()):
            line.tick(c)
        for i in range(seqs * pieces, share.turns):
            share.tick(i)
        line.finish()
        share.finish()

    nat = jax.ShapeDtypeStruct((rows, channels), f32)
    sums = jax.ShapeDtypeStruct((rows // piece, 8, piece * states), f32)
    return pl.pallas_call(
        kernel,
        out_shape=[nat, nat, sums, sums, jax.ShapeDtypeStruct((states, 8, 128), f32),
                   jax.ShapeDtypeStruct(partial.shape, bf16)] + share.results(),
        in_specs=[VMEM] * 6 + [HBM, VMEM] + [HBM] * (1 + n_ex + n_sc),
        out_specs=[VMEM] * (6 + n_sc),
        scratch_shapes=[pltpu.VMEM((rows * 8, 128), f32)] * 3
        + [
            pltpu.VMEM((seqs, states + 1, 8, 128), f32),
            pltpu.VMEM((width, seqs, states + 1, 8, 128), f32),
            pltpu.VMEM((2, piece, states, 8, 128), f32),
            pltpu.VMEM((piece * states, 128), f32),
            pltpu.VMEM((piece * states, 128), f32),
            pltpu.VMEM((states, 8, 128), f32),
            pltpu.SemaphoreType.DMA((seqs, width)),
            pltpu.SemaphoreType.DMA((seqs, width)),
            pltpu.SemaphoreType.DMA((2,)),
        ]
        + line.scratch()
        + share.scratch(),
        compiler_params=pltpu.CompilerParams(
            collective_id=ident, has_side_effects=True, vmem_limit_bytes=62 << 20
        ),
    )(size3, drive3, grad, b_row, c_row, rate, kept, enter, partial, *extras, *share.folded)


def body(
    hidden_in, lengths, cotangent, norm_gain, in_weight, conv_weight, conv_bias, low_weight, step_weight,
    step_bias, decay_log, skip_gain, out_weight, ffn_gain, gate_up, down_weight,
):
    seqs, local, width = hidden_in.shape
    rows = seqs * local
    shards, pieces = lax.axis_size("shard"), lax.axis_size("ctx")
    inner = in_weight.shape[2]
    taps = conv_weight.shape[0]
    rank = step_weight.shape[0]
    states = decay_log.shape[0]
    low_len = low_weight.shape[0]

    small = jnp.concatenate(
        [low_weight, step_weight, decay_log, conv_weight, conv_bias[None], step_bias[None], skip_gain[None]], axis=0
    )
    hidden_rows = hidden_in.reshape(rows, width)
    small = jnp.pad(small, ((0, -small.shape[0] % 16), (0, 0)))
    gains = jnp.stack([norm_gain, ffn_gain])
    gains = jnp.pad(gains, ((0, 14), (0, 0)))
    in_half = in_weight.transpose(1, 0, 2)
    in_w, small, gains, normed_one, gate_z, padded, pre_act, act_half, low_all = front(
        hidden_rows, in_half, small, gains, seqs, low_len + rank + states, taps, low_len, 0
    )
    out_parts = lax.all_gather(out_weight, "shard")
    gate_half = gate_up.transpose(1, 0, 2)
    gate_w = [lax.all_gather(gate_half[c], "shard", axis=0, tiled=True) for c in range(2)]
    down_parts = lax.all_gather(down_weight, "shard")
    part = width // shards

    low_w = small[:low_len]
    step_w = small[low_len : low_len + rank]
    at = low_len + rank
    decay_w = small[at : at + states].astype(f32)
    kernel = small[at + states : at + states + taps].astype(f32)
    conv_b = small[at + states + taps].astype(f32)
    step_b = small[at + states + taps + 1].astype(f32)
    skip_full = small[at + states + taps + 2].astype(f32)
    gain_one, gain_two = gains[0:1].astype(f32), gains[1:2].astype(f32)

    first_slot = lax.axis_index("ctx") * local
    positions = first_slot + jnp.arange(local, dtype=jnp.int32)
    pad_mask = (positions[None, :] < lengths[:, None]).astype(f32)

    source = hidden_rows.astype(f32)
    padded = padded.reshape(seqs, halo + local, inner)[:, halo - taps + 1 :].astype(f32)
    act_full = act_half.astype(f32)
    step_low = low_all[:rank].astype(bf16)
    b_in, c_out = low_all[rank : rank + states], low_all[rank + states :]
    b_row, c_row = (
        jnp.broadcast_to(v.T[:, :, None], (rows, states, 128)).reshape(rows * states, 128) for v in (b_in, c_out)
    )
    step_pre = inner_rows(step_low, step_w) + step_b
    step_size = jax.nn.softplus(step_pre)
    decay_rate = -jnp.exp(decay_w)
    rate = (decay_rate * log2e).reshape(states, 8, 128)
    scan_y, kept, enter, size3, drive3 = scan_forward(step_size, act_full, b_row, c_row, rate, seqs, 2)
    scan_out = scan_y + skip_full * act_full
    gate_act = jax.nn.silu(gate_z)
    gated_out = (scan_out * gate_act).astype(bf16)
    mixed_part = jnp.concatenate(
        [jnp.dot(gated_out, out_parts[k], preferred_element_type=f32) for k in range(shards)], axis=1
    ).astype(bf16)
    wide = jax.ShapeDtypeStruct((rows, width), f32)
    normed_two, middle = tp_sum(mixed_part, norm_end, [hidden_rows, gain_two], [wide], 32, 3)
    gate_lin, up_lin = (jnp.dot(normed_two, gate_w[c], preferred_element_type=f32) for c in range(2))
    hidden_ffn = (jax.nn.silu(gate_lin) * up_lin).astype(bf16)
    ffn_part = jnp.concatenate(
        [jnp.dot(hidden_ffn, down_parts[k], preferred_element_type=f32) for k in range(shards)], axis=1
    ).astype(bf16)

    upstream = cotangent.reshape(rows, width).astype(f32) * pad_mask.reshape(rows, 1)
    ffn_grad = upstream.astype(bf16)
    down_grad = inner_rows(ffn_grad, hidden_ffn).astype(bf16)
    hidden_grad = sum(outer_cols(ffn_grad[:, k * part : (k + 1) * part], down_parts[k]) for k in range(shards))
    gate_grad = (hidden_grad * up_lin * silu_grad(gate_lin)).astype(bf16)
    up_grad = (hidden_grad * jax.nn.silu(gate_lin)).astype(bf16)
    gate_up_grad = [inner_rows(normed_two, g).astype(bf16) for g in (gate_grad, up_grad)]
    back_part = (outer_cols(gate_grad, gate_w[0]) + outer_cols(up_grad, gate_w[1])).astype(bf16)
    mix_grad, middle_grad, *ffn_shares = tp_sum(
        back_part, norm_back_end, [middle, gain_two, ffn_grad], [wide], 32, 5, scatters=gate_up_grad + [down_grad]
    )
    ffn_gain_grad = jnp.sum(back_part.astype(f32) * normed_two.astype(f32), axis=0) / gain_two[0]

    out_weight_grad = inner_rows(mix_grad, gated_out).astype(bf16)
    gated_grad = sum(outer_cols(mix_grad[:, k * part : (k + 1) * part], out_parts[k]) for k in range(shards))
    scan_grad = gated_grad * gate_act
    z_grad = gated_grad * scan_out * silu_grad(gate_z)
    skip_gain_grad = jnp.sum(scan_grad * act_full, axis=0)
    through_b, through_decay, b_sums, c_sums, decay_sum, mixed_out, out_share = scan_backward(
        size3, drive3, scan_grad, b_row, c_row, rate, kept, enter, seqs, 6, ffn_part, add_end, [middle], 32,
        [out_weight_grad],
    )
    mixed_out = mixed_out.reshape(hidden_in.shape)
    decay_log_grad = decay_sum.reshape(states, inner) * decay_rate
    size_grad = act_full * through_b + through_decay * (1.0 / log2e)
    step_grad = (size_grad * jax.nn.sigmoid(step_pre)).astype(bf16)
    step_bias_grad = jnp.sum(step_grad.astype(f32), axis=0)
    step_weight_grad = jnp.dot(step_low, step_grad, preferred_element_type=f32)
    low_back = jnp.concatenate(
        [
            outer_cols(step_w, step_grad),
            b_sums[:, 0].reshape(rows, states).T,
            c_sums[:, 0].reshape(rows, states).T,
        ],
        axis=0,
    ).astype(bf16)
    low_grad = tp_sum(low_back, plain_end, [], [], 80, 7)[0]
    low_weight_grad = jnp.dot(low_grad, act_half, preferred_element_type=f32)
    act_grad = skip_full * scan_grad + step_size * through_b + inner_rows(low_grad, low_w)
    pre_grad = (act_grad * silu_grad(pre_act)).reshape(seqs, local, inner)
    conv_bias_grad = jnp.sum(pre_grad, axis=(0, 1))
    conv_weight_grad = jnp.stack(
        [jnp.sum(pre_grad * padded[:, k : k + local], axis=(0, 1)) for k in range(taps)]
    )
    behind = lax.ppermute(pre_grad[:, : taps - 1], "ctx", [(k + 1, k) for k in range(pieces - 1)])
    pre_long = jnp.concatenate([pre_grad, behind], axis=1)
    conv_grad = sum(kernel[k] * pre_long[:, taps - 1 - k : taps - 1 - k + local] for k in range(taps))
    conv_grad = conv_grad.reshape(rows, inner).astype(bf16)
    z_half = z_grad.astype(bf16)
    in_weight_grad = [inner_rows(normed_one, g).astype(bf16) for g in (conv_grad, z_half)]
    first_part = (outer_cols(conv_grad, in_w[0]) + outer_cols(z_half, in_w[1])).astype(bf16)
    norm_gain_grad = jnp.sum(first_part.astype(f32) * source * rms_scale(source), axis=0)
    small_grads = jnp.concatenate(
        [low_weight_grad, step_weight_grad, decay_log_grad, conv_weight_grad, conv_bias_grad[None],
         step_bias_grad[None], skip_gain_grad[None]], axis=0,
    )
    places = shards * pieces
    lines, lane, share = small_grads.shape[0], inner // places, width // places
    small_rows = -(-(lines * lane) // (16 * inner)) * 16
    if small_rows * inner - lines * lane < 8 * inner:
        small_rows += 16
    small_blocks = small_grads.reshape(lines, places, lane).transpose(1, 0, 2).reshape(places, lines * lane)
    gain_blocks = jnp.concatenate([norm_gain_grad.reshape(places, share), ffn_gain_grad.reshape(places, share)], axis=1)
    fill = (small_rows - 8) * inner - lines * lane
    small_blocks = jnp.concatenate(
        [small_blocks, jnp.zeros((places, fill), f32), gain_blocks, jnp.zeros((places, 8 * inner - 2 * share), f32)],
        axis=1,
    )
    small_blocks = small_blocks.reshape(places * small_rows, inner).astype(bf16)
    input_grad, in_share, z_share, small_share = tp_sum(
        first_part, norm_back_end, [hidden_rows, gain_one, middle_grad], [], 32, 8,
        scatters=in_weight_grad + [small_blocks], line_too=True,
    )
    gain_share = small_share[small_rows - 8]
    input_grad = input_grad.astype(f32).reshape(hidden_in.shape)
    small_out = small_share.reshape(-1)[: lines * lane].reshape(lines, lane)
    at = low_len + rank
    return (
        mixed_out,
        input_grad,
        gain_share[:share],
        jnp.stack([in_share, z_share], axis=1),
        small_out[at + states : at + states + taps],
        small_out[at + states + taps],
        small_out[:low_len],
        small_out[low_len : low_len + rank],
        small_out[at + states + taps + 1],
        small_out[at : at + states],
        small_out[at + states + taps + 2],
        out_share.T,
        gain_share[share : 2 * share],
        jnp.stack(ffn_shares[:2], axis=1),
        ffn_shares[2].T,
    )


def solution(mesh):
    placed = (
        P("shard", "ctx", None),
        P("shard"),
        P("shard", "ctx", None),
        P("shard"),
        P("shard", None, "tp"),
        P(None, ("tp", "shard")),
        P(("tp", "shard")),
        P(None, ("tp", "shard")),
        P(None, ("tp", "shard")),
        P(("tp", "shard")),
        P(None, ("tp", "shard")),
        P(("tp", "shard")),
        P("tp", "shard"),
        P("shard"),
        P("shard", None, "tp"),
        P("tp", "shard"),
    )
    return jax.shard_map(
        body,
        mesh=mesh,
        in_specs=placed,
        out_specs=(
            P("shard", "ctx", None),
            P("shard", "ctx", None),
            P(("shard", "ctx")),
            P(("shard", "ctx"), None, "tp"),
            P(None, ("tp", "shard", "ctx")),
            P(("tp", "shard", "ctx")),
            P(None, ("tp", "shard", "ctx")),
            P(None, ("tp", "shard", "ctx")),
            P(("tp", "shard", "ctx")),
            P(None, ("tp", "shard", "ctx")),
            P(("tp", "shard", "ctx")),
            P("tp", ("shard", "ctx")),
            P(("shard", "ctx")),
            P(("shard", "ctx"), None, "tp"),
            P("tp", ("shard", "ctx")),
        ),
        check_vma=False,
    )
```

```python
import functools

import jax
import jax.numpy as jnp
from jax import lax
from jax.experimental import pallas as pl
from jax.experimental.pallas import tpu as pltpu
from jax.sharding import PartitionSpec as P

MESH = pl.DeviceIdType.MESH
epsilon = 1e-05
log2e = 1.4426950408889634
bf16 = jnp.bfloat16
f32 = jnp.float32
VMEM = pl.BlockSpec(memory_space=pltpu.VMEM)
HBM = pl.BlockSpec(memory_space=pl.ANY)


def inner_rows(left, right):
    return lax.dot_general(left, right, (((0,), (0,)), ((), ())), preferred_element_type=f32)


def outer_cols(left, right):
    return lax.dot_general(left, right, (((1,), (1,)), ((), ())), preferred_element_type=f32)


def silu_grad(values):
    sig_val = jax.nn.sigmoid(values)
    return sig_val * (1.0 + values * (1.0 - sig_val))


def rms_scale(source):
    return lax.rsqrt(jnp.mean(source * source, axis=-1, keepdims=True) + epsilon)


class Line:
    lag = 3
    ahead = 4

    def __init__(self, shape, chunk, epilogue, extras, out_dtype):
        self.shape, self.chunk, self.epilogue, self.out_dtype = shape, chunk, epilogue, out_dtype
        self.count = shape[0] // chunk
        self.extras = [(e.shape, e.dtype) for e in extras]

    def scratch(self):
        return (
            [pltpu.VMEM(self.shape, bf16)] * 4
            + [pltpu.SemaphoreType.DMA((self.count,))] * 6
            + [pltpu.VMEM(shape, dtype) for shape, dtype in self.extras]
            + [pltpu.SemaphoreType.DMA((1 + len(self.extras),))]
        )

    def bind(self, p_ref, ins, out_ref, outs, scratch):
        self.p_ref, self.given, self.out_ref, self.outs = p_ref, ins, out_ref, outs
        (self.p, self.got_a, self.pair, self.got_b, self.a_send, self.a_recv, self.b_send, self.b_recv,
         self.c_send, self.c_recv) = scratch[:10]
        self.ins, self.in_sem = scratch[10:-1], scratch[-1]
        me = lax.axis_index("tp")
        self.mate = me + 1 - 2 * (me % 2)
        self.across = 3 - me
        self.middle = jnp.logical_or(me == 1, me == 2)

    def at(self, c):
        return pl.ds(pl.multiple_of(c * self.chunk, self.chunk), self.chunk)

    def remote(self, source, target, send, recv, c, to):
        return pltpu.make_async_remote_copy(
            source.at[self.at(c)], target.at[self.at(c)], send.at[c], recv.at[c], device_id={"tp": to}, device_id_type=MESH
        )

    def copy_a(self, c):
        return self.remote(self.p_ref, self.got_a, self.a_send, self.a_recv, c, self.mate)

    def copy_b(self, c):
        return self.remote(self.pair, self.got_b, self.b_send, self.b_recv, c, self.across)

    def copy_c(self, c):
        return self.remote(self.out_ref, self.out_ref, self.c_send, self.c_recv, c, self.mate)

    def loads(self):
        pairs = [(self.p_ref, self.p)] + list(zip(self.given, self.ins))
        return [pltpu.make_async_copy(a, b, self.in_sem.at[i]) for i, (a, b) in enumerate(pairs)]

    def begin(self, barrier, met, ends_meet=False):
        pl.semaphore_signal(barrier, inc=1, device_id={"tp": self.mate}, device_id_type=MESH)

        @pl.when(self.middle)
        def _():
            pl.semaphore_signal(barrier, inc=1, device_id={"tp": self.across}, device_id_type=MESH)
            for load in self.loads():
                load.start()
            pl.semaphore_wait(barrier, met + 2)
            for load in self.loads():
                load.wait()

        @pl.when(jnp.logical_not(self.middle))
        def _():
            if ends_meet:
                pl.semaphore_signal(barrier, inc=1, device_id={"tp": self.across}, device_id_type=MESH)
            pl.semaphore_wait(barrier, met + 2 if ends_meet else met + 1)

            for c in range(min(self.ahead, self.count)):
                self.copy_a(c).start()

    def greet(self, barrier, met):
        pl.semaphore_signal(barrier, inc=1, device_id={"tp": self.mate}, device_id_type=MESH)

        @pl.when(self.middle)
        def _():
            pl.semaphore_signal(barrier, inc=1, device_id={"tp": self.across}, device_id_type=MESH)
            pl.semaphore_wait(barrier, met + 2)

        @pl.when(jnp.logical_not(self.middle))
        def _():
            pl.semaphore_wait(barrier, met + 1)

    def start(self):
        @pl.when(jnp.logical_not(self.middle))
        def _():
            for c in range(min(self.ahead, self.count)):
                self.copy_a(c).start()

    def first(self, c):
        at = self.at(c)
        self.copy_a(c).wait_recv()
        self.pair[at, :] = (self.p[at, :].astype(f32) + self.got_a[at, :].astype(f32)).astype(bf16)
        self.copy_b(c).start()

    def second(self, c):
        at = self.at(c)
        self.copy_b(c).wait_recv()
        total = self.pair[at, :].astype(f32) + self.got_b[at, :].astype(f32)
        self.epilogue(c, at, total, self.ins, self.out_ref, self.outs)
        self.copy_c(c).start()

    def tick(self, c):
        lag = min(self.lag, self.count)

        @pl.when(jnp.logical_and(self.middle, c < self.count))
        def _():
            self.first(c)

        @pl.when(jnp.logical_and(self.middle, jnp.logical_and(c >= lag, c < self.count + lag)))
        def _():
            self.second(c - lag)

        @pl.when(jnp.logical_and(jnp.logical_not(self.middle), c + self.ahead < self.count))
        def _():
            self.copy_a(c + self.ahead).start()

    def ticks(self):
        return self.count + min(self.lag, self.count)

    def finish(self):
        @pl.when(self.middle)
        def _():
            def drain(c, _):
                self.copy_b(c).wait_send()
                self.copy_c(c).wait_send()
                return 0

            lax.fori_loop(0, self.count, drain, 0)

        @pl.when(jnp.logical_not(self.middle))
        def _():
            def take(c, _):
                self.copy_c(c).wait_recv()
                self.copy_a(c).wait_send()
                return 0

            lax.fori_loop(0, self.count, take, 0)


share_lag = 2
share_ahead = 2


class Halving:
    def __init__(self, arrays, step_rows=16):
        steps = [step_rows] * len(arrays) if isinstance(step_rows, int) else list(step_rows)
        self.steps = steps
        shards, pieces = lax.axis_size("shard"), lax.axis_size("ctx")
        self.n = len(arrays)
        self.bits = [
            (axis, 1 << k)
            for axis, size in (("shard", shards), ("ctx", pieces))
            for k in reversed(range(size.bit_length() - 1))
        ]
        self.depth = len(self.bits)
        head = shards.bit_length() - 1
        self.dims = list(range(self.depth))
        self.orders = (self.dims, self.dims[:head] + self.dims[head:][::-1])
        self.parts = [g.shape[0] // (shards * pieces) // k for g, k in zip(arrays, steps)]
        self.folded = [
            g.reshape((2,) * self.depth + (p * k, g.shape[1])) for g, p, k in zip(arrays, self.parts, steps)
        ]
        self.tails = [g.shape[self.depth :] for g in self.folded]
        self.pairs = (max(self.parts, default=0) + 1) // 2
        self.turns = self.pairs + share_lag * (self.depth - 1)

    def results(self):
        return [jax.ShapeDtypeStruct(tail, f32) for tail in self.tails]

    def scratch(self):
        if not self.n:
            return []
        held = [pltpu.VMEM((2,) * (self.depth - 1) + tail, bf16) for tail in self.tails]
        for j in range(self.depth):
            held += [pltpu.VMEM((2,) * (self.depth - 1 - j) + tail, bf16) for tail in self.tails]
        sem = pltpu.SemaphoreType.DMA((self.depth, self.n, max(self.parts)))
        return held + [sem, sem, pltpu.SemaphoreType.DMA((self.n, max(self.parts)))]

    def bind(self, full, shares, scratch):
        n = self.n
        self.partner, self.mine = [], []
        if not n:
            return
        self.full, self.shares, self.own = full, shares, scratch[:n]
        self.landed = [scratch[n * (j + 1) : n * (j + 2)] for j in range(self.depth)]
        self.send, self.recv, self.own_sem = scratch[n * (self.depth + 1) :]
        for axis, bit in self.bits:
            here = lax.axis_index(axis)
            self.mine.append((here // bit) % 2)
            self.partner.append({axis: here + bit - 2 * bit * ((here // bit) % 2)})

    def greet(self, barrier):
        for who in self.partner:
            pl.semaphore_signal(barrier, inc=1, device_id=who, device_id_type=MESH)
        return len(self.partner)

    def spot(self, a, c):
        return pl.ds(pl.multiple_of(c * self.steps[a], self.steps[a]), self.steps[a])

    def pick(self, remaining, dim, index, a, c):
        return tuple(index if d == dim else slice(None) for d in remaining) + (self.spot(a, c), slice(None))

    def rest(self, order, j):
        return [d for d in self.dims if d not in order[:j]]

    def copy(self, j, a, c, order):
        source = self.full[a] if j == 0 else self.landed[j - 1][a]
        d = order[j]
        return pltpu.make_async_remote_copy(
            source.at[self.pick(self.rest(order, j), d, 1 - self.mine[d], a, c)],
            self.landed[j][a].at[self.pick(self.rest(order, j + 1), None, None, a, c)],
            self.send.at[j, a, c],
            self.recv.at[j, a, c],
            device_id=self.partner[d],
            device_id_type=MESH,
        )

    def own_copy(self, a, c, order):
        return pltpu.make_async_copy(
            self.full[a].at[self.pick(self.dims, order[0], self.mine[order[0]], a, c)],
            self.own[a].at[self.pick(self.rest(order, 1), None, None, a, c)],
            self.own_sem.at[a, c],
        )

    def begin(self, a, c, order):
        self.copy(0, a, c, order).start()
        self.own_copy(a, c, order).start()

    def step(self, j, a, c, order):
        self.copy(j, a, c, order).wait_recv()
        where = self.pick(self.rest(order, j + 1), None, None, a, c)
        d = order[j]
        if j == 0:
            self.own_copy(a, c, order).wait()
            kept = self.own[a][where]
        else:
            kept = self.landed[j - 1][a][self.pick(self.rest(order, j), d, self.mine[d], a, c)]
        total = kept.astype(f32) + self.landed[j][a][where].astype(f32)
        if j == self.depth - 1:
            self.shares[a][self.spot(a, c), :] = total
        else:
            self.landed[j][a][where] = total.astype(bf16)
            self.copy(j + 1, a, c, order).start()

    def each(self, i, fn):
        for parity in (0, 1):
            c = 2 * i + parity
            for a in range(self.n):

                @pl.when(jnp.logical_and(c >= 0, c < self.parts[a]))
                def _():
                    fn(a, c, self.orders[parity])

    def start(self):
        for i in range(share_ahead if self.n else 0):
            self.each(i, self.begin)

    def tick(self, i):
        if self.n:
            self.each(i + share_ahead, self.begin)
            for j in range(self.depth):
                self.each(i - share_lag * j, functools.partial(self.step, j))

    def finish(self):
        def sent(i, _):
            for j in range(self.depth):
                self.each(i, lambda a, c, order: self.copy(j, a, c, order).wait_send())
            return 0

        if self.n:
            lax.fori_loop(0, self.pairs, sent, 0)


def tp_sum(partial, epilogue, extras, extra_outs, chunk, ident, out_dtype=bf16, scatters=(), line_too=False, steps=16):
    line = Line(partial.shape, chunk, epilogue, extras, out_dtype)
    share = Halving(scatters, steps)
    n_ex, n_out, n_sc = len(extras), len(extra_outs), len(scatters)
    n_line, n_share = len(line.scratch()), len(share.scratch())

    def kernel(*refs):
        refs = list(refs)

        def take_refs(n):
            taken = refs[:n]
            del refs[:n]
            return taken

        (p_ref,) = take_refs(1)
        ins = take_refs(n_ex)
        full = take_refs(n_sc)
        (out_ref,) = take_refs(1)
        outs = take_refs(n_out)
        shares = take_refs(n_sc)
        line.bind(p_ref, ins, out_ref, outs, take_refs(n_line))
        share.bind(full, shares, take_refs(n_share))
        tail, tail_send, tail_recv = take_refs(3) if line_too else (None, None, None)
        barrier = pltpu.get_barrier_semaphore()
        line.begin(barrier, share.greet(barrier), line_too)
        share.start()

        def turn(i, _):
            for parity in (0, 1):
                line.tick(2 * i + parity)
            share.tick(i)
            return 0

        turns = (line.ticks() + 1) // 2
        lax.fori_loop(0, max(turns, share.turns) if n_sc else turns, turn, 0)
        if line_too:
            height = shares[-1].shape[0]
            last = pl.ds(height - 8, 8)
            for k, to in enumerate((line.mate, line.across)):
                copy = pltpu.make_async_remote_copy(
                    shares[-1].at[last] if k == 0 else tail.at[2], tail.at[k], tail_send.at[k], tail_recv.at[k],
                    device_id={"tp": to}, device_id_type=MESH,
                )
                copy.start()
                copy.wait()
                if k == 0:
                    tail[2] = shares[-1][last, :] + tail[0]
            shares[-1][last, :] = tail[2] + tail[1]
        line.finish()
        share.finish()

    buffers = []
    if line_too:
        pair_sem = pltpu.SemaphoreType.DMA((2,))
        buffers += [pltpu.VMEM((3, 8, scatters[-1].shape[-1]), f32), pair_sem, pair_sem]
    return pl.pallas_call(
        kernel,
        out_shape=[jax.ShapeDtypeStruct(partial.shape, out_dtype)] + list(extra_outs) + share.results(),
        in_specs=[HBM] * (1 + n_ex + n_sc),
        out_specs=[VMEM] * (1 + n_out + n_sc),
        scratch_shapes=line.scratch() + share.scratch() + buffers,
        compiler_params=pltpu.CompilerParams(
            collective_id=ident, has_side_effects=True, vmem_limit_bytes=56 << 20
        ),
    )(partial, *extras, *share.folded)


def plain_end(c, rows, total, ins, out_ref, outs):
    out_ref[rows, :] = total.astype(out_ref.dtype)


def norm_end(c, rows, total, ins, out_ref, outs):
    source_ref, gain_ref = ins
    middle = source_ref[rows, :].astype(f32) + total
    outs[0][rows, :] = middle
    out_ref[rows, :] = (middle * rms_scale(middle) * gain_ref[...]).astype(bf16)


def add_end(c, rows, total, ins, out_ref, outs):
    out_ref[rows, :] = (ins[0][rows, :] + total).astype(bf16)


def norm_back_end(c, rows, total, ins, out_ref, outs):
    source = ins[0][rows, :].astype(f32)
    inv = rms_scale(source)
    weighted = total * ins[1][...]
    back = inv * weighted - source * (inv * inv * inv) * jnp.mean(weighted * source, axis=-1, keepdims=True)
    result = ins[2][rows, :] + back
    if outs:
        outs[0][rows, :] = result
    out_ref[rows, :] = result.astype(bf16)


halo = 16
tile_cols = 256


def front(hidden, in_half, small, gains, seqs, at_conv, taps, low_len, ident):
    rows, width = hidden.shape
    local = rows // seqs
    part, inner = in_half.shape[1:]
    shards, pieces = lax.axis_size("shard"), lax.axis_size("ctx")
    long = local + halo
    tiles = inner // tile_cols
    line = Line((low_len, rows), 80, plain_end, [], f32)
    n_line = len(line.scratch())

    def kernel(
        hid_ref, tail_ref, in_ref, small_ref, gain_ref,
        in_out, small_out, gain_out, normed_out, z_out, ext_out, pre_out, act_out, low_out,
        own_w, got_w, edge, normed, ext_n, acc, z_val, conv_f, ext_c, pre, act, low_acc, small_all, gain_all,
        send, recv, edge_sem, own_sem, out_sem, *rest
    ):
        me, ctx = lax.axis_index("shard"), lax.axis_index("ctx")
        barrier = pltpu.get_barrier_semaphore()
        line.bind(rest[0], [], low_out, [], list(rest))
        for step in range(1, shards):
            pl.semaphore_signal(barrier, inc=1, device_id={"shard": lax.rem(me + step, shards)}, device_id_type=MESH)
        pl.semaphore_signal(barrier, inc=1, device_id={"ctx": lax.rem(ctx + pieces - 1, pieces)}, device_id_type=MESH)
        load = pltpu.make_async_copy(in_ref, own_w, own_sem.at[0])
        load.start()
        small_size, gain_size = small_ref.shape[1], gain_ref.shape[1]
        small_at = pl.ds(pl.multiple_of(me * small_size, small_size), small_size)
        gain_at = pl.ds(pl.multiple_of(me * gain_size, gain_size), gain_size)
        small_all[:, small_at] = small_ref[...]
        gain_all[:, gain_at] = gain_ref[...]
        line.greet(barrier, shards)
        edge_copy = pltpu.make_async_remote_copy(
            tail_ref, edge, edge_sem.at[0], edge_sem.at[1],
            device_id={"ctx": lax.rem(ctx + 1, pieces)}, device_id_type=MESH,
        )
        copies = {}
        for step in range(1, shards):
            peer = {"shard": lax.rem(me + step, shards)}
            moves = [(gain_ref, gain_all.at[:, gain_at]), (small_ref, small_all.at[:, small_at])]
            moves += [(in_ref.at[c], got_w.at[step - 1, c]) for c in range(2)]
            for k, (source, target) in enumerate(moves):
                copies[step, k] = pltpu.make_async_remote_copy(
                    source, target, send.at[step, k], recv.at[step, k], device_id=peer, device_id_type=MESH
                )
        for k in range(4):
            for step in range(1, shards):
                copies[step, k].start()
            if k == 0:
                edge_copy.start()
        for step in range(1, shards):
            copies[step, 0].wait_recv()
        gain = gain_all[0:1, :].astype(f32)

        def norm_rows(i, _):
            at = pl.ds(pl.multiple_of(i * 16, 16), 16)
            source = hid_ref[at, :].astype(f32)
            value = (source * rms_scale(source) * gain).astype(bf16)
            normed[at, :] = value
            seq = i // (local // 16)
            ext_n[pl.ds(pl.multiple_of(i * 16 + (seq + 1) * halo, 16), 16), :] = value
            return 0

        lax.fori_loop(0, rows // 16, norm_rows, 0)
        edge_copy.wait_recv()
        for seq in range(seqs):
            source = edge[seq].astype(f32)
            value = source * rms_scale(source) * gain * (ctx > 0).astype(f32)
            ext_n[seq * long : seq * long + halo, :] = value.astype(bf16)
        outs = [(normed, normed_out)]
        pltpu.make_async_copy(normed, normed_out, out_sem.at[0]).start()

        def cols(c, j):
            return pl.ds(pl.multiple_of(c * inner + j * tile_cols, tile_cols), tile_cols)

        def finish_conv(j):
            here = pl.ds(pl.multiple_of(j * tile_cols, tile_cols), tile_cols)
            value = acc[:, cols(0, j)].astype(bf16)
            ext_c[:, here] = value
            conv_f[...] = value.astype(f32)
            weights = small_all[at_conv : at_conv + 16, here].astype(f32)
            for seq in range(seqs):
                for k in range(local // 64):
                    first = seq * long + halo + k * 64
                    total = weights[taps : taps + 1]
                    for tap in range(taps):
                        total = total + weights[tap : tap + 1] * conv_f[first - taps + 1 + tap : first - taps + 1 + tap + 64, :]
                    to = slice(seq * local + k * 64, seq * local + (k + 1) * 64)
                    pre[to, here] = total
                    act[to, here] = jax.nn.silu(total).astype(bf16)
            low = outer_cols(small_all[0:low_len, here], act[:, here])
            low_acc[...] = low_acc[...] + low

        def finish_gate(j):
            here = pl.ds(pl.multiple_of(j * tile_cols, tile_cols), tile_cols)
            for seq in range(seqs):
                z_val[seq * local : (seq + 1) * local, here] = acc[seq * long + halo : (seq + 1) * long, cols(1, j)]

        low_acc[...] = jnp.zeros_like(low_acc)
        own_place = pl.ds(pl.multiple_of(me * part, part), part)
        load.wait()
        own_save = pltpu.make_async_copy(own_w, in_out.at[:, own_place], own_sem.at[1])
        own_save.start()
        saves = []
        for step in range(shards):
            owner = lax.rem(me - step + shards, shards)
            place = pl.ds(pl.multiple_of(owner * part, part), part)
            last = step == shards - 1
            if last:
                for other in range(1, shards):
                    copies[other, 1].wait_recv()
            for c in range(2):
                weight = own_w.at[c] if step == 0 else got_w.at[step - 1, c]
                if step > 0:
                    copies[step, 2 + c].wait_recv()

                def matmul(j, _):
                    here = pl.ds(pl.multiple_of(j * tile_cols, tile_cols), tile_cols)
                    value = jnp.dot(ext_n[:, place], weight[:, here], preferred_element_type=f32)
                    acc[:, cols(c, j)] = value if step == 0 else acc[:, cols(c, j)] + value
                    if last:
                        (finish_conv, finish_gate)[c](j)
                    return 0

                lax.fori_loop(0, tiles, matmul, 0)
            if step > 0:
                saves.append(pltpu.make_async_copy(got_w.at[step - 1], in_out.at[:, place], own_sem.at[1 + step]))
                saves[-1].start()
        line.p[...] = low_acc[...].astype(bf16)
        outs += [(z_val, z_out), (ext_c, ext_out), (pre, pre_out), (act, act_out), (small_all, small_out), (gain_all, gain_out)]
        for k, (source, target) in enumerate(outs):
            if k:
                pltpu.make_async_copy(source, target, out_sem.at[k]).start()
        line.start()
        for c in range(line.ticks()):
            line.tick(c)
        line.finish()
        for save in saves + [own_save]:
            save.wait()
        for k, (source, target) in enumerate(outs):
            pltpu.make_async_copy(source, target, out_sem.at[k]).wait()
        for copy in copies.values():
            copy.wait_send()
        edge_copy.wait_send()

    sds = jax.ShapeDtypeStruct
    tails = hidden.reshape(seqs, local, width)[:, local - halo :]
    return pl.pallas_call(
        kernel,
        out_shape=[
            sds((2, shards * part, inner), bf16),
            sds((small.shape[0], small.shape[1] * shards), bf16),
            sds((gains.shape[0], gains.shape[1] * shards), bf16),
            sds((rows, width), bf16),
            sds((rows, inner), f32),
            sds((seqs * long, inner), bf16),
            sds((rows, inner), f32),
            sds((rows, inner), bf16),
            sds((low_len, rows), f32),
        ],
        in_specs=[VMEM, HBM, HBM, VMEM, VMEM],
        out_specs=[HBM] * 8 + [VMEM],
        scratch_shapes=[
            pltpu.VMEM((2, part, inner), bf16),
            pltpu.VMEM((max(shards - 1, 1), 2, part, inner), bf16),
            pltpu.VMEM((seqs, halo, width), bf16),
            pltpu.VMEM((rows, width), bf16),
            pltpu.VMEM((seqs * long, width), bf16),
            pltpu.VMEM((seqs * long, 2 * inner), f32),
            pltpu.VMEM((rows, inner), f32),
            pltpu.VMEM((seqs * long, tile_cols), f32),
            pltpu.VMEM((seqs * long, inner), bf16),
            pltpu.VMEM((rows, inner), f32),
            pltpu.VMEM((rows, inner), bf16),
            pltpu.VMEM((low_len, rows), f32),
            pltpu.VMEM((small.shape[0], small.shape[1] * shards), bf16),
            pltpu.VMEM((gains.shape[0], gains.shape[1] * shards), bf16),
            pltpu.SemaphoreType.DMA((shards, 4)),
            pltpu.SemaphoreType.DMA((shards, 4)),
            pltpu.SemaphoreType.DMA((2,)),
            pltpu.SemaphoreType.DMA((shards + 1,)),
            pltpu.SemaphoreType.DMA((7,)),
        ]
        + line.scratch(),
        compiler_params=pltpu.CompilerParams(
            collective_id=ident, has_side_effects=True, vmem_limit_bytes=56 << 20
        ),
    )(hidden, tails, in_half, small, gains)


piece = 32
unroll = 4


def spread(flat_ref, natural, first):
    for j in range(8):
        flat_ref[pl.ds(first * 8 + j, 8, stride=8), :] = natural[:, j * 128 : (j + 1) * 128]


def unspread(flat_ref, first):
    return jnp.concatenate([flat_ref[pl.ds(first * 8 + j, 8, stride=8), :] for j in range(8)], axis=1)


def tile(ref, t):
    return ref[pl.ds(pl.multiple_of(t * 8, 8), 8), :]


def row(ref, t, n, states):
    return ref[pl.ds(t * states + n, 8, stride=0), :]


def exchange(ends, got, send, recv, seq, width):
    me = lax.axis_index("ctx")
    copies = []
    for step in range(1, width):
        copies.append(
            pltpu.make_async_remote_copy(
                ends.at[seq],
                got.at[me, seq],
                send.at[seq, step],
                recv.at[seq, step],
                device_id={"ctx": lax.rem(me + step, width)},
                device_id_type=MESH,
            )
        )
        copies[-1].start()
    return copies


def ctx_greet(width):
    me = lax.axis_index("ctx")
    barrier = pltpu.get_barrier_semaphore()
    for step in range(1, width):
        pl.semaphore_signal(barrier, inc=1, device_id={"ctx": lax.rem(me + step, width)}, device_id_type=MESH)
    return barrier


def entering(got, seq, rate_ref, states, width, reverse):
    me = lax.axis_index("ctx")
    result = []
    for n in range(states):
        value = jnp.zeros((8, 128), f32)
        for k in reversed(range(width)) if reverse else range(width):
            new = jnp.exp2(got[k, seq, states] * rate_ref[n]) * value + got[k, seq, n]
            value = jnp.where(me < k if reverse else me > k, new, value)
        result.append(value)
    return result


def spread_rows(low_ref, first, out_ref):
    states, slots = 16, low_ref.shape[1]

    def lanes(k, _):
        block = low_ref[first : first + states, pl.ds(pl.multiple_of(k * 128, 128), 128)]
        for i in range(128):
            to = pl.ds(pl.multiple_of((k * 128 + i) * states, states), states)
            out_ref[to, :] = jnp.broadcast_to(block[:, i : i + 1], (states, 128))
        return 0

    lax.fori_loop(0, slots // 128, lanes, 0)


def scan_forward(low_all, act, gate_z, small, rate, out_parts, seqs, rank, at_step, at_bias, at_skip, ident):
    rows, channels = act.shape
    shards, _, part = out_parts.shape
    local = rows // seqs
    states = rate.shape[0]
    width = lax.axis_size("ctx")
    pieces = local // piece

    def kernel(
        low_ref, act_ref, z_ref, small_ref, rate_ref, w_ref,
        scan_ref, gated_ref, mixed_ref, pre_ref, kept_ref, enter_ref, size3, drive3,
        y3, ends, got, held, b_ref, c_ref, low_t, w_own, send, recv, out_sem, w_sem,
    ):
        barrier = ctx_greet(width)
        load = pltpu.make_async_copy(w_ref, w_own, w_sem)
        load.start()
        low_t[...] = low_ref[0:rank, :].T.astype(bf16)
        bias = small_ref[at_bias : at_bias + 16, :].astype(f32)[0:1]
        for j in range(channels // 256):
            here = slice(j * 256, (j + 1) * 256)
            value = jnp.dot(low_t[...], small_ref[at_step : at_step + rank, here], preferred_element_type=f32)
            pre_ref[:, here] = value + bias[:, here]
        spread_rows(low_ref, rank, b_ref)
        spread_rows(low_ref, rank + states, c_ref)

        def lay(i, _):
            first = pl.multiple_of(i * 16, 16)
            act_block = act_ref[pl.ds(first, 16), :].astype(f32)
            size = jax.nn.softplus(pre_ref[pl.ds(first, 16), :])
            drive = size * act_block
            for h in range(2):
                spread(size3, size[h * 8 : h * 8 + 8], first + h * 8)
                spread(drive3, drive[h * 8 : h * 8 + 8], first + h * 8)
            return 0

        lax.fori_loop(0, rows // 16, lay, 0)
        pl.semaphore_wait(barrier, width - 1)
        copies = []
        for seq in range(seqs):

            def first_pass(i, carried):
                values, total = list(carried[:-1]), carried[-1]
                for u in range(unroll):
                    t = seq * local + i * unroll + u
                    s, d = tile(size3, t), tile(drive3, t)
                    total = total + s
                    for n in range(states):
                        values[n] = jnp.exp2(s * rate_ref[n]) * values[n] + d * row(b_ref, t, n, states)
                return tuple(values) + (total,)

            zero = tuple(jnp.zeros((8, 128), f32) for _ in range(states + 1))
            done = lax.fori_loop(0, local // unroll, first_pass, zero)
            for n in range(states + 1):
                ends[seq, n] = done[n]
            copies.append(exchange(ends, got, send, recv, seq, width))
        me = lax.axis_index("ctx")
        for seq in range(seqs):
            for copy in copies[seq]:
                copy.wait()
            got[me, seq] = ends[seq]
            start = entering(got, seq, rate_ref, states, width, False)
            for n in range(states):
                enter_ref[seq, n] = start[n]

            def save(k, slot):
                return pltpu.make_async_copy(
                    held.at[slot], kept_ref.at[pl.ds(seq * local + k * piece, piece)], out_sem.at[slot]
                )

            def one_piece(k, carried):
                slot = lax.rem(k, 2)

                @pl.when(k >= 2)
                def _():
                    save(k - 2, slot).wait()

                def second_pass(i, values):
                    values = list(values)
                    for u in range(unroll):
                        inside = i * unroll + u
                        t = seq * local + k * piece + inside
                        s, d = tile(size3, t), tile(drive3, t)
                        acc = [None] * 4
                        for n in range(states):
                            values[n] = jnp.exp2(s * rate_ref[n]) * values[n] + d * row(b_ref, t, n, states)
                            held[slot, inside, n] = values[n]
                            part = values[n] * row(c_ref, t, n, states)
                            acc[n % 4] = part if acc[n % 4] is None else acc[n % 4] + part
                        y3[pl.ds(pl.multiple_of(t * 8, 8), 8), :] = (acc[0] + acc[1]) + (acc[2] + acc[3])
                    return tuple(values)

                carried = lax.fori_loop(0, piece // unroll, second_pass, carried)
                save(k, slot).start()
                return carried

            lax.fori_loop(0, pieces, one_piece, tuple(start))
            for k in (pieces - 2, pieces - 1):
                save(k, k % 2).wait()

        skip = small_ref[at_skip : at_skip + 16, :].astype(f32)[0:1]

        def back(i, _):
            first = pl.multiple_of(i * 16, 16)
            here = pl.ds(first, 16)
            value = jnp.concatenate([unspread(y3, first), unspread(y3, first + 8)], axis=0)
            value = value + skip * act_ref[here, :].astype(f32)
            scan_ref[here, :] = value
            gated_ref[here, :] = (value * jax.nn.silu(z_ref[here, :])).astype(bf16)
            return 0

        lax.fori_loop(0, rows // 16, back, 0)
        load.wait()
        for k in range(shards):
            for j in range(-(-part // 256)):
                span = min(256, part)
                value = jnp.dot(gated_ref[...], w_own[k, :, j * span : (j + 1) * span], preferred_element_type=f32)
                mixed_ref[:, k * part + j * span : k * part + (j + 1) * span] = value.astype(bf16)

    flat = jax.ShapeDtypeStruct((rows * 8, 128), f32)
    return pl.pallas_call(
        kernel,
        out_shape=[
            jax.ShapeDtypeStruct((rows, channels), f32),
            jax.ShapeDtypeStruct((rows, channels), bf16),
            jax.ShapeDtypeStruct((rows, shards * part), bf16),
            jax.ShapeDtypeStruct((rows, channels), f32),
            jax.ShapeDtypeStruct((rows, states, 8, 128), f32),
            jax.ShapeDtypeStruct((seqs, states, 8, 128), f32),
            flat,
            flat,
        ],
        in_specs=[VMEM] * 5 + [HBM],
        out_specs=[VMEM] * 4 + [HBM, VMEM, VMEM, VMEM],
        scratch_shapes=[
            pltpu.VMEM((rows * 8, 128), f32),
            pltpu.VMEM((seqs, states + 1, 8, 128), f32),
            pltpu.VMEM((width, seqs, states + 1, 8, 128), f32),
            pltpu.VMEM((2, piece, states, 8, 128), f32),
            pltpu.VMEM((rows * states, 128), f32),
            pltpu.VMEM((rows * states, 128), f32),
            pltpu.VMEM((rows, rank), bf16),
            pltpu.VMEM(out_parts.shape, bf16),
            pltpu.SemaphoreType.DMA((seqs, width)),
            pltpu.SemaphoreType.DMA((seqs, width)),
            pltpu.SemaphoreType.DMA((2,)),
            pltpu.SemaphoreType.DMA,
        ],
        compiler_params=pltpu.CompilerParams(
            collective_id=ident, has_side_effects=True, vmem_limit_bytes=48 << 20
        ),
    )(low_all, act, gate_z, small, rate, out_parts)


def sublane_sums(parts):
    at = lax.broadcasted_iota(jnp.int32, (8, 128), 0)
    for shift in (4, 2, 1):
        low = (at // shift) % 2 == 0
        half = len(parts) // 2
        merged = []
        for one, two in zip(parts[:half], parts[half:]):
            merged.append(
                jnp.where(low, one + pltpu.roll(one, 8 - shift, 0), two + pltpu.roll(two, shift, 0))
            )
        parts = merged
    return parts[0]


def scan_backward(size3, drive3, grad, low_all, rank, rate, kept, enter, seqs, ident, partial, epilogue, extras, chunk, scatters):
    rows, channels = grad.shape
    local = rows // seqs
    states = rate.shape[0]
    width = lax.axis_size("ctx")
    pieces = local // piece
    early = 2
    unroll_b = 2
    line = Line(partial.shape, chunk, epilogue, extras, bf16)
    share = Halving(scatters, 64)
    n_line, n_ex, n_sc = len(line.scratch()), len(extras), len(scatters)

    def kernel(*refs):
        refs = list(refs)

        def take_refs(n):
            taken = refs[:n]
            del refs[:n]
            return taken

        size_ref, drive_ref, grad_ref, low_ref, rate_ref, kept_ref, enter_ref, p_ref = take_refs(8)
        ins, full = take_refs(n_ex), take_refs(n_sc)
        tb_ref, sd_ref, bg_ref, cg_ref, dec_ref, sum_ref = take_refs(6)
        shares = take_refs(n_sc)
        grad3, tb3, sd3, b_ref, c_ref, ends, got, held, bpart, cpart, prior, send, recv, in_sem = take_refs(14)
        line.bind(p_ref, ins, sum_ref, [], take_refs(n_line))
        share.bind(full, shares, refs)
        barrier = ctx_greet(width)
        line.begin(barrier, width - 1 + share.greet(barrier))
        share.start()
        spread_rows(low_ref, rank, b_ref)
        spread_rows(low_ref, rank + states, c_ref)

        def lay(i, _):
            first = pl.multiple_of(i * 8, 8)
            spread(grad3, grad_ref[pl.ds(first, 8), :], first)
            return 0

        lax.fori_loop(0, rows // 8, lay, 0)

        def fetch(seq, k, slot):
            return pltpu.make_async_copy(
                kept_ref.at[pl.ds(seq * local + k * piece, piece)], held.at[slot], in_sem.at[slot]
            )

        copies = []
        for seq in range(seqs):

            def first_pass(i, carried):
                values, total = list(carried[:-1]), carried[-1]
                for u in range(unroll):
                    t = seq * local + local - 1 - (i * unroll + u)
                    s, g = tile(size_ref, t), tile(grad3, t)
                    total = total + s
                    for n in range(states):
                        values[n] = jnp.exp2(s * rate_ref[n]) * (values[n] + g * row(c_ref, t, n, states))
                return tuple(values) + (total,)

            zero = tuple(jnp.zeros((8, 128), f32) for _ in range(states + 1))
            done = zero
            for half in range(early):
                span = local // unroll // early
                done = lax.fori_loop(half * span, (half + 1) * span, first_pass, done)
                line.tick(seq * early + half)
            for n in range(states + 1):
                ends[seq, n] = done[n]
            copies.append(exchange(ends, got, send, recv, seq, width))
        me = lax.axis_index("ctx")
        for n in range(states):
            dec_ref[n] = jnp.zeros((8, 128), f32)
        for seq in range(seqs):
            fetch(seq, pieces - 1, (pieces - 1) % 2).start()
            for copy in copies[seq]:
                copy.wait()
            got[me, seq] = ends[seq]
            start = entering(got, seq, rate_ref, states, width, True)
            fetch(seq, pieces - 1, (pieces - 1) % 2).wait()

            def one_slot(slot, k, inside, adjoint, decays, prior_at):
                t = seq * local + k * piece + inside
                s, d, g = tile(size_ref, t), tile(drive_ref, t), tile(grad3, t)
                tb, sd = [None] * 2, [None] * 2
                b_parts, c_parts = [], []
                for n in range(states):
                    total = adjoint[n] + g * row(c_ref, t, n, states)
                    c_parts.append(held[slot, inside, n] * g)
                    b_parts.append(total * d)
                    through = total * row(b_ref, t, n, states)
                    adjoint[n] = jnp.exp2(s * rate_ref[n]) * total
                    kept_part = adjoint[n] * prior_at(n)
                    through_size = kept_part * rate_ref[n]
                    decays[n] = decays[n] + kept_part * s
                    tb[n % 2] = through if tb[n % 2] is None else tb[n % 2] + through
                    sd[n % 2] = through_size if sd[n % 2] is None else sd[n % 2] + through_size
                here = pl.ds(pl.multiple_of(t * 8, 8), 8)
                tb3[here, :] = tb[0] + tb[1]
                sd3[here, :] = sd[0] + sd[1]
                for h in range(states // 8):
                    spot = pl.ds(pl.multiple_of(inside * states + h * 8, 8), 8)
                    bpart[spot, :] = sublane_sums(b_parts[h * 8 : h * 8 + 8])
                    cpart[spot, :] = sublane_sums(c_parts[h * 8 : h * 8 + 8])

            def one_piece(back_k, carried):
                k = pieces - 1 - back_k
                slot = lax.rem(k, 2)

                @pl.when(k > 0)
                def _():
                    fetch(seq, k - 1, 1 - slot).start()

                def slots(i, carried):
                    adjoint, decays = list(carried[:states]), list(carried[states:])
                    for u in range(unroll_b):
                        inside = piece - 1 - (i * unroll_b + u)
                        one_slot(slot, k, inside, adjoint, decays, lambda n: held[slot, inside - 1, n])
                    return tuple(adjoint) + tuple(decays)

                carried = lax.fori_loop(0, piece // unroll_b - 1, slots, carried)
                adjoint, decays = list(carried[:states]), list(carried[states:])
                for inside in reversed(range(1, unroll_b)):
                    one_slot(slot, k, inside, adjoint, decays, lambda n: held[slot, inside - 1, n])

                @pl.when(k > 0)
                def _():
                    fetch(seq, k - 1, 1 - slot).wait()
                    prior[...] = held[1 - slot, piece - 1]

                @pl.when(k == 0)
                def _():
                    prior[...] = enter_ref[seq]

                one_slot(slot, k, 0, adjoint, decays, lambda n: prior[n])
                ones = jnp.ones((8, 128), bf16)
                for part, out in ((bpart, bg_ref), (cpart, cg_ref)):
                    sums = outer_cols(ones, part[...].astype(bf16))
                    out[pl.ds(seq * pieces + k, 1)] = sums[None]
                line.tick(seqs * early + seq * pieces + back_k)
                share.tick(seq * pieces + back_k)
                return tuple(adjoint) + tuple(decays)

            zero = tuple(jnp.zeros((8, 128), f32) for _ in range(states))
            carried = lax.fori_loop(0, pieces, one_piece, tuple(start) + zero)
            for n in range(states):
                dec_ref[n] = dec_ref[n] + carried[states + n]

        def back(i, _):
            first = pl.multiple_of(i * 8, 8)
            tb_ref[pl.ds(first, 8), :] = unspread(tb3, first)
            sd_ref[pl.ds(first, 8), :] = unspread(sd3, first)
            return 0

        lax.fori_loop(0, rows // 8, back, 0)
        for c in range(seqs * (early + pieces), line.ticks()):
            line.tick(c)
        for i in range(seqs * pieces, share.turns):
            share.tick(i)
        line.finish()
        share.finish()

    nat = jax.ShapeDtypeStruct((rows, channels), f32)
    sums = jax.ShapeDtypeStruct((rows // piece, 8, piece * states), f32)
    return pl.pallas_call(
        kernel,
        out_shape=[nat, nat, sums, sums, jax.ShapeDtypeStruct((states, 8, 128), f32),
                   jax.ShapeDtypeStruct(partial.shape, bf16)] + share.results(),
        in_specs=[VMEM] * 5 + [HBM, VMEM] + [HBM] * (1 + n_ex + n_sc),
        out_specs=[VMEM] * (6 + n_sc),
        scratch_shapes=[pltpu.VMEM((rows * 8, 128), f32)] * 3
        + [pltpu.VMEM((rows * states, 128), f32)] * 2
        + [
            pltpu.VMEM((seqs, states + 1, 8, 128), f32),
            pltpu.VMEM((width, seqs, states + 1, 8, 128), f32),
            pltpu.VMEM((2, piece, states, 8, 128), f32),
            pltpu.VMEM((piece * states, 128), f32),
            pltpu.VMEM((piece * states, 128), f32),
            pltpu.VMEM((states, 8, 128), f32),
            pltpu.SemaphoreType.DMA((seqs, width)),
            pltpu.SemaphoreType.DMA((seqs, width)),
            pltpu.SemaphoreType.DMA((2,)),
        ]
        + line.scratch()
        + share.scratch(),
        compiler_params=pltpu.CompilerParams(
            collective_id=ident, has_side_effects=True, vmem_limit_bytes=62 << 20
        ),
    )(size3, drive3, grad, low_all, rate, kept, enter, partial, *extras, *share.folded)


def scan_tail(through_b, through_decay, sums, decay_grad, scan_grad, step_pre, pre_act, act, padded, low_all, small, ident,
              seqs, low_len, rank, states, taps):
    rows, inner = act.shape
    local = rows // seqs
    long = local + halo
    shards, pieces = lax.axis_size("shard"), lax.axis_size("ctx")
    places = shards * pieces
    lane = inner // places
    line = Line((low_len, rows), 80, plain_end, [], bf16)
    tiles = inner // tile_cols
    at = low_len + rank
    lines = -(-(at + states + taps + 3) // 8) * 8
    height = -(-(lines + 8) // 32) * 32
    over = 8

    def kernel(
        tb_ref, sd_ref, sums_ref, dec_ref, sg_ref, sp_ref, pre_ref, act_ref, ext_ref, low_ref, small_ref,
        conv_ref, blocks_ref,
        low_out, low_t, step_g, low_acc, grads, pre_g, conv_f, edge, edge_out, edge_sem, *rest
    ):
        ctx = lax.axis_index("ctx")
        barrier = pltpu.get_barrier_semaphore()
        line.bind(rest[0], [], low_out, [], list(rest))
        pl.semaphore_signal(barrier, inc=1, device_id={"ctx": lax.rem(ctx + 1, pieces)}, device_id_type=MESH)

        def cols(j):
            return pl.ds(pl.multiple_of(j * tile_cols, tile_cols), tile_cols)

        low_acc[...] = jnp.zeros_like(low_acc)
        grads[...] = jnp.zeros_like(grads)
        low_t[...] = low_ref[0:rank, :].astype(bf16)

        def size_tile(j, _):
            here = cols(j)
            bias_grad = jnp.zeros((8, tile_cols), f32)
            skip_grad = jnp.zeros((8, tile_cols), f32)
            for k in range(rows // 64):
                to = slice(k * 64, (k + 1) * 64)
                act_block = act_ref[to, here].astype(f32)
                size_grad = act_block * tb_ref[to, here] + sd_ref[to, here] * (1.0 / log2e)
                value = (size_grad * jax.nn.sigmoid(sp_ref[to, here])).astype(bf16)
                step_g[to, here] = value
                wide = value.astype(f32)
                product = sg_ref[to, here] * act_block
                for h in range(8):
                    bias_grad = bias_grad + wide[h * 8 : h * 8 + 8]
                    skip_grad = skip_grad + product[h * 8 : h * 8 + 8]
            grads[at + states + taps + 1 : at + states + taps + 2, here] = jnp.sum(bias_grad, axis=0, keepdims=True)
            grads[at + states + taps + 2 : at + states + taps + 3, here] = jnp.sum(skip_grad, axis=0, keepdims=True)
            low_acc[...] = low_acc[...] + outer_cols(small_ref[low_len : low_len + rank, here], step_g[:, here])
            return 0

        lax.fori_loop(0, tiles, size_tile, 0)
        line.p[0:rank, :] = low_acc[...].astype(bf16)
        line.p[rank : rank + 2 * states, :] = sums_ref[...].astype(bf16)
        line.greet(barrier, 1)
        line.start()

        def step_tile(j, _):
            here = cols(j)
            grads[low_len:at, here] = jnp.dot(low_t[...], step_g[:, here], preferred_element_type=f32)
            return 0

        lax.fori_loop(0, tiles, step_tile, 0)
        grads[at : at + states, :] = dec_ref[...]
        for c in range(line.ticks()):
            line.tick(c)
        line.finish()

        def pre_tile(j, _):
            here = cols(j)
            grads[0:low_len, here] = jnp.dot(low_out[...], act_ref[:, here], preferred_element_type=f32)
            for seq in range(seqs):
                low = inner_rows(low_out[:, seq * local : (seq + 1) * local], small_ref[0:low_len, here])
                conv_f[seq * long : (seq + 1) * long, :] = ext_ref[seq * long : (seq + 1) * long, here].astype(f32)
                pre_g[seq * (local + over) : seq * (local + over) + local, here] = low
            skip = small_ref[at + states + 32 : at + states + 48, here].astype(f32)[0:1]
            bias_sum = jnp.zeros((8, tile_cols), f32)
            tap_sums = [jnp.zeros((8, tile_cols), f32) for _ in range(taps)]
            for seq in range(seqs):
                for k in range(local // 64):
                    to = slice(seq * local + k * 64, seq * local + (k + 1) * 64)
                    where = slice(seq * (local + over) + k * 64, seq * (local + over) + (k + 1) * 64)
                    act_grad = skip * sg_ref[to, here] + jax.nn.softplus(sp_ref[to, here]) * tb_ref[to, here]
                    value = (act_grad + pre_g[where, here]) * silu_grad(pre_ref[to, here])
                    pre_g[where, here] = value
                    first = seq * long + halo + k * 64 - taps + 1
                    products = [value * conv_f[first + tap : first + tap + 64, :] for tap in range(taps)]
                    for h in range(8):
                        bias_sum = bias_sum + value[h * 8 : h * 8 + 8]
                        for tap in range(taps):
                            tap_sums[tap] = tap_sums[tap] + products[tap][h * 8 : h * 8 + 8]
            for tap in range(taps):
                row = at + states + tap
                grads[row : row + 1, here] = jnp.sum(tap_sums[tap], axis=0, keepdims=True)
            row = at + states + taps
            grads[row : row + 1, here] = jnp.sum(bias_sum, axis=0, keepdims=True)
            return 0

        lax.fori_loop(0, tiles, pre_tile, 0)
        for seq in range(seqs):
            edge_out[seq] = pre_g[seq * (local + over) : seq * (local + over) + over, :]
        copy = pltpu.make_async_remote_copy(
            edge_out, edge, edge_sem.at[0], edge_sem.at[1],
            device_id={"ctx": lax.rem(ctx + pieces - 1, pieces)}, device_id_type=MESH,
        )
        copy.start()
        for p in range(places):
            blocks_ref[p * height : p * height + lines, :] = grads[:, p * lane : (p + 1) * lane].astype(bf16)
            blocks_ref[p * height + lines : (p + 1) * height, :] = jnp.zeros((height - lines, lane), bf16)
        copy.wait()
        inside = (ctx < pieces - 1).astype(f32)
        for seq in range(seqs):
            first = seq * (local + over) + local
            pre_g[first : first + over, :] = edge[seq] * inside

        def conv_tile(j, _):
            here = cols(j)
            weights = small_ref[at + states : at + states + 16, here].astype(f32)
            for seq in range(seqs):
                for k in range(local // 64):
                    first = seq * (local + over) + k * 64 + taps - 1
                    total = weights[0:1] * pre_g[first : first + 64, here]
                    for tap in range(1, taps):
                        total = total + weights[tap : tap + 1] * pre_g[first - tap : first - tap + 64, here]
                    conv_ref[seq * local + k * 64 : seq * local + (k + 1) * 64, here] = total.astype(bf16)
            return 0

        lax.fori_loop(0, tiles, conv_tile, 0)

    return pl.pallas_call(
        kernel,
        out_shape=[
            jax.ShapeDtypeStruct((rows, inner), bf16),
            jax.ShapeDtypeStruct((places * height, lane), bf16),
        ],
        in_specs=[VMEM] * 11,
        out_specs=[VMEM] * 2,
        scratch_shapes=[
            pltpu.VMEM((low_len, rows), bf16),
            pltpu.VMEM((rank, rows), bf16),
            pltpu.VMEM((rows, inner), bf16),
            pltpu.VMEM((rank, rows), f32),
            pltpu.VMEM((lines, inner), f32),
            pltpu.VMEM((seqs * (local + over), inner), f32),
            pltpu.VMEM((seqs * long, tile_cols), f32),
            pltpu.VMEM((seqs, over, inner), f32),
            pltpu.VMEM((seqs, over, inner), f32),
            pltpu.SemaphoreType.DMA((2,)),
        ]
        + line.scratch(),
        compiler_params=pltpu.CompilerParams(
            collective_id=ident, has_side_effects=True, vmem_limit_bytes=56 << 20
        ),
    )(through_b, through_decay, sums, decay_grad, scan_grad, step_pre, pre_act, act, padded, low_all, small), height


def body(
    hidden_in, lengths, cotangent, norm_gain, in_weight, conv_weight, conv_bias, low_weight, step_weight,
    step_bias, decay_log, skip_gain, out_weight, ffn_gain, gate_up, down_weight,
):
    seqs, local, width = hidden_in.shape
    rows = seqs * local
    shards, pieces = lax.axis_size("shard"), lax.axis_size("ctx")
    inner = in_weight.shape[2]
    taps = conv_weight.shape[0]
    rank = step_weight.shape[0]
    states = decay_log.shape[0]
    low_len = low_weight.shape[0]

    def rows16(v):
        return jnp.pad(v, ((0, 16 - v.shape[0]), (0, 0)))

    small = jnp.concatenate(
        [low_weight, step_weight, decay_log, rows16(jnp.concatenate([conv_weight, conv_bias[None]], axis=0)),
         rows16(step_bias[None]), rows16(skip_gain[None])], axis=0,
    )
    at_bias = low_len + rank + states + 16
    at_skip = at_bias + 16
    hidden_rows = hidden_in.reshape(rows, width)
    small = jnp.pad(small, ((0, -small.shape[0] % 16), (0, 0)))
    gains = jnp.stack([norm_gain, ffn_gain])
    gains = jnp.pad(gains, ((0, 14), (0, 0)))
    in_half = in_weight.transpose(1, 0, 2)
    in_w, small, gains, normed_one, gate_z, padded, pre_act, act_half, low_all = front(
        hidden_rows, in_half, small, gains, seqs, low_len + rank + states, taps, low_len, 0
    )
    out_parts = lax.all_gather(out_weight, "shard")
    gate_half = gate_up.transpose(1, 0, 2)
    gate_w = [lax.all_gather(gate_half[c], "shard", axis=0, tiled=True) for c in range(2)]
    down_parts = lax.all_gather(down_weight, "shard")
    part = width // shards

    low_w = small[:low_len]
    step_w = small[low_len : low_len + rank]
    at = low_len + rank
    decay_w = small[at : at + states].astype(f32)
    kernel = small[at + states : at + states + taps].astype(f32)
    skip_full = small[at_skip].astype(f32)
    gain_one, gain_two = gains[0:1].astype(f32), gains[1:2].astype(f32)

    first_slot = lax.axis_index("ctx") * local
    positions = first_slot + jnp.arange(local, dtype=jnp.int32)
    pad_mask = (positions[None, :] < lengths[:, None]).astype(f32)

    source = hidden_rows.astype(f32)
    act_full = act_half.astype(f32)
    step_low = low_all[:rank].astype(bf16)
    decay_rate = -jnp.exp(decay_w)
    rate = (decay_rate * log2e).reshape(states, 8, 128)
    scan_out, gated_out, mixed_part, step_pre, kept, enter, size3, drive3 = scan_forward(
        low_all, act_half, gate_z, small, rate, out_parts, seqs, rank, low_len, at_bias, at_skip, 2
    )
    step_size = jax.nn.softplus(step_pre)
    gate_act = jax.nn.silu(gate_z)
    wide = jax.ShapeDtypeStruct((rows, width), f32)
    normed_two, middle = tp_sum(mixed_part, norm_end, [hidden_rows, gain_two], [wide], 32, 3)
    gate_lin, up_lin = (jnp.dot(normed_two, gate_w[c], preferred_element_type=f32) for c in range(2))
    hidden_ffn = (jax.nn.silu(gate_lin) * up_lin).astype(bf16)
    ffn_part = jnp.concatenate(
        [jnp.dot(hidden_ffn, down_parts[k], preferred_element_type=f32) for k in range(shards)], axis=1
    ).astype(bf16)

    upstream = cotangent.reshape(rows, width).astype(f32) * pad_mask.reshape(rows, 1)
    ffn_grad = upstream.astype(bf16)
    down_grad = inner_rows(ffn_grad, hidden_ffn).astype(bf16)
    hidden_grad = sum(outer_cols(ffn_grad[:, k * part : (k + 1) * part], down_parts[k]) for k in range(shards))
    gate_grad = (hidden_grad * up_lin * silu_grad(gate_lin)).astype(bf16)
    up_grad = (hidden_grad * jax.nn.silu(gate_lin)).astype(bf16)
    gate_up_grad = [inner_rows(normed_two, g).astype(bf16) for g in (gate_grad, up_grad)]
    back_part = (outer_cols(gate_grad, gate_w[0]) + outer_cols(up_grad, gate_w[1])).astype(bf16)
    mix_grad, middle_grad, *ffn_shares = tp_sum(
        back_part, norm_back_end, [middle, gain_two, ffn_grad], [wide], 32, 5, scatters=gate_up_grad + [down_grad]
    )
    ffn_gain_grad = jnp.sum(back_part.astype(f32) * normed_two.astype(f32), axis=0) / gain_two[0]

    out_weight_grad = inner_rows(mix_grad, gated_out).astype(bf16)
    gated_grad = sum(outer_cols(mix_grad[:, k * part : (k + 1) * part], out_parts[k]) for k in range(shards))
    scan_grad = gated_grad * gate_act
    z_grad = gated_grad * scan_out * silu_grad(gate_z)
    through_b, through_decay, b_sums, c_sums, decay_sum, mixed_out, out_share = scan_backward(
        size3, drive3, scan_grad, low_all, rank, rate, kept, enter, seqs, 6, ffn_part, add_end, [middle], 32,
        [out_weight_grad],
    )
    mixed_out = mixed_out.reshape(hidden_in.shape)
    decay_log_grad = decay_sum.reshape(states, inner) * decay_rate
    sums = jnp.concatenate([v[:, 0].reshape(rows, states).T for v in (b_sums, c_sums)], axis=0)
    (conv_grad, small_blocks), small_height = scan_tail(
        through_b, through_decay, sums, decay_log_grad, scan_grad, step_pre, pre_act, act_half, padded, low_all, small, 7,
        seqs, low_len, rank, states, taps,
    )
    z_half = z_grad.astype(bf16)
    in_weight_grad = [inner_rows(normed_one, g).astype(bf16) for g in (conv_grad, z_half)]
    first_part = (outer_cols(conv_grad, in_w[0]) + outer_cols(z_half, in_w[1])).astype(bf16)
    norm_gain_grad = jnp.sum(first_part.astype(f32) * source * rms_scale(source), axis=0)
    places, share = shards * pieces, width // (shards * pieces)
    lane = inner // places
    gain_rows = -(-2 * share // lane)
    gain_blocks = jnp.concatenate([norm_gain_grad.reshape(places, share), ffn_gain_grad.reshape(places, share)], axis=1)
    gain_blocks = jnp.pad(gain_blocks, ((0, 0), (0, gain_rows * lane - 2 * share))).reshape(places, gain_rows, lane)
    gain_height = 16 * -(-gain_rows // 16)
    gain_blocks = jnp.pad(gain_blocks, ((0, 0), (gain_height - gain_rows, 0), (0, 0)))
    gain_blocks = gain_blocks.reshape(places * gain_height, lane).astype(bf16)
    input_grad, in_share, z_share, small_out, gain_share = tp_sum(
        first_part, norm_back_end, [hidden_rows, gain_one, middle_grad], [], 32, 8,
        scatters=in_weight_grad + [small_blocks, gain_blocks], line_too=True,
        steps=[16, 16, small_height // 2, gain_height],
    )
    gain_share = gain_share[gain_height - gain_rows :].reshape(-1)
    input_grad = input_grad.astype(f32).reshape(hidden_in.shape)
    at = low_len + rank
    return (
        mixed_out,
        input_grad,
        gain_share[:share],
        jnp.stack([in_share, z_share], axis=1),
        small_out[at + states : at + states + taps],
        small_out[at + states + taps],
        small_out[:low_len],
        small_out[low_len : low_len + rank],
        small_out[at + states + taps + 1],
        small_out[at : at + states],
        small_out[at + states + taps + 2],
        out_share.T,
        gain_share[share : 2 * share],
        jnp.stack(ffn_shares[:2], axis=1),
        ffn_shares[2].T,
    )


def solution(mesh):
    placed = (
        P("shard", "ctx", None),
        P("shard"),
        P("shard", "ctx", None),
        P("shard"),
        P("shard", None, "tp"),
        P(None, ("tp", "shard")),
        P(("tp", "shard")),
        P(None, ("tp", "shard")),
        P(None, ("tp", "shard")),
        P(("tp", "shard")),
        P(None, ("tp", "shard")),
        P(("tp", "shard")),
        P("tp", "shard"),
        P("shard"),
        P("shard", None, "tp"),
        P("tp", "shard"),
    )
    return jax.shard_map(
        body,
        mesh=mesh,
        in_specs=placed,
        out_specs=(
            P("shard", "ctx", None),
            P("shard", "ctx", None),
            P(("shard", "ctx")),
            P(("shard", "ctx"), None, "tp"),
            P(None, ("tp", "shard", "ctx")),
            P(("tp", "shard", "ctx")),
            P(None, ("tp", "shard", "ctx")),
            P(None, ("tp", "shard", "ctx")),
            P(("tp", "shard", "ctx")),
            P(None, ("tp", "shard", "ctx")),
            P(("tp", "shard", "ctx")),
            P("tp", ("shard", "ctx")),
            P(("shard", "ctx")),
            P(("shard", "ctx"), None, "tp"),
            P("tp", ("shard", "ctx")),
        ),
        check_vma=False,
    )
```

```python
import functools

import jax
import jax.numpy as jnp
from jax import lax
from jax.experimental import pallas as pl
from jax.experimental.pallas import tpu as pltpu
from jax.sharding import PartitionSpec as P

MESH = pl.DeviceIdType.MESH
epsilon = 1e-05
log2e = 1.4426950408889634
bf16 = jnp.bfloat16
f32 = jnp.float32
VMEM = pl.BlockSpec(memory_space=pltpu.VMEM)
HBM = pl.BlockSpec(memory_space=pl.ANY)


def inner_rows(left, right):
    return lax.dot_general(left, right, (((0,), (0,)), ((), ())), preferred_element_type=f32)


def outer_cols(left, right):
    return lax.dot_general(left, right, (((1,), (1,)), ((), ())), preferred_element_type=f32)


def silu_grad(values):
    sig_val = jax.nn.sigmoid(values)
    return sig_val * (1.0 + values * (1.0 - sig_val))


def rms_scale(source):
    return lax.rsqrt(jnp.mean(source * source, axis=-1, keepdims=True) + epsilon)


class Line:
    lag = 3
    ahead = 4

    def __init__(self, shape, chunk, epilogue, extras, out_dtype):
        self.shape, self.chunk, self.epilogue, self.out_dtype = shape, chunk, epilogue, out_dtype
        self.count = shape[0] // chunk
        self.extras = [(e.shape, e.dtype) for e in extras]

    def scratch(self):
        return (
            [pltpu.VMEM(self.shape, bf16)] * 4
            + [pltpu.SemaphoreType.DMA((self.count,))] * 6
            + [pltpu.VMEM(shape, dtype) for shape, dtype in self.extras]
            + [pltpu.SemaphoreType.DMA((1 + len(self.extras),))]
        )

    def bind(self, p_ref, ins, out_ref, outs, scratch):
        self.p_ref, self.given, self.out_ref, self.outs = p_ref, ins, out_ref, outs
        (self.p, self.got_a, self.pair, self.got_b, self.a_send, self.a_recv, self.b_send, self.b_recv,
         self.c_send, self.c_recv) = scratch[:10]
        self.ins, self.in_sem = scratch[10:-1], scratch[-1]
        me = lax.axis_index("tp")
        self.mate = me + 1 - 2 * (me % 2)
        self.across = 3 - me
        self.middle = jnp.logical_or(me == 1, me == 2)

    def at(self, c):
        return pl.ds(pl.multiple_of(c * self.chunk, self.chunk), self.chunk)

    def remote(self, source, target, send, recv, c, to):
        return pltpu.make_async_remote_copy(
            source.at[self.at(c)], target.at[self.at(c)], send.at[c], recv.at[c], device_id={"tp": to}, device_id_type=MESH
        )

    def copy_a(self, c):
        return self.remote(self.p_ref, self.got_a, self.a_send, self.a_recv, c, self.mate)

    def copy_b(self, c):
        return self.remote(self.pair, self.got_b, self.b_send, self.b_recv, c, self.across)

    def copy_c(self, c):
        return self.remote(self.out_ref, self.out_ref, self.c_send, self.c_recv, c, self.mate)

    def loads(self):
        pairs = [(self.p_ref, self.p)] + list(zip(self.given, self.ins))
        return [pltpu.make_async_copy(a, b, self.in_sem.at[i]) for i, (a, b) in enumerate(pairs)]

    def begin(self, barrier, met, ends_meet=False):
        pl.semaphore_signal(barrier, inc=1, device_id={"tp": self.mate}, device_id_type=MESH)

        @pl.when(self.middle)
        def _():
            pl.semaphore_signal(barrier, inc=1, device_id={"tp": self.across}, device_id_type=MESH)
            for load in self.loads():
                load.start()
            pl.semaphore_wait(barrier, met + 2)
            for load in self.loads():
                load.wait()

        @pl.when(jnp.logical_not(self.middle))
        def _():
            if ends_meet:
                pl.semaphore_signal(barrier, inc=1, device_id={"tp": self.across}, device_id_type=MESH)
            pl.semaphore_wait(barrier, met + 2 if ends_meet else met + 1)

            for c in range(min(self.ahead, self.count)):
                self.copy_a(c).start()

    def greet(self, barrier, met):
        pl.semaphore_signal(barrier, inc=1, device_id={"tp": self.mate}, device_id_type=MESH)

        @pl.when(self.middle)
        def _():
            pl.semaphore_signal(barrier, inc=1, device_id={"tp": self.across}, device_id_type=MESH)
            pl.semaphore_wait(barrier, met + 2)

        @pl.when(jnp.logical_not(self.middle))
        def _():
            pl.semaphore_wait(barrier, met + 1)

    def start(self):
        @pl.when(jnp.logical_not(self.middle))
        def _():
            for c in range(min(self.ahead, self.count)):
                self.copy_a(c).start()

    def first(self, c):
        at = self.at(c)
        self.copy_a(c).wait_recv()
        self.pair[at, :] = (self.p[at, :].astype(f32) + self.got_a[at, :].astype(f32)).astype(bf16)
        self.copy_b(c).start()

    def second(self, c):
        at = self.at(c)
        self.copy_b(c).wait_recv()
        total = self.pair[at, :].astype(f32) + self.got_b[at, :].astype(f32)
        self.epilogue(c, at, total, self.ins, self.out_ref, self.outs)
        self.copy_c(c).start()

    def tick(self, c):
        lag = min(self.lag, self.count)

        @pl.when(jnp.logical_and(self.middle, c < self.count))
        def _():
            self.first(c)

        @pl.when(jnp.logical_and(self.middle, jnp.logical_and(c >= lag, c < self.count + lag)))
        def _():
            self.second(c - lag)

        @pl.when(jnp.logical_and(jnp.logical_not(self.middle), c + self.ahead < self.count))
        def _():
            self.copy_a(c + self.ahead).start()

    def quiet_tick(self, c):
        lag = min(self.lag, self.count)

        @pl.when(jnp.logical_and(self.middle, jnp.logical_and(c >= 0, c < self.count)))
        def _():
            self.first(c)

        @pl.when(jnp.logical_and(self.middle, jnp.logical_and(c >= lag, c < self.count + lag)))
        def _():
            self.second(c - lag)

    def ticks(self):
        return self.count + min(self.lag, self.count)

    def finish(self, take_result=True):
        @pl.when(self.middle)
        def _():
            def drain(c, _):
                self.copy_b(c).wait_send()
                self.copy_c(c).wait_send()
                return 0

            lax.fori_loop(0, self.count, drain, 0)

        @pl.when(jnp.logical_not(self.middle))
        def _():
            def take(c, _):
                if take_result:
                    self.copy_c(c).wait_recv()
                self.copy_a(c).wait_send()
                return 0

            lax.fori_loop(0, self.count, take, 0)


share_lag = 2
share_ahead = 2


class Halving:
    def __init__(self, arrays, step_rows=16, lag=share_lag):
        self.lag = lag
        steps = [step_rows] * len(arrays) if isinstance(step_rows, int) else list(step_rows)
        self.steps = steps
        shards, pieces = lax.axis_size("shard"), lax.axis_size("ctx")
        self.n = len(arrays)
        self.bits = [
            (axis, 1 << k)
            for axis, size in (("shard", shards), ("ctx", pieces))
            for k in reversed(range(size.bit_length() - 1))
        ]
        self.depth = len(self.bits)
        head = shards.bit_length() - 1
        self.dims = list(range(self.depth))
        self.orders = (self.dims, self.dims[:head] + self.dims[head:][::-1])
        self.parts = [g.shape[0] // (shards * pieces) // k for g, k in zip(arrays, steps)]
        self.folded = [
            g.reshape((2,) * self.depth + (p * k, g.shape[1])) for g, p, k in zip(arrays, self.parts, steps)
        ]
        self.tails = [g.shape[self.depth :] for g in self.folded]
        self.pairs = (max(self.parts, default=0) + 1) // 2
        self.turns = self.pairs + lag * (self.depth - 1)

    def results(self):
        return [jax.ShapeDtypeStruct(tail, f32) for tail in self.tails]

    def scratch(self):
        if not self.n:
            return []
        held = [pltpu.VMEM((2,) * (self.depth - 1) + tail, bf16) for tail in self.tails]
        for j in range(self.depth):
            held += [pltpu.VMEM((2,) * (self.depth - 1 - j) + tail, bf16) for tail in self.tails]
        sem = pltpu.SemaphoreType.DMA((self.depth, self.n, max(self.parts)))
        return held + [sem, sem, pltpu.SemaphoreType.DMA((self.n, max(self.parts)))]

    def bind(self, full, shares, scratch):
        n = self.n
        self.partner, self.mine = [], []
        if not n:
            return
        self.full, self.shares, self.own = full, shares, scratch[:n]
        self.landed = [scratch[n * (j + 1) : n * (j + 2)] for j in range(self.depth)]
        self.send, self.recv, self.own_sem = scratch[n * (self.depth + 1) :]
        for axis, bit in self.bits:
            here = lax.axis_index(axis)
            self.mine.append((here // bit) % 2)
            self.partner.append({axis: here + bit - 2 * bit * ((here // bit) % 2)})

    def greet(self, barrier):
        for who in self.partner:
            pl.semaphore_signal(barrier, inc=1, device_id=who, device_id_type=MESH)
        return len(self.partner)

    def spot(self, a, c):
        return pl.ds(pl.multiple_of(c * self.steps[a], self.steps[a]), self.steps[a])

    def pick(self, remaining, dim, index, a, c):
        return tuple(index if d == dim else slice(None) for d in remaining) + (self.spot(a, c), slice(None))

    def rest(self, order, j):
        return [d for d in self.dims if d not in order[:j]]

    def copy(self, j, a, c, order):
        source = self.full[a] if j == 0 else self.landed[j - 1][a]
        d = order[j]
        return pltpu.make_async_remote_copy(
            source.at[self.pick(self.rest(order, j), d, 1 - self.mine[d], a, c)],
            self.landed[j][a].at[self.pick(self.rest(order, j + 1), None, None, a, c)],
            self.send.at[j, a, c],
            self.recv.at[j, a, c],
            device_id=self.partner[d],
            device_id_type=MESH,
        )

    def own_copy(self, a, c, order):
        return pltpu.make_async_copy(
            self.full[a].at[self.pick(self.dims, order[0], self.mine[order[0]], a, c)],
            self.own[a].at[self.pick(self.rest(order, 1), None, None, a, c)],
            self.own_sem.at[a, c],
        )

    def begin(self, a, c, order):
        self.copy(0, a, c, order).start()
        self.own_copy(a, c, order).start()

    def step(self, j, a, c, order):
        self.copy(j, a, c, order).wait_recv()
        where = self.pick(self.rest(order, j + 1), None, None, a, c)
        d = order[j]
        if j == 0:
            self.own_copy(a, c, order).wait()
            kept = self.own[a][where]
        else:
            kept = self.landed[j - 1][a][self.pick(self.rest(order, j), d, self.mine[d], a, c)]
        total = kept.astype(f32) + self.landed[j][a][where].astype(f32)
        if j == self.depth - 1:
            self.shares[a][self.spot(a, c), :] = total
        else:
            self.landed[j][a][where] = total.astype(bf16)
            self.copy(j + 1, a, c, order).start()

    def each(self, i, fn):
        for parity in (0, 1):
            c = 2 * i + parity
            for a in range(self.n):

                @pl.when(jnp.logical_and(c >= 0, c < self.parts[a]))
                def _():
                    fn(a, c, self.orders[parity])

    def start(self):
        for i in range(share_ahead if self.n else 0):
            self.each(i, self.begin)

    def tick(self, i):
        if self.n:
            self.each(i + share_ahead, self.begin)
            for j in range(self.depth):
                self.each(i - self.lag * j, functools.partial(self.step, j))

    def finish(self):
        def sent(i, _):
            for j in range(self.depth):
                self.each(i, lambda a, c, order: self.copy(j, a, c, order).wait_send())
            return 0

        if self.n:
            lax.fori_loop(0, self.pairs, sent, 0)


def tp_sum(partial, epilogue, extras, extra_outs, chunk, ident, out_dtype=bf16, scatters=(), line_too=False, steps=16):
    line = Line(partial.shape, chunk, epilogue, extras, out_dtype)
    share = Halving(scatters, steps)
    n_ex, n_out, n_sc = len(extras), len(extra_outs), len(scatters)
    n_line, n_share = len(line.scratch()), len(share.scratch())

    def kernel(*refs):
        refs = list(refs)

        def take_refs(n):
            taken = refs[:n]
            del refs[:n]
            return taken

        (p_ref,) = take_refs(1)
        ins = take_refs(n_ex)
        full = take_refs(n_sc)
        (out_ref,) = take_refs(1)
        outs = take_refs(n_out)
        shares = take_refs(n_sc)
        line.bind(p_ref, ins, out_ref, outs, take_refs(n_line))
        share.bind(full, shares, take_refs(n_share))
        tail, tail_send, tail_recv = take_refs(3) if line_too else (None, None, None)
        barrier = pltpu.get_barrier_semaphore()
        line.begin(barrier, share.greet(barrier), line_too)
        share.start()

        def turn(i, _):
            for parity in (0, 1):
                line.tick(2 * i + parity)
            share.tick(i)
            return 0

        turns = (line.ticks() + 1) // 2
        lax.fori_loop(0, max(turns, share.turns) if n_sc else turns, turn, 0)
        if line_too:
            height = shares[-1].shape[0]
            last = pl.ds(height - 8, 8)
            for k, to in enumerate((line.mate, line.across)):
                copy = pltpu.make_async_remote_copy(
                    shares[-1].at[last] if k == 0 else tail.at[2], tail.at[k], tail_send.at[k], tail_recv.at[k],
                    device_id={"tp": to}, device_id_type=MESH,
                )
                copy.start()
                copy.wait()
                if k == 0:
                    tail[2] = shares[-1][last, :] + tail[0]
            shares[-1][last, :] = tail[2] + tail[1]
        line.finish()
        share.finish()

    buffers = []
    if line_too:
        pair_sem = pltpu.SemaphoreType.DMA((2,))
        buffers += [pltpu.VMEM((3, 8, scatters[-1].shape[-1]), f32), pair_sem, pair_sem]
    return pl.pallas_call(
        kernel,
        out_shape=[jax.ShapeDtypeStruct(partial.shape, out_dtype)] + list(extra_outs) + share.results(),
        in_specs=[HBM] * (1 + n_ex + n_sc),
        out_specs=[VMEM] * (1 + n_out + n_sc),
        scratch_shapes=line.scratch() + share.scratch() + buffers,
        compiler_params=pltpu.CompilerParams(
            collective_id=ident, has_side_effects=True, vmem_limit_bytes=56 << 20
        ),
    )(partial, *extras, *share.folded)


def plain_end(c, rows, total, ins, out_ref, outs):
    out_ref[rows, :] = total.astype(out_ref.dtype)


def norm_end(c, rows, total, ins, out_ref, outs):
    source_ref, gain_ref = ins
    middle = source_ref[rows, :].astype(f32) + total
    outs[0][rows, :] = middle
    out_ref[rows, :] = (middle * rms_scale(middle) * gain_ref[...]).astype(bf16)


def add_end(c, rows, total, ins, out_ref, outs):
    out_ref[rows, :] = (ins[0][rows, :] + total).astype(bf16)


def norm_back_end(c, rows, total, ins, out_ref, outs):
    source = ins[0][rows, :].astype(f32)
    inv = rms_scale(source)
    weighted = total * ins[1][...]
    back = inv * weighted - source * (inv * inv * inv) * jnp.mean(weighted * source, axis=-1, keepdims=True)
    result = ins[2][rows, :] + back
    if outs:
        outs[0][rows, :] = result
    out_ref[rows, :] = result.astype(bf16)


halo = 16
tile_cols = 256


def front(hidden, in_half, small, gains, seqs, at_conv, taps, low_len, ident):
    rows, width = hidden.shape
    local = rows // seqs
    part, inner = in_half.shape[1:]
    shards, pieces = lax.axis_size("shard"), lax.axis_size("ctx")
    long = local + halo
    tiles = inner // tile_cols
    line = Line((low_len, rows), 80, plain_end, [], f32)
    n_line = len(line.scratch())

    def kernel(
        hid_ref, tail_ref, in_ref, small_ref, gain_ref,
        in_out, small_out, gain_out, normed_out, z_out, ext_out, pre_out, act_out, low_out,
        own_w, got_w, edge, normed, ext_n, acc, z_val, conv_f, ext_c, pre, act, low_acc, small_all, gain_all,
        send, recv, edge_sem, own_sem, out_sem, *rest
    ):
        me, ctx = lax.axis_index("shard"), lax.axis_index("ctx")
        barrier = pltpu.get_barrier_semaphore()
        line.bind(rest[0], [], low_out, [], list(rest))
        for step in range(1, shards):
            pl.semaphore_signal(barrier, inc=1, device_id={"shard": lax.rem(me + step, shards)}, device_id_type=MESH)
        pl.semaphore_signal(barrier, inc=1, device_id={"ctx": lax.rem(ctx + pieces - 1, pieces)}, device_id_type=MESH)
        load = pltpu.make_async_copy(in_ref, own_w, own_sem.at[0])
        load.start()
        small_size, gain_size = small_ref.shape[1], gain_ref.shape[1]
        small_at = pl.ds(pl.multiple_of(me * small_size, small_size), small_size)
        gain_at = pl.ds(pl.multiple_of(me * gain_size, gain_size), gain_size)
        small_all[:, small_at] = small_ref[...]
        gain_all[:, gain_at] = gain_ref[...]
        line.greet(barrier, shards)
        edge_copy = pltpu.make_async_remote_copy(
            tail_ref, edge, edge_sem.at[0], edge_sem.at[1],
            device_id={"ctx": lax.rem(ctx + 1, pieces)}, device_id_type=MESH,
        )
        copies = {}
        for step in range(1, shards):
            peer = {"shard": lax.rem(me + step, shards)}
            moves = [(gain_ref, gain_all.at[:, gain_at]), (small_ref, small_all.at[:, small_at])]
            moves += [(in_ref.at[c], got_w.at[step - 1, c]) for c in range(2)]
            for k, (source, target) in enumerate(moves):
                copies[step, k] = pltpu.make_async_remote_copy(
                    source, target, send.at[step, k], recv.at[step, k], device_id=peer, device_id_type=MESH
                )
        for k in range(4):
            for step in range(1, shards):
                copies[step, k].start()
            if k == 0:
                edge_copy.start()
        for step in range(1, shards):
            copies[step, 0].wait_recv()
        gain = gain_all[0:1, :].astype(f32)

        def norm_rows(i, _):
            at = pl.ds(pl.multiple_of(i * 16, 16), 16)
            source = hid_ref[at, :].astype(f32)
            value = (source * rms_scale(source) * gain).astype(bf16)
            normed[at, :] = value
            seq = i // (local // 16)
            ext_n[pl.ds(pl.multiple_of(i * 16 + (seq + 1) * halo, 16), 16), :] = value
            return 0

        lax.fori_loop(0, rows // 16, norm_rows, 0)
        edge_copy.wait_recv()
        for seq in range(seqs):
            source = edge[seq].astype(f32)
            value = source * rms_scale(source) * gain * (ctx > 0).astype(f32)
            ext_n[seq * long : seq * long + halo, :] = value.astype(bf16)
        outs = [(normed, normed_out)]
        pltpu.make_async_copy(normed, normed_out, out_sem.at[0]).start()

        def cols(c, j):
            return pl.ds(pl.multiple_of(c * inner + j * tile_cols, tile_cols), tile_cols)

        def finish_conv(j):
            here = pl.ds(pl.multiple_of(j * tile_cols, tile_cols), tile_cols)
            value = acc[:, cols(0, j)].astype(bf16)
            ext_c[:, here] = value
            conv_f[...] = value.astype(f32)
            weights = small_all[at_conv : at_conv + 16, here].astype(f32)
            for seq in range(seqs):
                for k in range(local // 64):
                    first = seq * long + halo + k * 64
                    total = weights[taps : taps + 1]
                    for tap in range(taps):
                        total = total + weights[tap : tap + 1] * conv_f[first - taps + 1 + tap : first - taps + 1 + tap + 64, :]
                    to = slice(seq * local + k * 64, seq * local + (k + 1) * 64)
                    pre[to, here] = total
                    act[to, here] = jax.nn.silu(total).astype(bf16)
            low = outer_cols(small_all[0:low_len, here], act[:, here])
            low_acc[...] = low_acc[...] + low

        def finish_gate(j):
            here = pl.ds(pl.multiple_of(j * tile_cols, tile_cols), tile_cols)
            for seq in range(seqs):
                z_val[seq * local : (seq + 1) * local, here] = acc[seq * long + halo : (seq + 1) * long, cols(1, j)]

        low_acc[...] = jnp.zeros_like(low_acc)
        own_place = pl.ds(pl.multiple_of(me * part, part), part)
        load.wait()
        own_save = pltpu.make_async_copy(own_w, in_out.at[:, own_place], own_sem.at[1])
        own_save.start()
        saves = []
        for step in range(shards):
            owner = lax.rem(me - step + shards, shards)
            place = pl.ds(pl.multiple_of(owner * part, part), part)
            last = step == shards - 1
            if last:
                for other in range(1, shards):
                    copies[other, 1].wait_recv()
            for c in range(2):
                weight = own_w.at[c] if step == 0 else got_w.at[step - 1, c]
                if step > 0:
                    copies[step, 2 + c].wait_recv()

                def matmul(j, _):
                    here = pl.ds(pl.multiple_of(j * tile_cols, tile_cols), tile_cols)
                    value = jnp.dot(ext_n[:, place], weight[:, here], preferred_element_type=f32)
                    acc[:, cols(c, j)] = value if step == 0 else acc[:, cols(c, j)] + value
                    if last:
                        (finish_conv, finish_gate)[c](j)
                    return 0

                lax.fori_loop(0, tiles, matmul, 0)
            if step > 0:
                saves.append(pltpu.make_async_copy(got_w.at[step - 1], in_out.at[:, place], own_sem.at[1 + step]))
                saves[-1].start()
        line.p[...] = low_acc[...].astype(bf16)
        outs += [(z_val, z_out), (ext_c, ext_out), (pre, pre_out), (act, act_out), (small_all, small_out), (gain_all, gain_out)]
        for k, (source, target) in enumerate(outs):
            if k:
                pltpu.make_async_copy(source, target, out_sem.at[k]).start()
        line.start()
        for c in range(line.ticks()):
            line.tick(c)
        line.finish()
        for save in saves + [own_save]:
            save.wait()
        for k, (source, target) in enumerate(outs):
            pltpu.make_async_copy(source, target, out_sem.at[k]).wait()
        for copy in copies.values():
            copy.wait_send()
        edge_copy.wait_send()

    sds = jax.ShapeDtypeStruct
    tails = hidden.reshape(seqs, local, width)[:, local - halo :]
    return pl.pallas_call(
        kernel,
        out_shape=[
            sds((2, shards * part, inner), bf16),
            sds((small.shape[0], small.shape[1] * shards), bf16),
            sds((gains.shape[0], gains.shape[1] * shards), bf16),
            sds((rows, width), bf16),
            sds((rows, inner), f32),
            sds((seqs * long, inner), bf16),
            sds((rows, inner), f32),
            sds((rows, inner), bf16),
            sds((low_len, rows), f32),
        ],
        in_specs=[VMEM, HBM, HBM, VMEM, VMEM],
        out_specs=[HBM] * 8 + [VMEM],
        scratch_shapes=[
            pltpu.VMEM((2, part, inner), bf16),
            pltpu.VMEM((max(shards - 1, 1), 2, part, inner), bf16),
            pltpu.VMEM((seqs, halo, width), bf16),
            pltpu.VMEM((rows, width), bf16),
            pltpu.VMEM((seqs * long, width), bf16),
            pltpu.VMEM((seqs * long, 2 * inner), f32),
            pltpu.VMEM((rows, inner), f32),
            pltpu.VMEM((seqs * long, tile_cols), f32),
            pltpu.VMEM((seqs * long, inner), bf16),
            pltpu.VMEM((rows, inner), f32),
            pltpu.VMEM((rows, inner), bf16),
            pltpu.VMEM((low_len, rows), f32),
            pltpu.VMEM((small.shape[0], small.shape[1] * shards), bf16),
            pltpu.VMEM((gains.shape[0], gains.shape[1] * shards), bf16),
            pltpu.SemaphoreType.DMA((shards, 4)),
            pltpu.SemaphoreType.DMA((shards, 4)),
            pltpu.SemaphoreType.DMA((2,)),
            pltpu.SemaphoreType.DMA((shards + 1,)),
            pltpu.SemaphoreType.DMA((7,)),
        ]
        + line.scratch(),
        compiler_params=pltpu.CompilerParams(
            collective_id=ident, has_side_effects=True, vmem_limit_bytes=56 << 20
        ),
    )(hidden, tails, in_half, small, gains)


piece = 16
slots_held = 4
unroll = 4


def spread(flat_ref, natural, first):
    for j in range(8):
        flat_ref[pl.ds(first * 8 + j, 8, stride=8), :] = natural[:, j * 128 : (j + 1) * 128]


def unspread(flat_ref, first):
    return jnp.concatenate([flat_ref[pl.ds(first * 8 + j, 8, stride=8), :] for j in range(8)], axis=1)


def tile(ref, t):
    return ref[pl.ds(pl.multiple_of(t * 8, 8), 8), :]


def row(ref, t, n, states):
    return ref[pl.ds(t * states + n, 8, stride=0), :]


def exchange(ends, got, send, recv, seq, width):
    me = lax.axis_index("ctx")
    copies = []
    for step in range(1, width):
        copies.append(
            pltpu.make_async_remote_copy(
                ends.at[seq],
                got.at[me, seq],
                send.at[seq, step],
                recv.at[seq, step],
                device_id={"ctx": lax.rem(me + step, width)},
                device_id_type=MESH,
            )
        )
        copies[-1].start()
    return copies


def ctx_greet(width):
    me = lax.axis_index("ctx")
    barrier = pltpu.get_barrier_semaphore()
    for step in range(1, width):
        pl.semaphore_signal(barrier, inc=1, device_id={"ctx": lax.rem(me + step, width)}, device_id_type=MESH)
    return barrier


def entering(got, seq, rate_ref, states, width, reverse):
    me = lax.axis_index("ctx")
    result = []
    for n in range(states):
        value = jnp.zeros((8, 128), f32)
        for k in reversed(range(width)) if reverse else range(width):
            new = jnp.exp2(got[k, seq, states] * rate_ref[n]) * value + got[k, seq, n]
            value = jnp.where(me < k if reverse else me > k, new, value)
        result.append(value)
    return result


def spread_rows(low_ref, first, out_ref):
    states, slots = 16, low_ref.shape[1]

    def lanes(k, _):
        block = low_ref[first : first + states, pl.ds(pl.multiple_of(k * 128, 128), 128)]
        for i in range(128):
            to = pl.ds(pl.multiple_of((k * 128 + i) * states, states), states)
            out_ref[to, :] = jnp.broadcast_to(block[:, i : i + 1], (states, 128))
        return 0

    lax.fori_loop(0, slots // 128, lanes, 0)


def scan_forward(low_all, act, gate_z, small, rate, out_parts, seqs, rank, at_step, at_bias, at_skip, ident):
    rows, channels = act.shape
    shards, _, part = out_parts.shape
    local = rows // seqs
    states = rate.shape[0]
    width = lax.axis_size("ctx")
    pieces = local // piece

    def kernel(
        low_ref, act_ref, z_ref, small_ref, rate_ref, w_ref,
        scan_ref, gated_ref, mixed_ref, pre_ref, kept_ref, enter_ref, size3, drive3,
        y3, ends, got, held, b_ref, c_ref, low_t, w_own, send, recv, out_sem, w_sem,
    ):
        barrier = ctx_greet(width)
        load = pltpu.make_async_copy(w_ref, w_own, w_sem)
        load.start()
        low_t[...] = low_ref[0:rank, :].T.astype(bf16)
        bias = small_ref[at_bias : at_bias + 16, :].astype(f32)[0:1]
        for j in range(channels // 256):
            here = slice(j * 256, (j + 1) * 256)
            value = jnp.dot(low_t[...], small_ref[at_step : at_step + rank, here], preferred_element_type=f32)
            pre_ref[:, here] = value + bias[:, here]
        spread_rows(low_ref, rank, b_ref)
        spread_rows(low_ref, rank + states, c_ref)

        def lay(i, _):
            first = pl.multiple_of(i * 16, 16)
            act_block = act_ref[pl.ds(first, 16), :].astype(f32)
            size = jax.nn.softplus(pre_ref[pl.ds(first, 16), :])
            drive = size * act_block
            for h in range(2):
                spread(size3, size[h * 8 : h * 8 + 8], first + h * 8)
                spread(drive3, drive[h * 8 : h * 8 + 8], first + h * 8)
            return 0

        lax.fori_loop(0, rows // 16, lay, 0)
        pl.semaphore_wait(barrier, width - 1)
        copies = []
        for seq in range(seqs):

            def first_pass(i, carried):
                values, total = list(carried[:-1]), carried[-1]
                for u in range(unroll):
                    t = seq * local + i * unroll + u
                    s, d = tile(size3, t), tile(drive3, t)
                    total = total + s
                    for n in range(states):
                        values[n] = jnp.exp2(s * rate_ref[n]) * values[n] + d * row(b_ref, t, n, states)
                return tuple(values) + (total,)

            zero = tuple(jnp.zeros((8, 128), f32) for _ in range(states + 1))
            done = lax.fori_loop(0, local // unroll, first_pass, zero)
            for n in range(states + 1):
                ends[seq, n] = done[n]
            copies.append(exchange(ends, got, send, recv, seq, width))
        me = lax.axis_index("ctx")
        for seq in range(seqs):
            for copy in copies[seq]:
                copy.wait()
            got[me, seq] = ends[seq]
            start = entering(got, seq, rate_ref, states, width, False)
            for n in range(states):
                enter_ref[seq, n] = start[n]

            def save(k, slot):
                return pltpu.make_async_copy(
                    held.at[slot], kept_ref.at[pl.ds(seq * local + k * piece, piece)], out_sem.at[slot]
                )

            def one_piece(k, carried):
                slot = lax.rem(k, 2)

                @pl.when(k >= 2)
                def _():
                    save(k - 2, slot).wait()

                def second_pass(i, values):
                    values = list(values)
                    for u in range(unroll):
                        inside = i * unroll + u
                        t = seq * local + k * piece + inside
                        s, d = tile(size3, t), tile(drive3, t)
                        acc = [None] * 4
                        for n in range(states):
                            values[n] = jnp.exp2(s * rate_ref[n]) * values[n] + d * row(b_ref, t, n, states)
                            held[slot, inside, n] = values[n]
                            part = values[n] * row(c_ref, t, n, states)
                            acc[n % 4] = part if acc[n % 4] is None else acc[n % 4] + part
                        y3[pl.ds(pl.multiple_of(t * 8, 8), 8), :] = (acc[0] + acc[1]) + (acc[2] + acc[3])
                    return tuple(values)

                carried = lax.fori_loop(0, piece // unroll, second_pass, carried)
                save(k, slot).start()
                return carried

            lax.fori_loop(0, pieces, one_piece, tuple(start))
            for k in (pieces - 2, pieces - 1):
                save(k, k % 2).wait()

        skip = small_ref[at_skip : at_skip + 16, :].astype(f32)[0:1]

        def back(i, _):
            first = pl.multiple_of(i * 16, 16)
            here = pl.ds(first, 16)
            value = jnp.concatenate([unspread(y3, first), unspread(y3, first + 8)], axis=0)
            value = value + skip * act_ref[here, :].astype(f32)
            scan_ref[here, :] = value
            gated_ref[here, :] = (value * jax.nn.silu(z_ref[here, :])).astype(bf16)
            return 0

        lax.fori_loop(0, rows // 16, back, 0)
        load.wait()
        for k in range(shards):
            for j in range(-(-part // 256)):
                span = min(256, part)
                value = jnp.dot(gated_ref[...], w_own[k, :, j * span : (j + 1) * span], preferred_element_type=f32)
                mixed_ref[:, k * part + j * span : k * part + (j + 1) * span] = value.astype(bf16)

    flat = jax.ShapeDtypeStruct((rows * 8, 128), f32)
    return pl.pallas_call(
        kernel,
        out_shape=[
            jax.ShapeDtypeStruct((rows, channels), f32),
            jax.ShapeDtypeStruct((rows, channels), bf16),
            jax.ShapeDtypeStruct((rows, shards * part), bf16),
            jax.ShapeDtypeStruct((rows, channels), f32),
            jax.ShapeDtypeStruct((rows, states, 8, 128), f32),
            jax.ShapeDtypeStruct((seqs, states, 8, 128), f32),
            flat,
            flat,
        ],
        in_specs=[VMEM] * 5 + [HBM],
        out_specs=[VMEM] * 4 + [HBM, VMEM, VMEM, VMEM],
        scratch_shapes=[
            pltpu.VMEM((rows * 8, 128), f32),
            pltpu.VMEM((seqs, states + 1, 8, 128), f32),
            pltpu.VMEM((width, seqs, states + 1, 8, 128), f32),
            pltpu.VMEM((2, piece, states, 8, 128), f32),
            pltpu.VMEM((rows * states, 128), f32),
            pltpu.VMEM((rows * states, 128), f32),
            pltpu.VMEM((rows, rank), bf16),
            pltpu.VMEM(out_parts.shape, bf16),
            pltpu.SemaphoreType.DMA((seqs, width)),
            pltpu.SemaphoreType.DMA((seqs, width)),
            pltpu.SemaphoreType.DMA((2,)),
            pltpu.SemaphoreType.DMA,
        ],
        compiler_params=pltpu.CompilerParams(
            collective_id=ident, has_side_effects=True, vmem_limit_bytes=48 << 20
        ),
    )(low_all, act, gate_z, small, rate, out_parts)


def sublane_sums(parts):
    at = lax.broadcasted_iota(jnp.int32, (8, 128), 0)
    for shift in (4, 2, 1):
        low = (at // shift) % 2 == 0
        half = len(parts) // 2
        merged = []
        for one, two in zip(parts[:half], parts[half:]):
            merged.append(
                jnp.where(low, one + pltpu.roll(one, 8 - shift, 0), two + pltpu.roll(two, shift, 0))
            )
        parts = merged
    return parts[0]


def scan_backward(size3, drive3, grad, low_all, rank, rate, kept, enter, seqs, ident, partial, epilogue, extras, chunk, scatters):
    rows, channels = grad.shape
    local = rows // seqs
    states = rate.shape[0]
    width = lax.axis_size("ctx")
    pieces = local // piece
    early = 2
    unroll_b = 2
    line = Line(partial.shape, chunk, epilogue, extras, bf16)
    share = Halving(scatters, 16, 1)
    n_line, n_ex, n_sc = len(line.scratch()), len(extras), len(scatters)

    def kernel(*refs):
        refs = list(refs)

        def take_refs(n):
            taken = refs[:n]
            del refs[:n]
            return taken

        size_ref, drive_ref, grad_ref, low_ref, rate_ref, kept_ref, enter_ref, p_ref = take_refs(8)
        ins, full = take_refs(n_ex), take_refs(n_sc)
        tb3, sd3, bg_ref, cg_ref, dec_ref, sum_ref = take_refs(6)
        shares = take_refs(n_sc)
        grad3, b_ref, c_ref, ends, got, held, bpart, cpart, prior, send, recv, in_sem = take_refs(12)
        line.bind(p_ref, ins, sum_ref, [], take_refs(n_line))
        share.bind(full, shares, refs)
        barrier = ctx_greet(width)
        line.begin(barrier, width - 1 + share.greet(barrier))
        share.start()
        spread_rows(low_ref, rank, b_ref)
        spread_rows(low_ref, rank + states, c_ref)
        share.tick(0)

        def lay(i, _):
            first = pl.multiple_of(i * 8, 8)
            spread(grad3, grad_ref[pl.ds(first, 8), :], first)
            return 0

        lax.fori_loop(0, rows // 8, lay, 0)

        def fetch(g):
            first = (g // pieces) * local + (pieces - 1 - g % pieces) * piece
            slot = g % slots_held
            return pltpu.make_async_copy(kept_ref.at[pl.ds(first, piece)], held.at[slot], in_sem.at[slot])

        for g in range(slots_held - 1):
            fetch(g).start()

        copies = []
        for seq in range(seqs):

            def first_pass(i, carried):
                values, total = list(carried[:-1]), carried[-1]
                for u in range(unroll):
                    t = seq * local + local - 1 - (i * unroll + u)
                    s, g = tile(size_ref, t), tile(grad3, t)
                    total = total + s
                    for n in range(states):
                        values[n] = jnp.exp2(s * rate_ref[n]) * (values[n] + g * row(c_ref, t, n, states))
                return tuple(values) + (total,)

            zero = tuple(jnp.zeros((8, 128), f32) for _ in range(states + 1))
            done = zero
            for half in range(early):
                span = local // unroll // early
                done = lax.fori_loop(half * span, (half + 1) * span, first_pass, done)
                line.tick(seq * early + half)
            for n in range(states + 1):
                ends[seq, n] = done[n]
            copies.append(exchange(ends, got, send, recv, seq, width))
            share.tick(1 + seq)
        me = lax.axis_index("ctx")
        for n in range(states):
            dec_ref[n] = jnp.zeros((8, 128), f32)
        for seq in range(seqs):
            for copy in copies[seq]:
                copy.wait()
            got[me, seq] = ends[seq]
            start = entering(got, seq, rate_ref, states, width, True)
            fetch(seq * pieces).wait()

            def one_slot(slot, k, inside, adjoint, decays, prior_at):
                t = seq * local + k * piece + inside
                s, d, g = tile(size_ref, t), tile(drive_ref, t), tile(grad3, t)
                tb, sd = [None] * 2, [None] * 2
                b_parts, c_parts = [], []
                for n in range(states):
                    total = adjoint[n] + g * row(c_ref, t, n, states)
                    c_parts.append(held[slot, inside, n] * g)
                    b_parts.append(total * d)
                    through = total * row(b_ref, t, n, states)
                    adjoint[n] = jnp.exp2(s * rate_ref[n]) * total
                    kept_part = adjoint[n] * prior_at(n)
                    through_size = kept_part * rate_ref[n]
                    decays[n] = decays[n] + kept_part * s
                    tb[n % 2] = through if tb[n % 2] is None else tb[n % 2] + through
                    sd[n % 2] = through_size if sd[n % 2] is None else sd[n % 2] + through_size
                here = pl.ds(pl.multiple_of(t * 8, 8), 8)
                tb3[here, :] = tb[0] + tb[1]
                sd3[here, :] = sd[0] + sd[1]
                for h in range(states // 8):
                    spot = pl.ds(pl.multiple_of(inside * states + h * 8, 8), 8)
                    bpart[spot, :] = sublane_sums(b_parts[h * 8 : h * 8 + 8])
                    cpart[spot, :] = sublane_sums(c_parts[h * 8 : h * 8 + 8])

            def one_piece(back_k, carried):
                k = pieces - 1 - back_k
                place = seq * pieces + back_k
                slot = place % slots_held

                @pl.when(place + slots_held - 1 < seqs * pieces)
                def _():
                    fetch(place + slots_held - 1).start()

                def slots(i, carried):
                    adjoint, decays = list(carried[:states]), list(carried[states:])
                    for u in range(unroll_b):
                        inside = piece - 1 - (i * unroll_b + u)
                        one_slot(slot, k, inside, adjoint, decays, lambda n: held[slot, inside - 1, n])
                    return tuple(adjoint) + tuple(decays)

                carried = lax.fori_loop(0, piece // unroll_b - 1, slots, carried)
                adjoint, decays = list(carried[:states]), list(carried[states:])
                for inside in reversed(range(1, unroll_b)):
                    one_slot(slot, k, inside, adjoint, decays, lambda n: held[slot, inside - 1, n])

                @pl.when(k > 0)
                def _():
                    fetch(place + 1).wait()
                    prior[...] = held[(place + 1) % slots_held, piece - 1]

                @pl.when(k == 0)
                def _():
                    prior[...] = enter_ref[seq]

                one_slot(slot, k, 0, adjoint, decays, lambda n: prior[n])
                ones = jnp.ones((8, 128), bf16)
                for part, out in ((bpart, bg_ref), (cpart, cg_ref)):
                    sums = outer_cols(ones, part[...].astype(bf16))
                    out[pl.ds(seq * pieces + k, 1)] = sums[None]
                @pl.when(place % 2 == 0)
                def _():
                    line.tick(seqs * early + place // 2)

                @pl.when(place % 5 == 0)
                def _():
                    share.tick(1 + seqs + place // 5)

                return tuple(adjoint) + tuple(decays)

            zero = tuple(jnp.zeros((8, 128), f32) for _ in range(states))
            carried = lax.fori_loop(0, pieces, one_piece, tuple(start) + zero)
            for n in range(states):
                dec_ref[n] = dec_ref[n] + carried[states + n]

        for c in range(seqs * early + (seqs * pieces + 1) // 2, line.ticks()):
            line.tick(c)
        for i in range(1 + seqs + (seqs * pieces + 4) // 5, share.turns):
            share.tick(i)
        line.finish()
        share.finish()

    flat = jax.ShapeDtypeStruct((rows * 8, 128), f32)
    sums = jax.ShapeDtypeStruct((rows // piece, 8, piece * states), f32)
    return pl.pallas_call(
        kernel,
        out_shape=[flat, flat, sums, sums, jax.ShapeDtypeStruct((states, 8, 128), f32),
                   jax.ShapeDtypeStruct(partial.shape, bf16)] + share.results(),
        in_specs=[VMEM] * 5 + [HBM, VMEM] + [HBM] * (1 + n_ex + n_sc),
        out_specs=[VMEM] * (6 + n_sc),
        scratch_shapes=[pltpu.VMEM((rows * 8, 128), f32)]
        + [pltpu.VMEM((rows * states, 128), f32)] * 2
        + [
            pltpu.VMEM((seqs, states + 1, 8, 128), f32),
            pltpu.VMEM((width, seqs, states + 1, 8, 128), f32),
            pltpu.VMEM((slots_held, piece, states, 8, 128), f32),
            pltpu.VMEM((piece * states, 128), f32),
            pltpu.VMEM((piece * states, 128), f32),
            pltpu.VMEM((states, 8, 128), f32),
            pltpu.SemaphoreType.DMA((seqs, width)),
            pltpu.SemaphoreType.DMA((seqs, width)),
            pltpu.SemaphoreType.DMA((slots_held,)),
        ]
        + line.scratch()
        + share.scratch(),
        compiler_params=pltpu.CompilerParams(
            collective_id=ident, has_side_effects=True, vmem_limit_bytes=62 << 20
        ),
    )(size3, drive3, grad, low_all, rate, kept, enter, partial, *extras, *share.folded)


def feed_forward(mixed_part, hidden, gain, ffn_grad, gate_w, down_parts, ident):
    rows, width = hidden.shape
    shards, ffn, part = down_parts.shape
    chunk = 32
    block = 4 * chunk
    tile = ffn // 4
    blocks = rows // block
    fore = Line(mixed_part.shape, chunk, norm_end, [], bf16)
    after = Line(mixed_part.shape, chunk, norm_back_end, [], bf16)
    n_line = len(fore.scratch())
    behind = 6
    wtile = 256

    def kernel(
        p_ref, hid_ref, gain_ref, fg_ref, gate_ref, up_ref, down_ref,
        ffn_out, mid_out, mix_ref, midg_ref, gsum_ref, both_out, dw_out,
        normed, middle, hid_v, gg_v, ug_v, ffn_v, ffn_acc, back_acc, gate_v, up_v, down_v, stage, stage_d, load_sem, save_sem, *rest
    ):
        barrier = pltpu.get_barrier_semaphore()
        fore.bind(p_ref, [], normed, [middle], rest[:n_line])
        after.bind(rest[n_line], [], mix_ref, [midg_ref], rest[n_line:])
        fore.ins = [hid_ref, gain_ref]
        after.ins = [middle, gain_ref, fg_ref]
        loads = [
            pltpu.make_async_copy(a, b, load_sem.at[i])
            for i, (a, b) in enumerate(((gate_ref, gate_v), (up_ref, up_v), (down_ref, down_v)))
        ]
        fore.begin(barrier, 0)
        for load in loads:
            load.start()
        gsum_ref[...] = jnp.zeros_like(gsum_ref)
        lead = 4 + fore.lag

        def warm(c, _):
            fore.tick(c)
            return 0

        lax.fori_loop(0, lead, warm, 0)
        for load in loads:
            load.wait()
        outer = jnp.logical_not(fore.middle)

        def step(s, _):
            b, j = s // 4, s % 4
            fore.tick(s + lead)
            at = pl.ds(pl.multiple_of(b * block, block), block)
            here = pl.ds(pl.multiple_of(j * tile, tile), tile)

            @pl.when(j == 0)
            def _():
                ffn_acc[...] = jnp.zeros_like(ffn_acc)
                back_acc[...] = jnp.zeros_like(back_acc)

                @pl.when(outer)
                def _():
                    for k in range(4):
                        fore.copy_c(4 * b + k).wait_recv()

            source, grad = normed[at, :], fg_ref[at, :]
            gate = jnp.dot(source, gate_v[:, here], preferred_element_type=f32)
            up = jnp.dot(source, up_v[:, here], preferred_element_type=f32)
            sig = jax.nn.sigmoid(gate)
            silu = gate * sig
            hidden_val = (silu * up).astype(bf16)
            back = sum(
                outer_cols(grad[:, k * part : (k + 1) * part], down_v[k, here, :]) for k in range(shards)
            )
            gate_back = (back * up * (sig * (1.0 + gate * (1.0 - sig)))).astype(bf16)
            up_back = (back * silu).astype(bf16)
            hid_v[at, here] = hidden_val
            gg_v[at, here] = gate_back
            ug_v[at, here] = up_back

            after.quiet_tick(s - behind)

            for k in range(shards):
                to = slice(k * part, (k + 1) * part)
                ffn_acc[:, to] += jnp.dot(hidden_val, down_v[k, here, :], preferred_element_type=f32)
            for k in range(width // 512):
                to = slice(k * 512, (k + 1) * 512)
                back_acc[:, to] += outer_cols(gate_back, gate_v[to, here]) + outer_cols(up_back, up_v[to, here])

            @pl.when(j == 3)
            def _():
                ffn_v[at, :] = ffn_acc[...].astype(bf16)
                after.p[at, :] = back_acc[...].astype(bf16)
                for k in range(block // 16):
                    product = after.p[pl.ds(pl.multiple_of(b * block + k * 16, 16), 16), :].astype(f32)
                    product = product * normed[pl.ds(pl.multiple_of(b * block + k * 16, 16), 16), :].astype(f32)
                    gsum_ref[...] += product[:8] + product[8:]

                @pl.when(outer)
                def _():
                    for k in range(4):
                        after.copy_a(4 * b + k).start()

            return 0

        steps = 4 * blocks
        lax.fori_loop(0, steps, step, 0)
        ffn_save = pltpu.make_async_copy(ffn_v, ffn_out, save_sem.at[3])
        ffn_save.start()
        mid_save = pltpu.make_async_copy(middle, mid_out, save_sem.at[4])
        mid_save.start()

        def saves(i):
            to = pl.ds(pl.multiple_of(i * wtile, wtile), wtile)
            return [
                pltpu.make_async_copy(held, out.at[to], save_sem.at[a])
                for a, (held, out) in enumerate(((stage, both_out), (stage_d, dw_out)))
            ]

        def weights(i, _):
            after.quiet_tick(steps - behind + i)
            here = pl.ds(pl.multiple_of(i * wtile, wtile), wtile)

            @pl.when(i > 0)
            def _():
                for save in saves(i - 1):
                    save.wait()

            source, grad = normed[:, here], fg_ref[:, here]
            stage[:, :ffn] = inner_rows(source, gg_v[...]).astype(bf16)
            stage[:, ffn:] = inner_rows(source, ug_v[...]).astype(bf16)
            stage_d[...] = inner_rows(grad, hid_v[...]).astype(bf16)
            for save in saves(i):
                save.start()
            return 0

        lax.fori_loop(0, width // wtile, weights, 0)
        for c in range(steps - behind + width // wtile, after.ticks()):
            after.quiet_tick(c)
        for save in saves(width // wtile - 1) + [ffn_save, mid_save]:
            save.wait()
        fore.finish(False)
        after.finish()

    sds = jax.ShapeDtypeStruct
    wide, half = sds((rows, width), f32), sds((rows, width), bf16)
    both, down = sds((width, 2 * ffn), bf16), sds((width, ffn), bf16)
    return pl.pallas_call(
        kernel,
        out_shape=[half, wide, half, wide, sds((8, width), f32), both, down],
        in_specs=[HBM, VMEM, VMEM, VMEM, HBM, HBM, HBM],
        out_specs=[HBM, HBM, VMEM, VMEM, VMEM, HBM, HBM],
        scratch_shapes=[
            pltpu.VMEM((rows, width), bf16),
            pltpu.VMEM((rows, width), f32),
            pltpu.VMEM((rows, ffn), bf16),
            pltpu.VMEM((rows, ffn), bf16),
            pltpu.VMEM((rows, ffn), bf16),
            pltpu.VMEM((rows, width), bf16),
            pltpu.VMEM((block, width), f32),
            pltpu.VMEM((block, width), f32),
            pltpu.VMEM((width, ffn), bf16),
            pltpu.VMEM((width, ffn), bf16),
            pltpu.VMEM(down_parts.shape, bf16),
            pltpu.VMEM((wtile, 2 * ffn), bf16),
            pltpu.VMEM((wtile, ffn), bf16),
            pltpu.SemaphoreType.DMA((3,)),
            pltpu.SemaphoreType.DMA((5,)),
        ]
        + fore.scratch()
        + after.scratch(),
        compiler_params=pltpu.CompilerParams(
            collective_id=ident, has_side_effects=True, vmem_limit_bytes=62 << 20
        ),
    )(mixed_part, hidden, gain, ffn_grad, gate_w[0], gate_w[1], down_parts)


def scan_tail(through_b, through_decay, sums, decay_grad, scan_grad, step_pre, pre_act, act, padded, z_half, low_all, small, ident,
              seqs, low_len, rank, states, taps):
    rows, inner = act.shape
    local = rows // seqs
    long = local + halo
    shards, pieces = lax.axis_size("shard"), lax.axis_size("ctx")
    places = shards * pieces
    lane = inner // places
    line = Line((low_len, rows), 80, plain_end, [], bf16)
    tiles = inner // tile_cols
    at = low_len + rank
    lines = -(-(at + states + taps + 3) // 8) * 8
    height = -(-(lines + 8) // 32) * 32
    over = 8

    def kernel(
        tb_ref, sd_ref, sums_ref, dec_ref, sg_ref, sp_ref, pre_ref, act_ref, ext_ref, zg_ref, low_ref, small_ref,
        conv_ref, blocks_ref,
        low_out, low_t, step_g, low_acc, grads, pre_g, conv_f, edge, edge_out, edge_sem, *rest
    ):
        ctx = lax.axis_index("ctx")
        barrier = pltpu.get_barrier_semaphore()
        line.bind(rest[0], [], low_out, [], list(rest))
        pl.semaphore_signal(barrier, inc=1, device_id={"ctx": lax.rem(ctx + 1, pieces)}, device_id_type=MESH)

        def flat(ref, j, first, count):
            parts = [ref[pl.ds(first * 8 + j * (tile_cols // 128) + h, count, stride=8), :] for h in range(tile_cols // 128)]
            return jnp.concatenate(parts, axis=1)

        def cols(j):
            return pl.ds(pl.multiple_of(j * tile_cols, tile_cols), tile_cols)

        low_acc[...] = jnp.zeros_like(low_acc)
        grads[...] = jnp.zeros_like(grads)
        low_t[...] = low_ref[0:rank, :].astype(bf16)

        def size_tile(j, _):
            here = cols(j)
            bias_grad = jnp.zeros((8, tile_cols), f32)
            skip_grad = jnp.zeros((8, tile_cols), f32)
            for k in range(rows // 64):
                to = slice(k * 64, (k + 1) * 64)
                act_block = act_ref[to, here].astype(f32)
                size_grad = act_block * flat(tb_ref, j, k * 64, 64) + flat(sd_ref, j, k * 64, 64) * (1.0 / log2e)
                value = (size_grad * jax.nn.sigmoid(sp_ref[to, here])).astype(bf16)
                step_g[to, here] = value
                wide = value.astype(f32)
                product = sg_ref[to, here] * act_block
                for h in range(8):
                    bias_grad = bias_grad + wide[h * 8 : h * 8 + 8]
                    skip_grad = skip_grad + product[h * 8 : h * 8 + 8]
            grads[at + states + taps + 1 : at + states + taps + 2, here] = jnp.sum(bias_grad, axis=0, keepdims=True)
            grads[at + states + taps + 2 : at + states + taps + 3, here] = jnp.sum(skip_grad, axis=0, keepdims=True)
            low_acc[...] = low_acc[...] + outer_cols(small_ref[low_len : low_len + rank, here], step_g[:, here])
            return 0

        lax.fori_loop(0, tiles, size_tile, 0)
        line.p[0:rank, :] = low_acc[...].astype(bf16)
        line.p[rank : rank + 2 * states, :] = sums_ref[...].astype(bf16)
        line.greet(barrier, 1)
        line.start()

        def step_tile(j, _):
            here = cols(j)
            grads[low_len:at, here] = jnp.dot(low_t[...], step_g[:, here], preferred_element_type=f32)
            return 0

        lax.fori_loop(0, tiles, step_tile, 0)
        grads[at : at + states, :] = dec_ref[...]
        for c in range(line.ticks()):
            line.tick(c)
        line.finish()

        def pre_tile(j, _):
            here = cols(j)
            grads[0:low_len, here] = jnp.dot(low_out[...], act_ref[:, here], preferred_element_type=f32)
            for seq in range(seqs):
                low = inner_rows(low_out[:, seq * local : (seq + 1) * local], small_ref[0:low_len, here])
                conv_f[seq * long : (seq + 1) * long, :] = ext_ref[seq * long : (seq + 1) * long, here].astype(f32)
                pre_g[seq * (local + over) : seq * (local + over) + local, here] = low
            skip = small_ref[at + states + 32 : at + states + 48, here].astype(f32)[0:1]
            bias_sum = jnp.zeros((8, tile_cols), f32)
            tap_sums = [jnp.zeros((8, tile_cols), f32) for _ in range(taps)]
            for seq in range(seqs):
                for k in range(local // 64):
                    to = slice(seq * local + k * 64, seq * local + (k + 1) * 64)
                    where = slice(seq * (local + over) + k * 64, seq * (local + over) + (k + 1) * 64)
                    act_grad = skip * sg_ref[to, here] + jax.nn.softplus(sp_ref[to, here]) * flat(tb_ref, j, seq * local + k * 64, 64)
                    value = (act_grad + pre_g[where, here]) * silu_grad(pre_ref[to, here])
                    pre_g[where, here] = value
                    first = seq * long + halo + k * 64 - taps + 1
                    products = [value * conv_f[first + tap : first + tap + 64, :] for tap in range(taps)]
                    for h in range(8):
                        bias_sum = bias_sum + value[h * 8 : h * 8 + 8]
                        for tap in range(taps):
                            tap_sums[tap] = tap_sums[tap] + products[tap][h * 8 : h * 8 + 8]
            for tap in range(taps):
                row = at + states + tap
                grads[row : row + 1, here] = jnp.sum(tap_sums[tap], axis=0, keepdims=True)
            row = at + states + taps
            grads[row : row + 1, here] = jnp.sum(bias_sum, axis=0, keepdims=True)
            return 0

        lax.fori_loop(0, tiles, pre_tile, 0)
        for seq in range(seqs):
            edge_out[seq] = pre_g[seq * (local + over) : seq * (local + over) + over, :]
        copy = pltpu.make_async_remote_copy(
            edge_out, edge, edge_sem.at[0], edge_sem.at[1],
            device_id={"ctx": lax.rem(ctx + pieces - 1, pieces)}, device_id_type=MESH,
        )
        copy.start()
        for p in range(places):
            blocks_ref[p * height : p * height + lines, :] = grads[:, p * lane : (p + 1) * lane].astype(bf16)
            blocks_ref[p * height + lines : (p + 1) * height, :] = jnp.zeros((height - lines, lane), bf16)
        copy.wait()
        inside = (ctx < pieces - 1).astype(f32)
        for seq in range(seqs):
            first = seq * (local + over) + local
            pre_g[first : first + over, :] = edge[seq] * inside

        def conv_tile(j, _):
            here = cols(j)
            weights = small_ref[at + states : at + states + 16, here].astype(f32)
            for seq in range(seqs):
                for k in range(local // 64):
                    first = seq * (local + over) + k * 64 + taps - 1
                    total = weights[0:1] * pre_g[first : first + 64, here]
                    for tap in range(1, taps):
                        total = total + weights[tap : tap + 1] * pre_g[first - tap : first - tap + 64, here]
                    conv_ref[seq * local + k * 64 : seq * local + (k + 1) * 64, here] = total.astype(bf16)
            return 0

        lax.fori_loop(0, tiles, conv_tile, 0)
        conv_ref[:, inner:] = zg_ref[...]

    return pl.pallas_call(
        kernel,
        out_shape=[
            jax.ShapeDtypeStruct((rows, 2 * inner), bf16),
            jax.ShapeDtypeStruct((places * height, lane), bf16),
        ],
        in_specs=[VMEM] * 12,
        out_specs=[VMEM] * 2,
        scratch_shapes=[
            pltpu.VMEM((low_len, rows), bf16),
            pltpu.VMEM((rank, rows), bf16),
            pltpu.VMEM((rows, inner), bf16),
            pltpu.VMEM((rank, rows), f32),
            pltpu.VMEM((lines, inner), f32),
            pltpu.VMEM((seqs * (local + over), inner), f32),
            pltpu.VMEM((seqs * long, tile_cols), f32),
            pltpu.VMEM((seqs, over, inner), f32),
            pltpu.VMEM((seqs, over, inner), f32),
            pltpu.SemaphoreType.DMA((2,)),
        ]
        + line.scratch(),
        compiler_params=pltpu.CompilerParams(
            collective_id=ident, has_side_effects=True, vmem_limit_bytes=56 << 20
        ),
    )(through_b, through_decay, sums, decay_grad, scan_grad, step_pre, pre_act, act, padded, z_half, low_all, small), height


def body(
    hidden_in, lengths, cotangent, norm_gain, in_weight, conv_weight, conv_bias, low_weight, step_weight,
    step_bias, decay_log, skip_gain, out_weight, ffn_gain, gate_up, down_weight,
):
    seqs, local, width = hidden_in.shape
    rows = seqs * local
    shards, pieces = lax.axis_size("shard"), lax.axis_size("ctx")
    inner = in_weight.shape[2]
    taps = conv_weight.shape[0]
    rank = step_weight.shape[0]
    states = decay_log.shape[0]
    low_len = low_weight.shape[0]

    def rows16(v):
        return jnp.pad(v, ((0, 16 - v.shape[0]), (0, 0)))

    small = jnp.concatenate(
        [low_weight, step_weight, decay_log, rows16(jnp.concatenate([conv_weight, conv_bias[None]], axis=0)),
         rows16(step_bias[None]), rows16(skip_gain[None])], axis=0,
    )
    at_bias = low_len + rank + states + 16
    at_skip = at_bias + 16
    hidden_rows = hidden_in.reshape(rows, width)
    small = jnp.pad(small, ((0, -small.shape[0] % 16), (0, 0)))
    gains = jnp.stack([norm_gain, ffn_gain])
    gains = jnp.pad(gains, ((0, 14), (0, 0)))
    in_half = in_weight.transpose(1, 0, 2)
    in_w, small, gains, normed_one, gate_z, padded, pre_act, act_half, low_all = front(
        hidden_rows, in_half, small, gains, seqs, low_len + rank + states, taps, low_len, 0
    )
    out_parts = lax.all_gather(out_weight, "shard")
    gate_half = gate_up.transpose(1, 0, 2)
    gate_w = [lax.all_gather(gate_half[c], "shard", axis=0, tiled=True) for c in range(2)]
    down_parts = lax.all_gather(down_weight, "shard")
    part = width // shards

    low_w = small[:low_len]
    step_w = small[low_len : low_len + rank]
    at = low_len + rank
    decay_w = small[at : at + states].astype(f32)
    kernel = small[at + states : at + states + taps].astype(f32)
    skip_full = small[at_skip].astype(f32)
    gain_one, gain_two = gains[0:1].astype(f32), gains[1:2].astype(f32)

    first_slot = lax.axis_index("ctx") * local
    positions = first_slot + jnp.arange(local, dtype=jnp.int32)
    pad_mask = (positions[None, :] < lengths[:, None]).astype(f32)

    source = hidden_rows.astype(f32)
    act_full = act_half.astype(f32)
    step_low = low_all[:rank].astype(bf16)
    decay_rate = -jnp.exp(decay_w)
    rate = (decay_rate * log2e).reshape(states, 8, 128)
    scan_out, gated_out, mixed_part, step_pre, kept, enter, size3, drive3 = scan_forward(
        low_all, act_half, gate_z, small, rate, out_parts, seqs, rank, low_len, at_bias, at_skip, 2
    )
    step_size = jax.nn.softplus(step_pre)
    gate_act = jax.nn.silu(gate_z)
    upstream = cotangent.reshape(rows, width).astype(f32) * pad_mask.reshape(rows, 1)
    ffn_grad = upstream.astype(bf16)
    ffn_part, middle, mix_grad, middle_grad, gain_sum, both_grad, down_grad = feed_forward(
        mixed_part, hidden_rows, gain_two, ffn_grad, gate_w, down_parts, 3
    )
    ffn_gain_grad = jnp.sum(gain_sum, axis=0) / gain_two[0]

    out_weight_grad = inner_rows(mix_grad, gated_out).astype(bf16)
    gated_grad = sum(outer_cols(mix_grad[:, k * part : (k + 1) * part], out_parts[k]) for k in range(shards))
    scan_grad = gated_grad * gate_act
    z_grad = gated_grad * scan_out * silu_grad(gate_z)
    through_b, through_decay, b_sums, c_sums, decay_sum, mixed_out, *ffn_shares = scan_backward(
        size3, drive3, scan_grad, low_all, rank, rate, kept, enter, seqs, 6, ffn_part, add_end, [middle], 32,
        [both_grad, down_grad],
    )
    mixed_out = mixed_out.reshape(hidden_in.shape)
    decay_log_grad = decay_sum.reshape(states, inner) * decay_rate
    sums = jnp.concatenate([v[:, 0].reshape(rows, states).T for v in (b_sums, c_sums)], axis=0)
    z_half = z_grad.astype(bf16)
    (project_grad, small_blocks), small_height = scan_tail(
        through_b, through_decay, sums, decay_log_grad, scan_grad, step_pre, pre_act, act_half, padded, z_half, low_all, small, 7,
        seqs, low_len, rank, states, taps,
    )
    in_weight_grad = inner_rows(normed_one, project_grad).astype(bf16)
    first_part = sum(outer_cols(project_grad[:, c * inner : (c + 1) * inner], in_w[c]) for c in range(2)).astype(bf16)
    norm_gain_grad = jnp.sum(first_part.astype(f32) * source * rms_scale(source), axis=0)
    places, share = shards * pieces, width // (shards * pieces)
    lane = inner // places
    gain_rows = -(-2 * share // lane)
    gain_blocks = jnp.concatenate([norm_gain_grad.reshape(places, share), ffn_gain_grad.reshape(places, share)], axis=1)
    gain_blocks = jnp.pad(gain_blocks, ((0, 0), (0, gain_rows * lane - 2 * share))).reshape(places, gain_rows, lane)
    gain_height = 16 * -(-gain_rows // 16)
    gain_blocks = jnp.pad(gain_blocks, ((0, 0), (gain_height - gain_rows, 0), (0, 0)))
    gain_blocks = gain_blocks.reshape(places * gain_height, lane).astype(bf16)
    input_grad, in_share, out_share, small_out, gain_share = tp_sum(
        first_part, norm_back_end, [hidden_rows, gain_one, middle_grad], [], 32, 8,
        scatters=[in_weight_grad, out_weight_grad, small_blocks, gain_blocks], line_too=True,
        steps=[16, 16, small_height // 2, gain_height],
    )
    gain_share = gain_share[gain_height - gain_rows :].reshape(-1)
    input_grad = input_grad.astype(f32).reshape(hidden_in.shape)
    at = low_len + rank
    return (
        mixed_out,
        input_grad,
        gain_share[:share],
        in_share.reshape((-1,) + in_weight.shape[1:]),
        small_out[at + states : at + states + taps],
        small_out[at + states + taps],
        small_out[:low_len],
        small_out[low_len : low_len + rank],
        small_out[at + states + taps + 1],
        small_out[at : at + states],
        small_out[at + states + taps + 2],
        out_share.T,
        gain_share[share : 2 * share],
        ffn_shares[0].reshape((-1,) + gate_up.shape[1:]),
        ffn_shares[1].T,
    )


def solution(mesh):
    placed = (
        P("shard", "ctx", None),
        P("shard"),
        P("shard", "ctx", None),
        P("shard"),
        P("shard", None, "tp"),
        P(None, ("tp", "shard")),
        P(("tp", "shard")),
        P(None, ("tp", "shard")),
        P(None, ("tp", "shard")),
        P(("tp", "shard")),
        P(None, ("tp", "shard")),
        P(("tp", "shard")),
        P("tp", "shard"),
        P("shard"),
        P("shard", None, "tp"),
        P("tp", "shard"),
    )
    return jax.shard_map(
        body,
        mesh=mesh,
        in_specs=placed,
        out_specs=(
            P("shard", "ctx", None),
            P("shard", "ctx", None),
            P(("shard", "ctx")),
            P(("shard", "ctx"), None, "tp"),
            P(None, ("tp", "shard", "ctx")),
            P(("tp", "shard", "ctx")),
            P(None, ("tp", "shard", "ctx")),
            P(None, ("tp", "shard", "ctx")),
            P(("tp", "shard", "ctx")),
            P(None, ("tp", "shard", "ctx")),
            P(("tp", "shard", "ctx")),
            P("tp", ("shard", "ctx")),
            P(("shard", "ctx")),
            P(("shard", "ctx"), None, "tp"),
            P("tp", ("shard", "ctx")),
        ),
        check_vma=False,
    )
```

```python
import functools

import jax
import jax.numpy as jnp
from jax import lax
from jax.experimental import pallas as pl
from jax.experimental.pallas import tpu as pltpu
from jax.sharding import PartitionSpec as P

MESH = pl.DeviceIdType.MESH
epsilon = 1e-05
log2e = 1.4426950408889634
bf16 = jnp.bfloat16
f32 = jnp.float32
VMEM = pl.BlockSpec(memory_space=pltpu.VMEM)
HBM = pl.BlockSpec(memory_space=pl.ANY)


def inner_rows(left, right):
    return lax.dot_general(left, right, (((0,), (0,)), ((), ())), preferred_element_type=f32)


def outer_cols(left, right):
    return lax.dot_general(left, right, (((1,), (1,)), ((), ())), preferred_element_type=f32)


def silu_grad(values):
    sig_val = jax.nn.sigmoid(values)
    return sig_val * (1.0 + values * (1.0 - sig_val))


def rms_scale(source):
    return lax.rsqrt(jnp.mean(source * source, axis=-1, keepdims=True) + epsilon)


class Line:
    lag = 2
    ahead = 4

    def __init__(self, shape, chunk, epilogue, extras, out_dtype):
        self.shape, self.chunk, self.epilogue, self.out_dtype = shape, chunk, epilogue, out_dtype
        self.count = shape[0] // chunk
        self.extras = [(e.shape, e.dtype) for e in extras]

    def scratch(self):
        return (
            [pltpu.VMEM(self.shape, bf16)] * 4
            + [pltpu.SemaphoreType.DMA((self.count,))] * 6
            + [pltpu.VMEM(shape, dtype) for shape, dtype in self.extras]
            + [pltpu.SemaphoreType.DMA((1 + len(self.extras),))]
        )

    def bind(self, p_ref, ins, out_ref, outs, scratch):
        self.p_ref, self.given, self.out_ref, self.outs = p_ref, ins, out_ref, outs
        (self.p, self.got_a, self.pair, self.got_b, self.a_send, self.a_recv, self.b_send, self.b_recv,
         self.c_send, self.c_recv) = scratch[:10]
        self.ins, self.in_sem = scratch[10:-1], scratch[-1]
        me = lax.axis_index("tp")
        self.mate = me + 1 - 2 * (me % 2)
        self.across = 3 - me
        self.middle = jnp.logical_or(me == 1, me == 2)

    def at(self, c):
        return pl.ds(pl.multiple_of(c * self.chunk, self.chunk), self.chunk)

    def remote(self, source, target, send, recv, c, to):
        return pltpu.make_async_remote_copy(
            source.at[self.at(c)], target.at[self.at(c)], send.at[c], recv.at[c], device_id={"tp": to}, device_id_type=MESH
        )

    def copy_a(self, c):
        return self.remote(self.p_ref, self.got_a, self.a_send, self.a_recv, c, self.mate)

    def copy_b(self, c):
        return self.remote(self.pair, self.got_b, self.b_send, self.b_recv, c, self.across)

    def copy_c(self, c):
        return self.remote(self.out_ref, self.out_ref, self.c_send, self.c_recv, c, self.mate)

    def loads(self):
        pairs = [(self.p_ref, self.p)] + list(zip(self.given, self.ins))
        return [pltpu.make_async_copy(a, b, self.in_sem.at[i]) for i, (a, b) in enumerate(pairs)]

    def begin(self, barrier, met, ends_meet=False):
        pl.semaphore_signal(barrier, inc=1, device_id={"tp": self.mate}, device_id_type=MESH)

        @pl.when(self.middle)
        def _():
            pl.semaphore_signal(barrier, inc=1, device_id={"tp": self.across}, device_id_type=MESH)
            for load in self.loads():
                load.start()
            pl.semaphore_wait(barrier, met + 2)
            for load in self.loads():
                load.wait()

        @pl.when(jnp.logical_not(self.middle))
        def _():
            if ends_meet:
                pl.semaphore_signal(barrier, inc=1, device_id={"tp": self.across}, device_id_type=MESH)
            pl.semaphore_wait(barrier, met + 2 if ends_meet else met + 1)

            for c in range(min(self.ahead, self.count)):
                self.copy_a(c).start()

    def greet(self, barrier, met):
        pl.semaphore_signal(barrier, inc=1, device_id={"tp": self.mate}, device_id_type=MESH)

        @pl.when(self.middle)
        def _():
            pl.semaphore_signal(barrier, inc=1, device_id={"tp": self.across}, device_id_type=MESH)
            pl.semaphore_wait(barrier, met + 2)

        @pl.when(jnp.logical_not(self.middle))
        def _():
            pl.semaphore_wait(barrier, met + 1)

    def start(self):
        @pl.when(jnp.logical_not(self.middle))
        def _():
            for c in range(min(self.ahead, self.count)):
                self.copy_a(c).start()

    def first(self, c):
        at = self.at(c)
        self.copy_a(c).wait_recv()
        self.pair[at, :] = self.p[at, :] + self.got_a[at, :]
        self.copy_b(c).start()

    def second(self, c):
        at = self.at(c)
        self.copy_b(c).wait_recv()
        total = self.pair[at, :].astype(f32) + self.got_b[at, :].astype(f32)
        self.epilogue(c, at, total, self.ins, self.out_ref, self.outs)
        self.copy_c(c).start()

    def tick(self, c):
        lag = min(self.lag, self.count)

        @pl.when(jnp.logical_and(self.middle, c < self.count))
        def _():
            self.first(c)

        @pl.when(jnp.logical_and(self.middle, jnp.logical_and(c >= lag, c < self.count + lag)))
        def _():
            self.second(c - lag)

        @pl.when(jnp.logical_and(jnp.logical_not(self.middle), c + self.ahead < self.count))
        def _():
            self.copy_a(c + self.ahead).start()

    def quiet_tick(self, c):
        lag = min(self.lag, self.count)

        @pl.when(jnp.logical_and(self.middle, jnp.logical_and(c >= 0, c < self.count)))
        def _():
            self.first(c)

        @pl.when(jnp.logical_and(self.middle, jnp.logical_and(c >= lag, c < self.count + lag)))
        def _():
            self.second(c - lag)

    def ticks(self):
        return self.count + min(self.lag, self.count)

    def finish(self, take_result=True):
        @pl.when(self.middle)
        def _():
            def drain(c, _):
                self.copy_b(c).wait_send()
                self.copy_c(c).wait_send()
                return 0

            lax.fori_loop(0, self.count, drain, 0)

        @pl.when(jnp.logical_not(self.middle))
        def _():
            def take(c, _):
                if take_result:
                    self.copy_c(c).wait_recv()
                self.copy_a(c).wait_send()
                return 0

            lax.fori_loop(0, self.count, take, 0)


share_lag = 2
share_ahead = 2


class Halving:
    def __init__(self, arrays, step_rows=16, lag=share_lag):
        self.lag = lag
        steps = [step_rows] * len(arrays) if isinstance(step_rows, int) else list(step_rows)
        self.steps = steps
        shards, pieces = lax.axis_size("shard"), lax.axis_size("ctx")
        self.n = len(arrays)
        self.bits = [
            (axis, 1 << k)
            for axis, size in (("shard", shards), ("ctx", pieces))
            for k in reversed(range(size.bit_length() - 1))
        ]
        self.depth = len(self.bits)
        head = shards.bit_length() - 1
        self.dims = list(range(self.depth))
        self.orders = (self.dims, self.dims[:head] + self.dims[head:][::-1])
        self.parts = [g.shape[0] // (shards * pieces) // k for g, k in zip(arrays, steps)]
        self.folded = [
            g.reshape((2,) * self.depth + (p * k, g.shape[1])) for g, p, k in zip(arrays, self.parts, steps)
        ]
        self.tails = [g.shape[self.depth :] for g in self.folded]
        self.pairs = (max(self.parts, default=0) + 1) // 2
        self.turns = self.pairs + lag * (self.depth - 1)

    def results(self):
        return [jax.ShapeDtypeStruct(tail, f32) for tail in self.tails]

    def scratch(self):
        if not self.n:
            return []
        held = [pltpu.VMEM((2,) * (self.depth - 1) + tail, bf16) for tail in self.tails]
        for j in range(self.depth):
            held += [pltpu.VMEM((2,) * (self.depth - 1 - j) + tail, bf16) for tail in self.tails]
        sem = pltpu.SemaphoreType.DMA((self.depth, self.n, max(self.parts)))
        return held + [sem, sem, pltpu.SemaphoreType.DMA((self.n, max(self.parts)))]

    def bind(self, full, shares, scratch):
        n = self.n
        self.partner, self.mine = [], []
        if not n:
            return
        self.full, self.shares, self.own = full, shares, scratch[:n]
        self.landed = [scratch[n * (j + 1) : n * (j + 2)] for j in range(self.depth)]
        self.send, self.recv, self.own_sem = scratch[n * (self.depth + 1) :]
        for axis, bit in self.bits:
            here = lax.axis_index(axis)
            self.mine.append((here // bit) % 2)
            self.partner.append({axis: here + bit - 2 * bit * ((here // bit) % 2)})

    def greet(self, barrier):
        for who in self.partner:
            pl.semaphore_signal(barrier, inc=1, device_id=who, device_id_type=MESH)
        return len(self.partner)

    def spot(self, a, c):
        return pl.ds(pl.multiple_of(c * self.steps[a], self.steps[a]), self.steps[a])

    def pick(self, remaining, dim, index, a, c):
        return tuple(index if d == dim else slice(None) for d in remaining) + (self.spot(a, c), slice(None))

    def rest(self, order, j):
        return [d for d in self.dims if d not in order[:j]]

    def copy(self, j, a, c, order):
        source = self.full[a] if j == 0 else self.landed[j - 1][a]
        d = order[j]
        return pltpu.make_async_remote_copy(
            source.at[self.pick(self.rest(order, j), d, 1 - self.mine[d], a, c)],
            self.landed[j][a].at[self.pick(self.rest(order, j + 1), None, None, a, c)],
            self.send.at[j, a, c],
            self.recv.at[j, a, c],
            device_id=self.partner[d],
            device_id_type=MESH,
        )

    def own_copy(self, a, c, order):
        return pltpu.make_async_copy(
            self.full[a].at[self.pick(self.dims, order[0], self.mine[order[0]], a, c)],
            self.own[a].at[self.pick(self.rest(order, 1), None, None, a, c)],
            self.own_sem.at[a, c],
        )

    def begin(self, a, c, order):
        self.copy(0, a, c, order).start()
        self.own_copy(a, c, order).start()

    def step(self, j, a, c, order):
        self.copy(j, a, c, order).wait_recv()
        where = self.pick(self.rest(order, j + 1), None, None, a, c)
        d = order[j]
        if j == 0:
            self.own_copy(a, c, order).wait()
            kept = self.own[a][where]
        else:
            kept = self.landed[j - 1][a][self.pick(self.rest(order, j), d, self.mine[d], a, c)]
        if j == self.depth - 1:
            self.shares[a][self.spot(a, c), :] = kept.astype(f32) + self.landed[j][a][where].astype(f32)
        else:
            self.landed[j][a][where] = kept + self.landed[j][a][where]
            self.copy(j + 1, a, c, order).start()

    def each(self, i, fn):
        for parity in (0, 1):
            c = 2 * i + parity
            for a in range(self.n):

                @pl.when(jnp.logical_and(c >= 0, c < self.parts[a]))
                def _():
                    fn(a, c, self.orders[parity])

    def start(self):
        for i in range(share_ahead if self.n else 0):
            self.each(i, self.begin)

    def tick(self, i):
        if self.n:
            self.each(i + share_ahead, self.begin)
            for j in range(self.depth):
                self.each(i - self.lag * j, functools.partial(self.step, j))

    def finish(self):
        def sent(i, _):
            for j in range(self.depth):
                self.each(i, lambda a, c, order: self.copy(j, a, c, order).wait_send())
            return 0

        if self.n:
            lax.fori_loop(0, self.pairs, sent, 0)


def tp_sum(partial, epilogue, extras, extra_outs, chunk, ident, out_dtype=bf16, scatters=(), line_too=False, steps=16):
    line = Line(partial.shape, chunk, epilogue, extras, out_dtype)
    share = Halving(scatters, steps)
    n_ex, n_out, n_sc = len(extras), len(extra_outs), len(scatters)
    n_line, n_share = len(line.scratch()), len(share.scratch())

    def kernel(*refs):
        refs = list(refs)

        def take_refs(n):
            taken = refs[:n]
            del refs[:n]
            return taken

        (p_ref,) = take_refs(1)
        ins = take_refs(n_ex)
        full = take_refs(n_sc)
        (out_ref,) = take_refs(1)
        outs = take_refs(n_out)
        shares = take_refs(n_sc)
        line.bind(p_ref, ins, out_ref, outs, take_refs(n_line))
        share.bind(full, shares, take_refs(n_share))
        tail, tail_send, tail_recv = take_refs(3) if line_too else (None, None, None)
        barrier = pltpu.get_barrier_semaphore()
        line.begin(barrier, share.greet(barrier), line_too)
        share.start()

        def tail_copy(k):
            to = (line.mate, line.across)[k]
            source = shares[-1].at[pl.ds(shares[-1].shape[0] - 8, 8)] if k == 0 else tail.at[2]
            return pltpu.make_async_remote_copy(
                source, tail.at[k], tail_send.at[k], tail_recv.at[k], device_id={"tp": to}, device_id_type=MESH
            )

        def tail_step(k):
            last = pl.ds(shares[-1].shape[0] - 8, 8)
            if k > 0:
                tail_copy(k - 1).wait()
            if k == 1:
                tail[2] = shares[-1][last, :] + tail[0]
            if k == 2:
                shares[-1][last, :] = tail[2] + tail[1]
            else:
                tail_copy(k).start()

        ready = (share.parts[-1] + 1) // 2 + share.lag * (share.depth - 1) if n_sc else 0

        def turn(i, _):
            for parity in (0, 1):
                line.tick(2 * i + parity)
            share.tick(i)
            for k in range(3 if line_too else 0):

                @pl.when(i == ready + k)
                def _():
                    tail_step(k)

            return 0

        turns = max((line.ticks() + 1) // 2, share.turns if n_sc else 0, ready + 3 if line_too else 0)
        lax.fori_loop(0, turns, turn, 0)
        line.finish()
        share.finish()

    buffers = []
    if line_too:
        pair_sem = pltpu.SemaphoreType.DMA((2,))
        buffers += [pltpu.VMEM((3, 8, scatters[-1].shape[-1]), f32), pair_sem, pair_sem]
    return pl.pallas_call(
        kernel,
        out_shape=[jax.ShapeDtypeStruct(partial.shape, out_dtype)] + list(extra_outs) + share.results(),
        in_specs=[HBM] * (1 + n_ex + n_sc),
        out_specs=[VMEM] * (1 + n_out + n_sc),
        scratch_shapes=line.scratch() + share.scratch() + buffers,
        compiler_params=pltpu.CompilerParams(
            collective_id=ident, has_side_effects=True, vmem_limit_bytes=56 << 20
        ),
    )(partial, *extras, *share.folded)


def plain_end(c, rows, total, ins, out_ref, outs):
    out_ref[rows, :] = total.astype(out_ref.dtype)


def norm_end(c, rows, total, ins, out_ref, outs):
    source_ref, gain_ref = ins
    middle = source_ref[rows, :].astype(f32) + total
    outs[0][rows, :] = middle
    out_ref[rows, :] = (middle * rms_scale(middle) * gain_ref[...]).astype(bf16)


def add_end(c, rows, total, ins, out_ref, outs):
    out_ref[rows, :] = (ins[0][rows, :] + total).astype(bf16)


def norm_back_end(c, rows, total, ins, out_ref, outs):
    source = ins[0][rows, :].astype(f32)
    inv = rms_scale(source)
    weighted = total * ins[1][...]
    back = inv * weighted - source * (inv * inv * inv) * jnp.mean(weighted * source, axis=-1, keepdims=True)
    result = ins[2][rows, :] + back
    if outs:
        outs[0][rows, :] = result
    out_ref[rows, :] = result.astype(bf16)


halo = 16
tile_cols = 256


def front(hidden, in_half, small, gains, seqs, at_conv, taps, low_len, ident):
    rows, width = hidden.shape
    local = rows // seqs
    part, inner = in_half.shape[1:]
    shards, pieces = lax.axis_size("shard"), lax.axis_size("ctx")
    long = local + halo
    tiles = inner // tile_cols
    line = Line((low_len, rows), 80, plain_end, [], f32)
    n_line = len(line.scratch())

    def kernel(
        hid_ref, tail_ref, in_ref, small_ref, gain_ref,
        in_out, small_out, gain_out, normed_out, z_out, ext_out, pre_out, act_out, low_out,
        own_w, got_w, edge, normed, ext_n, acc, z_val, conv_f, ext_c, pre, act, low_acc, small_all, gain_all,
        send, recv, edge_sem, own_sem, out_sem, *rest
    ):
        me, ctx = lax.axis_index("shard"), lax.axis_index("ctx")
        barrier = pltpu.get_barrier_semaphore()
        line.bind(rest[0], [], low_out, [], list(rest))
        for step in range(1, shards):
            pl.semaphore_signal(barrier, inc=1, device_id={"shard": lax.rem(me + step, shards)}, device_id_type=MESH)
        pl.semaphore_signal(barrier, inc=1, device_id={"ctx": lax.rem(ctx + pieces - 1, pieces)}, device_id_type=MESH)
        load = pltpu.make_async_copy(in_ref, own_w, own_sem.at[0])
        load.start()
        small_size, gain_size = small_ref.shape[1], gain_ref.shape[1]
        small_at = pl.ds(pl.multiple_of(me * small_size, small_size), small_size)
        gain_at = pl.ds(pl.multiple_of(me * gain_size, gain_size), gain_size)
        small_all[:, small_at] = small_ref[...]
        gain_all[:, gain_at] = gain_ref[...]
        line.greet(barrier, shards)
        edge_copy = pltpu.make_async_remote_copy(
            tail_ref, edge, edge_sem.at[0], edge_sem.at[1],
            device_id={"ctx": lax.rem(ctx + 1, pieces)}, device_id_type=MESH,
        )
        copies = {}
        for step in range(1, shards):
            peer = {"shard": lax.rem(me + step, shards)}
            moves = [(gain_ref, gain_all.at[:, gain_at]), (small_ref, small_all.at[:, small_at])]
            moves += [(in_ref.at[c], got_w.at[step - 1, c]) for c in range(2)]
            for k, (source, target) in enumerate(moves):
                copies[step, k] = pltpu.make_async_remote_copy(
                    source, target, send.at[step, k], recv.at[step, k], device_id=peer, device_id_type=MESH
                )
        for k in range(4):
            for step in range(1, shards):
                copies[step, k].start()
            if k == 0:
                edge_copy.start()
        for step in range(1, shards):
            copies[step, 0].wait_recv()
        gain = gain_all[0:1, :].astype(f32)

        def norm_rows(i, _):
            at = pl.ds(pl.multiple_of(i * 16, 16), 16)
            source = hid_ref[at, :].astype(f32)
            value = (source * rms_scale(source) * gain).astype(bf16)
            normed[at, :] = value
            seq = i // (local // 16)
            ext_n[pl.ds(pl.multiple_of(i * 16 + (seq + 1) * halo, 16), 16), :] = value
            return 0

        lax.fori_loop(0, rows // 16, norm_rows, 0)
        edge_copy.wait_recv()
        for seq in range(seqs):
            source = edge[seq].astype(f32)
            value = source * rms_scale(source) * gain * (ctx > 0).astype(f32)
            ext_n[seq * long : seq * long + halo, :] = value.astype(bf16)
        outs = [(normed, normed_out)]
        pltpu.make_async_copy(normed, normed_out, out_sem.at[0]).start()

        def cols(c, j):
            return pl.ds(pl.multiple_of(c * inner + j * tile_cols, tile_cols), tile_cols)

        def finish_conv(j):
            here = pl.ds(pl.multiple_of(j * tile_cols, tile_cols), tile_cols)
            value = acc[:, cols(0, j)].astype(bf16)
            ext_c[:, here] = value
            conv_f[...] = value.astype(f32)
            weights = small_all[at_conv : at_conv + 16, here].astype(f32)
            for seq in range(seqs):
                for k in range(local // 64):
                    first = seq * long + halo + k * 64
                    total = weights[taps : taps + 1]
                    for tap in range(taps):
                        total = total + weights[tap : tap + 1] * conv_f[first - taps + 1 + tap : first - taps + 1 + tap + 64, :]
                    to = slice(seq * local + k * 64, seq * local + (k + 1) * 64)
                    pre[to, here] = total
                    act[to, here] = jax.nn.silu(total).astype(bf16)
            low = outer_cols(small_all[0:low_len, here], act[:, here])
            low_acc[...] = low_acc[...] + low

        def finish_gate(j):
            here = pl.ds(pl.multiple_of(j * tile_cols, tile_cols), tile_cols)
            for seq in range(seqs):
                z_val[seq * local : (seq + 1) * local, here] = acc[seq * long + halo : (seq + 1) * long, cols(1, j)]

        low_acc[...] = jnp.zeros_like(low_acc)
        own_place = pl.ds(pl.multiple_of(me * part, part), part)
        load.wait()
        own_save = pltpu.make_async_copy(own_w, in_out.at[:, own_place], own_sem.at[1])
        own_save.start()
        saves = []
        for step in range(shards):
            owner = lax.rem(me - step + shards, shards)
            place = pl.ds(pl.multiple_of(owner * part, part), part)
            last = step == shards - 1
            if last:
                for other in range(1, shards):
                    copies[other, 1].wait_recv()
            for c in range(2):
                weight = own_w.at[c] if step == 0 else got_w.at[step - 1, c]
                if step > 0:
                    copies[step, 2 + c].wait_recv()

                def matmul(j, _):
                    here = pl.ds(pl.multiple_of(j * tile_cols, tile_cols), tile_cols)
                    value = jnp.dot(ext_n[:, place], weight[:, here], preferred_element_type=f32)
                    acc[:, cols(c, j)] = value if step == 0 else acc[:, cols(c, j)] + value
                    if last:
                        (finish_conv, finish_gate)[c](j)
                    return 0

                lax.fori_loop(0, tiles, matmul, 0)
            if step > 0:
                saves.append(pltpu.make_async_copy(got_w.at[step - 1], in_out.at[:, place], own_sem.at[1 + step]))
                saves[-1].start()
        line.p[...] = low_acc[...].astype(bf16)
        outs += [(z_val, z_out), (ext_c, ext_out), (pre, pre_out), (act, act_out), (small_all, small_out), (gain_all, gain_out)]
        for k, (source, target) in enumerate(outs):
            if k:
                pltpu.make_async_copy(source, target, out_sem.at[k]).start()
        line.start()
        for c in range(line.ticks()):
            line.tick(c)
        line.finish()
        for save in saves + [own_save]:
            save.wait()
        for k, (source, target) in enumerate(outs):
            pltpu.make_async_copy(source, target, out_sem.at[k]).wait()
        for copy in copies.values():
            copy.wait_send()
        edge_copy.wait_send()

    sds = jax.ShapeDtypeStruct
    tails = hidden.reshape(seqs, local, width)[:, local - halo :]
    return pl.pallas_call(
        kernel,
        out_shape=[
            sds((2, shards * part, inner), bf16),
            sds((small.shape[0], small.shape[1] * shards), bf16),
            sds((gains.shape[0], gains.shape[1] * shards), bf16),
            sds((rows, width), bf16),
            sds((rows, inner), f32),
            sds((seqs * long, inner), bf16),
            sds((rows, inner), f32),
            sds((rows, inner), bf16),
            sds((low_len, rows), f32),
        ],
        in_specs=[VMEM, HBM, HBM, VMEM, VMEM],
        out_specs=[HBM] * 8 + [VMEM],
        scratch_shapes=[
            pltpu.VMEM((2, part, inner), bf16),
            pltpu.VMEM((max(shards - 1, 1), 2, part, inner), bf16),
            pltpu.VMEM((seqs, halo, width), bf16),
            pltpu.VMEM((rows, width), bf16),
            pltpu.VMEM((seqs * long, width), bf16),
            pltpu.VMEM((seqs * long, 2 * inner), f32),
            pltpu.VMEM((rows, inner), f32),
            pltpu.VMEM((seqs * long, tile_cols), f32),
            pltpu.VMEM((seqs * long, inner), bf16),
            pltpu.VMEM((rows, inner), f32),
            pltpu.VMEM((rows, inner), bf16),
            pltpu.VMEM((low_len, rows), f32),
            pltpu.VMEM((small.shape[0], small.shape[1] * shards), bf16),
            pltpu.VMEM((gains.shape[0], gains.shape[1] * shards), bf16),
            pltpu.SemaphoreType.DMA((shards, 4)),
            pltpu.SemaphoreType.DMA((shards, 4)),
            pltpu.SemaphoreType.DMA((2,)),
            pltpu.SemaphoreType.DMA((shards + 1,)),
            pltpu.SemaphoreType.DMA((7,)),
        ]
        + line.scratch(),
        compiler_params=pltpu.CompilerParams(
            collective_id=ident, has_side_effects=True, vmem_limit_bytes=56 << 20
        ),
    )(hidden, tails, in_half, small, gains)


piece = 16
slots_held = 4
unroll = 4


def spread(flat_ref, natural, first):
    for j in range(8):
        flat_ref[pl.ds(first * 8 + j, 8, stride=8), :] = natural[:, j * 128 : (j + 1) * 128]


def unspread(flat_ref, first):
    return jnp.concatenate([flat_ref[pl.ds(first * 8 + j, 8, stride=8), :] for j in range(8)], axis=1)


def tile(ref, t):
    return ref[pl.ds(pl.multiple_of(t * 8, 8), 8), :]


def row(ref, t, n, states):
    return ref[pl.ds(t * states + n, 8, stride=0), :]


def exchange(ends, got, send, recv, seq, width):
    me = lax.axis_index("ctx")
    copies = []
    for step in range(1, width):
        copies.append(
            pltpu.make_async_remote_copy(
                ends.at[seq],
                got.at[me, seq],
                send.at[seq, step],
                recv.at[seq, step],
                device_id={"ctx": lax.rem(me + step, width)},
                device_id_type=MESH,
            )
        )
        copies[-1].start()
    return copies


def ctx_greet(width):
    me = lax.axis_index("ctx")
    barrier = pltpu.get_barrier_semaphore()
    for step in range(1, width):
        pl.semaphore_signal(barrier, inc=1, device_id={"ctx": lax.rem(me + step, width)}, device_id_type=MESH)
    return barrier


def entering(got, seq, rate_ref, states, width, reverse):
    me = lax.axis_index("ctx")
    result = []
    for n in range(states):
        value = jnp.zeros((8, 128), f32)
        for k in reversed(range(width)) if reverse else range(width):
            new = jnp.exp2(got[k, seq, states] * rate_ref[n]) * value + got[k, seq, n]
            value = jnp.where(me < k if reverse else me > k, new, value)
        result.append(value)
    return result


def spread_rows(low_ref, first, out_ref):
    states, slots = 16, low_ref.shape[1]

    def lanes(k, _):
        block = low_ref[first : first + states, pl.ds(pl.multiple_of(k * 128, 128), 128)]
        for i in range(128):
            to = pl.ds(pl.multiple_of((k * 128 + i) * states, states), states)
            out_ref[to, :] = jnp.broadcast_to(block[:, i : i + 1], (states, 128))
        return 0

    lax.fori_loop(0, slots // 128, lanes, 0)


def scan_forward(low_all, act, gate_z, small, rate, out_parts, seqs, rank, at_step, at_bias, at_skip, ident):
    rows, channels = act.shape
    shards, _, part = out_parts.shape
    local = rows // seqs
    states = rate.shape[0]
    width = lax.axis_size("ctx")
    pieces = local // piece

    def kernel(
        low_ref, act_ref, z_ref, small_ref, rate_ref, w_ref,
        scan_ref, gated_ref, mixed_ref, pre_ref, kept_ref, enter_ref, size3, drive3,
        y3, ends, got, held, b_ref, c_ref, low_t, w_own, send, recv, out_sem, w_sem,
    ):
        barrier = ctx_greet(width)
        load = pltpu.make_async_copy(w_ref, w_own, w_sem)
        load.start()
        low_t[...] = low_ref[0:rank, :].T.astype(bf16)
        bias = small_ref[at_bias : at_bias + 16, :].astype(f32)[0:1]
        for j in range(channels // 256):
            here = slice(j * 256, (j + 1) * 256)
            value = jnp.dot(low_t[...], small_ref[at_step : at_step + rank, here], preferred_element_type=f32)
            pre_ref[:, here] = value + bias[:, here]
        spread_rows(low_ref, rank, b_ref)
        spread_rows(low_ref, rank + states, c_ref)

        def lay(i, _):
            first = pl.multiple_of(i * 16, 16)
            act_block = act_ref[pl.ds(first, 16), :].astype(f32)
            size = jax.nn.softplus(pre_ref[pl.ds(first, 16), :])
            drive = size * act_block
            for h in range(2):
                spread(size3, size[h * 8 : h * 8 + 8], first + h * 8)
                spread(drive3, drive[h * 8 : h * 8 + 8], first + h * 8)
            return 0

        lax.fori_loop(0, rows // 16, lay, 0)
        pl.semaphore_wait(barrier, width - 1)
        copies = []
        for seq in range(seqs):

            def first_pass(i, carried):
                values, total = list(carried[:-1]), carried[-1]
                for u in range(unroll):
                    t = seq * local + i * unroll + u
                    s, d = tile(size3, t), tile(drive3, t)
                    total = total + s
                    for n in range(states):
                        values[n] = jnp.exp2(s * rate_ref[n]) * values[n] + d * row(b_ref, t, n, states)
                return tuple(values) + (total,)

            zero = tuple(jnp.zeros((8, 128), f32) for _ in range(states + 1))
            done = lax.fori_loop(0, local // unroll, first_pass, zero)
            for n in range(states + 1):
                ends[seq, n] = done[n]
            copies.append(exchange(ends, got, send, recv, seq, width))
        me = lax.axis_index("ctx")
        for seq in range(seqs):
            for copy in copies[seq]:
                copy.wait()
            got[me, seq] = ends[seq]
            start = entering(got, seq, rate_ref, states, width, False)
            for n in range(states):
                enter_ref[seq, n] = start[n]

            def save(k, slot):
                return pltpu.make_async_copy(
                    held.at[slot], kept_ref.at[pl.ds(seq * local + k * piece, piece)], out_sem.at[slot]
                )

            def one_piece(k, carried):
                slot = lax.rem(k, 2)

                @pl.when(k >= 2)
                def _():
                    save(k - 2, slot).wait()

                def second_pass(i, values):
                    values = list(values)
                    for u in range(unroll):
                        inside = i * unroll + u
                        t = seq * local + k * piece + inside
                        s, d = tile(size3, t), tile(drive3, t)
                        acc = [None] * 4
                        for n in range(states):
                            values[n] = jnp.exp2(s * rate_ref[n]) * values[n] + d * row(b_ref, t, n, states)
                            held[slot, inside, n] = values[n]
                            part = values[n] * row(c_ref, t, n, states)
                            acc[n % 4] = part if acc[n % 4] is None else acc[n % 4] + part
                        y3[pl.ds(pl.multiple_of(t * 8, 8), 8), :] = (acc[0] + acc[1]) + (acc[2] + acc[3])
                    return tuple(values)

                carried = lax.fori_loop(0, piece // unroll, second_pass, carried)
                save(k, slot).start()
                return carried

            lax.fori_loop(0, pieces, one_piece, tuple(start))
            for k in (pieces - 2, pieces - 1):
                save(k, k % 2).wait()

        skip = small_ref[at_skip : at_skip + 16, :].astype(f32)[0:1]

        def back(i, _):
            first = pl.multiple_of(i * 16, 16)
            here = pl.ds(first, 16)
            value = jnp.concatenate([unspread(y3, first), unspread(y3, first + 8)], axis=0)
            value = value + skip * act_ref[here, :].astype(f32)
            scan_ref[here, :] = value
            gated_ref[here, :] = (value * jax.nn.silu(z_ref[here, :])).astype(bf16)
            return 0

        lax.fori_loop(0, rows // 16, back, 0)
        load.wait()
        for k in range(shards):
            for j in range(-(-part // 256)):
                span = min(256, part)
                value = jnp.dot(gated_ref[...], w_own[k, :, j * span : (j + 1) * span], preferred_element_type=f32)
                mixed_ref[:, k * part + j * span : k * part + (j + 1) * span] = value.astype(bf16)

    flat = jax.ShapeDtypeStruct((rows * 8, 128), f32)
    return pl.pallas_call(
        kernel,
        out_shape=[
            jax.ShapeDtypeStruct((rows, channels), f32),
            jax.ShapeDtypeStruct((rows, channels), bf16),
            jax.ShapeDtypeStruct((rows, shards * part), bf16),
            jax.ShapeDtypeStruct((rows, channels), f32),
            jax.ShapeDtypeStruct((rows, states, 8, 128), f32),
            jax.ShapeDtypeStruct((seqs, states, 8, 128), f32),
            flat,
            flat,
        ],
        in_specs=[VMEM] * 5 + [HBM],
        out_specs=[VMEM] * 4 + [HBM, VMEM, VMEM, VMEM],
        scratch_shapes=[
            pltpu.VMEM((rows * 8, 128), f32),
            pltpu.VMEM((seqs, states + 1, 8, 128), f32),
            pltpu.VMEM((width, seqs, states + 1, 8, 128), f32),
            pltpu.VMEM((2, piece, states, 8, 128), f32),
            pltpu.VMEM((rows * states, 128), f32),
            pltpu.VMEM((rows * states, 128), f32),
            pltpu.VMEM((rows, rank), bf16),
            pltpu.VMEM(out_parts.shape, bf16),
            pltpu.SemaphoreType.DMA((seqs, width)),
            pltpu.SemaphoreType.DMA((seqs, width)),
            pltpu.SemaphoreType.DMA((2,)),
            pltpu.SemaphoreType.DMA,
        ],
        compiler_params=pltpu.CompilerParams(
            collective_id=ident, has_side_effects=True, vmem_limit_bytes=48 << 20
        ),
    )(low_all, act, gate_z, small, rate, out_parts)


def sublane_sums(parts):
    at = lax.broadcasted_iota(jnp.int32, (8, 128), 0)
    for shift in (4, 2, 1):
        low = (at // shift) % 2 == 0
        half = len(parts) // 2
        merged = []
        for one, two in zip(parts[:half], parts[half:]):
            merged.append(
                jnp.where(low, one + pltpu.roll(one, 8 - shift, 0), two + pltpu.roll(two, shift, 0))
            )
        parts = merged
    return parts[0]


def scan_backward(size3, drive3, grad, low_all, rank, rate, kept, enter, seqs, ident, partial, epilogue, extras, chunk, scatters):
    rows, channels = grad.shape
    local = rows // seqs
    states = rate.shape[0]
    width = lax.axis_size("ctx")
    pieces = local // piece
    early = 2
    unroll_b = 2
    line = Line(partial.shape, chunk, epilogue, extras, bf16)
    share = Halving(scatters, 16, 1)
    n_line, n_ex, n_sc = len(line.scratch()), len(extras), len(scatters)

    def kernel(*refs):
        refs = list(refs)

        def take_refs(n):
            taken = refs[:n]
            del refs[:n]
            return taken

        size_ref, drive_ref, grad_ref, low_ref, rate_ref, kept_ref, enter_ref, p_ref = take_refs(8)
        ins, full = take_refs(n_ex), take_refs(n_sc)
        tb3, sd3, bg_ref, cg_ref, dec_ref, sum_ref = take_refs(6)
        shares = take_refs(n_sc)
        grad3, b_ref, c_ref, ends, got, held, bpart, cpart, prior, send, recv, in_sem = take_refs(12)
        line.bind(p_ref, ins, sum_ref, [], take_refs(n_line))
        share.bind(full, shares, refs)
        barrier = ctx_greet(width)
        line.begin(barrier, width - 1 + share.greet(barrier))
        share.start()
        spread_rows(low_ref, rank, b_ref)
        spread_rows(low_ref, rank + states, c_ref)
        share.tick(0)

        def lay(i, _):
            first = pl.multiple_of(i * 8, 8)
            spread(grad3, grad_ref[pl.ds(first, 8), :], first)
            return 0

        lax.fori_loop(0, rows // 8, lay, 0)

        def fetch(g):
            first = (g // pieces) * local + (pieces - 1 - g % pieces) * piece
            slot = g % slots_held
            return pltpu.make_async_copy(kept_ref.at[pl.ds(first, piece)], held.at[slot], in_sem.at[slot])

        for g in range(slots_held - 1):
            fetch(g).start()

        copies = []
        for seq in range(seqs):

            def first_pass(i, carried):
                values, total = list(carried[:-1]), carried[-1]
                for u in range(unroll):
                    t = seq * local + local - 1 - (i * unroll + u)
                    s, g = tile(size_ref, t), tile(grad3, t)
                    total = total + s
                    for n in range(states):
                        values[n] = jnp.exp2(s * rate_ref[n]) * (values[n] + g * row(c_ref, t, n, states))
                return tuple(values) + (total,)

            zero = tuple(jnp.zeros((8, 128), f32) for _ in range(states + 1))
            done = zero
            for half in range(early):
                span = local // unroll // early
                done = lax.fori_loop(half * span, (half + 1) * span, first_pass, done)
                line.tick(seq * early + half)
            for n in range(states + 1):
                ends[seq, n] = done[n]
            copies.append(exchange(ends, got, send, recv, seq, width))
            share.tick(1 + seq)
        me = lax.axis_index("ctx")
        for n in range(states):
            dec_ref[n] = jnp.zeros((8, 128), f32)
        for seq in range(seqs):
            for copy in copies[seq]:
                copy.wait()
            got[me, seq] = ends[seq]
            start = entering(got, seq, rate_ref, states, width, True)
            fetch(seq * pieces).wait()

            def one_slot(slot, k, inside, adjoint, decays, prior_at):
                t = seq * local + k * piece + inside
                s, d, g = tile(size_ref, t), tile(drive_ref, t), tile(grad3, t)
                tb, sd = [None] * 2, [None] * 2
                b_parts, c_parts = [], []
                for n in range(states):
                    total = adjoint[n] + g * row(c_ref, t, n, states)
                    c_parts.append(held[slot, inside, n] * g)
                    b_parts.append(total * d)
                    through = total * row(b_ref, t, n, states)
                    adjoint[n] = jnp.exp2(s * rate_ref[n]) * total
                    kept_part = adjoint[n] * prior_at(n)
                    through_size = kept_part * rate_ref[n]
                    decays[n] = decays[n] + kept_part * s
                    tb[n % 2] = through if tb[n % 2] is None else tb[n % 2] + through
                    sd[n % 2] = through_size if sd[n % 2] is None else sd[n % 2] + through_size
                here = pl.ds(pl.multiple_of(t * 8, 8), 8)
                tb3[here, :] = tb[0] + tb[1]
                sd3[here, :] = sd[0] + sd[1]
                for h in range(states // 8):
                    spot = pl.ds(pl.multiple_of(inside * states + h * 8, 8), 8)
                    bpart[spot, :] = sublane_sums(b_parts[h * 8 : h * 8 + 8])
                    cpart[spot, :] = sublane_sums(c_parts[h * 8 : h * 8 + 8])

            def one_piece(back_k, carried):
                k = pieces - 1 - back_k
                place = seq * pieces + back_k
                slot = place % slots_held

                @pl.when(place + slots_held - 1 < seqs * pieces)
                def _():
                    fetch(place + slots_held - 1).start()

                def slots(i, carried):
                    adjoint, decays = list(carried[:states]), list(carried[states:])
                    for u in range(unroll_b):
                        inside = piece - 1 - (i * unroll_b + u)
                        one_slot(slot, k, inside, adjoint, decays, lambda n: held[slot, inside - 1, n])
                    return tuple(adjoint) + tuple(decays)

                carried = lax.fori_loop(0, piece // unroll_b - 1, slots, carried)
                adjoint, decays = list(carried[:states]), list(carried[states:])
                for inside in reversed(range(1, unroll_b)):
                    one_slot(slot, k, inside, adjoint, decays, lambda n: held[slot, inside - 1, n])

                @pl.when(k > 0)
                def _():
                    fetch(place + 1).wait()
                    prior[...] = held[(place + 1) % slots_held, piece - 1]

                @pl.when(k == 0)
                def _():
                    prior[...] = enter_ref[seq]

                one_slot(slot, k, 0, adjoint, decays, lambda n: prior[n])
                ones = jnp.ones((8, 128), bf16)
                for part, out in ((bpart, bg_ref), (cpart, cg_ref)):
                    sums = outer_cols(ones, part[...].astype(bf16))
                    out[pl.ds(seq * pieces + k, 1)] = sums[None]
                @pl.when(place % 2 == 0)
                def _():
                    line.tick(seqs * early + place // 2)

                @pl.when(place % 5 == 0)
                def _():
                    share.tick(1 + seqs + place // 5)

                return tuple(adjoint) + tuple(decays)

            zero = tuple(jnp.zeros((8, 128), f32) for _ in range(states))
            carried = lax.fori_loop(0, pieces, one_piece, tuple(start) + zero)
            for n in range(states):
                dec_ref[n] = dec_ref[n] + carried[states + n]

        for c in range(seqs * early + (seqs * pieces + 1) // 2, line.ticks()):
            line.tick(c)
        for i in range(1 + seqs + (seqs * pieces + 4) // 5, share.turns):
            share.tick(i)
        line.finish()
        share.finish()

    flat = jax.ShapeDtypeStruct((rows * 8, 128), f32)
    sums = jax.ShapeDtypeStruct((rows // piece, 8, piece * states), f32)
    return pl.pallas_call(
        kernel,
        out_shape=[flat, flat, sums, sums, jax.ShapeDtypeStruct((states, 8, 128), f32),
                   jax.ShapeDtypeStruct(partial.shape, bf16)] + share.results(),
        in_specs=[VMEM] * 5 + [HBM, VMEM] + [HBM] * (1 + n_ex + n_sc),
        out_specs=[VMEM] * (6 + n_sc),
        scratch_shapes=[pltpu.VMEM((rows * 8, 128), f32)]
        + [pltpu.VMEM((rows * states, 128), f32)] * 2
        + [
            pltpu.VMEM((seqs, states + 1, 8, 128), f32),
            pltpu.VMEM((width, seqs, states + 1, 8, 128), f32),
            pltpu.VMEM((slots_held, piece, states, 8, 128), f32),
            pltpu.VMEM((piece * states, 128), f32),
            pltpu.VMEM((piece * states, 128), f32),
            pltpu.VMEM((states, 8, 128), f32),
            pltpu.SemaphoreType.DMA((seqs, width)),
            pltpu.SemaphoreType.DMA((seqs, width)),
            pltpu.SemaphoreType.DMA((slots_held,)),
        ]
        + line.scratch()
        + share.scratch(),
        compiler_params=pltpu.CompilerParams(
            collective_id=ident, has_side_effects=True, vmem_limit_bytes=62 << 20
        ),
    )(size3, drive3, grad, low_all, rate, kept, enter, partial, *extras, *share.folded)


def feed_forward(mixed_part, hidden, gain, ffn_grad, gate_w, down_parts, ident):
    rows, width = hidden.shape
    shards, ffn, part = down_parts.shape
    chunk = 32
    block = 4 * chunk
    tile = ffn // 4
    blocks = rows // block
    fore = Line(mixed_part.shape, chunk, norm_end, [], bf16)
    after = Line(mixed_part.shape, chunk, norm_back_end, [], bf16)
    n_line = len(fore.scratch())
    behind = 5
    wtile = 256

    def kernel(
        p_ref, hid_ref, gain_ref, fg_ref, gate_ref, up_ref, down_ref,
        ffn_out, mid_out, mix_ref, midg_ref, gsum_ref, both_out, dw_out,
        normed, middle, hid_v, gg_v, ug_v, ffn_v, ffn_acc, back_acc, gate_v, up_v, down_v, stage, stage_d, load_sem, save_sem, *rest
    ):
        barrier = pltpu.get_barrier_semaphore()
        fore.bind(p_ref, [], normed, [middle], rest[:n_line])
        after.bind(rest[n_line], [], mix_ref, [midg_ref], rest[n_line:])
        fore.ins = [hid_ref, gain_ref]
        after.ins = [middle, gain_ref, fg_ref]
        loads = [
            pltpu.make_async_copy(a, b, load_sem.at[i])
            for i, (a, b) in enumerate(((gate_ref, gate_v), (up_ref, up_v), (down_ref, down_v)))
        ]
        fore.begin(barrier, 0)
        for load in loads:
            load.start()
        gsum_ref[...] = jnp.zeros_like(gsum_ref)
        lead = 4 + fore.lag

        def warm(c, _):
            fore.tick(c)
            return 0

        lax.fori_loop(0, lead, warm, 0)
        for load in loads:
            load.wait()
        outer = jnp.logical_not(fore.middle)

        def step(s, _):
            b, j = s // 4, s % 4
            fore.tick(s + lead)
            at = pl.ds(pl.multiple_of(b * block, block), block)
            here = pl.ds(pl.multiple_of(j * tile, tile), tile)

            @pl.when(j == 0)
            def _():
                ffn_acc[...] = jnp.zeros_like(ffn_acc)
                back_acc[...] = jnp.zeros_like(back_acc)

                @pl.when(outer)
                def _():
                    for k in range(4):
                        fore.copy_c(4 * b + k).wait_recv()

            source, grad = normed[at, :], fg_ref[at, :]
            gate = jnp.dot(source, gate_v[:, here], preferred_element_type=f32)
            up = jnp.dot(source, up_v[:, here], preferred_element_type=f32)
            sig = jax.nn.sigmoid(gate)
            silu = gate * sig
            hidden_val = (silu * up).astype(bf16)
            back = sum(
                outer_cols(grad[:, k * part : (k + 1) * part], down_v[k, here, :]) for k in range(shards)
            )
            gate_back = (back * up * (sig * (1.0 + gate * (1.0 - sig)))).astype(bf16)
            up_back = (back * silu).astype(bf16)
            hid_v[at, here] = hidden_val
            gg_v[at, here] = gate_back
            ug_v[at, here] = up_back

            after.quiet_tick(s - behind)

            for k in range(shards):
                to = slice(k * part, (k + 1) * part)
                ffn_acc[:, to] += jnp.dot(hidden_val, down_v[k, here, :], preferred_element_type=f32)
            for k in range(width // 512):
                to = slice(k * 512, (k + 1) * 512)
                back_acc[:, to] += outer_cols(gate_back, gate_v[to, here]) + outer_cols(up_back, up_v[to, here])

            @pl.when(j == 3)
            def _():
                ffn_v[at, :] = ffn_acc[...].astype(bf16)
                after.p[at, :] = back_acc[...].astype(bf16)
                for k in range(block // 16):
                    product = after.p[pl.ds(pl.multiple_of(b * block + k * 16, 16), 16), :].astype(f32)
                    product = product * normed[pl.ds(pl.multiple_of(b * block + k * 16, 16), 16), :].astype(f32)
                    gsum_ref[...] += product[:8] + product[8:]

                @pl.when(outer)
                def _():
                    for k in range(4):
                        after.copy_a(4 * b + k).start()

            return 0

        steps = 4 * blocks
        lax.fori_loop(0, steps, step, 0)
        ffn_save = pltpu.make_async_copy(ffn_v, ffn_out, save_sem.at[3])
        ffn_save.start()
        mid_save = pltpu.make_async_copy(middle, mid_out, save_sem.at[4])
        mid_save.start()

        def saves(i):
            to = pl.ds(pl.multiple_of(i * wtile, wtile), wtile)
            return [
                pltpu.make_async_copy(held, out.at[to], save_sem.at[a])
                for a, (held, out) in enumerate(((stage, both_out), (stage_d, dw_out)))
            ]

        def weights(i, _):
            after.quiet_tick(steps - behind + i)
            here = pl.ds(pl.multiple_of(i * wtile, wtile), wtile)

            @pl.when(i > 0)
            def _():
                for save in saves(i - 1):
                    save.wait()

            source, grad = normed[:, here], fg_ref[:, here]
            stage[:, :ffn] = inner_rows(source, gg_v[...]).astype(bf16)
            stage[:, ffn:] = inner_rows(source, ug_v[...]).astype(bf16)
            stage_d[...] = inner_rows(grad, hid_v[...]).astype(bf16)
            for save in saves(i):
                save.start()
            return 0

        lax.fori_loop(0, width // wtile, weights, 0)
        for c in range(steps - behind + width // wtile, after.ticks()):
            after.quiet_tick(c)
        for save in saves(width // wtile - 1) + [ffn_save, mid_save]:
            save.wait()
        fore.finish(False)
        after.finish()

    sds = jax.ShapeDtypeStruct
    wide, half = sds((rows, width), f32), sds((rows, width), bf16)
    both, down = sds((width, 2 * ffn), bf16), sds((width, ffn), bf16)
    return pl.pallas_call(
        kernel,
        out_shape=[half, wide, half, wide, sds((8, width), f32), both, down],
        in_specs=[HBM, VMEM, VMEM, VMEM, HBM, HBM, HBM],
        out_specs=[HBM, HBM, VMEM, VMEM, VMEM, HBM, HBM],
        scratch_shapes=[
            pltpu.VMEM((rows, width), bf16),
            pltpu.VMEM((rows, width), f32),
            pltpu.VMEM((rows, ffn), bf16),
            pltpu.VMEM((rows, ffn), bf16),
            pltpu.VMEM((rows, ffn), bf16),
            pltpu.VMEM((rows, width), bf16),
            pltpu.VMEM((block, width), f32),
            pltpu.VMEM((block, width), f32),
            pltpu.VMEM((width, ffn), bf16),
            pltpu.VMEM((width, ffn), bf16),
            pltpu.VMEM(down_parts.shape, bf16),
            pltpu.VMEM((wtile, 2 * ffn), bf16),
            pltpu.VMEM((wtile, ffn), bf16),
            pltpu.SemaphoreType.DMA((3,)),
            pltpu.SemaphoreType.DMA((5,)),
        ]
        + fore.scratch()
        + after.scratch(),
        compiler_params=pltpu.CompilerParams(
            collective_id=ident, has_side_effects=True, vmem_limit_bytes=62 << 20
        ),
    )(mixed_part, hidden, gain, ffn_grad, gate_w[0], gate_w[1], down_parts)


def scan_tail(through_b, through_decay, sums, decay_grad, scan_grad, step_pre, pre_act, act, padded, z_half, low_all, small, normed, in_w, scatters, ident,
              seqs, low_len, rank, states, taps):
    rows, inner = act.shape
    local = rows // seqs
    long = local + halo
    shards, pieces = lax.axis_size("shard"), lax.axis_size("ctx")
    places = shards * pieces
    lane = inner // places
    line = Line((low_len, rows), 80, plain_end, [], bf16)
    tiles = inner // tile_cols
    at = low_len + rank
    lines = -(-(at + states + taps + 3) // 8) * 8
    height = -(-(lines + 8) // 32) * 32
    over = 8
    width = normed.shape[1]
    dtile = width // 8
    share = Halving(scatters, 32, 1)
    n_sc, n_share = len(scatters), len(share.scratch())

    def kernel(*refs):
        n_in = 14 + n_sc
        main(*refs[:14], *refs[n_in : n_in + 4], refs[14:n_in], refs[n_in + 4 : n_in + 4 + n_sc],
             refs[n_in + 4 + n_sc : n_in + 4 + n_sc + n_share], *refs[n_in + 4 + n_sc + n_share :])

    def main(
        tb_ref, sd_ref, sums_ref, dec_ref, sg_ref, sp_ref, pre_ref, act_ref, ext_ref, zg_ref, low_ref, small_ref, n_ref, w_ref,
        iw_out, first_ref, gsum_ref, blocks_ref, full, shares, share_scratch,
        conv_ref, w_v, acc, stage, w_sem, stage_sem, low_out, low_t, step_g, low_acc, grads, pre_g, conv_f, edge, edge_out, edge_sem, *rest
    ):
        ctx = lax.axis_index("ctx")
        barrier = pltpu.get_barrier_semaphore()
        line.bind(rest[0], [], low_out, [], list(rest))
        share.bind(full, shares, share_scratch)
        w_load = pltpu.make_async_copy(w_ref, w_v, w_sem)
        w_load.start()
        met = share.greet(barrier)
        pl.semaphore_signal(barrier, inc=1, device_id={"ctx": lax.rem(ctx + 1, pieces)}, device_id_type=MESH)

        def flat(ref, j, first, count):
            parts = [ref[pl.ds(first * 8 + j * (tile_cols // 128) + h, count, stride=8), :] for h in range(tile_cols // 128)]
            return jnp.concatenate(parts, axis=1)

        def cols(j):
            return pl.ds(pl.multiple_of(j * tile_cols, tile_cols), tile_cols)

        low_acc[...] = jnp.zeros_like(low_acc)
        grads[...] = jnp.zeros_like(grads)
        low_t[...] = low_ref[0:rank, :].astype(bf16)

        def size_tile(j, _):
            here = cols(j)
            bias_grad = jnp.zeros((8, tile_cols), f32)
            skip_grad = jnp.zeros((8, tile_cols), f32)
            for k in range(rows // 64):
                to = slice(k * 64, (k + 1) * 64)
                act_block = act_ref[to, here].astype(f32)
                size_grad = act_block * flat(tb_ref, j, k * 64, 64) + flat(sd_ref, j, k * 64, 64) * (1.0 / log2e)
                value = (size_grad * jax.nn.sigmoid(sp_ref[to, here])).astype(bf16)
                step_g[to, here] = value
                wide = value.astype(f32)
                product = sg_ref[to, here] * act_block
                for h in range(8):
                    bias_grad = bias_grad + wide[h * 8 : h * 8 + 8]
                    skip_grad = skip_grad + product[h * 8 : h * 8 + 8]
            grads[at + states + taps + 1 : at + states + taps + 2, here] = jnp.sum(bias_grad, axis=0, keepdims=True)
            grads[at + states + taps + 2 : at + states + taps + 3, here] = jnp.sum(skip_grad, axis=0, keepdims=True)
            low_acc[...] = low_acc[...] + outer_cols(small_ref[low_len : low_len + rank, here], step_g[:, here])
            return 0

        lax.fori_loop(0, tiles, size_tile, 0)
        line.p[0:rank, :] = low_acc[...].astype(bf16)
        line.p[rank : rank + 2 * states, :] = sums_ref[...].astype(bf16)
        line.greet(barrier, 1 + met)
        line.start()
        share.start()

        def save(i):
            c, d = 1 - i // 8, i % 8
            return pltpu.make_async_copy(
                stage.at[i % 2], iw_out.at[pl.ds(d * dtile, dtile), pl.ds(c * inner, inner)], stage_sem.at[i % 2]
            )

        def weight_piece(i, right):
            c, here = 1 - i // 8, slice((i % 8) * dtile, (i % 8 + 1) * dtile)
            if i >= 2:
                save(i - 2).wait()
            stage[i % 2] = inner_rows(n_ref[:, here], right[...]).astype(bf16)
            save(i).start()
            value = outer_cols(right[...], w_v[c, here, :])
            if i < 8:
                acc[:, here] = value
            else:
                value = (acc[:, here] + value).astype(bf16)
                first_ref[:, here] = value
                product = value.astype(f32) * n_ref[:, here].astype(f32)
                gsum_ref[:, here] = jnp.sum(product.reshape(rows // 8, 8, dtile), axis=0)

        def step_tile(j, _):
            here = cols(j)
            grads[low_len:at, here] = jnp.dot(low_t[...], step_g[:, here], preferred_element_type=f32)
            return 0

        lax.fori_loop(0, tiles, step_tile, 0)
        grads[at : at + states, :] = dec_ref[...]
        w_load.wait()
        early = 8 // line.ticks()
        for c in range(line.ticks()):
            for i in range(early):
                weight_piece(c * early + i, zg_ref)
            line.tick(c)
            share.tick(c)
        for i in range(early * line.ticks(), 8):
            weight_piece(i, zg_ref)
        line.finish()

        def pre_tile(j, _):
            here = cols(j)
            grads[0:low_len, here] = jnp.dot(low_out[...], act_ref[:, here], preferred_element_type=f32)
            for seq in range(seqs):
                low = inner_rows(low_out[:, seq * local : (seq + 1) * local], small_ref[0:low_len, here])
                conv_f[seq * long : (seq + 1) * long, :] = ext_ref[seq * long : (seq + 1) * long, here].astype(f32)
                pre_g[seq * (local + over) : seq * (local + over) + local, here] = low
            skip = small_ref[at + states + 32 : at + states + 48, here].astype(f32)[0:1]
            bias_sum = jnp.zeros((8, tile_cols), f32)
            tap_sums = [jnp.zeros((8, tile_cols), f32) for _ in range(taps)]
            for seq in range(seqs):
                for k in range(local // 64):
                    to = slice(seq * local + k * 64, seq * local + (k + 1) * 64)
                    where = slice(seq * (local + over) + k * 64, seq * (local + over) + (k + 1) * 64)
                    act_grad = skip * sg_ref[to, here] + jax.nn.softplus(sp_ref[to, here]) * flat(tb_ref, j, seq * local + k * 64, 64)
                    value = (act_grad + pre_g[where, here]) * silu_grad(pre_ref[to, here])
                    pre_g[where, here] = value
                    first = seq * long + halo + k * 64 - taps + 1
                    products = [value * conv_f[first + tap : first + tap + 64, :] for tap in range(taps)]
                    for h in range(8):
                        bias_sum = bias_sum + value[h * 8 : h * 8 + 8]
                        for tap in range(taps):
                            tap_sums[tap] = tap_sums[tap] + products[tap][h * 8 : h * 8 + 8]
            for tap in range(taps):
                row = at + states + tap
                grads[row : row + 1, here] = jnp.sum(tap_sums[tap], axis=0, keepdims=True)
            row = at + states + taps
            grads[row : row + 1, here] = jnp.sum(bias_sum, axis=0, keepdims=True)
            return 0

        lax.fori_loop(0, tiles, pre_tile, 0)
        share.tick(line.ticks())
        for seq in range(seqs):
            edge_out[seq] = pre_g[seq * (local + over) : seq * (local + over) + over, :]
        copy = pltpu.make_async_remote_copy(
            edge_out, edge, edge_sem.at[0], edge_sem.at[1],
            device_id={"ctx": lax.rem(ctx + pieces - 1, pieces)}, device_id_type=MESH,
        )
        copy.start()
        for p in range(places):
            blocks_ref[p * height : p * height + lines, :] = grads[:, p * lane : (p + 1) * lane].astype(bf16)
            blocks_ref[p * height + lines : (p + 1) * height, :] = jnp.zeros((height - lines, lane), bf16)
        copy.wait()
        inside = (ctx < pieces - 1).astype(f32)
        for seq in range(seqs):
            first = seq * (local + over) + local
            pre_g[first : first + over, :] = edge[seq] * inside

        def conv_tile(j, _):
            here = cols(j)
            weights = small_ref[at + states : at + states + 16, here].astype(f32)
            for seq in range(seqs):
                for k in range(local // 64):
                    first = seq * (local + over) + k * 64 + taps - 1
                    total = weights[0:1] * pre_g[first : first + 64, here]
                    for tap in range(1, taps):
                        total = total + weights[tap : tap + 1] * pre_g[first - tap : first - tap + 64, here]
                    conv_ref[seq * local + k * 64 : seq * local + (k + 1) * 64, here] = total.astype(bf16)
            return 0

        lax.fori_loop(0, tiles, conv_tile, 0)
        for i in range(8, 16):
            if line.ticks() + i - 7 < share.turns:
                share.tick(line.ticks() + i - 7)
            weight_piece(i, conv_ref)
        for i in range(line.ticks() + 9, share.turns):
            share.tick(i)
        save(14).wait()
        save(15).wait()
        share.finish()

    return pl.pallas_call(
        kernel,
        out_shape=[
            jax.ShapeDtypeStruct((width, 2 * inner), bf16),
            jax.ShapeDtypeStruct((rows, width), bf16),
            jax.ShapeDtypeStruct((8, width), f32),
            jax.ShapeDtypeStruct((places * height, lane), bf16),
        ]
        + share.results(),
        in_specs=[VMEM] * 13 + [HBM] * (1 + n_sc),
        out_specs=[HBM] + [VMEM] * (3 + n_sc),
        scratch_shapes=share.scratch()
        + [
            pltpu.VMEM((rows, inner), bf16),
            pltpu.VMEM(in_w.shape, bf16),
            pltpu.VMEM((rows, width), f32),
            pltpu.VMEM((2, dtile, inner), bf16),
            pltpu.SemaphoreType.DMA,
            pltpu.SemaphoreType.DMA((2,)),
            pltpu.VMEM((low_len, rows), bf16),
            pltpu.VMEM((rank, rows), bf16),
            pltpu.VMEM((rows, inner), bf16),
            pltpu.VMEM((rank, rows), f32),
            pltpu.VMEM((lines, inner), f32),
            pltpu.VMEM((seqs * (local + over), inner), f32),
            pltpu.VMEM((seqs * long, tile_cols), f32),
            pltpu.VMEM((seqs, over, inner), f32),
            pltpu.VMEM((seqs, over, inner), f32),
            pltpu.SemaphoreType.DMA((2,)),
        ]
        + line.scratch(),
        compiler_params=pltpu.CompilerParams(
            collective_id=ident, has_side_effects=True, vmem_limit_bytes=60 << 20
        ),
    )(through_b, through_decay, sums, decay_grad, scan_grad, step_pre, pre_act, act, padded, z_half, low_all, small, normed, in_w, *share.folded), height


def body(
    hidden_in, lengths, cotangent, norm_gain, in_weight, conv_weight, conv_bias, low_weight, step_weight,
    step_bias, decay_log, skip_gain, out_weight, ffn_gain, gate_up, down_weight,
):
    seqs, local, width = hidden_in.shape
    rows = seqs * local
    shards, pieces = lax.axis_size("shard"), lax.axis_size("ctx")
    inner = in_weight.shape[2]
    taps = conv_weight.shape[0]
    rank = step_weight.shape[0]
    states = decay_log.shape[0]
    low_len = low_weight.shape[0]

    def rows16(v):
        return jnp.pad(v, ((0, 16 - v.shape[0]), (0, 0)))

    small = jnp.concatenate(
        [low_weight, step_weight, decay_log, rows16(jnp.concatenate([conv_weight, conv_bias[None]], axis=0)),
         rows16(step_bias[None]), rows16(skip_gain[None])], axis=0,
    )
    at_bias = low_len + rank + states + 16
    at_skip = at_bias + 16
    hidden_rows = hidden_in.reshape(rows, width)
    small = jnp.pad(small, ((0, -small.shape[0] % 16), (0, 0)))
    gains = jnp.stack([norm_gain, ffn_gain])
    gains = jnp.pad(gains, ((0, 14), (0, 0)))
    in_half = in_weight.transpose(1, 0, 2)
    in_w, small, gains, normed_one, gate_z, padded, pre_act, act_half, low_all = front(
        hidden_rows, in_half, small, gains, seqs, low_len + rank + states, taps, low_len, 0
    )
    out_parts = lax.all_gather(out_weight, "shard")
    gate_half = gate_up.transpose(1, 0, 2)
    gate_w = [lax.all_gather(gate_half[c], "shard", axis=0, tiled=True) for c in range(2)]
    down_parts = lax.all_gather(down_weight, "shard")
    part = width // shards

    low_w = small[:low_len]
    step_w = small[low_len : low_len + rank]
    at = low_len + rank
    decay_w = small[at : at + states].astype(f32)
    kernel = small[at + states : at + states + taps].astype(f32)
    skip_full = small[at_skip].astype(f32)
    gain_one, gain_two = gains[0:1].astype(f32), gains[1:2].astype(f32)

    first_slot = lax.axis_index("ctx") * local
    positions = first_slot + jnp.arange(local, dtype=jnp.int32)
    pad_mask = (positions[None, :] < lengths[:, None]).astype(f32)

    source = hidden_rows.astype(f32)
    act_full = act_half.astype(f32)
    step_low = low_all[:rank].astype(bf16)
    decay_rate = -jnp.exp(decay_w)
    rate = (decay_rate * log2e).reshape(states, 8, 128)
    scan_out, gated_out, mixed_part, step_pre, kept, enter, size3, drive3 = scan_forward(
        low_all, act_half, gate_z, small, rate, out_parts, seqs, rank, low_len, at_bias, at_skip, 2
    )
    step_size = jax.nn.softplus(step_pre)
    gate_act = jax.nn.silu(gate_z)
    upstream = cotangent.reshape(rows, width).astype(f32) * pad_mask.reshape(rows, 1)
    ffn_grad = upstream.astype(bf16)
    ffn_part, middle, mix_grad, middle_grad, gain_sum, both_grad, down_grad = feed_forward(
        mixed_part, hidden_rows, gain_two, ffn_grad, gate_w, down_parts, 3
    )
    ffn_gain_grad = jnp.sum(gain_sum, axis=0) / gain_two[0]

    out_weight_grad = inner_rows(mix_grad, gated_out).astype(bf16)
    gated_grad = sum(outer_cols(mix_grad[:, k * part : (k + 1) * part], out_parts[k]) for k in range(shards))
    scan_grad = gated_grad * gate_act
    z_grad = gated_grad * scan_out * silu_grad(gate_z)
    through_b, through_decay, b_sums, c_sums, decay_sum, mixed_out, *ffn_shares = scan_backward(
        size3, drive3, scan_grad, low_all, rank, rate, kept, enter, seqs, 6, ffn_part, add_end, [middle], 32,
        [both_grad, down_grad],
    )
    mixed_out = mixed_out.reshape(hidden_in.shape)
    decay_log_grad = decay_sum.reshape(states, inner) * decay_rate
    sums = jnp.concatenate([v[:, 0].reshape(rows, states).T for v in (b_sums, c_sums)], axis=0)
    z_half = z_grad.astype(bf16)
    (in_weight_grad, first_part, gain_one_sum, small_blocks), small_height = scan_tail(
        through_b, through_decay, sums, decay_log_grad, scan_grad, step_pre, pre_act, act_half, padded, z_half, low_all, small, normed_one, in_w,
        [], 7,
        seqs, low_len, rank, states, taps,
    )
    norm_gain_grad = jnp.sum(gain_one_sum, axis=0) / gain_one[0]
    places, share = shards * pieces, width // (shards * pieces)
    lane = inner // places
    gain_rows = -(-2 * share // lane)
    gain_blocks = jnp.concatenate([norm_gain_grad.reshape(places, share), ffn_gain_grad.reshape(places, share)], axis=1)
    gain_blocks = jnp.pad(gain_blocks, ((0, 0), (0, gain_rows * lane - 2 * share))).reshape(places, gain_rows, lane)
    gain_height = 16 * -(-gain_rows // 16)
    gain_blocks = jnp.pad(gain_blocks, ((0, 0), (gain_height - gain_rows, 0), (0, 0)))
    gain_blocks = gain_blocks.reshape(places * gain_height, lane).astype(bf16)
    input_grad, in_share, out_share, small_out, gain_share = tp_sum(
        first_part, norm_back_end, [hidden_rows, gain_one, middle_grad], [], 32, 8,
        scatters=[in_weight_grad, out_weight_grad, small_blocks, gain_blocks], line_too=True,
        steps=[16, 16, small_height // 2, gain_height],
    )
    gain_share = gain_share[gain_height - gain_rows :].reshape(-1)
    input_grad = input_grad.astype(f32).reshape(hidden_in.shape)
    at = low_len + rank
    return (
        mixed_out,
        input_grad,
        gain_share[:share],
        in_share.reshape((-1,) + in_weight.shape[1:]),
        small_out[at + states : at + states + taps],
        small_out[at + states + taps],
        small_out[:low_len],
        small_out[low_len : low_len + rank],
        small_out[at + states + taps + 1],
        small_out[at : at + states],
        small_out[at + states + taps + 2],
        out_share.T,
        gain_share[share : 2 * share],
        ffn_shares[0].reshape((-1,) + gate_up.shape[1:]),
        ffn_shares[1].T,
    )


def solution(mesh):
    placed = (
        P("shard", "ctx", None),
        P("shard"),
        P("shard", "ctx", None),
        P("shard"),
        P("shard", None, "tp"),
        P(None, ("tp", "shard")),
        P(("tp", "shard")),
        P(None, ("tp", "shard")),
        P(None, ("tp", "shard")),
        P(("tp", "shard")),
        P(None, ("tp", "shard")),
        P(("tp", "shard")),
        P("tp", "shard"),
        P("shard"),
        P("shard", None, "tp"),
        P("tp", "shard"),
    )
    return jax.shard_map(
        body,
        mesh=mesh,
        in_specs=placed,
        out_specs=(
            P("shard", "ctx", None),
            P("shard", "ctx", None),
            P(("shard", "ctx")),
            P(("shard", "ctx"), None, "tp"),
            P(None, ("tp", "shard", "ctx")),
            P(("tp", "shard", "ctx")),
            P(None, ("tp", "shard", "ctx")),
            P(None, ("tp", "shard", "ctx")),
            P(("tp", "shard", "ctx")),
            P(None, ("tp", "shard", "ctx")),
            P(("tp", "shard", "ctx")),
            P("tp", ("shard", "ctx")),
            P(("shard", "ctx")),
            P(("shard", "ctx"), None, "tp"),
            P("tp", ("shard", "ctx")),
        ),
        check_vma=False,
    )
```

```python
import functools

import jax
import jax.numpy as jnp
from jax import lax
from jax.experimental import pallas as pl
from jax.experimental.pallas import tpu as pltpu
from jax.sharding import PartitionSpec as P

MESH = pl.DeviceIdType.MESH
epsilon = 1e-05
log2e = 1.4426950408889634
bf16 = jnp.bfloat16
f32 = jnp.float32
VMEM = pl.BlockSpec(memory_space=pltpu.VMEM)
HBM = pl.BlockSpec(memory_space=pl.ANY)


def inner_rows(left, right):
    return lax.dot_general(left, right, (((0,), (0,)), ((), ())), preferred_element_type=f32)


def outer_cols(left, right):
    return lax.dot_general(left, right, (((1,), (1,)), ((), ())), preferred_element_type=f32)


def silu_grad(values):
    sig_val = jax.nn.sigmoid(values)
    return sig_val * (1.0 + values * (1.0 - sig_val))


def rms_scale(source):
    return lax.rsqrt(jnp.mean(source * source, axis=-1, keepdims=True) + epsilon)


class Line:
    lag = 2
    ahead = 4

    def __init__(self, shape, chunk, epilogue, extras, out_dtype):
        self.shape, self.chunk, self.epilogue, self.out_dtype = shape, chunk, epilogue, out_dtype
        self.count = shape[0] // chunk
        self.extras = [(e.shape, e.dtype) for e in extras]

    def scratch(self):
        return (
            [pltpu.VMEM(self.shape, bf16)] * 4
            + [pltpu.SemaphoreType.DMA((self.count,))] * 6
            + [pltpu.VMEM(shape, dtype) for shape, dtype in self.extras]
            + [pltpu.SemaphoreType.DMA((1 + len(self.extras),))]
        )

    def bind(self, p_ref, ins, out_ref, outs, scratch):
        self.p_ref, self.given, self.out_ref, self.outs = p_ref, ins, out_ref, outs
        (self.p, self.got_a, self.pair, self.got_b, self.a_send, self.a_recv, self.b_send, self.b_recv,
         self.c_send, self.c_recv) = scratch[:10]
        self.ins, self.in_sem = scratch[10:-1], scratch[-1]
        me = lax.axis_index("tp")
        self.mate = me + 1 - 2 * (me % 2)
        self.across = 3 - me
        self.middle = jnp.logical_or(me == 1, me == 2)

    def at(self, c):
        return pl.ds(pl.multiple_of(c * self.chunk, self.chunk), self.chunk)

    def remote(self, source, target, send, recv, c, to):
        return pltpu.make_async_remote_copy(
            source.at[self.at(c)], target.at[self.at(c)], send.at[c], recv.at[c], device_id={"tp": to}, device_id_type=MESH
        )

    def copy_a(self, c):
        return self.remote(self.p_ref, self.got_a, self.a_send, self.a_recv, c, self.mate)

    def copy_b(self, c):
        return self.remote(self.pair, self.got_b, self.b_send, self.b_recv, c, self.across)

    def copy_c(self, c):
        return self.remote(self.out_ref, self.out_ref, self.c_send, self.c_recv, c, self.mate)

    def loads(self):
        pairs = [(self.p_ref, self.p)] + list(zip(self.given, self.ins))
        return [pltpu.make_async_copy(a, b, self.in_sem.at[i]) for i, (a, b) in enumerate(pairs)]

    def begin(self, barrier, met, ends_meet=False):
        pl.semaphore_signal(barrier, inc=1, device_id={"tp": self.mate}, device_id_type=MESH)

        @pl.when(self.middle)
        def _():
            pl.semaphore_signal(barrier, inc=1, device_id={"tp": self.across}, device_id_type=MESH)
            for load in self.loads():
                load.start()
            pl.semaphore_wait(barrier, met + 2)
            for load in self.loads():
                load.wait()

        @pl.when(jnp.logical_not(self.middle))
        def _():
            if ends_meet:
                pl.semaphore_signal(barrier, inc=1, device_id={"tp": self.across}, device_id_type=MESH)
            pl.semaphore_wait(barrier, met + 2 if ends_meet else met + 1)

            for c in range(min(self.ahead, self.count)):
                self.copy_a(c).start()

    def greet(self, barrier, met):
        pl.semaphore_signal(barrier, inc=1, device_id={"tp": self.mate}, device_id_type=MESH)

        @pl.when(self.middle)
        def _():
            pl.semaphore_signal(barrier, inc=1, device_id={"tp": self.across}, device_id_type=MESH)
            pl.semaphore_wait(barrier, met + 2)

        @pl.when(jnp.logical_not(self.middle))
        def _():
            pl.semaphore_wait(barrier, met + 1)

    def start(self):
        @pl.when(jnp.logical_not(self.middle))
        def _():
            for c in range(min(self.ahead, self.count)):
                self.copy_a(c).start()

    def first(self, c):
        at = self.at(c)
        self.copy_a(c).wait_recv()
        self.pair[at, :] = self.p[at, :] + self.got_a[at, :]
        self.copy_b(c).start()

    def second(self, c):
        at = self.at(c)
        self.copy_b(c).wait_recv()
        total = self.pair[at, :].astype(f32) + self.got_b[at, :].astype(f32)
        self.epilogue(c, at, total, self.ins, self.out_ref, self.outs)
        self.copy_c(c).start()

    def tick(self, c):
        lag = min(self.lag, self.count)

        @pl.when(jnp.logical_and(self.middle, c < self.count))
        def _():
            self.first(c)

        @pl.when(jnp.logical_and(self.middle, jnp.logical_and(c >= lag, c < self.count + lag)))
        def _():
            self.second(c - lag)

        @pl.when(jnp.logical_and(jnp.logical_not(self.middle), c + self.ahead < self.count))
        def _():
            self.copy_a(c + self.ahead).start()

    def quiet_tick(self, c):
        lag = min(self.lag, self.count)

        @pl.when(jnp.logical_and(self.middle, jnp.logical_and(c >= 0, c < self.count)))
        def _():
            self.first(c)

        @pl.when(jnp.logical_and(self.middle, jnp.logical_and(c >= lag, c < self.count + lag)))
        def _():
            self.second(c - lag)

    def ticks(self):
        return self.count + min(self.lag, self.count)

    def finish(self, take_result=True):
        @pl.when(self.middle)
        def _():
            def drain(c, _):
                self.copy_b(c).wait_send()
                self.copy_c(c).wait_send()
                return 0

            lax.fori_loop(0, self.count, drain, 0)

        @pl.when(jnp.logical_not(self.middle))
        def _():
            def take(c, _):
                if take_result:
                    self.copy_c(c).wait_recv()
                self.copy_a(c).wait_send()
                return 0

            lax.fori_loop(0, self.count, take, 0)


share_lag = 2
share_ahead = 2


class Halving:
    def __init__(self, arrays, step_rows=16, lag=share_lag):
        self.lag = lag
        steps = [step_rows] * len(arrays) if isinstance(step_rows, int) else list(step_rows)
        self.steps = steps
        shards, pieces = lax.axis_size("shard"), lax.axis_size("ctx")
        self.n = len(arrays)
        self.bits = [
            (axis, 1 << k)
            for axis, size in (("shard", shards), ("ctx", pieces))
            for k in reversed(range(size.bit_length() - 1))
        ]
        self.depth = len(self.bits)
        head = shards.bit_length() - 1
        self.dims = list(range(self.depth))
        self.orders = (self.dims, self.dims[:head] + self.dims[head:][::-1])
        self.parts = [g.shape[0] // (shards * pieces) // k for g, k in zip(arrays, steps)]
        self.folded = [
            g.reshape((2,) * self.depth + (p * k, g.shape[1])) for g, p, k in zip(arrays, self.parts, steps)
        ]
        self.tails = [g.shape[self.depth :] for g in self.folded]
        self.pairs = (max(self.parts, default=0) + 1) // 2
        self.turns = self.pairs + lag * (self.depth - 1)

    def results(self):
        return [jax.ShapeDtypeStruct(tail, f32) for tail in self.tails]

    def scratch(self):
        if not self.n:
            return []
        held = [pltpu.VMEM((2,) * (self.depth - 1) + tail, bf16) for tail in self.tails]
        for j in range(self.depth):
            held += [pltpu.VMEM((2,) * (self.depth - 1 - j) + tail, bf16) for tail in self.tails]
        sem = pltpu.SemaphoreType.DMA((self.depth, self.n, max(self.parts)))
        return held + [sem, sem, pltpu.SemaphoreType.DMA((self.n, max(self.parts)))]

    def bind(self, full, shares, scratch):
        n = self.n
        self.partner, self.mine = [], []
        if not n:
            return
        self.full, self.shares, self.own = full, shares, scratch[:n]
        self.landed = [scratch[n * (j + 1) : n * (j + 2)] for j in range(self.depth)]
        self.send, self.recv, self.own_sem = scratch[n * (self.depth + 1) :]
        for axis, bit in self.bits:
            here = lax.axis_index(axis)
            self.mine.append((here // bit) % 2)
            self.partner.append({axis: here + bit - 2 * bit * ((here // bit) % 2)})

    def greet(self, barrier):
        for who in self.partner:
            pl.semaphore_signal(barrier, inc=1, device_id=who, device_id_type=MESH)
        return len(self.partner)

    def spot(self, a, c):
        return pl.ds(pl.multiple_of(c * self.steps[a], self.steps[a]), self.steps[a])

    def pick(self, remaining, dim, index, a, c):
        return tuple(index if d == dim else slice(None) for d in remaining) + (self.spot(a, c), slice(None))

    def rest(self, order, j):
        return [d for d in self.dims if d not in order[:j]]

    def copy(self, j, a, c, order):
        source = self.full[a] if j == 0 else self.landed[j - 1][a]
        d = order[j]
        return pltpu.make_async_remote_copy(
            source.at[self.pick(self.rest(order, j), d, 1 - self.mine[d], a, c)],
            self.landed[j][a].at[self.pick(self.rest(order, j + 1), None, None, a, c)],
            self.send.at[j, a, c],
            self.recv.at[j, a, c],
            device_id=self.partner[d],
            device_id_type=MESH,
        )

    def own_copy(self, a, c, order):
        return pltpu.make_async_copy(
            self.full[a].at[self.pick(self.dims, order[0], self.mine[order[0]], a, c)],
            self.own[a].at[self.pick(self.rest(order, 1), None, None, a, c)],
            self.own_sem.at[a, c],
        )

    def begin(self, a, c, order):
        self.copy(0, a, c, order).start()
        self.own_copy(a, c, order).start()

    def step(self, j, a, c, order):
        self.copy(j, a, c, order).wait_recv()
        where = self.pick(self.rest(order, j + 1), None, None, a, c)
        d = order[j]
        if j == 0:
            self.own_copy(a, c, order).wait()
            kept = self.own[a][where]
        else:
            kept = self.landed[j - 1][a][self.pick(self.rest(order, j), d, self.mine[d], a, c)]
        if j == self.depth - 1:
            self.shares[a][self.spot(a, c), :] = kept.astype(f32) + self.landed[j][a][where].astype(f32)
        else:
            self.landed[j][a][where] = kept + self.landed[j][a][where]
            self.copy(j + 1, a, c, order).start()

    def each(self, i, fn):
        for parity in (0, 1):
            c = 2 * i + parity
            for a in range(self.n):

                @pl.when(jnp.logical_and(c >= 0, c < self.parts[a]))
                def _():
                    fn(a, c, self.orders[parity])

    def start(self):
        for i in range(share_ahead if self.n else 0):
            self.each(i, self.begin)

    def tick(self, i):
        if self.n:
            self.each(i + share_ahead, self.begin)
            for j in range(self.depth):
                self.each(i - self.lag * j, functools.partial(self.step, j))

    def finish(self):
        def sent(i, _):
            for j in range(self.depth):
                self.each(i, lambda a, c, order: self.copy(j, a, c, order).wait_send())
            return 0

        if self.n:
            lax.fori_loop(0, self.pairs, sent, 0)


def tp_sum(partial, epilogue, extras, extra_outs, chunk, ident, out_dtype=bf16, scatters=(), line_too=False, steps=16):
    line = Line(partial.shape, chunk, epilogue, extras, out_dtype)
    share = Halving(scatters, steps)
    n_ex, n_out, n_sc = len(extras), len(extra_outs), len(scatters)
    n_line, n_share = len(line.scratch()), len(share.scratch())

    def kernel(*refs):
        refs = list(refs)

        def take_refs(n):
            taken = refs[:n]
            del refs[:n]
            return taken

        (p_ref,) = take_refs(1)
        ins = take_refs(n_ex)
        full = take_refs(n_sc)
        (out_ref,) = take_refs(1)
        outs = take_refs(n_out)
        shares = take_refs(n_sc)
        line.bind(p_ref, ins, out_ref, outs, take_refs(n_line))
        share.bind(full, shares, take_refs(n_share))
        tail, tail_send, tail_recv = take_refs(3) if line_too else (None, None, None)
        barrier = pltpu.get_barrier_semaphore()
        line.begin(barrier, share.greet(barrier), line_too)
        share.start()

        def tail_copy(k):
            to = (line.mate, line.across)[k]
            source = shares[-1].at[pl.ds(shares[-1].shape[0] - 8, 8)] if k == 0 else tail.at[2]
            return pltpu.make_async_remote_copy(
                source, tail.at[k], tail_send.at[k], tail_recv.at[k], device_id={"tp": to}, device_id_type=MESH
            )

        def tail_step(k):
            last = pl.ds(shares[-1].shape[0] - 8, 8)
            if k > 0:
                tail_copy(k - 1).wait()
            if k == 1:
                tail[2] = shares[-1][last, :] + tail[0]
            if k == 2:
                shares[-1][last, :] = tail[2] + tail[1]
            else:
                tail_copy(k).start()

        ready = (share.parts[-1] + 1) // 2 + share.lag * (share.depth - 1) if n_sc else 0

        def turn(i, _):
            for parity in (0, 1):
                line.tick(2 * i + parity)
            share.tick(i)
            for k in range(3 if line_too else 0):

                @pl.when(i == ready + k)
                def _():
                    tail_step(k)

            return 0

        turns = max((line.ticks() + 1) // 2, share.turns if n_sc else 0, ready + 3 if line_too else 0)
        lax.fori_loop(0, turns, turn, 0)
        line.finish()
        share.finish()

    buffers = []
    if line_too:
        pair_sem = pltpu.SemaphoreType.DMA((2,))
        buffers += [pltpu.VMEM((3, 8, scatters[-1].shape[-1]), f32), pair_sem, pair_sem]
    return pl.pallas_call(
        kernel,
        out_shape=[jax.ShapeDtypeStruct(partial.shape, out_dtype)] + list(extra_outs) + share.results(),
        in_specs=[HBM] * (1 + n_ex + n_sc),
        out_specs=[VMEM] * (1 + n_out + n_sc),
        scratch_shapes=line.scratch() + share.scratch() + buffers,
        compiler_params=pltpu.CompilerParams(
            collective_id=ident, has_side_effects=True, vmem_limit_bytes=56 << 20
        ),
    )(partial, *extras, *share.folded)


def plain_end(c, rows, total, ins, out_ref, outs):
    out_ref[rows, :] = total.astype(out_ref.dtype)


def norm_end(c, rows, total, ins, out_ref, outs):
    source_ref, gain_ref = ins
    middle = source_ref[rows, :].astype(f32) + total
    outs[0][rows, :] = middle
    out_ref[rows, :] = (middle * rms_scale(middle) * gain_ref[...]).astype(bf16)


def add_end(c, rows, total, ins, out_ref, outs):
    out_ref[rows, :] = (ins[0][rows, :] + total).astype(bf16)


def norm_back_end(c, rows, total, ins, out_ref, outs):
    source = ins[0][rows, :].astype(f32)
    inv = rms_scale(source)
    weighted = total * ins[1][...]
    back = inv * weighted - source * (inv * inv * inv) * jnp.mean(weighted * source, axis=-1, keepdims=True)
    result = ins[2][rows, :] + back
    if outs:
        outs[0][rows, :] = result
    out_ref[rows, :] = result.astype(bf16)


halo = 16
tile_cols = 256


def front(hidden, in_half, small, gains, seqs, at_conv, taps, low_len, ident):
    rows, width = hidden.shape
    local = rows // seqs
    part, inner = in_half.shape[1:]
    shards, pieces = lax.axis_size("shard"), lax.axis_size("ctx")
    long = local + halo
    tiles = inner // tile_cols
    line = Line((low_len, rows), 80, plain_end, [], f32)
    n_line = len(line.scratch())

    def kernel(
        hid_ref, tail_ref, in_ref, small_ref, gain_ref,
        in_out, small_out, gain_out, normed_out, z_out, ext_out, pre_out, act_out, low_out,
        own_w, got_w, edge, normed, ext_n, acc, z_val, conv_f, ext_c, pre, act, low_acc, small_all, gain_all,
        send, recv, edge_sem, own_sem, out_sem, *rest
    ):
        me, ctx = lax.axis_index("shard"), lax.axis_index("ctx")
        barrier = pltpu.get_barrier_semaphore()
        line.bind(rest[0], [], low_out, [], list(rest))
        for step in range(1, shards):
            pl.semaphore_signal(barrier, inc=1, device_id={"shard": lax.rem(me + step, shards)}, device_id_type=MESH)
        pl.semaphore_signal(barrier, inc=1, device_id={"ctx": lax.rem(ctx + pieces - 1, pieces)}, device_id_type=MESH)
        load = pltpu.make_async_copy(in_ref, own_w, own_sem.at[0])
        load.start()
        small_size, gain_size = small_ref.shape[1], gain_ref.shape[1]
        small_at = pl.ds(pl.multiple_of(me * small_size, small_size), small_size)
        gain_at = pl.ds(pl.multiple_of(me * gain_size, gain_size), gain_size)
        small_all[:, small_at] = small_ref[...]
        gain_all[:, gain_at] = gain_ref[...]
        line.greet(barrier, shards)
        edge_copy = pltpu.make_async_remote_copy(
            tail_ref, edge, edge_sem.at[0], edge_sem.at[1],
            device_id={"ctx": lax.rem(ctx + 1, pieces)}, device_id_type=MESH,
        )
        copies = {}
        for step in range(1, shards):
            peer = {"shard": lax.rem(me + step, shards)}
            moves = [(gain_ref, gain_all.at[:, gain_at]), (small_ref, small_all.at[:, small_at])]
            moves += [(in_ref.at[c], got_w.at[step - 1, c]) for c in range(2)]
            for k, (source, target) in enumerate(moves):
                copies[step, k] = pltpu.make_async_remote_copy(
                    source, target, send.at[step, k], recv.at[step, k], device_id=peer, device_id_type=MESH
                )
        for k in range(4):
            for step in range(1, shards):
                copies[step, k].start()
            if k == 0:
                edge_copy.start()
        for step in range(1, shards):
            copies[step, 0].wait_recv()
        gain = gain_all[0:1, :].astype(f32)

        def norm_rows(i, _):
            at = pl.ds(pl.multiple_of(i * 16, 16), 16)
            source = hid_ref[at, :].astype(f32)
            value = (source * rms_scale(source) * gain).astype(bf16)
            normed[at, :] = value
            seq = i // (local // 16)
            ext_n[pl.ds(pl.multiple_of(i * 16 + (seq + 1) * halo, 16), 16), :] = value
            return 0

        lax.fori_loop(0, rows // 16, norm_rows, 0)
        edge_copy.wait_recv()
        for seq in range(seqs):
            source = edge[seq].astype(f32)
            value = source * rms_scale(source) * gain * (ctx > 0).astype(f32)
            ext_n[seq * long : seq * long + halo, :] = value.astype(bf16)
        outs = [(normed, normed_out)]
        pltpu.make_async_copy(normed, normed_out, out_sem.at[0]).start()

        def cols(c, j):
            return pl.ds(pl.multiple_of(c * inner + j * tile_cols, tile_cols), tile_cols)

        def finish_conv(j):
            here = pl.ds(pl.multiple_of(j * tile_cols, tile_cols), tile_cols)
            value = acc[:, cols(0, j)].astype(bf16)
            ext_c[:, here] = value
            conv_f[...] = value.astype(f32)
            weights = small_all[at_conv : at_conv + 16, here].astype(f32)
            for seq in range(seqs):
                for k in range(local // 64):
                    first = seq * long + halo + k * 64
                    total = weights[taps : taps + 1]
                    for tap in range(taps):
                        total = total + weights[tap : tap + 1] * conv_f[first - taps + 1 + tap : first - taps + 1 + tap + 64, :]
                    to = slice(seq * local + k * 64, seq * local + (k + 1) * 64)
                    pre[to, here] = total
                    act[to, here] = jax.nn.silu(total).astype(bf16)
            low = outer_cols(small_all[0:low_len, here], act[:, here])
            low_acc[...] = low_acc[...] + low

        def finish_gate(j):
            here = pl.ds(pl.multiple_of(j * tile_cols, tile_cols), tile_cols)
            for seq in range(seqs):
                z_val[seq * local : (seq + 1) * local, here] = acc[seq * long + halo : (seq + 1) * long, cols(1, j)]

        low_acc[...] = jnp.zeros_like(low_acc)
        own_place = pl.ds(pl.multiple_of(me * part, part), part)
        load.wait()
        own_save = pltpu.make_async_copy(own_w, in_out.at[:, own_place], own_sem.at[1])
        own_save.start()
        saves = []
        for step in range(shards):
            owner = lax.rem(me - step + shards, shards)
            place = pl.ds(pl.multiple_of(owner * part, part), part)
            last = step == shards - 1
            if last:
                for other in range(1, shards):
                    copies[other, 1].wait_recv()
            for c in range(2):
                weight = own_w.at[c] if step == 0 else got_w.at[step - 1, c]
                if step > 0:
                    copies[step, 2 + c].wait_recv()

                def matmul(j, _):
                    here = pl.ds(pl.multiple_of(j * tile_cols, tile_cols), tile_cols)
                    value = jnp.dot(ext_n[:, place], weight[:, here], preferred_element_type=f32)
                    acc[:, cols(c, j)] = value if step == 0 else acc[:, cols(c, j)] + value
                    if last:
                        (finish_conv, finish_gate)[c](j)
                    return 0

                lax.fori_loop(0, tiles, matmul, 0)
            if step > 0:
                saves.append(pltpu.make_async_copy(got_w.at[step - 1], in_out.at[:, place], own_sem.at[1 + step]))
                saves[-1].start()
        line.p[...] = low_acc[...].astype(bf16)
        outs += [(z_val, z_out), (ext_c, ext_out), (pre, pre_out), (act, act_out), (small_all, small_out), (gain_all, gain_out)]
        for k, (source, target) in enumerate(outs):
            if k:
                pltpu.make_async_copy(source, target, out_sem.at[k]).start()
        line.start()
        for c in range(line.ticks()):
            line.tick(c)
        line.finish()
        for save in saves + [own_save]:
            save.wait()
        for k, (source, target) in enumerate(outs):
            pltpu.make_async_copy(source, target, out_sem.at[k]).wait()
        for copy in copies.values():
            copy.wait_send()
        edge_copy.wait_send()

    sds = jax.ShapeDtypeStruct
    tails = hidden.reshape(seqs, local, width)[:, local - halo :]
    return pl.pallas_call(
        kernel,
        out_shape=[
            sds((2, shards * part, inner), bf16),
            sds((small.shape[0], small.shape[1] * shards), bf16),
            sds((gains.shape[0], gains.shape[1] * shards), bf16),
            sds((rows, width), bf16),
            sds((rows, inner), f32),
            sds((seqs * long, inner), bf16),
            sds((rows, inner), f32),
            sds((rows, inner), bf16),
            sds((low_len, rows), f32),
        ],
        in_specs=[VMEM, HBM, HBM, VMEM, VMEM],
        out_specs=[HBM] * 8 + [VMEM],
        scratch_shapes=[
            pltpu.VMEM((2, part, inner), bf16),
            pltpu.VMEM((max(shards - 1, 1), 2, part, inner), bf16),
            pltpu.VMEM((seqs, halo, width), bf16),
            pltpu.VMEM((rows, width), bf16),
            pltpu.VMEM((seqs * long, width), bf16),
            pltpu.VMEM((seqs * long, 2 * inner), f32),
            pltpu.VMEM((rows, inner), f32),
            pltpu.VMEM((seqs * long, tile_cols), f32),
            pltpu.VMEM((seqs * long, inner), bf16),
            pltpu.VMEM((rows, inner), f32),
            pltpu.VMEM((rows, inner), bf16),
            pltpu.VMEM((low_len, rows), f32),
            pltpu.VMEM((small.shape[0], small.shape[1] * shards), bf16),
            pltpu.VMEM((gains.shape[0], gains.shape[1] * shards), bf16),
            pltpu.SemaphoreType.DMA((shards, 4)),
            pltpu.SemaphoreType.DMA((shards, 4)),
            pltpu.SemaphoreType.DMA((2,)),
            pltpu.SemaphoreType.DMA((shards + 1,)),
            pltpu.SemaphoreType.DMA((7,)),
        ]
        + line.scratch(),
        compiler_params=pltpu.CompilerParams(
            collective_id=ident, has_side_effects=True, vmem_limit_bytes=56 << 20
        ),
    )(hidden, tails, in_half, small, gains)


piece = 16
slots_held = 4
unroll = 4


def spread(flat_ref, natural, first):
    for j in range(8):
        flat_ref[pl.ds(first * 8 + j, 8, stride=8), :] = natural[:, j * 128 : (j + 1) * 128]


def unspread(flat_ref, first):
    return jnp.concatenate([flat_ref[pl.ds(first * 8 + j, 8, stride=8), :] for j in range(8)], axis=1)


def tile(ref, t):
    return ref[pl.ds(pl.multiple_of(t * 8, 8), 8), :]


def row(ref, t, n, states):
    return ref[pl.ds(t * states + n, 8, stride=0), :]


def exchange(ends, got, send, recv, seq, width):
    me = lax.axis_index("ctx")
    copies = []
    for step in range(1, width):
        copies.append(
            pltpu.make_async_remote_copy(
                ends.at[seq],
                got.at[me, seq],
                send.at[seq, step],
                recv.at[seq, step],
                device_id={"ctx": lax.rem(me + step, width)},
                device_id_type=MESH,
            )
        )
        copies[-1].start()
    return copies


def ctx_greet(width):
    me = lax.axis_index("ctx")
    barrier = pltpu.get_barrier_semaphore()
    for step in range(1, width):
        pl.semaphore_signal(barrier, inc=1, device_id={"ctx": lax.rem(me + step, width)}, device_id_type=MESH)
    return barrier


def entering(got, seq, rate_ref, states, width, reverse):
    me = lax.axis_index("ctx")
    result = []
    for n in range(states):
        value = jnp.zeros((8, 128), f32)
        for k in reversed(range(width)) if reverse else range(width):
            new = jnp.exp2(got[k, seq, states] * rate_ref[n]) * value + got[k, seq, n]
            value = jnp.where(me < k if reverse else me > k, new, value)
        result.append(value)
    return result


def spread_rows(low_ref, first, out_ref):
    states, slots = 16, low_ref.shape[1]

    def lanes(k, _):
        block = low_ref[first : first + states, pl.ds(pl.multiple_of(k * 128, 128), 128)]
        for i in range(128):
            to = pl.ds(pl.multiple_of((k * 128 + i) * states, states), states)
            out_ref[to, :] = jnp.broadcast_to(block[:, i : i + 1], (states, 128))
        return 0

    lax.fori_loop(0, slots // 128, lanes, 0)


def scan_forward(low_all, act, gate_z, small, rate, out_parts, seqs, rank, at_step, at_bias, at_skip, ident):
    rows, channels = act.shape
    shards, _, part = out_parts.shape
    local = rows // seqs
    states = rate.shape[0]
    width = lax.axis_size("ctx")
    pieces = local // piece

    def kernel(
        low_ref, act_ref, z_ref, small_ref, rate_ref, w_ref,
        scan_ref, gated_ref, mixed_ref, pre_ref, kept_ref, enter_ref, size3, drive3,
        y3, ends, got, held, b_ref, c_ref, low_t, w_own, send, recv, out_sem, w_sem,
    ):
        barrier = ctx_greet(width)
        load = pltpu.make_async_copy(w_ref, w_own, w_sem)
        load.start()
        low_t[...] = low_ref[0:rank, :].T.astype(bf16)
        bias = small_ref[at_bias : at_bias + 16, :].astype(f32)[0:1]
        for j in range(channels // 256):
            here = slice(j * 256, (j + 1) * 256)
            value = jnp.dot(low_t[...], small_ref[at_step : at_step + rank, here], preferred_element_type=f32)
            pre_ref[:, here] = value + bias[:, here]
        spread_rows(low_ref, rank, b_ref)
        spread_rows(low_ref, rank + states, c_ref)

        def lay(i, _):
            first = pl.multiple_of(i * 16, 16)
            act_block = act_ref[pl.ds(first, 16), :].astype(f32)
            size = jax.nn.softplus(pre_ref[pl.ds(first, 16), :])
            drive = size * act_block
            for h in range(2):
                spread(size3, size[h * 8 : h * 8 + 8], first + h * 8)
                spread(drive3, drive[h * 8 : h * 8 + 8], first + h * 8)
            return 0

        lax.fori_loop(0, rows // 16, lay, 0)
        pl.semaphore_wait(barrier, width - 1)
        copies = []
        for seq in range(seqs):

            def first_pass(i, carried):
                values, total = list(carried[:-1]), carried[-1]
                for u in range(unroll):
                    t = seq * local + i * unroll + u
                    s, d = tile(size3, t), tile(drive3, t)
                    total = total + s
                    for n in range(states):
                        values[n] = jnp.exp2(s * rate_ref[n]) * values[n] + d * row(b_ref, t, n, states)
                return tuple(values) + (total,)

            zero = tuple(jnp.zeros((8, 128), f32) for _ in range(states + 1))
            done = lax.fori_loop(0, local // unroll, first_pass, zero)
            for n in range(states + 1):
                ends[seq, n] = done[n]
            copies.append(exchange(ends, got, send, recv, seq, width))
        me = lax.axis_index("ctx")
        for seq in range(seqs):
            for copy in copies[seq]:
                copy.wait()
            got[me, seq] = ends[seq]
            start = entering(got, seq, rate_ref, states, width, False)
            for n in range(states):
                enter_ref[seq, n] = start[n]

            def save(k, slot):
                return pltpu.make_async_copy(
                    held.at[slot], kept_ref.at[pl.ds(seq * local + k * piece, piece)], out_sem.at[slot]
                )

            def one_piece(k, carried):
                slot = lax.rem(k, 2)

                @pl.when(k >= 2)
                def _():
                    save(k - 2, slot).wait()

                def second_pass(i, values):
                    values = list(values)
                    for u in range(unroll):
                        inside = i * unroll + u
                        t = seq * local + k * piece + inside
                        s, d = tile(size3, t), tile(drive3, t)
                        acc = [None] * 4
                        for n in range(states):
                            values[n] = jnp.exp2(s * rate_ref[n]) * values[n] + d * row(b_ref, t, n, states)
                            held[slot, inside, n] = values[n]
                            part = values[n] * row(c_ref, t, n, states)
                            acc[n % 4] = part if acc[n % 4] is None else acc[n % 4] + part
                        y3[pl.ds(pl.multiple_of(t * 8, 8), 8), :] = (acc[0] + acc[1]) + (acc[2] + acc[3])
                    return tuple(values)

                carried = lax.fori_loop(0, piece // unroll, second_pass, carried)
                save(k, slot).start()
                return carried

            lax.fori_loop(0, pieces, one_piece, tuple(start))
            for k in (pieces - 2, pieces - 1):
                save(k, k % 2).wait()

        skip = small_ref[at_skip : at_skip + 16, :].astype(f32)[0:1]

        def back(i, _):
            first = pl.multiple_of(i * 16, 16)
            here = pl.ds(first, 16)
            value = jnp.concatenate([unspread(y3, first), unspread(y3, first + 8)], axis=0)
            value = value + skip * act_ref[here, :].astype(f32)
            scan_ref[here, :] = value
            gated_ref[here, :] = (value * jax.nn.silu(z_ref[here, :])).astype(bf16)
            return 0

        lax.fori_loop(0, rows // 16, back, 0)
        load.wait()
        for k in range(shards):
            for j in range(-(-part // 256)):
                span = min(256, part)
                value = jnp.dot(gated_ref[...], w_own[k, :, j * span : (j + 1) * span], preferred_element_type=f32)
                mixed_ref[:, k * part + j * span : k * part + (j + 1) * span] = value.astype(bf16)

    flat = jax.ShapeDtypeStruct((rows * 8, 128), f32)
    return pl.pallas_call(
        kernel,
        out_shape=[
            jax.ShapeDtypeStruct((rows, channels), f32),
            jax.ShapeDtypeStruct((rows, channels), bf16),
            jax.ShapeDtypeStruct((rows, shards * part), bf16),
            jax.ShapeDtypeStruct((rows, channels), f32),
            jax.ShapeDtypeStruct((rows, states, 8, 128), f32),
            jax.ShapeDtypeStruct((seqs, states, 8, 128), f32),
            flat,
            flat,
        ],
        in_specs=[VMEM] * 5 + [HBM],
        out_specs=[VMEM] * 4 + [HBM, VMEM, VMEM, VMEM],
        scratch_shapes=[
            pltpu.VMEM((rows * 8, 128), f32),
            pltpu.VMEM((seqs, states + 1, 8, 128), f32),
            pltpu.VMEM((width, seqs, states + 1, 8, 128), f32),
            pltpu.VMEM((2, piece, states, 8, 128), f32),
            pltpu.VMEM((rows * states, 128), f32),
            pltpu.VMEM((rows * states, 128), f32),
            pltpu.VMEM((rows, rank), bf16),
            pltpu.VMEM(out_parts.shape, bf16),
            pltpu.SemaphoreType.DMA((seqs, width)),
            pltpu.SemaphoreType.DMA((seqs, width)),
            pltpu.SemaphoreType.DMA((2,)),
            pltpu.SemaphoreType.DMA,
        ],
        compiler_params=pltpu.CompilerParams(
            collective_id=ident, has_side_effects=True, vmem_limit_bytes=48 << 20
        ),
    )(low_all, act, gate_z, small, rate, out_parts)


def sublane_sums(parts):
    at = lax.broadcasted_iota(jnp.int32, (8, 128), 0)
    for shift in (4, 2, 1):
        low = (at // shift) % 2 == 0
        half = len(parts) // 2
        merged = []
        for one, two in zip(parts[:half], parts[half:]):
            merged.append(
                jnp.where(low, one + pltpu.roll(one, 8 - shift, 0), two + pltpu.roll(two, shift, 0))
            )
        parts = merged
    return parts[0]


def scan_backward(size3, drive3, grad, low_all, rank, rate, kept, enter, seqs, ident, partial, epilogue, extras, chunk, scatters):
    rows, channels = grad.shape
    local = rows // seqs
    states = rate.shape[0]
    width = lax.axis_size("ctx")
    pieces = local // piece
    early = 2
    unroll_b = 2
    line = Line(partial.shape, chunk, epilogue, extras, bf16)
    share = Halving(scatters, 16, 1)
    n_line, n_ex, n_sc = len(line.scratch()), len(extras), len(scatters)

    def kernel(*refs):
        refs = list(refs)

        def take_refs(n):
            taken = refs[:n]
            del refs[:n]
            return taken

        size_ref, drive_ref, grad_ref, low_ref, rate_ref, kept_ref, enter_ref, p_ref = take_refs(8)
        ins, full = take_refs(n_ex), take_refs(n_sc)
        tb3, sd3, bg_ref, cg_ref, dec_ref, sum_ref = take_refs(6)
        shares = take_refs(n_sc)
        grad3, b_ref, c_ref, ends, got, held, bpart, cpart, prior, send, recv, in_sem = take_refs(12)
        line.bind(p_ref, ins, sum_ref, [], take_refs(n_line))
        share.bind(full, shares, refs)
        barrier = ctx_greet(width)
        line.begin(barrier, width - 1 + share.greet(barrier))
        share.start()
        spread_rows(low_ref, rank, b_ref)
        spread_rows(low_ref, rank + states, c_ref)
        share.tick(0)

        def lay(i, _):
            first = pl.multiple_of(i * 8, 8)
            spread(grad3, grad_ref[pl.ds(first, 8), :], first)
            return 0

        lax.fori_loop(0, rows // 8, lay, 0)

        def fetch(g):
            first = (g // pieces) * local + (pieces - 1 - g % pieces) * piece
            slot = g % slots_held
            return pltpu.make_async_copy(kept_ref.at[pl.ds(first, piece)], held.at[slot], in_sem.at[slot])

        for g in range(slots_held - 1):
            fetch(g).start()

        copies = []
        for seq in range(seqs):

            def first_pass(i, carried):
                values, total = list(carried[:-1]), carried[-1]
                for u in range(unroll):
                    t = seq * local + local - 1 - (i * unroll + u)
                    s, g = tile(size_ref, t), tile(grad3, t)
                    total = total + s
                    for n in range(states):
                        values[n] = jnp.exp2(s * rate_ref[n]) * (values[n] + g * row(c_ref, t, n, states))
                return tuple(values) + (total,)

            zero = tuple(jnp.zeros((8, 128), f32) for _ in range(states + 1))
            done = zero
            for half in range(early):
                span = local // unroll // early
                done = lax.fori_loop(half * span, (half + 1) * span, first_pass, done)
                line.tick(seq * early + half)
            for n in range(states + 1):
                ends[seq, n] = done[n]
            copies.append(exchange(ends, got, send, recv, seq, width))
            share.tick(1 + seq)
        me = lax.axis_index("ctx")
        for n in range(states):
            dec_ref[n] = jnp.zeros((8, 128), f32)
        for seq in range(seqs):
            for copy in copies[seq]:
                copy.wait()
            got[me, seq] = ends[seq]
            start = entering(got, seq, rate_ref, states, width, True)
            fetch(seq * pieces).wait()

            def one_slot(slot, k, inside, adjoint, decays, prior_at):
                t = seq * local + k * piece + inside
                s, d, g = tile(size_ref, t), tile(drive_ref, t), tile(grad3, t)
                tb, sd = [None] * 2, [None] * 2
                b_parts, c_parts = [], []
                for n in range(states):
                    total = adjoint[n] + g * row(c_ref, t, n, states)
                    c_parts.append(held[slot, inside, n] * g)
                    b_parts.append(total * d)
                    through = total * row(b_ref, t, n, states)
                    adjoint[n] = jnp.exp2(s * rate_ref[n]) * total
                    kept_part = adjoint[n] * prior_at(n)
                    through_size = kept_part * rate_ref[n]
                    decays[n] = decays[n] + kept_part * s
                    tb[n % 2] = through if tb[n % 2] is None else tb[n % 2] + through
                    sd[n % 2] = through_size if sd[n % 2] is None else sd[n % 2] + through_size
                here = pl.ds(pl.multiple_of(t * 8, 8), 8)
                tb3[here, :] = tb[0] + tb[1]
                sd3[here, :] = sd[0] + sd[1]
                for h in range(states // 8):
                    spot = pl.ds(pl.multiple_of(inside * states + h * 8, 8), 8)
                    bpart[spot, :] = sublane_sums(b_parts[h * 8 : h * 8 + 8])
                    cpart[spot, :] = sublane_sums(c_parts[h * 8 : h * 8 + 8])

            def one_piece(back_k, carried):
                k = pieces - 1 - back_k
                place = seq * pieces + back_k
                slot = place % slots_held

                @pl.when(place + slots_held - 1 < seqs * pieces)
                def _():
                    fetch(place + slots_held - 1).start()

                def slots(i, carried):
                    adjoint, decays = list(carried[:states]), list(carried[states:])
                    for u in range(unroll_b):
                        inside = piece - 1 - (i * unroll_b + u)
                        one_slot(slot, k, inside, adjoint, decays, lambda n: held[slot, inside - 1, n])
                    return tuple(adjoint) + tuple(decays)

                carried = lax.fori_loop(0, piece // unroll_b - 1, slots, carried)
                adjoint, decays = list(carried[:states]), list(carried[states:])
                for inside in reversed(range(1, unroll_b)):
                    one_slot(slot, k, inside, adjoint, decays, lambda n: held[slot, inside - 1, n])

                @pl.when(k > 0)
                def _():
                    fetch(place + 1).wait()
                    prior[...] = held[(place + 1) % slots_held, piece - 1]

                @pl.when(k == 0)
                def _():
                    prior[...] = enter_ref[seq]

                one_slot(slot, k, 0, adjoint, decays, lambda n: prior[n])
                ones = jnp.ones((8, 128), bf16)
                for part, out in ((bpart, bg_ref), (cpart, cg_ref)):
                    sums = outer_cols(ones, part[...].astype(bf16))
                    out[pl.ds(seq * pieces + k, 1)] = sums[None]
                @pl.when(place % 2 == 0)
                def _():
                    line.tick(seqs * early + place // 2)

                @pl.when(place % 5 == 0)
                def _():
                    share.tick(1 + seqs + place // 5)

                return tuple(adjoint) + tuple(decays)

            zero = tuple(jnp.zeros((8, 128), f32) for _ in range(states))
            carried = lax.fori_loop(0, pieces, one_piece, tuple(start) + zero)
            for n in range(states):
                dec_ref[n] = dec_ref[n] + carried[states + n]

        for c in range(seqs * early + (seqs * pieces + 1) // 2, line.ticks()):
            line.tick(c)
        for i in range(1 + seqs + (seqs * pieces + 4) // 5, share.turns):
            share.tick(i)
        line.finish()
        share.finish()

    flat = jax.ShapeDtypeStruct((rows * 8, 128), f32)
    sums = jax.ShapeDtypeStruct((rows // piece, 8, piece * states), f32)
    return pl.pallas_call(
        kernel,
        out_shape=[flat, flat, sums, sums, jax.ShapeDtypeStruct((states, 8, 128), f32),
                   jax.ShapeDtypeStruct(partial.shape, bf16)] + share.results(),
        in_specs=[VMEM] * 5 + [HBM, VMEM] + [HBM] * (1 + n_ex + n_sc),
        out_specs=[VMEM] * (6 + n_sc),
        scratch_shapes=[pltpu.VMEM((rows * 8, 128), f32)]
        + [pltpu.VMEM((rows * states, 128), f32)] * 2
        + [
            pltpu.VMEM((seqs, states + 1, 8, 128), f32),
            pltpu.VMEM((width, seqs, states + 1, 8, 128), f32),
            pltpu.VMEM((slots_held, piece, states, 8, 128), f32),
            pltpu.VMEM((piece * states, 128), f32),
            pltpu.VMEM((piece * states, 128), f32),
            pltpu.VMEM((states, 8, 128), f32),
            pltpu.SemaphoreType.DMA((seqs, width)),
            pltpu.SemaphoreType.DMA((seqs, width)),
            pltpu.SemaphoreType.DMA((slots_held,)),
        ]
        + line.scratch()
        + share.scratch(),
        compiler_params=pltpu.CompilerParams(
            collective_id=ident, has_side_effects=True, vmem_limit_bytes=62 << 20
        ),
    )(size3, drive3, grad, low_all, rate, kept, enter, partial, *extras, *share.folded)


def feed_forward(mixed_part, hidden, gain, ffn_grad, gate_w, down_parts, ident):
    rows, width = hidden.shape
    shards, ffn, part = down_parts.shape
    chunk = 32
    block = 4 * chunk
    tile = ffn // 4
    blocks = rows // block
    fore = Line(mixed_part.shape, chunk, norm_end, [], bf16)
    after = Line(mixed_part.shape, chunk, norm_back_end, [], bf16)
    n_line = len(fore.scratch())
    behind = 5
    wtile = 256

    def kernel(
        p_ref, hid_ref, gain_ref, fg_ref, gate_ref, up_ref, down_ref,
        ffn_out, mid_out, mix_ref, midg_ref, gsum_ref, both_out, dw_out,
        normed, middle, hid_v, gg_v, ug_v, ffn_v, ffn_acc, back_acc, gate_v, up_v, down_v, stage, stage_d, load_sem, save_sem, *rest
    ):
        barrier = pltpu.get_barrier_semaphore()
        fore.bind(p_ref, [], normed, [middle], rest[:n_line])
        after.bind(rest[n_line], [], mix_ref, [midg_ref], rest[n_line:])
        fore.ins = [hid_ref, gain_ref]
        after.ins = [middle, gain_ref, fg_ref]
        loads = [
            pltpu.make_async_copy(a, b, load_sem.at[i])
            for i, (a, b) in enumerate(((gate_ref, gate_v), (up_ref, up_v), (down_ref, down_v)))
        ]
        fore.begin(barrier, 0)
        for load in loads:
            load.start()
        gsum_ref[...] = jnp.zeros_like(gsum_ref)
        lead = 4 + fore.lag

        def warm(c, _):
            fore.tick(c)
            return 0

        lax.fori_loop(0, lead, warm, 0)
        for load in loads:
            load.wait()
        outer = jnp.logical_not(fore.middle)

        def step(s, _):
            b, j = s // 4, s % 4
            fore.tick(s + lead)
            at = pl.ds(pl.multiple_of(b * block, block), block)
            here = pl.ds(pl.multiple_of(j * tile, tile), tile)

            @pl.when(j == 0)
            def _():
                ffn_acc[...] = jnp.zeros_like(ffn_acc)
                back_acc[...] = jnp.zeros_like(back_acc)

                @pl.when(outer)
                def _():
                    for k in range(4):
                        fore.copy_c(4 * b + k).wait_recv()

            source, grad = normed[at, :], fg_ref[at, :]
            gate = jnp.dot(source, gate_v[:, here], preferred_element_type=f32)
            up = jnp.dot(source, up_v[:, here], preferred_element_type=f32)
            sig = jax.nn.sigmoid(gate)
            silu = gate * sig
            hidden_val = (silu * up).astype(bf16)
            back = sum(
                outer_cols(grad[:, k * part : (k + 1) * part], down_v[k, here, :]) for k in range(shards)
            )
            gate_back = (back * up * (sig * (1.0 + gate * (1.0 - sig)))).astype(bf16)
            up_back = (back * silu).astype(bf16)
            hid_v[at, here] = hidden_val
            gg_v[at, here] = gate_back
            ug_v[at, here] = up_back

            after.quiet_tick(s - behind)

            for k in range(shards):
                to = slice(k * part, (k + 1) * part)
                ffn_acc[:, to] += jnp.dot(hidden_val, down_v[k, here, :], preferred_element_type=f32)
            for k in range(width // 512):
                to = slice(k * 512, (k + 1) * 512)
                back_acc[:, to] += outer_cols(gate_back, gate_v[to, here]) + outer_cols(up_back, up_v[to, here])

            @pl.when(j == 3)
            def _():
                ffn_v[at, :] = ffn_acc[...].astype(bf16)
                after.p[at, :] = back_acc[...].astype(bf16)
                for k in range(block // 16):
                    product = after.p[pl.ds(pl.multiple_of(b * block + k * 16, 16), 16), :].astype(f32)
                    product = product * normed[pl.ds(pl.multiple_of(b * block + k * 16, 16), 16), :].astype(f32)
                    gsum_ref[...] += product[:8] + product[8:]

                @pl.when(outer)
                def _():
                    for k in range(4):
                        after.copy_a(4 * b + k).start()

            return 0

        steps = 4 * blocks
        lax.fori_loop(0, steps, step, 0)
        ffn_save = pltpu.make_async_copy(ffn_v, ffn_out, save_sem.at[3])
        ffn_save.start()
        mid_save = pltpu.make_async_copy(middle, mid_out, save_sem.at[4])
        mid_save.start()

        def saves(i):
            to = pl.ds(pl.multiple_of(i * wtile, wtile), wtile)
            return [
                pltpu.make_async_copy(held, out.at[to], save_sem.at[a])
                for a, (held, out) in enumerate(((stage, both_out), (stage_d, dw_out)))
            ]

        def weights(i, _):
            after.quiet_tick(steps - behind + i)
            here = pl.ds(pl.multiple_of(i * wtile, wtile), wtile)

            @pl.when(i > 0)
            def _():
                for save in saves(i - 1):
                    save.wait()

            source, grad = normed[:, here], fg_ref[:, here]
            stage[:, :ffn] = inner_rows(source, gg_v[...]).astype(bf16)
            stage[:, ffn:] = inner_rows(source, ug_v[...]).astype(bf16)
            stage_d[...] = inner_rows(grad, hid_v[...]).astype(bf16)
            for save in saves(i):
                save.start()
            return 0

        lax.fori_loop(0, width // wtile, weights, 0)
        for c in range(steps - behind + width // wtile, after.ticks()):
            after.quiet_tick(c)
        for save in saves(width // wtile - 1) + [ffn_save, mid_save]:
            save.wait()
        fore.finish(False)
        after.finish()

    sds = jax.ShapeDtypeStruct
    wide, half = sds((rows, width), f32), sds((rows, width), bf16)
    both, down = sds((width, 2 * ffn), bf16), sds((width, ffn), bf16)
    return pl.pallas_call(
        kernel,
        out_shape=[half, wide, half, wide, sds((8, width), f32), both, down],
        in_specs=[HBM, VMEM, VMEM, VMEM, HBM, HBM, HBM],
        out_specs=[HBM, HBM, VMEM, VMEM, VMEM, HBM, HBM],
        scratch_shapes=[
            pltpu.VMEM((rows, width), bf16),
            pltpu.VMEM((rows, width), f32),
            pltpu.VMEM((rows, ffn), bf16),
            pltpu.VMEM((rows, ffn), bf16),
            pltpu.VMEM((rows, ffn), bf16),
            pltpu.VMEM((rows, width), bf16),
            pltpu.VMEM((block, width), f32),
            pltpu.VMEM((block, width), f32),
            pltpu.VMEM((width, ffn), bf16),
            pltpu.VMEM((width, ffn), bf16),
            pltpu.VMEM(down_parts.shape, bf16),
            pltpu.VMEM((wtile, 2 * ffn), bf16),
            pltpu.VMEM((wtile, ffn), bf16),
            pltpu.SemaphoreType.DMA((3,)),
            pltpu.SemaphoreType.DMA((5,)),
        ]
        + fore.scratch()
        + after.scratch(),
        compiler_params=pltpu.CompilerParams(
            collective_id=ident, has_side_effects=True, vmem_limit_bytes=62 << 20
        ),
    )(mixed_part, hidden, gain, ffn_grad, gate_w[0], gate_w[1], down_parts)


def scan_tail(through_b, through_decay, sums, decay_grad, scan_grad, step_pre, pre_act, act, padded, z_half, low_all, small, normed, in_w, scatters, ident,
              seqs, low_len, rank, states, taps):
    rows, inner = act.shape
    local = rows // seqs
    long = local + halo
    shards, pieces = lax.axis_size("shard"), lax.axis_size("ctx")
    places = shards * pieces
    lane = inner // places
    line = Line((low_len, rows), 80, plain_end, [], bf16)
    tiles = inner // tile_cols
    at = low_len + rank
    lines = -(-(at + states + taps + 3) // 8) * 8
    height = -(-(lines + 8) // 32) * 32
    over = 8
    width = normed.shape[1]
    dtile = width // 8
    share = Halving(scatters, 32, 1)
    n_sc, n_share = len(scatters), len(share.scratch())

    def kernel(*refs):
        n_in = 14 + n_sc
        main(*refs[:14], *refs[n_in : n_in + 4], refs[14:n_in], refs[n_in + 4 : n_in + 4 + n_sc],
             refs[n_in + 4 + n_sc : n_in + 4 + n_sc + n_share], *refs[n_in + 4 + n_sc + n_share :])

    def main(
        tb_ref, sd_ref, sums_ref, dec_ref, sg_ref, sp_ref, pre_ref, act_ref, ext_ref, zg_ref, low_ref, small_ref, n_ref, w_ref,
        iw_out, first_ref, gsum_ref, blocks_ref, full, shares, share_scratch,
        conv_ref, w_v, acc, stage, w_sem, stage_sem, low_out, low_t, step_g, low_acc, grads, pre_g, conv_f, edge, edge_out, edge_sem, *rest
    ):
        ctx = lax.axis_index("ctx")
        barrier = pltpu.get_barrier_semaphore()
        line.bind(rest[0], [], low_out, [], list(rest))
        share.bind(full, shares, share_scratch)
        w_load = pltpu.make_async_copy(w_ref, w_v, w_sem)
        w_load.start()
        met = share.greet(barrier)
        pl.semaphore_signal(barrier, inc=1, device_id={"ctx": lax.rem(ctx + 1, pieces)}, device_id_type=MESH)

        def flat(ref, j, first, count):
            parts = [ref[pl.ds(first * 8 + j * (tile_cols // 128) + h, count, stride=8), :] for h in range(tile_cols // 128)]
            return jnp.concatenate(parts, axis=1)

        def cols(j):
            return pl.ds(pl.multiple_of(j * tile_cols, tile_cols), tile_cols)

        low_acc[...] = jnp.zeros_like(low_acc)
        grads[...] = jnp.zeros_like(grads)
        low_t[...] = low_ref[0:rank, :].astype(bf16)

        def size_tile(j, _):
            here = cols(j)
            bias_grad = jnp.zeros((8, tile_cols), f32)
            skip_grad = jnp.zeros((8, tile_cols), f32)
            for k in range(rows // 64):
                to = slice(k * 64, (k + 1) * 64)
                act_block = act_ref[to, here].astype(f32)
                size_grad = act_block * flat(tb_ref, j, k * 64, 64) + flat(sd_ref, j, k * 64, 64) * (1.0 / log2e)
                value = (size_grad * jax.nn.sigmoid(sp_ref[to, here])).astype(bf16)
                step_g[to, here] = value
                wide = value.astype(f32)
                product = sg_ref[to, here] * act_block
                for h in range(8):
                    bias_grad = bias_grad + wide[h * 8 : h * 8 + 8]
                    skip_grad = skip_grad + product[h * 8 : h * 8 + 8]
            grads[at + states + taps + 1 : at + states + taps + 2, here] = jnp.sum(bias_grad, axis=0, keepdims=True)
            grads[at + states + taps + 2 : at + states + taps + 3, here] = jnp.sum(skip_grad, axis=0, keepdims=True)
            low_acc[...] = low_acc[...] + outer_cols(small_ref[low_len : low_len + rank, here], step_g[:, here])
            return 0

        lax.fori_loop(0, tiles, size_tile, 0)
        line.p[0:rank, :] = low_acc[...].astype(bf16)
        line.p[rank : rank + 2 * states, :] = sums_ref[...].astype(bf16)
        line.greet(barrier, 1 + met)
        line.start()
        share.start()

        def save(i, c):
            return pltpu.make_async_copy(
                stage.at[i % 2],
                iw_out.at[pl.ds(pl.multiple_of(i * dtile, dtile), dtile), pl.ds(c * inner, inner)],
                stage_sem.at[i % 2],
            )

        def weight_piece(i, right, c):
            here = pl.ds(pl.multiple_of(i * dtile, dtile), dtile)
            if c == 0:
                save(i, c).wait()
            else:

                @pl.when(i >= 2)
                def _():
                    save(i, c).wait()

            stage[i % 2] = inner_rows(n_ref[:, here], right[...]).astype(bf16)
            save(i, c).start()
            value = outer_cols(right[...], w_v[c, here, :])
            if c == 1:
                acc[:, here] = value
            else:
                value = (acc[:, here] + value).astype(bf16)
                first_ref[:, here] = value
                product = value.astype(f32) * n_ref[:, here].astype(f32)
                gsum_ref[:, here] = jnp.sum(product.reshape(rows // 8, 8, dtile), axis=0)

        def step_tile(j, _):
            here = cols(j)
            grads[low_len:at, here] = jnp.dot(low_t[...], step_g[:, here], preferred_element_type=f32)
            return 0

        lax.fori_loop(0, tiles, step_tile, 0)
        grads[at : at + states, :] = dec_ref[...]
        w_load.wait()
        early = 8 // line.ticks()

        def beside(c, _):
            for i in range(early):
                weight_piece(c * early + i, zg_ref, 1)
            line.tick(c)
            return 0

        lax.fori_loop(0, line.ticks(), beside, 0)
        for i in range(early * line.ticks(), 8):
            weight_piece(i, zg_ref, 1)
        line.finish()

        def pre_tile(j, _):
            here = cols(j)
            grads[0:low_len, here] = jnp.dot(low_out[...], act_ref[:, here], preferred_element_type=f32)
            for seq in range(seqs):
                low = inner_rows(low_out[:, seq * local : (seq + 1) * local], small_ref[0:low_len, here])
                conv_f[seq * long : (seq + 1) * long, :] = ext_ref[seq * long : (seq + 1) * long, here].astype(f32)
                pre_g[seq * (local + over) : seq * (local + over) + local, here] = low
            skip = small_ref[at + states + 32 : at + states + 48, here].astype(f32)[0:1]
            bias_sum = jnp.zeros((8, tile_cols), f32)
            tap_sums = [jnp.zeros((8, tile_cols), f32) for _ in range(taps)]
            for seq in range(seqs):
                for k in range(local // 64):
                    to = slice(seq * local + k * 64, seq * local + (k + 1) * 64)
                    where = slice(seq * (local + over) + k * 64, seq * (local + over) + (k + 1) * 64)
                    act_grad = skip * sg_ref[to, here] + jax.nn.softplus(sp_ref[to, here]) * flat(tb_ref, j, seq * local + k * 64, 64)
                    value = (act_grad + pre_g[where, here]) * silu_grad(pre_ref[to, here])
                    pre_g[where, here] = value
                    first = seq * long + halo + k * 64 - taps + 1
                    products = [value * conv_f[first + tap : first + tap + 64, :] for tap in range(taps)]
                    for h in range(8):
                        bias_sum = bias_sum + value[h * 8 : h * 8 + 8]
                        for tap in range(taps):
                            tap_sums[tap] = tap_sums[tap] + products[tap][h * 8 : h * 8 + 8]
            for tap in range(taps):
                row = at + states + tap
                grads[row : row + 1, here] = jnp.sum(tap_sums[tap], axis=0, keepdims=True)
            row = at + states + taps
            grads[row : row + 1, here] = jnp.sum(bias_sum, axis=0, keepdims=True)
            return 0

        lax.fori_loop(0, tiles, pre_tile, 0)
        for seq in range(seqs):
            edge_out[seq] = pre_g[seq * (local + over) : seq * (local + over) + over, :]
        copy = pltpu.make_async_remote_copy(
            edge_out, edge, edge_sem.at[0], edge_sem.at[1],
            device_id={"ctx": lax.rem(ctx + pieces - 1, pieces)}, device_id_type=MESH,
        )
        copy.start()
        for p in range(places):
            blocks_ref[p * height : p * height + lines, :] = grads[:, p * lane : (p + 1) * lane].astype(bf16)
            blocks_ref[p * height + lines : (p + 1) * height, :] = jnp.zeros((height - lines, lane), bf16)
        copy.wait()
        inside = (ctx < pieces - 1).astype(f32)
        for seq in range(seqs):
            first = seq * (local + over) + local
            pre_g[first : first + over, :] = edge[seq] * inside

        def conv_tile(j, _):
            here = cols(j)
            weights = small_ref[at + states : at + states + 16, here].astype(f32)
            for seq in range(seqs):
                for k in range(local // 64):
                    first = seq * (local + over) + k * 64 + taps - 1
                    total = weights[0:1] * pre_g[first : first + 64, here]
                    for tap in range(1, taps):
                        total = total + weights[tap : tap + 1] * pre_g[first - tap : first - tap + 64, here]
                    conv_ref[seq * local + k * 64 : seq * local + (k + 1) * 64, here] = total.astype(bf16)
            return 0

        lax.fori_loop(0, tiles, conv_tile, 0)

        def conv_piece(i, _):
            weight_piece(i, conv_ref, 0)
            return 0

        lax.fori_loop(0, 8, conv_piece, 0)
        for i in range(share.turns if n_sc else 0):
            share.tick(i)
        save(6, 0).wait()
        save(7, 0).wait()
        share.finish()

    return pl.pallas_call(
        kernel,
        out_shape=[
            jax.ShapeDtypeStruct((width, 2 * inner), bf16),
            jax.ShapeDtypeStruct((rows, width), bf16),
            jax.ShapeDtypeStruct((8, width), f32),
            jax.ShapeDtypeStruct((places * height, lane), bf16),
        ]
        + share.results(),
        in_specs=[VMEM] * 13 + [HBM] * (1 + n_sc),
        out_specs=[HBM] + [VMEM] * (3 + n_sc),
        scratch_shapes=share.scratch()
        + [
            pltpu.VMEM((rows, inner), bf16),
            pltpu.VMEM(in_w.shape, bf16),
            pltpu.VMEM((rows, width), f32),
            pltpu.VMEM((2, dtile, inner), bf16),
            pltpu.SemaphoreType.DMA,
            pltpu.SemaphoreType.DMA((2,)),
            pltpu.VMEM((low_len, rows), bf16),
            pltpu.VMEM((rank, rows), bf16),
            pltpu.VMEM((rows, inner), bf16),
            pltpu.VMEM((rank, rows), f32),
            pltpu.VMEM((lines, inner), f32),
            pltpu.VMEM((seqs * (local + over), inner), f32),
            pltpu.VMEM((seqs * long, tile_cols), f32),
            pltpu.VMEM((seqs, over, inner), f32),
            pltpu.VMEM((seqs, over, inner), f32),
            pltpu.SemaphoreType.DMA((2,)),
        ]
        + line.scratch(),
        compiler_params=pltpu.CompilerParams(
            collective_id=ident, has_side_effects=True, vmem_limit_bytes=60 << 20
        ),
    )(through_b, through_decay, sums, decay_grad, scan_grad, step_pre, pre_act, act, padded, z_half, low_all, small, normed, in_w, *share.folded), height


def body(
    hidden_in, lengths, cotangent, norm_gain, in_weight, conv_weight, conv_bias, low_weight, step_weight,
    step_bias, decay_log, skip_gain, out_weight, ffn_gain, gate_up, down_weight,
):
    seqs, local, width = hidden_in.shape
    rows = seqs * local
    shards, pieces = lax.axis_size("shard"), lax.axis_size("ctx")
    inner = in_weight.shape[2]
    taps = conv_weight.shape[0]
    rank = step_weight.shape[0]
    states = decay_log.shape[0]
    low_len = low_weight.shape[0]

    def rows16(v):
        return jnp.pad(v, ((0, 16 - v.shape[0]), (0, 0)))

    small = jnp.concatenate(
        [low_weight, step_weight, decay_log, rows16(jnp.concatenate([conv_weight, conv_bias[None]], axis=0)),
         rows16(step_bias[None]), rows16(skip_gain[None])], axis=0,
    )
    at_bias = low_len + rank + states + 16
    at_skip = at_bias + 16
    hidden_rows = hidden_in.reshape(rows, width)
    small = jnp.pad(small, ((0, -small.shape[0] % 16), (0, 0)))
    gains = jnp.stack([norm_gain, ffn_gain])
    gains = jnp.pad(gains, ((0, 14), (0, 0)))
    in_half = in_weight.transpose(1, 0, 2)
    in_w, small, gains, normed_one, gate_z, padded, pre_act, act_half, low_all = front(
        hidden_rows, in_half, small, gains, seqs, low_len + rank + states, taps, low_len, 0
    )
    out_parts = lax.all_gather(out_weight, "shard")
    gate_half = gate_up.transpose(1, 0, 2)
    gate_w = [lax.all_gather(gate_half[c], "shard", axis=0, tiled=True) for c in range(2)]
    down_parts = lax.all_gather(down_weight, "shard")
    part = width // shards

    low_w = small[:low_len]
    step_w = small[low_len : low_len + rank]
    at = low_len + rank
    decay_w = small[at : at + states].astype(f32)
    kernel = small[at + states : at + states + taps].astype(f32)
    skip_full = small[at_skip].astype(f32)
    gain_one, gain_two = gains[0:1].astype(f32), gains[1:2].astype(f32)

    first_slot = lax.axis_index("ctx") * local
    positions = first_slot + jnp.arange(local, dtype=jnp.int32)
    pad_mask = (positions[None, :] < lengths[:, None]).astype(f32)

    source = hidden_rows.astype(f32)
    act_full = act_half.astype(f32)
    step_low = low_all[:rank].astype(bf16)
    decay_rate = -jnp.exp(decay_w)
    rate = (decay_rate * log2e).reshape(states, 8, 128)
    scan_out, gated_out, mixed_part, step_pre, kept, enter, size3, drive3 = scan_forward(
        low_all, act_half, gate_z, small, rate, out_parts, seqs, rank, low_len, at_bias, at_skip, 2
    )
    step_size = jax.nn.softplus(step_pre)
    gate_act = jax.nn.silu(gate_z)
    upstream = cotangent.reshape(rows, width).astype(f32) * pad_mask.reshape(rows, 1)
    ffn_grad = upstream.astype(bf16)
    ffn_part, middle, mix_grad, middle_grad, gain_sum, both_grad, down_grad = feed_forward(
        mixed_part, hidden_rows, gain_two, ffn_grad, gate_w, down_parts, 3
    )
    ffn_gain_grad = jnp.sum(gain_sum, axis=0) / gain_two[0]

    out_weight_grad = inner_rows(mix_grad, gated_out).astype(bf16)
    gated_grad = sum(outer_cols(mix_grad[:, k * part : (k + 1) * part], out_parts[k]) for k in range(shards))
    scan_grad = gated_grad * gate_act
    z_grad = gated_grad * scan_out * silu_grad(gate_z)
    through_b, through_decay, b_sums, c_sums, decay_sum, mixed_out, *ffn_shares = scan_backward(
        size3, drive3, scan_grad, low_all, rank, rate, kept, enter, seqs, 6, ffn_part, add_end, [middle], 32,
        [both_grad, down_grad],
    )
    mixed_out = mixed_out.reshape(hidden_in.shape)
    decay_log_grad = decay_sum.reshape(states, inner) * decay_rate
    sums = jnp.concatenate([v[:, 0].reshape(rows, states).T for v in (b_sums, c_sums)], axis=0)
    z_half = z_grad.astype(bf16)
    (in_weight_grad, first_part, gain_one_sum, small_blocks), small_height = scan_tail(
        through_b, through_decay, sums, decay_log_grad, scan_grad, step_pre, pre_act, act_half, padded, z_half, low_all, small, normed_one, in_w,
        [], 7,
        seqs, low_len, rank, states, taps,
    )
    norm_gain_grad = jnp.sum(gain_one_sum, axis=0) / gain_one[0]
    places, share = shards * pieces, width // (shards * pieces)
    lane = inner // places
    gain_rows = -(-2 * share // lane)
    gain_blocks = jnp.concatenate([norm_gain_grad.reshape(places, share), ffn_gain_grad.reshape(places, share)], axis=1)
    gain_blocks = jnp.pad(gain_blocks, ((0, 0), (0, gain_rows * lane - 2 * share))).reshape(places, gain_rows, lane)
    gain_height = 16 * -(-gain_rows // 16)
    gain_blocks = jnp.pad(gain_blocks, ((0, 0), (gain_height - gain_rows, 0), (0, 0)))
    gain_blocks = gain_blocks.reshape(places * gain_height, lane).astype(bf16)
    input_grad, in_share, out_share, small_out, gain_share = tp_sum(
        first_part, norm_back_end, [hidden_rows, gain_one, middle_grad], [], 32, 8,
        scatters=[in_weight_grad, out_weight_grad, small_blocks, gain_blocks], line_too=True,
        steps=[16, 16, small_height // 2, gain_height],
    )
    gain_share = gain_share[gain_height - gain_rows :].reshape(-1)
    input_grad = input_grad.astype(f32).reshape(hidden_in.shape)
    at = low_len + rank
    return (
        mixed_out,
        input_grad,
        gain_share[:share],
        in_share.reshape((-1,) + in_weight.shape[1:]),
        small_out[at + states : at + states + taps],
        small_out[at + states + taps],
        small_out[:low_len],
        small_out[low_len : low_len + rank],
        small_out[at + states + taps + 1],
        small_out[at : at + states],
        small_out[at + states + taps + 2],
        out_share.T,
        gain_share[share : 2 * share],
        ffn_shares[0].reshape((-1,) + gate_up.shape[1:]),
        ffn_shares[1].T,
    )


def solution(mesh):
    placed = (
        P("shard", "ctx", None),
        P("shard"),
        P("shard", "ctx", None),
        P("shard"),
        P("shard", None, "tp"),
        P(None, ("tp", "shard")),
        P(("tp", "shard")),
        P(None, ("tp", "shard")),
        P(None, ("tp", "shard")),
        P(("tp", "shard")),
        P(None, ("tp", "shard")),
        P(("tp", "shard")),
        P("tp", "shard"),
        P("shard"),
        P("shard", None, "tp"),
        P("tp", "shard"),
    )
    return jax.shard_map(
        body,
        mesh=mesh,
        in_specs=placed,
        out_specs=(
            P("shard", "ctx", None),
            P("shard", "ctx", None),
            P(("shard", "ctx")),
            P(("shard", "ctx"), None, "tp"),
            P(None, ("tp", "shard", "ctx")),
            P(("tp", "shard", "ctx")),
            P(None, ("tp", "shard", "ctx")),
            P(None, ("tp", "shard", "ctx")),
            P(("tp", "shard", "ctx")),
            P(None, ("tp", "shard", "ctx")),
            P(("tp", "shard", "ctx")),
            P("tp", ("shard", "ctx")),
            P(("shard", "ctx")),
            P(("shard", "ctx"), None, "tp"),
            P("tp", ("shard", "ctx")),
        ),
        check_vma=False,
    )
```

```python
import functools

import jax
import jax.numpy as jnp
from jax import lax
from jax.experimental import pallas as pl
from jax.experimental.pallas import tpu as pltpu
from jax.sharding import PartitionSpec as P

MESH = pl.DeviceIdType.MESH
epsilon = 1e-05
log2e = 1.4426950408889634
bf16 = jnp.bfloat16
f32 = jnp.float32
VMEM = pl.BlockSpec(memory_space=pltpu.VMEM)
HBM = pl.BlockSpec(memory_space=pl.ANY)


def inner_rows(left, right):
    return lax.dot_general(left, right, (((0,), (0,)), ((), ())), preferred_element_type=f32)


def outer_cols(left, right):
    return lax.dot_general(left, right, (((1,), (1,)), ((), ())), preferred_element_type=f32)


def silu_grad(values):
    sig_val = jax.nn.sigmoid(values)
    return sig_val * (1.0 + values * (1.0 - sig_val))


def rms_scale(source):
    return lax.rsqrt(jnp.mean(source * source, axis=-1, keepdims=True) + epsilon)


class Line:
    lag = 2
    ahead = 4

    def __init__(self, shape, chunk, epilogue, extras, out_dtype):
        self.shape, self.chunk, self.epilogue, self.out_dtype = shape, chunk, epilogue, out_dtype
        self.count = shape[0] // chunk
        self.extras = [(e.shape, e.dtype) for e in extras]

    def scratch(self):
        return (
            [pltpu.VMEM(self.shape, bf16)] * 4
            + [pltpu.SemaphoreType.DMA((self.count,))] * 6
            + [pltpu.VMEM(shape, dtype) for shape, dtype in self.extras]
            + [pltpu.SemaphoreType.DMA((1 + len(self.extras),))]
        )

    def bind(self, p_ref, ins, out_ref, outs, scratch):
        self.p_ref, self.given, self.out_ref, self.outs = p_ref, ins, out_ref, outs
        (self.p, self.got_a, self.pair, self.got_b, self.a_send, self.a_recv, self.b_send, self.b_recv,
         self.c_send, self.c_recv) = scratch[:10]
        self.ins, self.in_sem = scratch[10:-1], scratch[-1]
        me = lax.axis_index("tp")
        self.mate = me + 1 - 2 * (me % 2)
        self.across = 3 - me
        self.middle = jnp.logical_or(me == 1, me == 2)

    def at(self, c):
        return pl.ds(pl.multiple_of(c * self.chunk, self.chunk), self.chunk)

    def remote(self, source, target, send, recv, c, to):
        return pltpu.make_async_remote_copy(
            source.at[self.at(c)], target.at[self.at(c)], send.at[c], recv.at[c], device_id={"tp": to}, device_id_type=MESH
        )

    def copy_a(self, c):
        return self.remote(self.p_ref, self.got_a, self.a_send, self.a_recv, c, self.mate)

    def copy_b(self, c):
        return self.remote(self.pair, self.got_b, self.b_send, self.b_recv, c, self.across)

    def copy_c(self, c):
        return self.remote(self.out_ref, self.out_ref, self.c_send, self.c_recv, c, self.mate)

    def loads(self):
        pairs = [(self.p_ref, self.p)] + list(zip(self.given, self.ins))
        return [pltpu.make_async_copy(a, b, self.in_sem.at[i]) for i, (a, b) in enumerate(pairs)]

    def begin(self, barrier, met, ends_meet=False):
        pl.semaphore_signal(barrier, inc=1, device_id={"tp": self.mate}, device_id_type=MESH)

        @pl.when(self.middle)
        def _():
            pl.semaphore_signal(barrier, inc=1, device_id={"tp": self.across}, device_id_type=MESH)
            for load in self.loads():
                load.start()
            pl.semaphore_wait(barrier, met + 2)
            for load in self.loads():
                load.wait()

        @pl.when(jnp.logical_not(self.middle))
        def _():
            if ends_meet:
                pl.semaphore_signal(barrier, inc=1, device_id={"tp": self.across}, device_id_type=MESH)
            pl.semaphore_wait(barrier, met + 2 if ends_meet else met + 1)

            for c in range(min(self.ahead, self.count)):
                self.copy_a(c).start()

    def greet(self, barrier, met):
        pl.semaphore_signal(barrier, inc=1, device_id={"tp": self.mate}, device_id_type=MESH)

        @pl.when(self.middle)
        def _():
            pl.semaphore_signal(barrier, inc=1, device_id={"tp": self.across}, device_id_type=MESH)
            pl.semaphore_wait(barrier, met + 2)

        @pl.when(jnp.logical_not(self.middle))
        def _():
            pl.semaphore_wait(barrier, met + 1)

    def start(self):
        @pl.when(jnp.logical_not(self.middle))
        def _():
            for c in range(min(self.ahead, self.count)):
                self.copy_a(c).start()

    def first(self, c):
        at = self.at(c)
        self.copy_a(c).wait_recv()
        self.pair[at, :] = self.p[at, :] + self.got_a[at, :]
        self.copy_b(c).start()

    def second(self, c):
        at = self.at(c)
        self.copy_b(c).wait_recv()
        total = self.pair[at, :].astype(f32) + self.got_b[at, :].astype(f32)
        self.epilogue(c, at, total, self.ins, self.out_ref, self.outs)
        self.copy_c(c).start()

    def tick(self, c):
        lag = min(self.lag, self.count)

        @pl.when(jnp.logical_and(self.middle, c < self.count))
        def _():
            self.first(c)

        @pl.when(jnp.logical_and(self.middle, jnp.logical_and(c >= lag, c < self.count + lag)))
        def _():
            self.second(c - lag)

        @pl.when(jnp.logical_and(jnp.logical_not(self.middle), c + self.ahead < self.count))
        def _():
            self.copy_a(c + self.ahead).start()

    def quiet_tick(self, c):
        lag = min(self.lag, self.count)

        @pl.when(jnp.logical_and(self.middle, jnp.logical_and(c >= 0, c < self.count)))
        def _():
            self.first(c)

        @pl.when(jnp.logical_and(self.middle, jnp.logical_and(c >= lag, c < self.count + lag)))
        def _():
            self.second(c - lag)

    def ticks(self):
        return self.count + min(self.lag, self.count)

    def finish(self, take_result=True):
        @pl.when(self.middle)
        def _():
            def drain(c, _):
                self.copy_b(c).wait_send()
                self.copy_c(c).wait_send()
                return 0

            lax.fori_loop(0, self.count, drain, 0)

        @pl.when(jnp.logical_not(self.middle))
        def _():
            def take(c, _):
                if take_result:
                    self.copy_c(c).wait_recv()
                self.copy_a(c).wait_send()
                return 0

            lax.fori_loop(0, self.count, take, 0)


share_lag = 2
share_ahead = 2


class Halving:
    def __init__(self, arrays, step_rows=16, lag=share_lag):
        self.lag = lag
        steps = [step_rows] * len(arrays) if isinstance(step_rows, int) else list(step_rows)
        self.steps = steps
        shards, pieces = lax.axis_size("shard"), lax.axis_size("ctx")
        self.n = len(arrays)
        self.bits = [
            (axis, 1 << k)
            for axis, size in (("shard", shards), ("ctx", pieces))
            for k in reversed(range(size.bit_length() - 1))
        ]
        self.depth = len(self.bits)
        head = shards.bit_length() - 1
        self.dims = list(range(self.depth))
        self.orders = (self.dims, self.dims[:head] + self.dims[head:][::-1])
        self.parts = [g.shape[0] // (shards * pieces) // k for g, k in zip(arrays, steps)]
        self.folded = [
            g.reshape((2,) * self.depth + (p * k, g.shape[1])) for g, p, k in zip(arrays, self.parts, steps)
        ]
        self.tails = [g.shape[self.depth :] for g in self.folded]
        self.pairs = (max(self.parts, default=0) + 1) // 2
        self.turns = self.pairs + lag * (self.depth - 1)

    def results(self):
        return [jax.ShapeDtypeStruct(tail, f32) for tail in self.tails]

    def scratch(self):
        if not self.n:
            return []
        held = [pltpu.VMEM((2,) * (self.depth - 1) + tail, bf16) for tail in self.tails]
        for j in range(self.depth):
            held += [pltpu.VMEM((2,) * (self.depth - 1 - j) + tail, bf16) for tail in self.tails]
        sem = pltpu.SemaphoreType.DMA((self.depth, self.n, max(self.parts)))
        return held + [sem, sem, pltpu.SemaphoreType.DMA((self.n, max(self.parts)))]

    def bind(self, full, shares, scratch):
        n = self.n
        self.partner, self.mine = [], []
        if not n:
            return
        self.full, self.shares, self.own = full, shares, scratch[:n]
        self.landed = [scratch[n * (j + 1) : n * (j + 2)] for j in range(self.depth)]
        self.send, self.recv, self.own_sem = scratch[n * (self.depth + 1) :]
        for axis, bit in self.bits:
            here = lax.axis_index(axis)
            self.mine.append((here // bit) % 2)
            self.partner.append({axis: here + bit - 2 * bit * ((here // bit) % 2)})

    def greet(self, barrier):
        for who in self.partner:
            pl.semaphore_signal(barrier, inc=1, device_id=who, device_id_type=MESH)
        return len(self.partner)

    def spot(self, a, c):
        return pl.ds(pl.multiple_of(c * self.steps[a], self.steps[a]), self.steps[a])

    def pick(self, remaining, dim, index, a, c):
        return tuple(index if d == dim else slice(None) for d in remaining) + (self.spot(a, c), slice(None))

    def rest(self, order, j):
        return [d for d in self.dims if d not in order[:j]]

    def copy(self, j, a, c, order):
        source = self.full[a] if j == 0 else self.landed[j - 1][a]
        d = order[j]
        return pltpu.make_async_remote_copy(
            source.at[self.pick(self.rest(order, j), d, 1 - self.mine[d], a, c)],
            self.landed[j][a].at[self.pick(self.rest(order, j + 1), None, None, a, c)],
            self.send.at[j, a, c],
            self.recv.at[j, a, c],
            device_id=self.partner[d],
            device_id_type=MESH,
        )

    def own_copy(self, a, c, order):
        return pltpu.make_async_copy(
            self.full[a].at[self.pick(self.dims, order[0], self.mine[order[0]], a, c)],
            self.own[a].at[self.pick(self.rest(order, 1), None, None, a, c)],
            self.own_sem.at[a, c],
        )

    def begin(self, a, c, order):
        self.copy(0, a, c, order).start()
        self.own_copy(a, c, order).start()

    def step(self, j, a, c, order):
        self.copy(j, a, c, order).wait_recv()
        where = self.pick(self.rest(order, j + 1), None, None, a, c)
        d = order[j]
        if j == 0:
            self.own_copy(a, c, order).wait()
            kept = self.own[a][where]
        else:
            kept = self.landed[j - 1][a][self.pick(self.rest(order, j), d, self.mine[d], a, c)]
        if j == self.depth - 1:
            self.shares[a][self.spot(a, c), :] = kept.astype(f32) + self.landed[j][a][where].astype(f32)
        else:
            self.landed[j][a][where] = kept + self.landed[j][a][where]
            self.copy(j + 1, a, c, order).start()

    def each(self, i, fn):
        for parity in (0, 1):
            c = 2 * i + parity
            for a in range(self.n):

                @pl.when(jnp.logical_and(c >= 0, c < self.parts[a]))
                def _():
                    fn(a, c, self.orders[parity])

    def start(self):
        for i in range(share_ahead if self.n else 0):
            self.each(i, self.begin)

    def tick(self, i):
        if self.n:
            self.each(i + share_ahead, self.begin)
            for j in range(self.depth):
                self.each(i - self.lag * j, functools.partial(self.step, j))

    def finish(self):
        def sent(i, _):
            for j in range(self.depth):
                self.each(i, lambda a, c, order: self.copy(j, a, c, order).wait_send())
            return 0

        if self.n:
            lax.fori_loop(0, self.pairs, sent, 0)


def tp_sum(partial, epilogue, extras, extra_outs, chunk, ident, out_dtype=bf16, scatters=(), line_too=False, steps=16):
    line = Line(partial.shape, chunk, epilogue, extras, out_dtype)
    share = Halving(scatters, steps)
    n_ex, n_out, n_sc = len(extras), len(extra_outs), len(scatters)
    n_line, n_share = len(line.scratch()), len(share.scratch())

    def kernel(*refs):
        refs = list(refs)

        def take_refs(n):
            taken = refs[:n]
            del refs[:n]
            return taken

        (p_ref,) = take_refs(1)
        ins = take_refs(n_ex)
        full = take_refs(n_sc)
        (out_ref,) = take_refs(1)
        outs = take_refs(n_out)
        shares = take_refs(n_sc)
        line.bind(p_ref, ins, out_ref, outs, take_refs(n_line))
        share.bind(full, shares, take_refs(n_share))
        tail, tail_send, tail_recv = take_refs(3) if line_too else (None, None, None)
        barrier = pltpu.get_barrier_semaphore()
        line.begin(barrier, share.greet(barrier), line_too)
        share.start()

        def tail_copy(k):
            to = (line.mate, line.across)[k]
            source = shares[-1].at[pl.ds(shares[-1].shape[0] - 8, 8)] if k == 0 else tail.at[2]
            return pltpu.make_async_remote_copy(
                source, tail.at[k], tail_send.at[k], tail_recv.at[k], device_id={"tp": to}, device_id_type=MESH
            )

        def tail_step(k):
            last = pl.ds(shares[-1].shape[0] - 8, 8)
            if k > 0:
                tail_copy(k - 1).wait()
            if k == 1:
                tail[2] = shares[-1][last, :] + tail[0]
            if k == 2:
                shares[-1][last, :] = tail[2] + tail[1]
            else:
                tail_copy(k).start()

        ready = (share.parts[-1] + 1) // 2 + share.lag * (share.depth - 1) if n_sc else 0

        def turn(i, _):
            for parity in (0, 1):
                line.tick(2 * i + parity)
            share.tick(i)
            for k in range(3 if line_too else 0):

                @pl.when(i == ready + k)
                def _():
                    tail_step(k)

            return 0

        turns = max((line.ticks() + 1) // 2, share.turns if n_sc else 0, ready + 3 if line_too else 0)
        lax.fori_loop(0, turns, turn, 0)
        line.finish()
        share.finish()

    buffers = []
    if line_too:
        pair_sem = pltpu.SemaphoreType.DMA((2,))
        buffers += [pltpu.VMEM((3, 8, scatters[-1].shape[-1]), f32), pair_sem, pair_sem]
    return pl.pallas_call(
        kernel,
        out_shape=[jax.ShapeDtypeStruct(partial.shape, out_dtype)] + list(extra_outs) + share.results(),
        in_specs=[HBM] * (1 + n_ex + n_sc),
        out_specs=[VMEM] * (1 + n_out + n_sc),
        scratch_shapes=line.scratch() + share.scratch() + buffers,
        compiler_params=pltpu.CompilerParams(
            collective_id=ident, has_side_effects=True, vmem_limit_bytes=56 << 20
        ),
    )(partial, *extras, *share.folded)


def plain_end(c, rows, total, ins, out_ref, outs):
    out_ref[rows, :] = total.astype(out_ref.dtype)


def norm_end(c, rows, total, ins, out_ref, outs):
    source_ref, gain_ref = ins
    middle = source_ref[rows, :].astype(f32) + total
    outs[0][rows, :] = middle
    out_ref[rows, :] = (middle * rms_scale(middle) * gain_ref[...]).astype(bf16)


def add_end(c, rows, total, ins, out_ref, outs):
    out_ref[rows, :] = (ins[0][rows, :] + total).astype(bf16)


def norm_back_end(c, rows, total, ins, out_ref, outs):
    source = ins[0][rows, :].astype(f32)
    inv = rms_scale(source)
    weighted = total * ins[1][...]
    back = inv * weighted - source * (inv * inv * inv) * jnp.mean(weighted * source, axis=-1, keepdims=True)
    result = ins[2][rows, :] + back
    if outs:
        outs[0][rows, :] = result
    out_ref[rows, :] = result.astype(bf16)


halo = 16
tile_cols = 256


def front(hidden, in_half, small, gains, seqs, at_conv, taps, low_len, ident):
    rows, width = hidden.shape
    local = rows // seqs
    part, inner = in_half.shape[1:]
    shards, pieces = lax.axis_size("shard"), lax.axis_size("ctx")
    long = local + halo
    tiles = inner // tile_cols
    line = Line((low_len, rows), 80, plain_end, [], f32)
    n_line = len(line.scratch())

    def kernel(
        hid_ref, tail_ref, in_ref, small_ref, gain_ref,
        in_out, small_out, gain_out, normed_out, z_out, ext_out, pre_out, act_out, low_out,
        own_w, got_w, edge, normed, ext_n, acc, z_val, conv_f, ext_c, pre, act, low_acc, small_all, gain_all,
        send, recv, edge_sem, own_sem, out_sem, *rest
    ):
        me, ctx = lax.axis_index("shard"), lax.axis_index("ctx")
        barrier = pltpu.get_barrier_semaphore()
        line.bind(rest[0], [], low_out, [], list(rest))
        for step in range(1, shards):
            pl.semaphore_signal(barrier, inc=1, device_id={"shard": lax.rem(me + step, shards)}, device_id_type=MESH)
        pl.semaphore_signal(barrier, inc=1, device_id={"ctx": lax.rem(ctx + pieces - 1, pieces)}, device_id_type=MESH)
        load = pltpu.make_async_copy(in_ref, own_w, own_sem.at[0])
        load.start()
        small_size, gain_size = small_ref.shape[1], gain_ref.shape[1]
        small_at = pl.ds(pl.multiple_of(me * small_size, small_size), small_size)
        gain_at = pl.ds(pl.multiple_of(me * gain_size, gain_size), gain_size)
        small_all[:, small_at] = small_ref[...]
        gain_all[:, gain_at] = gain_ref[...]
        line.greet(barrier, shards)
        edge_copy = pltpu.make_async_remote_copy(
            tail_ref, edge, edge_sem.at[0], edge_sem.at[1],
            device_id={"ctx": lax.rem(ctx + 1, pieces)}, device_id_type=MESH,
        )
        copies = {}
        for step in range(1, shards):
            peer = {"shard": lax.rem(me + step, shards)}
            moves = [(gain_ref, gain_all.at[:, gain_at]), (small_ref, small_all.at[:, small_at])]
            moves += [(in_ref.at[c], got_w.at[step - 1, c]) for c in range(2)]
            for k, (source, target) in enumerate(moves):
                copies[step, k] = pltpu.make_async_remote_copy(
                    source, target, send.at[step, k], recv.at[step, k], device_id=peer, device_id_type=MESH
                )
        for k in range(4):
            for step in range(1, shards):
                copies[step, k].start()
            if k == 0:
                edge_copy.start()
        for step in range(1, shards):
            copies[step, 0].wait_recv()
        gain = gain_all[0:1, :].astype(f32)

        def norm_rows(i, _):
            at = pl.ds(pl.multiple_of(i * 16, 16), 16)
            source = hid_ref[at, :].astype(f32)
            value = (source * rms_scale(source) * gain).astype(bf16)
            normed[at, :] = value
            seq = i // (local // 16)
            ext_n[pl.ds(pl.multiple_of(i * 16 + (seq + 1) * halo, 16), 16), :] = value
            return 0

        lax.fori_loop(0, rows // 16, norm_rows, 0)
        edge_copy.wait_recv()
        for seq in range(seqs):
            source = edge[seq].astype(f32)
            value = source * rms_scale(source) * gain * (ctx > 0).astype(f32)
            ext_n[seq * long : seq * long + halo, :] = value.astype(bf16)
        outs = [(normed, normed_out)]
        pltpu.make_async_copy(normed, normed_out, out_sem.at[0]).start()

        def cols(c, j):
            return pl.ds(pl.multiple_of(c * inner + j * tile_cols, tile_cols), tile_cols)

        def finish_conv(j):
            here = pl.ds(pl.multiple_of(j * tile_cols, tile_cols), tile_cols)
            value = acc[:, cols(0, j)].astype(bf16)
            ext_c[:, here] = value
            conv_f[...] = value.astype(f32)
            weights = small_all[at_conv : at_conv + 16, here].astype(f32)
            for seq in range(seqs):
                for k in range(local // 64):
                    first = seq * long + halo + k * 64
                    total = weights[taps : taps + 1]
                    for tap in range(taps):
                        total = total + weights[tap : tap + 1] * conv_f[first - taps + 1 + tap : first - taps + 1 + tap + 64, :]
                    to = slice(seq * local + k * 64, seq * local + (k + 1) * 64)
                    pre[to, here] = total
                    act[to, here] = jax.nn.silu(total).astype(bf16)
            low = outer_cols(small_all[0:low_len, here], act[:, here])
            low_acc[...] = low_acc[...] + low

        def finish_gate(j):
            here = pl.ds(pl.multiple_of(j * tile_cols, tile_cols), tile_cols)
            for seq in range(seqs):
                z_val[seq * local : (seq + 1) * local, here] = acc[seq * long + halo : (seq + 1) * long, cols(1, j)]

        low_acc[...] = jnp.zeros_like(low_acc)
        own_place = pl.ds(pl.multiple_of(me * part, part), part)
        load.wait()
        own_save = pltpu.make_async_copy(own_w, in_out.at[:, own_place], own_sem.at[1])
        own_save.start()
        saves = []
        for step in range(shards):
            owner = lax.rem(me - step + shards, shards)
            place = pl.ds(pl.multiple_of(owner * part, part), part)
            last = step == shards - 1
            if last:
                for other in range(1, shards):
                    copies[other, 1].wait_recv()
            for c in range(2):
                weight = own_w.at[c] if step == 0 else got_w.at[step - 1, c]
                if step > 0:
                    copies[step, 2 + c].wait_recv()

                def matmul(j, _):
                    here = pl.ds(pl.multiple_of(j * tile_cols, tile_cols), tile_cols)
                    value = jnp.dot(ext_n[:, place], weight[:, here], preferred_element_type=f32)
                    acc[:, cols(c, j)] = value if step == 0 else acc[:, cols(c, j)] + value
                    if last:
                        (finish_conv, finish_gate)[c](j)
                    return 0

                lax.fori_loop(0, tiles, matmul, 0)
            if step > 0:
                saves.append(pltpu.make_async_copy(got_w.at[step - 1], in_out.at[:, place], own_sem.at[1 + step]))
                saves[-1].start()
        line.p[...] = low_acc[...].astype(bf16)
        outs += [(z_val, z_out), (ext_c, ext_out), (pre, pre_out), (act, act_out), (small_all, small_out), (gain_all, gain_out)]
        for k, (source, target) in enumerate(outs):
            if k:
                pltpu.make_async_copy(source, target, out_sem.at[k]).start()
        line.start()
        for c in range(line.ticks()):
            line.tick(c)
        line.finish()
        for save in saves + [own_save]:
            save.wait()
        for k, (source, target) in enumerate(outs):
            pltpu.make_async_copy(source, target, out_sem.at[k]).wait()
        for copy in copies.values():
            copy.wait_send()
        edge_copy.wait_send()

    sds = jax.ShapeDtypeStruct
    tails = hidden.reshape(seqs, local, width)[:, local - halo :]
    return pl.pallas_call(
        kernel,
        out_shape=[
            sds((2, shards * part, inner), bf16),
            sds((small.shape[0], small.shape[1] * shards), bf16),
            sds((gains.shape[0], gains.shape[1] * shards), bf16),
            sds((rows, width), bf16),
            sds((rows, inner), f32),
            sds((seqs * long, inner), bf16),
            sds((rows, inner), f32),
            sds((rows, inner), bf16),
            sds((low_len, rows), f32),
        ],
        in_specs=[VMEM, HBM, HBM, VMEM, VMEM],
        out_specs=[HBM] * 8 + [VMEM],
        scratch_shapes=[
            pltpu.VMEM((2, part, inner), bf16),
            pltpu.VMEM((max(shards - 1, 1), 2, part, inner), bf16),
            pltpu.VMEM((seqs, halo, width), bf16),
            pltpu.VMEM((rows, width), bf16),
            pltpu.VMEM((seqs * long, width), bf16),
            pltpu.VMEM((seqs * long, 2 * inner), f32),
            pltpu.VMEM((rows, inner), f32),
            pltpu.VMEM((seqs * long, tile_cols), f32),
            pltpu.VMEM((seqs * long, inner), bf16),
            pltpu.VMEM((rows, inner), f32),
            pltpu.VMEM((rows, inner), bf16),
            pltpu.VMEM((low_len, rows), f32),
            pltpu.VMEM((small.shape[0], small.shape[1] * shards), bf16),
            pltpu.VMEM((gains.shape[0], gains.shape[1] * shards), bf16),
            pltpu.SemaphoreType.DMA((shards, 4)),
            pltpu.SemaphoreType.DMA((shards, 4)),
            pltpu.SemaphoreType.DMA((2,)),
            pltpu.SemaphoreType.DMA((shards + 1,)),
            pltpu.SemaphoreType.DMA((7,)),
        ]
        + line.scratch(),
        compiler_params=pltpu.CompilerParams(
            collective_id=ident, has_side_effects=True, vmem_limit_bytes=56 << 20
        ),
    )(hidden, tails, in_half, small, gains)


piece = 16
forward_piece = 32
slots_held = 4
unroll = 4


def spread(flat_ref, natural, first):
    for j in range(8):
        flat_ref[pl.ds(first * 8 + j, 8, stride=8), :] = natural[:, j * 128 : (j + 1) * 128]


def unspread(flat_ref, first):
    return jnp.concatenate([flat_ref[pl.ds(first * 8 + j, 8, stride=8), :] for j in range(8)], axis=1)


def tile(ref, t):
    return ref[pl.ds(pl.multiple_of(t * 8, 8), 8), :]


def row(ref, t, n, states):
    return ref[pl.ds(t * states + n, 8, stride=0), :]


def exchange(ends, got, send, recv, seq, width):
    me = lax.axis_index("ctx")
    copies = []
    for step in range(1, width):
        copies.append(
            pltpu.make_async_remote_copy(
                ends.at[seq],
                got.at[me, seq],
                send.at[seq, step],
                recv.at[seq, step],
                device_id={"ctx": lax.rem(me + step, width)},
                device_id_type=MESH,
            )
        )
        copies[-1].start()
    return copies


def ctx_greet(width):
    me = lax.axis_index("ctx")
    barrier = pltpu.get_barrier_semaphore()
    for step in range(1, width):
        pl.semaphore_signal(barrier, inc=1, device_id={"ctx": lax.rem(me + step, width)}, device_id_type=MESH)
    return barrier


def entering(got, seq, rate_ref, states, width, reverse):
    me = lax.axis_index("ctx")
    result = []
    for n in range(states):
        value = jnp.zeros((8, 128), f32)
        for k in reversed(range(width)) if reverse else range(width):
            new = jnp.exp2(got[k, seq, states] * rate_ref[n]) * value + got[k, seq, n]
            value = jnp.where(me < k if reverse else me > k, new, value)
        result.append(value)
    return result


def spread_rows(low_ref, first, out_ref):
    states, slots = 16, low_ref.shape[1]

    def lanes(k, _):
        block = low_ref[first : first + states, pl.ds(pl.multiple_of(k * 128, 128), 128)]
        for i in range(128):
            to = pl.ds(pl.multiple_of((k * 128 + i) * states, states), states)
            out_ref[to, :] = jnp.broadcast_to(block[:, i : i + 1], (states, 128))
        return 0

    lax.fori_loop(0, slots // 128, lanes, 0)


def scan_forward(low_all, act, gate_z, small, rate, out_parts, seqs, rank, at_step, at_bias, at_skip, ident):
    rows, channels = act.shape
    shards, _, part = out_parts.shape
    local = rows // seqs
    states = rate.shape[0]
    width = lax.axis_size("ctx")
    pieces = local // forward_piece

    def kernel(
        low_ref, act_ref, z_ref, small_ref, rate_ref, w_ref,
        scan_ref, gated_ref, mixed_ref, pre_ref, kept_ref, enter_ref, size3, drive3,
        y3, ends, got, held, b_ref, c_ref, low_t, w_own, send, recv, out_sem, w_sem,
    ):
        barrier = ctx_greet(width)
        load = pltpu.make_async_copy(w_ref, w_own, w_sem)
        load.start()
        low_t[...] = low_ref[0:rank, :].T.astype(bf16)
        bias = small_ref[at_bias : at_bias + 16, :].astype(f32)[0:1]
        for j in range(channels // 256):
            here = slice(j * 256, (j + 1) * 256)
            value = jnp.dot(low_t[...], small_ref[at_step : at_step + rank, here], preferred_element_type=f32)
            pre_ref[:, here] = value + bias[:, here]
        spread_rows(low_ref, rank, b_ref)
        spread_rows(low_ref, rank + states, c_ref)

        def lay(i, _):
            first = pl.multiple_of(i * 16, 16)
            act_block = act_ref[pl.ds(first, 16), :].astype(f32)
            size = jax.nn.softplus(pre_ref[pl.ds(first, 16), :])
            drive = size * act_block
            for h in range(2):
                spread(size3, size[h * 8 : h * 8 + 8], first + h * 8)
                spread(drive3, drive[h * 8 : h * 8 + 8], first + h * 8)
            return 0

        lax.fori_loop(0, rows // 16, lay, 0)
        pl.semaphore_wait(barrier, width - 1)
        copies = []
        for seq in range(seqs):

            def first_pass(i, carried):
                values, total = list(carried[:-1]), carried[-1]
                for u in range(unroll):
                    t = seq * local + i * unroll + u
                    s, d = tile(size3, t), tile(drive3, t)
                    total = total + s
                    for n in range(states):
                        values[n] = jnp.exp2(s * rate_ref[n]) * values[n] + d * row(b_ref, t, n, states)
                return tuple(values) + (total,)

            zero = tuple(jnp.zeros((8, 128), f32) for _ in range(states + 1))
            done = lax.fori_loop(0, local // unroll, first_pass, zero)
            for n in range(states + 1):
                ends[seq, n] = done[n]
            copies.append(exchange(ends, got, send, recv, seq, width))
        me = lax.axis_index("ctx")
        for seq in range(seqs):
            for copy in copies[seq]:
                copy.wait()
            got[me, seq] = ends[seq]
            start = entering(got, seq, rate_ref, states, width, False)
            for n in range(states):
                enter_ref[seq, n] = start[n]

            def save(k, slot):
                return pltpu.make_async_copy(
                    held.at[slot], kept_ref.at[pl.ds(seq * local + k * forward_piece, forward_piece)], out_sem.at[slot]
                )

            def one_piece(k, carried):
                slot = lax.rem(k, 2)

                @pl.when(k >= 2)
                def _():
                    save(k - 2, slot).wait()

                def second_pass(i, values):
                    values = list(values)
                    for u in range(unroll):
                        inside = i * unroll + u
                        t = seq * local + k * forward_piece + inside
                        s, d = tile(size3, t), tile(drive3, t)
                        acc = [None] * 4
                        for n in range(states):
                            values[n] = jnp.exp2(s * rate_ref[n]) * values[n] + d * row(b_ref, t, n, states)
                            held[slot, inside, n] = values[n]
                            part = values[n] * row(c_ref, t, n, states)
                            acc[n % 4] = part if acc[n % 4] is None else acc[n % 4] + part
                        y3[pl.ds(pl.multiple_of(t * 8, 8), 8), :] = (acc[0] + acc[1]) + (acc[2] + acc[3])
                    return tuple(values)

                carried = lax.fori_loop(0, forward_piece // unroll, second_pass, carried)
                save(k, slot).start()
                return carried

            lax.fori_loop(0, pieces, one_piece, tuple(start))
            for k in (pieces - 2, pieces - 1):
                save(k, k % 2).wait()

        skip = small_ref[at_skip : at_skip + 16, :].astype(f32)[0:1]

        def back(i, _):
            first = pl.multiple_of(i * 16, 16)
            here = pl.ds(first, 16)
            value = jnp.concatenate([unspread(y3, first), unspread(y3, first + 8)], axis=0)
            value = value + skip * act_ref[here, :].astype(f32)
            scan_ref[here, :] = value
            gated_ref[here, :] = (value * jax.nn.silu(z_ref[here, :])).astype(bf16)
            return 0

        lax.fori_loop(0, rows // 16, back, 0)
        load.wait()
        for k in range(shards):
            for j in range(-(-part // 256)):
                span = min(256, part)
                value = jnp.dot(gated_ref[...], w_own[k, :, j * span : (j + 1) * span], preferred_element_type=f32)
                mixed_ref[:, k * part + j * span : k * part + (j + 1) * span] = value.astype(bf16)

    flat = jax.ShapeDtypeStruct((rows * 8, 128), f32)
    return pl.pallas_call(
        kernel,
        out_shape=[
            jax.ShapeDtypeStruct((rows, channels), f32),
            jax.ShapeDtypeStruct((rows, channels), bf16),
            jax.ShapeDtypeStruct((rows, shards * part), bf16),
            jax.ShapeDtypeStruct((rows, channels), f32),
            jax.ShapeDtypeStruct((rows, states, 8, 128), f32),
            jax.ShapeDtypeStruct((seqs, states, 8, 128), f32),
            flat,
            flat,
        ],
        in_specs=[VMEM] * 5 + [HBM],
        out_specs=[VMEM] * 4 + [HBM, VMEM, VMEM, VMEM],
        scratch_shapes=[
            pltpu.VMEM((rows * 8, 128), f32),
            pltpu.VMEM((seqs, states + 1, 8, 128), f32),
            pltpu.VMEM((width, seqs, states + 1, 8, 128), f32),
            pltpu.VMEM((2, forward_piece, states, 8, 128), f32),
            pltpu.VMEM((rows * states, 128), f32),
            pltpu.VMEM((rows * states, 128), f32),
            pltpu.VMEM((rows, rank), bf16),
            pltpu.VMEM(out_parts.shape, bf16),
            pltpu.SemaphoreType.DMA((seqs, width)),
            pltpu.SemaphoreType.DMA((seqs, width)),
            pltpu.SemaphoreType.DMA((2,)),
            pltpu.SemaphoreType.DMA,
        ],
        compiler_params=pltpu.CompilerParams(
            collective_id=ident, has_side_effects=True, vmem_limit_bytes=48 << 20
        ),
    )(low_all, act, gate_z, small, rate, out_parts)


def sublane_sums(parts):
    at = lax.broadcasted_iota(jnp.int32, (8, 128), 0)
    for shift in (4, 2, 1):
        low = (at // shift) % 2 == 0
        half = len(parts) // 2
        merged = []
        for one, two in zip(parts[:half], parts[half:]):
            merged.append(
                jnp.where(low, one + pltpu.roll(one, 8 - shift, 0), two + pltpu.roll(two, shift, 0))
            )
        parts = merged
    return parts[0]


def scan_backward(size3, drive3, grad, low_all, rank, rate, kept, enter, seqs, ident, partial, epilogue, extras, chunk, scatters):
    rows, channels = grad.shape
    local = rows // seqs
    states = rate.shape[0]
    width = lax.axis_size("ctx")
    pieces = local // piece
    early = 2
    unroll_b = 2
    line = Line(partial.shape, chunk, epilogue, extras, bf16)
    share = Halving(scatters, 16, 1)
    n_line, n_ex, n_sc = len(line.scratch()), len(extras), len(scatters)

    def kernel(*refs):
        refs = list(refs)

        def take_refs(n):
            taken = refs[:n]
            del refs[:n]
            return taken

        size_ref, drive_ref, grad_ref, low_ref, rate_ref, kept_ref, enter_ref, p_ref = take_refs(8)
        ins, full = take_refs(n_ex), take_refs(n_sc)
        tb3, sd3, bg_ref, cg_ref, dec_ref, sum_ref = take_refs(6)
        shares = take_refs(n_sc)
        grad3, b_ref, c_ref, ends, got, held, bpart, cpart, prior, send, recv, in_sem = take_refs(12)
        line.bind(p_ref, ins, sum_ref, [], take_refs(n_line))
        share.bind(full, shares, refs)
        barrier = ctx_greet(width)
        line.begin(barrier, width - 1 + share.greet(barrier))
        share.start()
        spread_rows(low_ref, rank, b_ref)
        spread_rows(low_ref, rank + states, c_ref)
        share.tick(0)

        def lay(i, _):
            first = pl.multiple_of(i * 8, 8)
            spread(grad3, grad_ref[pl.ds(first, 8), :], first)
            return 0

        lax.fori_loop(0, rows // 8, lay, 0)

        def fetch(g):
            first = (g // pieces) * local + (pieces - 1 - g % pieces) * piece
            slot = g % slots_held
            return pltpu.make_async_copy(kept_ref.at[pl.ds(first, piece)], held.at[slot], in_sem.at[slot])

        for g in range(slots_held - 1):
            fetch(g).start()

        copies = []
        for seq in range(seqs):

            def first_pass(i, carried):
                values, total = list(carried[:-1]), carried[-1]
                for u in range(unroll):
                    t = seq * local + local - 1 - (i * unroll + u)
                    s, g = tile(size_ref, t), tile(grad3, t)
                    total = total + s
                    for n in range(states):
                        values[n] = jnp.exp2(s * rate_ref[n]) * (values[n] + g * row(c_ref, t, n, states))
                return tuple(values) + (total,)

            zero = tuple(jnp.zeros((8, 128), f32) for _ in range(states + 1))
            done = zero
            for half in range(early):
                span = local // unroll // early
                done = lax.fori_loop(half * span, (half + 1) * span, first_pass, done)
                line.tick(seq * early + half)
            for n in range(states + 1):
                ends[seq, n] = done[n]
            copies.append(exchange(ends, got, send, recv, seq, width))
            share.tick(1 + seq)
        me = lax.axis_index("ctx")
        for n in range(states):
            dec_ref[n] = jnp.zeros((8, 128), f32)
        for seq in range(seqs):
            for copy in copies[seq]:
                copy.wait()
            got[me, seq] = ends[seq]
            start = entering(got, seq, rate_ref, states, width, True)
            fetch(seq * pieces).wait()

            def one_slot(slot, k, inside, adjoint, decays, prior_at):
                t = seq * local + k * piece + inside
                s, d, g = tile(size_ref, t), tile(drive_ref, t), tile(grad3, t)
                tb, sd = [None] * 2, [None] * 2
                b_parts, c_parts = [], []
                for n in range(states):
                    total = adjoint[n] + g * row(c_ref, t, n, states)
                    c_parts.append(held[slot, inside, n] * g)
                    b_parts.append(total * d)
                    through = total * row(b_ref, t, n, states)
                    adjoint[n] = jnp.exp2(s * rate_ref[n]) * total
                    kept_part = adjoint[n] * prior_at(n)
                    through_size = kept_part * rate_ref[n]
                    decays[n] = decays[n] + kept_part * s
                    tb[n % 2] = through if tb[n % 2] is None else tb[n % 2] + through
                    sd[n % 2] = through_size if sd[n % 2] is None else sd[n % 2] + through_size
                here = pl.ds(pl.multiple_of(t * 8, 8), 8)
                tb3[here, :] = tb[0] + tb[1]
                sd3[here, :] = sd[0] + sd[1]
                for h in range(states // 8):
                    spot = pl.ds(pl.multiple_of(inside * states + h * 8, 8), 8)
                    bpart[spot, :] = sublane_sums(b_parts[h * 8 : h * 8 + 8])
                    cpart[spot, :] = sublane_sums(c_parts[h * 8 : h * 8 + 8])

            def one_piece(back_k, carried):
                k = pieces - 1 - back_k
                place = seq * pieces + back_k
                slot = place % slots_held

                @pl.when(place + slots_held - 1 < seqs * pieces)
                def _():
                    fetch(place + slots_held - 1).start()

                def slots(i, carried):
                    adjoint, decays = list(carried[:states]), list(carried[states:])
                    for u in range(unroll_b):
                        inside = piece - 1 - (i * unroll_b + u)
                        one_slot(slot, k, inside, adjoint, decays, lambda n: held[slot, inside - 1, n])
                    return tuple(adjoint) + tuple(decays)

                carried = lax.fori_loop(0, piece // unroll_b - 1, slots, carried)
                adjoint, decays = list(carried[:states]), list(carried[states:])
                for inside in reversed(range(1, unroll_b)):
                    one_slot(slot, k, inside, adjoint, decays, lambda n: held[slot, inside - 1, n])

                @pl.when(k > 0)
                def _():
                    fetch(place + 1).wait()
                    prior[...] = held[(place + 1) % slots_held, piece - 1]

                @pl.when(k == 0)
                def _():
                    prior[...] = enter_ref[seq]

                one_slot(slot, k, 0, adjoint, decays, lambda n: prior[n])
                ones = jnp.ones((8, 128), bf16)
                for part, out in ((bpart, bg_ref), (cpart, cg_ref)):
                    sums = outer_cols(ones, part[...].astype(bf16))
                    out[pl.ds(seq * pieces + k, 1)] = sums[None]
                @pl.when(place % 2 == 0)
                def _():
                    line.tick(seqs * early + place // 2)

                @pl.when(place % 5 == 0)
                def _():
                    share.tick(1 + seqs + place // 5)

                return tuple(adjoint) + tuple(decays)

            zero = tuple(jnp.zeros((8, 128), f32) for _ in range(states))
            carried = lax.fori_loop(0, pieces, one_piece, tuple(start) + zero)
            for n in range(states):
                dec_ref[n] = dec_ref[n] + carried[states + n]

        for c in range(seqs * early + (seqs * pieces + 1) // 2, line.ticks()):
            line.tick(c)
        for i in range(1 + seqs + (seqs * pieces + 4) // 5, share.turns):
            share.tick(i)
        line.finish()
        share.finish()

    flat = jax.ShapeDtypeStruct((rows * 8, 128), f32)
    sums = jax.ShapeDtypeStruct((rows // piece, 8, piece * states), f32)
    return pl.pallas_call(
        kernel,
        out_shape=[flat, flat, sums, sums, jax.ShapeDtypeStruct((states, 8, 128), f32),
                   jax.ShapeDtypeStruct(partial.shape, bf16)] + share.results(),
        in_specs=[VMEM] * 5 + [HBM, VMEM] + [HBM] * (1 + n_ex + n_sc),
        out_specs=[VMEM] * (6 + n_sc),
        scratch_shapes=[pltpu.VMEM((rows * 8, 128), f32)]
        + [pltpu.VMEM((rows * states, 128), f32)] * 2
        + [
            pltpu.VMEM((seqs, states + 1, 8, 128), f32),
            pltpu.VMEM((width, seqs, states + 1, 8, 128), f32),
            pltpu.VMEM((slots_held, piece, states, 8, 128), f32),
            pltpu.VMEM((piece * states, 128), f32),
            pltpu.VMEM((piece * states, 128), f32),
            pltpu.VMEM((states, 8, 128), f32),
            pltpu.SemaphoreType.DMA((seqs, width)),
            pltpu.SemaphoreType.DMA((seqs, width)),
            pltpu.SemaphoreType.DMA((slots_held,)),
        ]
        + line.scratch()
        + share.scratch(),
        compiler_params=pltpu.CompilerParams(
            collective_id=ident, has_side_effects=True, vmem_limit_bytes=62 << 20
        ),
    )(size3, drive3, grad, low_all, rate, kept, enter, partial, *extras, *share.folded)


def feed_forward(mixed_part, hidden, gain, ffn_grad, gate_w, down_parts, ident):
    rows, width = hidden.shape
    shards, ffn, part = down_parts.shape
    chunk = 32
    block = 4 * chunk
    tile = ffn // 4
    blocks = rows // block
    fore = Line(mixed_part.shape, chunk, norm_end, [], bf16)
    after = Line(mixed_part.shape, chunk, norm_back_end, [], bf16)
    n_line = len(fore.scratch())
    behind = 5
    wtile = 256

    def kernel(
        p_ref, hid_ref, gain_ref, fg_ref, gate_ref, up_ref, down_ref,
        ffn_out, mid_out, mix_ref, midg_ref, gsum_ref, both_out, dw_out,
        normed, middle, hid_v, gg_v, ug_v, ffn_v, ffn_acc, back_acc, gate_v, up_v, down_v, stage, stage_d, load_sem, save_sem, *rest
    ):
        barrier = pltpu.get_barrier_semaphore()
        fore.bind(p_ref, [], normed, [middle], rest[:n_line])
        after.bind(rest[n_line], [], mix_ref, [midg_ref], rest[n_line:])
        fore.ins = [hid_ref, gain_ref]
        after.ins = [middle, gain_ref, fg_ref]
        loads = [
            pltpu.make_async_copy(a, b, load_sem.at[i])
            for i, (a, b) in enumerate(((gate_ref, gate_v), (up_ref, up_v), (down_ref, down_v)))
        ]
        fore.begin(barrier, 0)
        for load in loads:
            load.start()
        gsum_ref[...] = jnp.zeros_like(gsum_ref)
        lead = 4 + fore.lag

        def warm(c, _):
            fore.tick(c)
            return 0

        lax.fori_loop(0, lead, warm, 0)
        for load in loads:
            load.wait()
        outer = jnp.logical_not(fore.middle)

        def step(s, _):
            b, j = s // 4, s % 4
            fore.tick(s + lead)
            at = pl.ds(pl.multiple_of(b * block, block), block)
            here = pl.ds(pl.multiple_of(j * tile, tile), tile)

            @pl.when(j == 0)
            def _():
                ffn_acc[...] = jnp.zeros_like(ffn_acc)
                back_acc[...] = jnp.zeros_like(back_acc)

                @pl.when(outer)
                def _():
                    for k in range(4):
                        fore.copy_c(4 * b + k).wait_recv()

            source, grad = normed[at, :], fg_ref[at, :]
            gate = jnp.dot(source, gate_v[:, here], preferred_element_type=f32)
            up = jnp.dot(source, up_v[:, here], preferred_element_type=f32)
            sig = jax.nn.sigmoid(gate)
            silu = gate * sig
            hidden_val = (silu * up).astype(bf16)
            back = sum(
                outer_cols(grad[:, k * part : (k + 1) * part], down_v[k, here, :]) for k in range(shards)
            )
            gate_back = (back * up * (sig * (1.0 + gate * (1.0 - sig)))).astype(bf16)
            up_back = (back * silu).astype(bf16)
            hid_v[at, here] = hidden_val
            gg_v[at, here] = gate_back
            ug_v[at, here] = up_back

            after.quiet_tick(s - behind)

            for k in range(shards):
                to = slice(k * part, (k + 1) * part)
                ffn_acc[:, to] += jnp.dot(hidden_val, down_v[k, here, :], preferred_element_type=f32)
            for k in range(width // 512):
                to = slice(k * 512, (k + 1) * 512)
                back_acc[:, to] += outer_cols(gate_back, gate_v[to, here]) + outer_cols(up_back, up_v[to, here])

            @pl.when(j == 3)
            def _():
                ffn_v[at, :] = ffn_acc[...].astype(bf16)
                after.p[at, :] = back_acc[...].astype(bf16)
                for k in range(block // 16):
                    product = after.p[pl.ds(pl.multiple_of(b * block + k * 16, 16), 16), :].astype(f32)
                    product = product * normed[pl.ds(pl.multiple_of(b * block + k * 16, 16), 16), :].astype(f32)
                    gsum_ref[...] += product[:8] + product[8:]

                @pl.when(outer)
                def _():
                    for k in range(4):
                        after.copy_a(4 * b + k).start()

            return 0

        steps = 4 * blocks
        lax.fori_loop(0, steps, step, 0)
        ffn_save = pltpu.make_async_copy(ffn_v, ffn_out, save_sem.at[3])
        ffn_save.start()
        mid_save = pltpu.make_async_copy(middle, mid_out, save_sem.at[4])
        mid_save.start()

        def saves(i):
            to = pl.ds(pl.multiple_of(i * wtile, wtile), wtile)
            return [
                pltpu.make_async_copy(held, out.at[to], save_sem.at[a])
                for a, (held, out) in enumerate(((stage, both_out), (stage_d, dw_out)))
            ]

        def weights(i, _):
            after.quiet_tick(steps - behind + i)
            here = pl.ds(pl.multiple_of(i * wtile, wtile), wtile)

            @pl.when(i > 0)
            def _():
                for save in saves(i - 1):
                    save.wait()

            source, grad = normed[:, here], fg_ref[:, here]
            stage[:, :ffn] = inner_rows(source, gg_v[...]).astype(bf16)
            stage[:, ffn:] = inner_rows(source, ug_v[...]).astype(bf16)
            stage_d[...] = inner_rows(grad, hid_v[...]).astype(bf16)
            for save in saves(i):
                save.start()
            return 0

        lax.fori_loop(0, width // wtile, weights, 0)
        for c in range(steps - behind + width // wtile, after.ticks()):
            after.quiet_tick(c)
        for save in saves(width // wtile - 1) + [ffn_save, mid_save]:
            save.wait()
        fore.finish(False)
        after.finish()

    sds = jax.ShapeDtypeStruct
    wide, half = sds((rows, width), f32), sds((rows, width), bf16)
    both, down = sds((width, 2 * ffn), bf16), sds((width, ffn), bf16)
    return pl.pallas_call(
        kernel,
        out_shape=[half, wide, half, wide, sds((8, width), f32), both, down],
        in_specs=[HBM, VMEM, VMEM, VMEM, HBM, HBM, HBM],
        out_specs=[HBM, HBM, VMEM, VMEM, VMEM, HBM, HBM],
        scratch_shapes=[
            pltpu.VMEM((rows, width), bf16),
            pltpu.VMEM((rows, width), f32),
            pltpu.VMEM((rows, ffn), bf16),
            pltpu.VMEM((rows, ffn), bf16),
            pltpu.VMEM((rows, ffn), bf16),
            pltpu.VMEM((rows, width), bf16),
            pltpu.VMEM((block, width), f32),
            pltpu.VMEM((block, width), f32),
            pltpu.VMEM((width, ffn), bf16),
            pltpu.VMEM((width, ffn), bf16),
            pltpu.VMEM(down_parts.shape, bf16),
            pltpu.VMEM((wtile, 2 * ffn), bf16),
            pltpu.VMEM((wtile, ffn), bf16),
            pltpu.SemaphoreType.DMA((3,)),
            pltpu.SemaphoreType.DMA((5,)),
        ]
        + fore.scratch()
        + after.scratch(),
        compiler_params=pltpu.CompilerParams(
            collective_id=ident, has_side_effects=True, vmem_limit_bytes=62 << 20
        ),
    )(mixed_part, hidden, gain, ffn_grad, gate_w[0], gate_w[1], down_parts)


def scan_tail(through_b, through_decay, sums, decay_grad, scan_grad, step_pre, pre_act, act, padded, z_half, low_all, small, normed, in_w, scatters, ident,
              seqs, low_len, rank, states, taps):
    rows, inner = act.shape
    local = rows // seqs
    long = local + halo
    shards, pieces = lax.axis_size("shard"), lax.axis_size("ctx")
    places = shards * pieces
    lane = inner // places
    line = Line((low_len, rows), 80, plain_end, [], bf16)
    tiles = inner // tile_cols
    at = low_len + rank
    lines = -(-(at + states + taps + 3) // 8) * 8
    height = -(-(lines + 8) // 32) * 32
    over = 8
    width = normed.shape[1]
    dtile = width // 8
    share = Halving(scatters, 32, 1)
    n_sc, n_share = len(scatters), len(share.scratch())

    def kernel(*refs):
        n_in = 14 + n_sc
        main(*refs[:14], *refs[n_in : n_in + 4], refs[14:n_in], refs[n_in + 4 : n_in + 4 + n_sc],
             refs[n_in + 4 + n_sc : n_in + 4 + n_sc + n_share], *refs[n_in + 4 + n_sc + n_share :])

    def main(
        tb_ref, sd_ref, sums_ref, dec_ref, sg_ref, sp_ref, pre_ref, act_ref, ext_ref, zg_ref, low_ref, small_ref, n_ref, w_ref,
        iw_out, first_ref, gsum_ref, blocks_ref, full, shares, share_scratch,
        conv_ref, w_v, acc, stage, w_sem, stage_sem, low_out, low_t, step_g, low_acc, grads, pre_g, conv_f, edge, edge_out, edge_sem, *rest
    ):
        ctx = lax.axis_index("ctx")
        barrier = pltpu.get_barrier_semaphore()
        line.bind(rest[0], [], low_out, [], list(rest))
        share.bind(full, shares, share_scratch)
        w_load = pltpu.make_async_copy(w_ref, w_v, w_sem)
        w_load.start()
        met = share.greet(barrier)
        pl.semaphore_signal(barrier, inc=1, device_id={"ctx": lax.rem(ctx + 1, pieces)}, device_id_type=MESH)

        def flat(ref, j, first, count):
            parts = [ref[pl.ds(first * 8 + j * (tile_cols // 128) + h, count, stride=8), :] for h in range(tile_cols // 128)]
            return jnp.concatenate(parts, axis=1)

        def cols(j):
            return pl.ds(pl.multiple_of(j * tile_cols, tile_cols), tile_cols)

        low_acc[...] = jnp.zeros_like(low_acc)
        grads[...] = jnp.zeros_like(grads)
        low_t[...] = low_ref[0:rank, :].astype(bf16)

        def size_tile(j, _):
            here = cols(j)
            bias_grad = jnp.zeros((8, tile_cols), f32)
            skip_grad = jnp.zeros((8, tile_cols), f32)
            for k in range(rows // 64):
                to = slice(k * 64, (k + 1) * 64)
                act_block = act_ref[to, here].astype(f32)
                size_grad = act_block * flat(tb_ref, j, k * 64, 64) + flat(sd_ref, j, k * 64, 64) * (1.0 / log2e)
                value = (size_grad * jax.nn.sigmoid(sp_ref[to, here])).astype(bf16)
                step_g[to, here] = value
                wide = value.astype(f32)
                product = sg_ref[to, here] * act_block
                for h in range(8):
                    bias_grad = bias_grad + wide[h * 8 : h * 8 + 8]
                    skip_grad = skip_grad + product[h * 8 : h * 8 + 8]
            grads[at + states + taps + 1 : at + states + taps + 2, here] = jnp.sum(bias_grad, axis=0, keepdims=True)
            grads[at + states + taps + 2 : at + states + taps + 3, here] = jnp.sum(skip_grad, axis=0, keepdims=True)
            low_acc[...] = low_acc[...] + outer_cols(small_ref[low_len : low_len + rank, here], step_g[:, here])
            return 0

        lax.fori_loop(0, tiles, size_tile, 0)
        line.p[0:rank, :] = low_acc[...].astype(bf16)
        line.p[rank : rank + 2 * states, :] = sums_ref[...].astype(bf16)
        line.greet(barrier, 1 + met)
        line.start()
        share.start()

        def save(i, c):
            return pltpu.make_async_copy(
                stage.at[i % 2],
                iw_out.at[pl.ds(pl.multiple_of(i * dtile, dtile), dtile), pl.ds(c * inner, inner)],
                stage_sem.at[i % 2],
            )

        def weight_piece(i, right, c):
            here = pl.ds(pl.multiple_of(i * dtile, dtile), dtile)
            if c == 0:
                save(i, c).wait()
            else:

                @pl.when(i >= 2)
                def _():
                    save(i, c).wait()

            stage[i % 2] = inner_rows(n_ref[:, here], right[...]).astype(bf16)
            save(i, c).start()
            value = outer_cols(right[...], w_v[c, here, :])
            if c == 1:
                acc[:, here] = value
            else:
                value = (acc[:, here] + value).astype(bf16)
                first_ref[:, here] = value
                product = value.astype(f32) * n_ref[:, here].astype(f32)
                gsum_ref[:, here] = jnp.sum(product.reshape(rows // 8, 8, dtile), axis=0)

        def step_tile(j, _):
            here = cols(j)
            grads[low_len:at, here] = jnp.dot(low_t[...], step_g[:, here], preferred_element_type=f32)
            return 0

        lax.fori_loop(0, tiles, step_tile, 0)
        grads[at : at + states, :] = dec_ref[...]
        w_load.wait()
        early = 8 // line.ticks()

        def beside(c, _):
            for i in range(early):
                weight_piece(c * early + i, zg_ref, 1)
            line.tick(c)
            return 0

        lax.fori_loop(0, line.ticks(), beside, 0)
        for i in range(early * line.ticks(), 8):
            weight_piece(i, zg_ref, 1)
        line.finish()

        def pre_tile(j, _):
            here = cols(j)
            grads[0:low_len, here] = jnp.dot(low_out[...], act_ref[:, here], preferred_element_type=f32)
            for seq in range(seqs):
                low = inner_rows(low_out[:, seq * local : (seq + 1) * local], small_ref[0:low_len, here])
                conv_f[seq * long : (seq + 1) * long, :] = ext_ref[seq * long : (seq + 1) * long, here].astype(f32)
                pre_g[seq * (local + over) : seq * (local + over) + local, here] = low
            skip = small_ref[at + states + 32 : at + states + 48, here].astype(f32)[0:1]
            bias_sum = jnp.zeros((8, tile_cols), f32)
            tap_sums = [jnp.zeros((8, tile_cols), f32) for _ in range(taps)]
            for seq in range(seqs):
                for k in range(local // 64):
                    to = slice(seq * local + k * 64, seq * local + (k + 1) * 64)
                    where = slice(seq * (local + over) + k * 64, seq * (local + over) + (k + 1) * 64)
                    act_grad = skip * sg_ref[to, here] + jax.nn.softplus(sp_ref[to, here]) * flat(tb_ref, j, seq * local + k * 64, 64)
                    value = (act_grad + pre_g[where, here]) * silu_grad(pre_ref[to, here])
                    pre_g[where, here] = value
                    first = seq * long + halo + k * 64 - taps + 1
                    products = [value * conv_f[first + tap : first + tap + 64, :] for tap in range(taps)]
                    for h in range(8):
                        bias_sum = bias_sum + value[h * 8 : h * 8 + 8]
                        for tap in range(taps):
                            tap_sums[tap] = tap_sums[tap] + products[tap][h * 8 : h * 8 + 8]
            for tap in range(taps):
                row = at + states + tap
                grads[row : row + 1, here] = jnp.sum(tap_sums[tap], axis=0, keepdims=True)
            row = at + states + taps
            grads[row : row + 1, here] = jnp.sum(bias_sum, axis=0, keepdims=True)
            return 0

        lax.fori_loop(0, tiles, pre_tile, 0)
        for seq in range(seqs):
            edge_out[seq] = pre_g[seq * (local + over) : seq * (local + over) + over, :]
        copy = pltpu.make_async_remote_copy(
            edge_out, edge, edge_sem.at[0], edge_sem.at[1],
            device_id={"ctx": lax.rem(ctx + pieces - 1, pieces)}, device_id_type=MESH,
        )
        copy.start()
        for p in range(places):
            blocks_ref[p * height : p * height + lines, :] = grads[:, p * lane : (p + 1) * lane].astype(bf16)
            blocks_ref[p * height + lines : (p + 1) * height, :] = jnp.zeros((height - lines, lane), bf16)
        copy.wait()
        inside = (ctx < pieces - 1).astype(f32)
        for seq in range(seqs):
            first = seq * (local + over) + local
            pre_g[first : first + over, :] = edge[seq] * inside

        def conv_tile(j, _):
            here = cols(j)
            weights = small_ref[at + states : at + states + 16, here].astype(f32)
            for seq in range(seqs):
                for k in range(local // 64):
                    first = seq * (local + over) + k * 64 + taps - 1
                    total = weights[0:1] * pre_g[first : first + 64, here]
                    for tap in range(1, taps):
                        total = total + weights[tap : tap + 1] * pre_g[first - tap : first - tap + 64, here]
                    conv_ref[seq * local + k * 64 : seq * local + (k + 1) * 64, here] = total.astype(bf16)
            return 0

        lax.fori_loop(0, tiles, conv_tile, 0)

        def conv_piece(i, _):
            weight_piece(i, conv_ref, 0)
            return 0

        lax.fori_loop(0, 8, conv_piece, 0)
        for i in range(share.turns if n_sc else 0):
            share.tick(i)
        save(6, 0).wait()
        save(7, 0).wait()
        share.finish()

    return pl.pallas_call(
        kernel,
        out_shape=[
            jax.ShapeDtypeStruct((width, 2 * inner), bf16),
            jax.ShapeDtypeStruct((rows, width), bf16),
            jax.ShapeDtypeStruct((8, width), f32),
            jax.ShapeDtypeStruct((places * height, lane), bf16),
        ]
        + share.results(),
        in_specs=[VMEM] * 13 + [HBM] * (1 + n_sc),
        out_specs=[HBM] + [VMEM] * (3 + n_sc),
        scratch_shapes=share.scratch()
        + [
            pltpu.VMEM((rows, inner), bf16),
            pltpu.VMEM(in_w.shape, bf16),
            pltpu.VMEM((rows, width), f32),
            pltpu.VMEM((2, dtile, inner), bf16),
            pltpu.SemaphoreType.DMA,
            pltpu.SemaphoreType.DMA((2,)),
            pltpu.VMEM((low_len, rows), bf16),
            pltpu.VMEM((rank, rows), bf16),
            pltpu.VMEM((rows, inner), bf16),
            pltpu.VMEM((rank, rows), f32),
            pltpu.VMEM((lines, inner), f32),
            pltpu.VMEM((seqs * (local + over), inner), f32),
            pltpu.VMEM((seqs * long, tile_cols), f32),
            pltpu.VMEM((seqs, over, inner), f32),
            pltpu.VMEM((seqs, over, inner), f32),
            pltpu.SemaphoreType.DMA((2,)),
        ]
        + line.scratch(),
        compiler_params=pltpu.CompilerParams(
            collective_id=ident, has_side_effects=True, vmem_limit_bytes=60 << 20
        ),
    )(through_b, through_decay, sums, decay_grad, scan_grad, step_pre, pre_act, act, padded, z_half, low_all, small, normed, in_w, *share.folded), height


def body(
    hidden_in, lengths, cotangent, norm_gain, in_weight, conv_weight, conv_bias, low_weight, step_weight,
    step_bias, decay_log, skip_gain, out_weight, ffn_gain, gate_up, down_weight,
):
    seqs, local, width = hidden_in.shape
    rows = seqs * local
    shards, pieces = lax.axis_size("shard"), lax.axis_size("ctx")
    inner = in_weight.shape[2]
    taps = conv_weight.shape[0]
    rank = step_weight.shape[0]
    states = decay_log.shape[0]
    low_len = low_weight.shape[0]

    def rows16(v):
        return jnp.pad(v, ((0, 16 - v.shape[0]), (0, 0)))

    small = jnp.concatenate(
        [low_weight, step_weight, decay_log, rows16(jnp.concatenate([conv_weight, conv_bias[None]], axis=0)),
         rows16(step_bias[None]), rows16(skip_gain[None])], axis=0,
    )
    at_bias = low_len + rank + states + 16
    at_skip = at_bias + 16
    hidden_rows = hidden_in.reshape(rows, width)
    small = jnp.pad(small, ((0, -small.shape[0] % 16), (0, 0)))
    gains = jnp.stack([norm_gain, ffn_gain])
    gains = jnp.pad(gains, ((0, 14), (0, 0)))
    in_half = in_weight.transpose(1, 0, 2)
    in_w, small, gains, normed_one, gate_z, padded, pre_act, act_half, low_all = front(
        hidden_rows, in_half, small, gains, seqs, low_len + rank + states, taps, low_len, 0
    )
    out_parts = lax.all_gather(out_weight, "shard")
    gate_half = gate_up.transpose(1, 0, 2)
    gate_w = [lax.all_gather(gate_half[c], "shard", axis=0, tiled=True) for c in range(2)]
    down_parts = lax.all_gather(down_weight, "shard")
    part = width // shards

    low_w = small[:low_len]
    step_w = small[low_len : low_len + rank]
    at = low_len + rank
    decay_w = small[at : at + states].astype(f32)
    kernel = small[at + states : at + states + taps].astype(f32)
    skip_full = small[at_skip].astype(f32)
    gain_one, gain_two = gains[0:1].astype(f32), gains[1:2].astype(f32)

    first_slot = lax.axis_index("ctx") * local
    positions = first_slot + jnp.arange(local, dtype=jnp.int32)
    pad_mask = (positions[None, :] < lengths[:, None]).astype(f32)

    source = hidden_rows.astype(f32)
    act_full = act_half.astype(f32)
    step_low = low_all[:rank].astype(bf16)
    decay_rate = -jnp.exp(decay_w)
    rate = (decay_rate * log2e).reshape(states, 8, 128)
    scan_out, gated_out, mixed_part, step_pre, kept, enter, size3, drive3 = scan_forward(
        low_all, act_half, gate_z, small, rate, out_parts, seqs, rank, low_len, at_bias, at_skip, 2
    )
    step_size = jax.nn.softplus(step_pre)
    gate_act = jax.nn.silu(gate_z)
    upstream = cotangent.reshape(rows, width).astype(f32) * pad_mask.reshape(rows, 1)
    ffn_grad = upstream.astype(bf16)
    ffn_part, middle, mix_grad, middle_grad, gain_sum, both_grad, down_grad = feed_forward(
        mixed_part, hidden_rows, gain_two, ffn_grad, gate_w, down_parts, 3
    )
    ffn_gain_grad = jnp.sum(gain_sum, axis=0) / gain_two[0]

    out_weight_grad = inner_rows(mix_grad, gated_out).astype(bf16)
    gated_grad = sum(outer_cols(mix_grad[:, k * part : (k + 1) * part], out_parts[k]) for k in range(shards))
    scan_grad = gated_grad * gate_act
    z_grad = gated_grad * scan_out * silu_grad(gate_z)
    through_b, through_decay, b_sums, c_sums, decay_sum, mixed_out, *ffn_shares = scan_backward(
        size3, drive3, scan_grad, low_all, rank, rate, kept, enter, seqs, 6, ffn_part, add_end, [middle], 32,
        [both_grad, down_grad],
    )
    mixed_out = mixed_out.reshape(hidden_in.shape)
    decay_log_grad = decay_sum.reshape(states, inner) * decay_rate
    sums = jnp.concatenate([v[:, 0].reshape(rows, states).T for v in (b_sums, c_sums)], axis=0)
    z_half = z_grad.astype(bf16)
    (in_weight_grad, first_part, gain_one_sum, small_blocks), small_height = scan_tail(
        through_b, through_decay, sums, decay_log_grad, scan_grad, step_pre, pre_act, act_half, padded, z_half, low_all, small, normed_one, in_w,
        [], 7,
        seqs, low_len, rank, states, taps,
    )
    norm_gain_grad = jnp.sum(gain_one_sum, axis=0) / gain_one[0]
    places, share = shards * pieces, width // (shards * pieces)
    lane = inner // places
    gain_rows = -(-2 * share // lane)
    gain_blocks = jnp.concatenate([norm_gain_grad.reshape(places, share), ffn_gain_grad.reshape(places, share)], axis=1)
    gain_blocks = jnp.pad(gain_blocks, ((0, 0), (0, gain_rows * lane - 2 * share))).reshape(places, gain_rows, lane)
    gain_height = 16 * -(-gain_rows // 16)
    gain_blocks = jnp.pad(gain_blocks, ((0, 0), (gain_height - gain_rows, 0), (0, 0)))
    gain_blocks = gain_blocks.reshape(places * gain_height, lane).astype(bf16)
    input_grad, in_share, out_share, small_out, gain_share = tp_sum(
        first_part, norm_back_end, [hidden_rows, gain_one, middle_grad], [], 32, 8,
        scatters=[in_weight_grad, out_weight_grad, small_blocks, gain_blocks], line_too=True,
        steps=[16, 16, small_height // 2, gain_height],
    )
    gain_share = gain_share[gain_height - gain_rows :].reshape(-1)
    input_grad = input_grad.astype(f32).reshape(hidden_in.shape)
    at = low_len + rank
    return (
        mixed_out,
        input_grad,
        gain_share[:share],
        in_share.reshape((-1,) + in_weight.shape[1:]),
        small_out[at + states : at + states + taps],
        small_out[at + states + taps],
        small_out[:low_len],
        small_out[low_len : low_len + rank],
        small_out[at + states + taps + 1],
        small_out[at : at + states],
        small_out[at + states + taps + 2],
        out_share.T,
        gain_share[share : 2 * share],
        ffn_shares[0].reshape((-1,) + gate_up.shape[1:]),
        ffn_shares[1].T,
    )


def solution(mesh):
    placed = (
        P("shard", "ctx", None),
        P("shard"),
        P("shard", "ctx", None),
        P("shard"),
        P("shard", None, "tp"),
        P(None, ("tp", "shard")),
        P(("tp", "shard")),
        P(None, ("tp", "shard")),
        P(None, ("tp", "shard")),
        P(("tp", "shard")),
        P(None, ("tp", "shard")),
        P(("tp", "shard")),
        P("tp", "shard"),
        P("shard"),
        P("shard", None, "tp"),
        P("tp", "shard"),
    )
    return jax.shard_map(
        body,
        mesh=mesh,
        in_specs=placed,
        out_specs=(
            P("shard", "ctx", None),
            P("shard", "ctx", None),
            P(("shard", "ctx")),
            P(("shard", "ctx"), None, "tp"),
            P(None, ("tp", "shard", "ctx")),
            P(("tp", "shard", "ctx")),
            P(None, ("tp", "shard", "ctx")),
            P(None, ("tp", "shard", "ctx")),
            P(("tp", "shard", "ctx")),
            P(None, ("tp", "shard", "ctx")),
            P(("tp", "shard", "ctx")),
            P("tp", ("shard", "ctx")),
            P(("shard", "ctx")),
            P(("shard", "ctx"), None, "tp"),
            P("tp", ("shard", "ctx")),
        ),
        check_vma=False,
    )
```
